32 devices in a mesh: dp: 4 (over y, core), fsdp: 8 (over z, x).
Axes of the slice: x: 2, y: 2, z: 4, core: 2. Of those that a mesh axis runs over, the one named last changes fastest.
Arguments:
- tokens: bfloat16 [32, 1024, 1024], P(('dp', 'fsdp')), may hold values from -6 to 6
- doc_ids: int32 [32, 1024], P(('dp', 'fsdp')), may hold values from 0 to 7, never falling along the last dimension, each value on 1 to 512 neighbouring positions
- norm_gain: bfloat16 [1024], P(('dp', 'fsdp')), may hold values from 0.25 to 1.75
- w_query_heads: bfloat16 [1024, 96], P(('dp', 'fsdp')), may hold values from -0.625 to 0.625
- w_query_dims: bfloat16 [1024, 384], P(('dp', 'fsdp')), may hold values from -0.1875 to 0.1875
- w_key_heads: bfloat16 [1024, 32], P(('dp', 'fsdp')), may hold values from -0.375 to 0.375
- w_key_dims: bfloat16 [1024, 128], P(('dp', 'fsdp')), may hold values from -0.1875 to 0.1875
- w_value_heads: bfloat16 [1024, 32], P(('dp', 'fsdp')), may hold values from -0.1875 to 0.1875
- w_value_dims: bfloat16 [1024, 128], P(('dp', 'fsdp')), may hold values from -0.1875 to 0.1875
- w_output: bfloat16 [1024, 1024], P(('dp', 'fsdp')), may hold values from -1.5 to 1.5
- mlp_gain: bfloat16 [1024], P(('dp', 'fsdp')), may hold values from 0.25 to 1.75
- w_gate: bfloat16 [1024, 2816], P(('dp', 'fsdp')), may hold values from -0.1875 to 0.1875
- w_up: bfloat16 [1024, 2816], P(('dp', 'fsdp')), may hold values from -0.1875 to 0.1875
- w_down: bfloat16 [2816, 1024], P(('dp', 'fsdp')), may hold values from -0.109375 to 0.109375
- out_grad: bfloat16 [32, 1024, 1024], P(('dp', 'fsdp')), may hold values from -6 to 6
Outputs:
- output: bfloat16 [32, 1024, 1024], P(('dp', 'fsdp'))
- grad_tokens: bfloat16 [32, 1024, 1024], P(('dp', 'fsdp'))
- grad_norm_gain: float32 [1024], P(('dp', 'fsdp'))
- grad_w_query_heads: float32 [1024, 96], P(('dp', 'fsdp'))
- grad_w_query_dims: float32 [1024, 384], P(('dp', 'fsdp'))
- grad_w_key_heads: float32 [1024, 32], P(('dp', 'fsdp'))
- grad_w_key_dims: float32 [1024, 128], P(('dp', 'fsdp'))
- grad_w_value_heads: float32 [1024, 32], P(('dp', 'fsdp'))
- grad_w_value_dims: float32 [1024, 128], P(('dp', 'fsdp'))
- grad_w_output: float32 [1024, 1024], P(('dp', 'fsdp'))
- grad_mlp_gain: float32 [1024], P(('dp', 'fsdp'))
- grad_w_gate: float32 [1024, 2816], P(('dp', 'fsdp'))
- grad_w_up: float32 [1024, 2816], P(('dp', 'fsdp'))
- grad_w_down: float32 [2816, 1024], P(('dp', 'fsdp'))
The draws below stay inside these ranges and needn't reach their ends.
Inputs may be any that keep to these rules, and one draw needn't show every extreme that they name: `doc_ids`: along each row the document numbers never fall; a document holds at most 512 tokens.
All inputs are finite; a program needn't handle non-finite values.
Results may differ from the reference program's by a relative error of at most 0.015.
The reference program's roundings to bfloat16 on the way count: a program that leaves them out, or rounds other values in their place, can miss the bound.
Values may be sent and summed in bfloat16 or wider, within the bound.
A program may use at most 320 MiB of HBM per device.

```python
import math
import jax
import jax.numpy as jnp
import numpy as np
from jax import lax

D = 1024
H = 16
DH = 64
RQ = 6
RK = 2
FF = 2816
SEQ = 1024
ROWS = 32


def levels(key, dims, cuts, least, top_value):
    def one(axis_at, blocks):
        steps = jax.random.uniform(jax.random.fold_in(jax.random.fold_in(key, 6), axis_at), (blocks,), jnp.float32, least / len(cuts), top_value / len(cuts))
        return jnp.repeat(jnp.exp(steps), dims[axis_at] // blocks).reshape((-1,) + (1,) * (len(dims) - axis_at - 1))

    factor_of = one(*cuts[0])
    for cut in cuts[1:]:
        factor_of = factor_of * one(*cut)
    return factor_of


def length_profile(amount, total, bound, skew):
    weights = [(1 << 20) // math.isqrt(grade ** skew) + 1 for grade in range(2, amount + 1)]
    spare, holding = total - bound - (amount - 1), [1] * (amount - 1)
    while spare > 0:
        free = [i for i in range(amount - 1) if holding[i] < bound]
        whole, budget = sum([weights[i] for i in free]), spare
        for i in free:
            extra = min(bound - holding[i], max(1, budget * weights[i] // whole), spare)
            holding[i] = holding[i] + extra
            spare = spare - extra
    return np.array([bound] + holding)


def ragged(own_key, amount, total, most, skew):
    if amount == 2:
        one = jax.random.randint(own_key, (), max(1, total - most), min(most, total - 1) + 1)
        return jnp.stack([one, total - one])
    sizes = jnp.asarray(length_profile(amount, total, most, skew), jnp.int32)
    twos = (amount - 1) // 2
    donor, sink = sizes[1:1 + 2 * twos:2], sizes[2:2 + 2 * twos:2]
    room = jnp.minimum(donor - 1, most - sink)
    moved = jax.random.randint(jax.random.fold_in(own_key, 1), (twos,), 0, 1 << 20) % (room + 1)
    sizes = sizes.at[1:1 + 2 * twos:2].set(donor - moved).at[2:2 + 2 * twos:2].set(sink + moved)
    return sizes[jax.random.permutation(jax.random.fold_in(own_key, 2), amount)]


def scatter_about(stream_key, dims, spread, most, cuts=(), kind=jnp.bfloat16):
    values = jax.random.normal(stream_key, dims, jnp.float32) * spread
    if len(cuts) > 0:
        values = levels(stream_key, dims, cuts, -0.22, 0.18) * values
    return jnp.clip(values, min=-most, max=most).astype(kind)


def setup_inputs(seed: int = 0) -> dict:
    seeds = jax.random.split(jax.random.key(seed), 16)
    tokens = scatter_about(seeds[0], (ROWS, SEQ, D), 1.0, 6.0, ((0, 32),))
    doc_ids = jax.vmap(lambda own: jnp.searchsorted(jnp.cumsum(ragged(own, max(4, SEQ // 128), SEQ, SEQ // 2, 2)), jnp.arange(SEQ), side="right"))(jax.random.split(seeds[1], ROWS)).reshape((ROWS, SEQ)).astype(jnp.int32)
    norm_gain = jnp.clip(1.0 + 0.15 * jax.random.normal(seeds[2], (D,), jnp.float32), 0.25, 1.75).astype(jnp.bfloat16)
    w_query_heads = scatter_about(seeds[3], (D, RQ * H), (D // 12) ** -0.5, 0.625, ((0, 32),))
    w_query_dims = scatter_about(seeds[4], (D, RQ * DH), D ** -0.5, 0.1875, ((0, 32),))
    w_key_heads = scatter_about(seeds[5], (D, RK * H), (D // 4) ** -0.5, 0.375, ((0, 32),))
    w_key_dims = scatter_about(seeds[6], (D, RK * DH), D ** -0.5, 0.1875, ((0, 32),))
    w_value_heads = scatter_about(seeds[7], (D, RK * H), D ** -0.5, 0.1875, ((0, 32),))
    w_value_dims = scatter_about(seeds[8], (D, RK * DH), D ** -0.5, 0.1875, ((0, 32),))
    w_output = scatter_about(seeds[9], (H * DH, D), (max(4, H * DH // 64)) ** -0.5, 1.5, ((0, 32),))
    mlp_gain = jnp.clip(1.0 + 0.15 * jax.random.normal(seeds[10], (D,), jnp.float32), 0.25, 1.75).astype(jnp.bfloat16)
    w_gate = scatter_about(seeds[11], (D, FF), D ** -0.5, 0.1875, ((0, 32),))
    w_up = scatter_about(seeds[12], (D, FF), D ** -0.5, 0.1875, ((0, 32),))
    w_down = scatter_about(seeds[13], (FF, D), FF ** -0.5, 0.109375, ((0, 32),))
    out_grad = scatter_about(seeds[14], (ROWS, SEQ, D), 1.0, 6.0, ((0, 32),))
    return dict(tokens=tokens, doc_ids=doc_ids, norm_gain=norm_gain, w_query_heads=w_query_heads, w_query_dims=w_query_dims, w_key_heads=w_key_heads, w_key_dims=w_key_dims, w_value_heads=w_value_heads, w_value_dims=w_value_dims, w_output=w_output, mlp_gain=mlp_gain, w_gate=w_gate, w_up=w_up, w_down=w_down, out_grad=out_grad)


@jax.custom_vjp
def low(v):
    return lax.optimization_barrier(v.astype(jnp.bfloat16)).astype(jnp.float32)

@jax.custom_vjp
def low_back(v):
    return v

def low_keep(v):
    return (low(v), None)

def low_pass(kept, grad):
    return (grad,)

def back_keep(v):
    return (v, None)

def back_low(kept, grad):
    return (low(grad),)
low.defvjp(low_keep, low_pass)
low_back.defvjp(back_keep, back_low)
epsilon = 1e-06
theta_base = 10000.0
highest = lax.Precision.HIGHEST

def rotary_tables(seq_len, half_dim):
    position = jnp.arange(seq_len, dtype=jnp.float32)
    inverse = jnp.exp(-math.log(theta_base) * 2.0 * jnp.arange(half_dim, dtype=jnp.float32) / (2.0 * half_dim))
    angle = position[:, None] * inverse[None, :]
    return (jnp.cos(angle), jnp.sin(angle))

def rotate(factor, cosine_table, sine_table):
    half_dim = factor.shape[-1] // 2
    first_half = factor[..., :half_dim]
    second_half = factor[..., half_dim:]
    cosine_part = cosine_table[:, None, :]
    sine_part = sine_table[:, None, :]
    return jnp.concatenate([first_half * cosine_part - second_half * sine_part, first_half * sine_part + second_half * cosine_part], axis=-1)

def rms_scale(values):
    return lax.rsqrt(lax.optimization_barrier(jnp.mean(values * values, axis=-1, keepdims=True)) + epsilon)

def matmul(left, right):
    return jnp.dot(left, right, precision=highest, preferred_element_type=jnp.float32)

def attention(query_full, key_full, value_full, doc_piece):
    group_rows = query_full.shape[0]
    seq_len = query_full.shape[1]
    block_len = min(512, seq_len)
    block_count = seq_len // block_len
    score_scale = 1.0 / math.sqrt(DH)
    positions = jnp.arange(seq_len, dtype=jnp.int32)

    def one_block(block_start):
        query_block = lax.dynamic_slice_in_dim(query_full, block_start, block_len, 1)
        query_doc = lax.dynamic_slice_in_dim(doc_piece, block_start, block_len, 1)
        scores = low_back(jnp.einsum('bqhd,bkhd->bhqk', query_block, key_full, precision=highest) * score_scale)
        query_pos = block_start + jnp.arange(block_len, dtype=jnp.int32)
        allowed = (positions[None, None, :] <= query_pos[None, :, None]) & (query_doc[:, :, None] == doc_piece[:, None, :])
        masked = jnp.where(allowed[:, None, :, :], scores, -1e+30)
        row_max = lax.optimization_barrier(jnp.max(masked, axis=-1, keepdims=True))
        exp_terms = jnp.exp(masked - row_max)
        attn_probs = low(exp_terms / lax.optimization_barrier(jnp.sum(exp_terms, axis=-1, keepdims=True)))
        return jnp.einsum('bhqk,bkhd->bqhd', attn_probs, value_full, precision=highest)
    starts = (jnp.arange(block_count) * block_len).astype(jnp.int32)
    mixed_blocks = lax.map(jax.checkpoint(one_block), starts)
    return jnp.moveaxis(mixed_blocks, 0, 1).reshape(group_rows, seq_len, H * DH)

def layer_forward(inputs, doc_piece, norm_gain, w_query_heads, w_query_dims, w_key_heads, w_key_dims, w_value_heads, w_value_dims, w_output, mlp_gain, w_gate, w_up, w_down):
    group_rows, seq_len, width_dim = inputs.shape
    token_count = group_rows * seq_len
    inputs_flat = inputs.reshape(token_count, width_dim)
    cosine_table, sine_table = rotary_tables(seq_len, DH // 2)
    normed = low(inputs_flat * rms_scale(inputs_flat) * norm_gain)
    heads_query = low_back(matmul(normed, w_query_heads)).reshape(group_rows, seq_len, RQ, H)
    dims_query = rotate(low_back(matmul(normed, w_query_dims)).reshape(group_rows, seq_len, RQ, DH), cosine_table, sine_table)
    heads_key = low_back(matmul(normed, w_key_heads)).reshape(group_rows, seq_len, RK, H)
    dims_key = rotate(low_back(matmul(normed, w_key_dims)).reshape(group_rows, seq_len, RK, DH), cosine_table, sine_table)
    heads_value = low_back(matmul(normed, w_value_heads)).reshape(group_rows, seq_len, RK, H)
    dims_value = low_back(matmul(normed, w_value_dims)).reshape(group_rows, seq_len, RK, DH)
    query_full = low(jnp.einsum('bsrh,bsrd->bshd', heads_query, dims_query, precision=highest) / RQ)
    key_full = low(jnp.einsum('bsrh,bsrd->bshd', heads_key, dims_key, precision=highest) / RK)
    value_full = low(jnp.einsum('bsrh,bsrd->bshd', heads_value, dims_value, precision=highest) / RK)
    mixed_heads = low_back(low(attention(query_full, key_full, value_full, doc_piece))).reshape(token_count, H * DH)
    middle = inputs_flat + low_back(matmul(mixed_heads, w_output))
    normed_two = low(middle * rms_scale(middle) * mlp_gain)
    gate_proj = low_back(matmul(normed_two, w_gate))
    up_proj = low_back(matmul(normed_two, w_up))
    inner_act = low(jax.nn.silu(gate_proj) * up_proj)
    result = middle + low_back(matmul(inner_act, w_down))
    return result.reshape(group_rows, seq_len, width_dim)

def reference(tokens, doc_ids, norm_gain, w_query_heads, w_query_dims, w_key_heads, w_key_dims, w_value_heads, w_value_dims, w_output, mlp_gain, w_gate, w_up, w_down, out_grad):
    weights = tuple((weight.astype(jnp.float32) for weight in (norm_gain, w_query_heads, w_query_dims, w_key_heads, w_key_dims, w_value_heads, w_value_dims, w_output, mlp_gain, w_gate, w_up, w_down)))
    group_rows = math.gcd(ROWS, max(1, 4096 // SEQ))
    group_count = ROWS // group_rows
    token_groups = tokens.astype(jnp.float32).reshape(group_count, group_rows, SEQ, D)
    doc_groups = doc_ids.astype(jnp.int32).reshape(group_count, group_rows, SEQ)
    grad_groups = out_grad.astype(jnp.float32).reshape(group_count, group_rows, SEQ, D)

    def scan_step(totals_carry, pieces):
        token_piece, doc_piece, grad_piece = pieces

        def forward_fn(inputs, *params):
            return layer_forward(inputs, doc_piece, *params)
        result, pullback = jax.vjp(forward_fn, token_piece, *weights)
        gradients = pullback(grad_piece)
        new_totals = tuple((total + gradient for total, gradient in zip(totals_carry, gradients[1:])))
        return (new_totals, (result.astype(jnp.bfloat16), gradients[0].astype(jnp.bfloat16)))
    initial = tuple((jnp.zeros(weight.shape, jnp.float32) for weight in weights))
    totals, outputs = lax.scan(scan_step, initial, (token_groups, doc_groups, grad_groups))
    layer_out = outputs[0].reshape(ROWS, SEQ, D)
    input_grads = outputs[1].reshape(ROWS, SEQ, D)
    return (layer_out, input_grads, totals[0], totals[1], totals[2], totals[3], totals[4], totals[5], totals[6], totals[7], totals[8], totals[9], totals[10], totals[11])
```

```python
import functools
import math

import jax
import jax.numpy as jnp
from jax import lax
from jax.experimental import pallas as pl
from jax.experimental.pallas import tpu as pltpu
from jax.sharding import PartitionSpec as P

MESH = pl.DeviceIdType.MESH

D = 1024
H = 16
DH = 64
RQ = 6
RK = 2
PACKED = 896


epsilon = 1e-06
theta_base = 10000.0
highest = lax.Precision.HIGHEST


def rotary_tables(seq_len, half_dim):
    position = jnp.arange(seq_len, dtype=jnp.float32)
    inverse = jnp.exp(
        -math.log(theta_base) * 2.0 * jnp.arange(half_dim, dtype=jnp.float32) / (2.0 * half_dim)
    )
    angle = position[:, None] * inverse[None, :]
    return (jnp.cos(angle), jnp.sin(angle))


def rotate(factor, cosine_table, sine_table):
    half_dim = factor.shape[-1] // 2
    first_half = factor[..., :half_dim]
    second_half = factor[..., half_dim:]
    cosine_part = cosine_table[:, None, :]
    sine_part = sine_table[:, None, :]
    return jnp.concatenate(
        [
            first_half * cosine_part - second_half * sine_part,
            first_half * sine_part + second_half * cosine_part,
        ],
        axis=-1,
    )


def rotate_back(grad_factor, cosine_table, sine_table):
    half_dim = grad_factor.shape[-1] // 2
    first_half = grad_factor[..., :half_dim]
    second_half = grad_factor[..., half_dim:]
    cosine_part = cosine_table[:, None, :]
    sine_part = sine_table[:, None, :]
    return jnp.concatenate(
        [
            first_half * cosine_part + second_half * sine_part,
            second_half * cosine_part - first_half * sine_part,
        ],
        axis=-1,
    )


def rms_scale(values):
    return lax.rsqrt(jnp.mean(values * values, axis=-1, keepdims=True) + epsilon)


def forward_dot(left, right):
    return jnp.dot(left, right, preferred_element_type=jnp.float32)


def outer_sum(left, right):
    return lax.dot_general(
        left, right, (((0,), (0,)), ((), ())), preferred_element_type=jnp.float32
    )


def back_dot(grad_rows, weight):
    return lax.dot_general(
        grad_rows, weight, (((1,), (1,)), ((), ())), preferred_element_type=jnp.float32
    )


def combine_factors(heads_act, dims_act, rank_count):
    return jnp.einsum("bsrh,bsrd->bshd", heads_act, dims_act, precision=highest) / rank_count


def split_factors(grad_full, heads_act, dims_act, rank_count):
    grad_heads = jnp.einsum("bshd,bsrd->bsrh", grad_full, dims_act, precision=highest) / rank_count
    grad_dims = jnp.einsum("bshd,bsrh->bsrd", grad_full, heads_act, precision=highest) / rank_count
    return (grad_heads, grad_dims)
ANY = pl.BlockSpec(memory_space=pl.ANY)


def grid_of(mesh):
    nd, nf = mesh.shape["dp"], mesh.shape["fsdp"]
    nc = math.gcd(2, nd)
    nz = math.gcd(4, nf)
    return (nd // nc, nc, nz, nf // nz)


class Place:
    def __init__(self, dims):
        self.dims = dims
        ny, nc, nz, nx = dims
        dp, fs = lax.axis_index("dp"), lax.axis_index("fsdp")
        self.y, self.c = lax.div(dp, nc), lax.rem(dp, nc)
        self.z, self.x = lax.div(fs, nx), lax.rem(fs, nx)

    def at(self, axis, k):
        n = self.dims["yczx".index(axis)]
        return lax.rem(getattr(self, axis) + k + n, n)

    def device(self, axis=None, k=0):
        ny, nc, nz, nx = self.dims
        put = {a: getattr(self, a) for a in "yczx"}
        if axis is not None:
            put[axis] = self.at(axis, k)
        return (put["y"] * nc + put["c"], put["z"] * nx + put["x"])


def peers_of(dims):
    ny, nc, nz, nx = dims
    return [(a, k) for a, n in (("y", ny), ("c", nc), ("z", nz), ("x", nx)) for k in range(1, n)]


def enter(place):
    barrier = pltpu.get_barrier_semaphore()
    peers = peers_of(place.dims)
    for axis, k in peers:
        pl.semaphore_signal(barrier, inc=1, device_id=place.device(axis, k), device_id_type=MESH)
    pl.semaphore_wait(barrier, len(peers))


class Gather:
    def __init__(self, place, src, dst, sems, i):
        self.p, self.src, self.dst, self.i = place, src, dst, i
        self.local, self.zs, self.zr, self.as_, self.ar, self.bs, self.br, self.cs, self.cr = sems

    @staticmethod
    def sem_shapes(dims, n):
        ny, nc, nz, nx = dims
        dma = pltpu.SemaphoreType.DMA
        m = max(nx, ny) - 1
        one = lambda k: dma((n, max(1, k)))
        return [dma((n,)), one(nz - 1), one(nz - 1), one(m), one(m), one(m), one(m), one(nx + ny - 1), one(nx + ny - 1)]

    def copy(self, ref_src, ref_dst, send, recv, axis, k):
        return pltpu.make_async_remote_copy(
            src_ref=ref_src, dst_ref=ref_dst, send_sem=send, recv_sem=recv,
            device_id=self.p.device(axis, k), device_id_type=MESH,
        )

    def z_copies(self):
        p, i = self.p, self.i
        nz = p.dims[2]
        mine = self.dst.at[p.y, p.c, p.z, p.x]
        def one(k, back):
            if back:
                ref = self.dst.at[p.y, p.c, p.at("z", -k), p.x]
                return self.copy(ref, ref, self.zs.at[i, k - 1], self.zr.at[i, k - 1], "z", k)
            return self.copy(self.src, mine, self.zs.at[i, k - 1], self.zr.at[i, k - 1], "z", k)

        return [[functools.partial(one, k, back) for k in range(1, nz)] for back in (False, True)]

    def part(self, first, step, y, x, c):
        every = slice(None)
        if step == 0:
            return self.dst.at[y, c, :, x]
        return self.dst.at[y, c] if first == "x" else self.dst.at[:, c, :, x]

    def side_copies(self, first, step):
        p, i = self.p, self.i
        axis = first if step == 0 else {"x": "y", "y": "x"}[first]
        n = p.dims["yczx".index(axis)]
        s, r = ((self.as_, self.ar), (self.bs, self.br))[step]

        def one(k, back):
            y, x = p.y, p.x
            if back:
                y, x = (p.y, p.at("x", -k)) if axis == "x" else (p.at("y", -k), p.x)
            ref = self.part(first, step, y, x, p.c)
            return self.copy(ref, ref, s.at[i, k - 1], r.at[i, k - 1], axis, k)

        return [[functools.partial(one, k, back) for k in range(1, n)] for back in (False, True)]

    def core_copies(self, first, c):
        p, i = self.p, self.i
        second = {"x": "y", "y": "x"}[first]
        lists, j = [], 0
        for step, axis in ((0, None), (0, first), (1, second)):
            now = []
            count = 1 if axis is None else p.dims["yczx".index(axis)] - 1
            for k in range(1, count + 1):
                def one(axis=axis, step=step, k=k, j=j):
                    y = p.at("y", -k) if axis == "y" else p.y
                    x = p.at("x", -k) if axis == "x" else p.x
                    ref = self.part(first, step, y, x, c)
                    return self.copy(ref, ref, self.cs.at[i, j], self.cr.at[i, j], "c", 1)

                now.append(one)
                j += 1
            lists.append(now)
        return lists

    def start(self):
        p = self.p
        mine = self.dst.at[p.y, p.c, p.z, p.x]
        pltpu.make_async_copy(self.src, mine, self.local.at[self.i]).start()
        for copy in self.z_copies()[0]:
            copy().start()

    def by_core(self, body):
        if self.p.dims[1] == 1:
            body("x")
            return
        pl.when(self.p.c == 0)(lambda: body("x"))
        pl.when(self.p.c == 1)(lambda: body("y"))

    def after_z(self):
        p = self.p
        mine = self.dst.at[p.y, p.c, p.z, p.x]
        pltpu.make_async_copy(self.src, mine, self.local.at[self.i]).wait()
        for copy in self.z_copies()[1]:
            copy().wait_recv()

        def body(first):
            for copy in self.side_copies(first, 0)[0]:
                copy().start()
            if p.dims[1] > 1:
                for copy in self.core_copies(first, p.c)[0]:
                    copy().start()

        self.by_core(body)

    def after_first(self):
        p = self.p

        def body(first):
            for copy in self.side_copies(first, 0)[1]:
                copy().wait_recv()
            for copy in self.side_copies(first, 1)[0]:
                copy().start()
            if p.dims[1] > 1:
                for copy in self.core_copies(first, p.c)[1]:
                    copy().start()

        self.by_core(body)

    def after_second(self):
        p = self.p

        def body(first):
            for copy in self.side_copies(first, 1)[1]:
                copy().wait_recv()
            if p.dims[1] > 1:
                for copy in self.core_copies(first, p.c)[2]:
                    copy().start()

        self.by_core(body)

    def finish(self):
        p = self.p
        for copy in self.z_copies()[0]:
            copy().wait_send()

        def body(first):
            for step in (0, 1):
                for copy in self.side_copies(first, step)[0]:
                    copy().wait_send()
            if p.dims[1] > 1:
                for now in self.core_copies(first, p.c):
                    for copy in now:
                        copy().wait_send()
                other = {"x": "y", "y": "x"}[first]
                for now in self.core_copies(other, p.at("c", 1)):
                    for copy in now:
                        copy().wait_recv()

        self.by_core(body)

    def stages(self):
        return [self.start, self.after_z, self.after_first, self.after_second, self.finish]


def gather_kernel(dims, n, *refs):
    place = Place(dims)
    src, dst, sems = refs[:n], refs[n:2 * n], refs[2 * n:]
    enter(place)
    jobs = [Gather(place, src[i], dst[i], sems, i).stages() for i in range(n)]
    run_stages(jobs)


def gather(dims, arrays, collective_id):
    n = len(arrays)
    outs = pl.pallas_call(
        functools.partial(gather_kernel, dims, n),
        out_shape=[jax.ShapeDtypeStruct(dims + a.shape, a.dtype) for a in arrays],
        in_specs=[ANY] * n,
        out_specs=[ANY] * n,
        scratch_shapes=Gather.sem_shapes(dims, n),
        compiler_params=pltpu.CompilerParams(collective_id=collective_id, has_side_effects=True),
        name="gather_weights",
    )(*arrays)
    return [o.reshape((-1,) + a.shape[1:]) for o, a in zip(outs, arrays)]


class Scatter:
    def __init__(self, place, src, out, bufs, sems, i):
        self.p, self.src, self.out, self.i = place, src, out, i
        self.own, self.from_core, self.from_a, self.from_b, self.from_z = bufs
        self.local, self.cs, self.cr, self.as_, self.ar, self.bs, self.br, self.zs, self.zr = sems

    @staticmethod
    def sem_shapes(dims, n):
        ny, nc, nz, nx = dims
        dma = pltpu.SemaphoreType.DMA
        m = max(nx, ny, 2) - 1
        return [dma((n, nx))] * 3 + [dma((n, m))] * 4 + [dma((n, max(1, nz - 1)))] * 2

    @staticmethod
    def buf_shapes(dims, block):
        ny, nc, nz, nx = dims
        m = max(nx, ny, 2)
        buf = lambda *s: pltpu.VMEM(s + block, jnp.bfloat16)
        return [buf(ny, nx, nz), buf(ny, nx, nz), buf(m - 1, m, nz), buf(m - 1, nz), buf(max(1, nz - 1))]

    def copy(self, src, dst, send, recv, axis, k):
        return pltpu.make_async_remote_copy(
            src_ref=src, dst_ref=dst, send_sem=send, recv_sem=recv,
            device_id=self.p.device(axis, k), device_id_type=MESH,
        )

    def loads(self):
        p, i = self.p, self.i
        for x in range(p.dims[3]):
            yield lambda x=x: pltpu.make_async_copy(self.src.at[:, p.c, :, x], self.own.at[:, x], self.local.at[i, x])

    def core_copies(self):
        p, i = self.p, self.i
        if p.dims[1] == 1:
            return
        for x in range(p.dims[3]):
            yield lambda x=x: self.copy(
                self.src.at[:, p.at("c", 1), :, x], self.from_core.at[:, x], self.cs.at[i, x], self.cr.at[i, x], "c", 1)

    def a_copies(self, first):
        p, i = self.p, self.i
        ny, nc, nz, nx = p.dims
        for k in range(1, ny if first == "y" else nx):
            def copy(k=k):
                if first == "y":
                    src, dst = self.own.at[p.at("y", k)], self.from_a.at[k - 1, pl.ds(0, nx)]
                else:
                    src, dst = self.own.at[:, p.at("x", k)], self.from_a.at[k - 1, pl.ds(0, ny)]
                return self.copy(src, dst, self.as_.at[i, k - 1], self.ar.at[i, k - 1], first, k)
            yield copy

    def b_copies(self, first):
        p, i = self.p, self.i
        ny, nc, nz, nx = p.dims
        second = {"x": "y", "y": "x"}[first]
        for k in range(1, ny if second == "y" else nx):
            def copy(k=k):
                src = self.own.at[p.at("y", k), p.x] if second == "y" else self.own.at[p.y, p.at("x", k)]
                return self.copy(src, self.from_b.at[k - 1], self.bs.at[i, k - 1], self.br.at[i, k - 1], second, k)
            yield copy

    def z_copies(self):
        p, i = self.p, self.i
        for k in range(1, p.dims[2]):
            yield lambda k=k: self.copy(
                self.own.at[p.y, p.x, p.at("z", k)], self.from_z.at[k - 1], self.zs.at[i, k - 1], self.zr.at[i, k - 1], "z", k)

    def by_core(self, body):
        if self.p.dims[1] == 1:
            body("y")
            return
        pl.when(self.p.c == 0)(lambda: body("y"))
        pl.when(self.p.c == 1)(lambda: body("x"))

    @staticmethod
    def add(total, terms):
        value = total[...].astype(jnp.float32)
        for term in terms:
            value = value + term[...].astype(jnp.float32)
        return value

    def start(self):
        for copy in self.core_copies():
            copy().start()
        for copy in self.loads():
            copy().start()

    def after_core(self):
        p = self.p
        ny, nc, nz, nx = p.dims
        for copy in self.loads():
            copy().wait()
        for copy in self.core_copies():
            copy().wait_recv()
        if nc > 1:
            def body(t, carry):
                at = (lax.div(t, nx * nz), lax.rem(lax.div(t, nz), nx), lax.rem(t, nz))
                self.own[at] = self.add(self.own.at[at], [self.from_core.at[at]]).astype(jnp.bfloat16)
                return carry
            lax.fori_loop(0, ny * nx * nz, body, 0)

        def go(first):
            for copy in self.a_copies(first):
                copy().start()
        self.by_core(go)

    def after_a(self):
        p = self.p
        ny, nc, nz, nx = p.dims

        def go(first):
            for copy in self.a_copies(first):
                copy().wait_recv()
            n = ny if first == "y" else nx

            def body(t, carry):
                j, z = lax.div(t, nz), lax.rem(t, nz)
                at = (p.y, j, z) if first == "y" else (j, p.x, z)
                terms = [self.from_a.at[k, j, z] for k in range(n - 1)]
                self.own[at] = self.add(self.own.at[at], terms).astype(jnp.bfloat16)
                return carry
            if n > 1:
                lax.fori_loop(0, (nx if first == "y" else ny) * nz, body, 0)
            for copy in self.b_copies(first):
                copy().start()
        self.by_core(go)

    def after_b(self):
        p = self.p
        ny, nc, nz, nx = p.dims

        def go(first):
            for copy in self.b_copies(first):
                copy().wait_recv()
            n = nx if first == "y" else ny

            def body(z, carry):
                at = (p.y, p.x, z)
                terms = [self.from_b.at[k, z] for k in range(n - 1)]
                self.own[at] = self.add(self.own.at[at], terms).astype(jnp.bfloat16)
                return carry
            if n > 1:
                lax.fori_loop(0, nz, body, 0)
        self.by_core(go)
        for copy in self.z_copies():
            copy().start()

    def after_z(self):
        p = self.p
        for copy in self.z_copies():
            copy().wait_recv()
        terms = [self.from_z.at[k] for k in range(p.dims[2] - 1)]
        self.out[...] = self.add(self.own.at[p.y, p.x, p.z], terms)

    def finish(self):
        for copy in self.core_copies():
            copy().wait_send()

        def go(first):
            for copy in self.a_copies(first):
                copy().wait_send()
            for copy in self.b_copies(first):
                copy().wait_send()
        self.by_core(go)
        for copy in self.z_copies():
            copy().wait_send()

    def stages(self):
        return [self.start, self.after_core, self.after_a, self.after_b, self.after_z, self.finish]


def run_stages(jobs):
    n, depth = len(jobs), len(jobs[0])
    for t in range(n + depth - 1):
        for i in range(n):
            if 0 <= t - i < depth:
                jobs[i][t - i]()


def scatter_kernel(dims, n, *refs):
    place = Place(dims)
    src, out, rest = refs[:n], refs[n:2 * n], refs[2 * n:]
    bufs, sems = rest[:5 * n], rest[5 * n:]
    enter(place)
    run_stages([Scatter(place, src[i], out[i], bufs[5 * i:5 * i + 5], sems, i).stages() for i in range(n)])


def scatter(dims, arrays, collective_id):
    n = len(arrays)
    devices = math.prod(dims)
    blocks = [(a.shape[0] // devices,) + a.shape[1:] for a in arrays]
    shaped = [a.reshape(dims + b) for a, b in zip(arrays, blocks)]
    scratch = []
    for b in blocks:
        scratch += Scatter.buf_shapes(dims, b)
    return pl.pallas_call(
        functools.partial(scatter_kernel, dims, n),
        out_shape=[jax.ShapeDtypeStruct(b, jnp.float32) for b in blocks],
        in_specs=[ANY] * n,
        out_specs=[pl.BlockSpec(memory_space=pltpu.VMEM)] * n,
        scratch_shapes=scratch + Scatter.sem_shapes(dims, n),
        compiler_params=pltpu.CompilerParams(
            collective_id=collective_id, has_side_effects=True, vmem_limit_bytes=56 << 20),
        name="scatter_gradients",
    )(*shaped)


def on_device(
    dims,
    tokens,
    doc_ids,
    norm_gain,
    w_query_heads,
    w_query_dims,
    w_key_heads,
    w_key_dims,
    w_value_heads,
    w_value_dims,
    w_output,
    mlp_gain,
    w_gate,
    w_up,
    w_down,
    out_grad,
):
    row_count = tokens.shape[0]
    seq_len = tokens.shape[1]
    token_count = row_count * seq_len
    score_scale = 1.0 / math.sqrt(DH)
    cosine_table, sine_table = rotary_tables(seq_len, DH // 2)
    block_len = min(512, seq_len)
    block_count = seq_len // block_len
    positions = jnp.arange(seq_len, dtype=jnp.int32)
    starts = jnp.arange(block_count) * block_len
    parts = (w_query_heads, w_query_dims, w_key_heads, w_key_dims, w_value_heads, w_value_dims)
    edges = [0]
    for part in parts:
        edges.append(edges[-1] + part.shape[1])
    packed = jnp.concatenate(
        parts
        + (norm_gain[:, None], mlp_gain[:, None])
        + (jnp.zeros((norm_gain.shape[0], PACKED - edges[-1] - 2), jnp.bfloat16),),
        axis=1,
    )
    packed_w, output_w, gate_w, up_w, down_w = gather(
        dims, [packed, w_output, w_gate, w_up, w_down], 0
    )
    query_heads_w, query_dims_w, key_heads_w, key_dims_w, value_heads_w, value_dims_w = [
        packed_w[:, lo:hi] for lo, hi in zip(edges, edges[1:])
    ]
    gain_one, gain_two = packed_w[:, edges[-1]], packed_w[:, edges[-1] + 1]
    inputs_flat = tokens.astype(jnp.float32).reshape(token_count, D)
    scale_one = rms_scale(inputs_flat)
    normed = (inputs_flat * scale_one * gain_one.astype(jnp.float32)).astype(jnp.bfloat16)
    heads_query = forward_dot(normed, query_heads_w).reshape(row_count, seq_len, RQ, H)
    dims_query = rotate(
        forward_dot(normed, query_dims_w).reshape(row_count, seq_len, RQ, DH),
        cosine_table,
        sine_table,
    )
    heads_key = forward_dot(normed, key_heads_w).reshape(row_count, seq_len, RK, H)
    dims_key = rotate(
        forward_dot(normed, key_dims_w).reshape(row_count, seq_len, RK, DH),
        cosine_table,
        sine_table,
    )
    heads_value = forward_dot(normed, value_heads_w).reshape(row_count, seq_len, RK, H)
    dims_value = forward_dot(normed, value_dims_w).reshape(row_count, seq_len, RK, DH)
    query_full = combine_factors(heads_query, dims_query, RQ).astype(jnp.bfloat16)
    key_full = combine_factors(heads_key, dims_key, RK).astype(jnp.bfloat16)
    value_full = combine_factors(heads_value, dims_value, RK).astype(jnp.bfloat16)

    def block_scores(block_start):
        query_block = lax.dynamic_slice_in_dim(query_full, block_start, block_len, 1)
        query_doc = lax.dynamic_slice_in_dim(doc_ids, block_start, block_len, 1)
        scores = (
            jnp.einsum("bqhd,bkhd->bhqk", query_block, key_full, preferred_element_type=jnp.float32)
            * score_scale
        )
        query_pos = block_start + jnp.arange(block_len, dtype=jnp.int32)
        allowed = (positions[None, None, :] <= query_pos[None, :, None]) & (
            query_doc[:, :, None] == doc_ids[:, None, :]
        )
        return (jnp.where(allowed[:, None, :, :], scores, -1e30), query_block)

    def forward_block(block_start):
        masked, query_block = block_scores(block_start)
        row_max = jnp.max(masked, axis=-1, keepdims=True)
        exp_terms = jnp.exp(masked - row_max)
        row_total = jnp.sum(exp_terms, axis=-1, keepdims=True)
        attn_probs = (exp_terms / row_total).astype(jnp.bfloat16)
        mixed_block = jnp.einsum(
            "bhqk,bkhd->bqhd", attn_probs, value_full, preferred_element_type=jnp.float32
        )
        return (mixed_block.astype(jnp.bfloat16), (row_max + jnp.log(row_total))[..., 0])

    mixed_blocks, lse_blocks = lax.map(forward_block, starts)
    mixed_heads = jnp.moveaxis(mixed_blocks, 0, 1).reshape(token_count, H * DH)
    middle = inputs_flat + forward_dot(mixed_heads, output_w)
    scale_two = rms_scale(middle)
    gain_two_f = gain_two.astype(jnp.float32)
    normed_two = (middle * scale_two * gain_two_f).astype(jnp.bfloat16)
    gate_proj = forward_dot(normed_two, gate_w)
    up_proj = forward_dot(normed_two, up_w)
    sigmoid_gate = jax.nn.sigmoid(gate_proj)
    silu_gate = gate_proj * sigmoid_gate
    inner_act = (silu_gate * up_proj).astype(jnp.bfloat16)
    result = middle + forward_dot(inner_act, down_w)
    output = result.astype(jnp.bfloat16).reshape(tokens.shape)
    cotangent = out_grad.reshape(token_count, D)
    grad_inner = back_dot(cotangent, down_w)
    grad_gate = (
        grad_inner * up_proj * sigmoid_gate * (1.0 + gate_proj * (1.0 - sigmoid_gate))
    ).astype(jnp.bfloat16)
    grad_up = (grad_inner * silu_gate).astype(jnp.bfloat16)
    grad_normed_two = back_dot(grad_gate, gate_w) + back_dot(grad_up, up_w)
    gained_two = grad_normed_two * gain_two.astype(jnp.float32)
    grad_mlp_gain = jnp.sum(grad_normed_two * middle * scale_two, axis=0)
    grad_middle = (
        cotangent.astype(jnp.float32)
        + scale_two * gained_two
        - middle * scale_two**3 * jnp.mean(gained_two * middle, axis=-1, keepdims=True)
    )
    normed_cols = normed_two
    grad_branch = grad_middle.astype(jnp.bfloat16)
    grad_mixed = (
        back_dot(grad_branch, output_w).astype(jnp.bfloat16).reshape(row_count, seq_len, H, DH)
    )

    def backward_block(carry_grads, block_inputs):
        grad_key_sum, grad_value_sum = carry_grads
        block_start, lse_block = block_inputs
        masked, query_block = block_scores(block_start)
        probs = jnp.exp(masked - lse_block[..., None])
        grad_mixed_block = lax.dynamic_slice_in_dim(grad_mixed, block_start, block_len, 1)
        grad_probs = jnp.einsum(
            "bqhd,bkhd->bhqk", grad_mixed_block, value_full, preferred_element_type=jnp.float32
        )
        grad_value_sum = grad_value_sum + jnp.einsum(
            "bhqk,bqhd->bkhd",
            probs.astype(jnp.bfloat16),
            grad_mixed_block,
            preferred_element_type=jnp.float32,
        )
        row_delta = jnp.sum(probs * grad_probs, axis=-1, keepdims=True)
        grad_scores = (probs * (grad_probs - row_delta)).astype(jnp.bfloat16)
        grad_query_block = (
            jnp.einsum("bhqk,bkhd->bqhd", grad_scores, key_full, preferred_element_type=jnp.float32)
            * score_scale
        )
        grad_key_sum = (
            grad_key_sum
            + jnp.einsum(
                "bhqk,bqhd->bkhd", grad_scores, query_block, preferred_element_type=jnp.float32
            )
            * score_scale
        )
        return ((grad_key_sum, grad_value_sum), grad_query_block)

    zeros_full = jnp.zeros((row_count, seq_len, H, DH), jnp.float32)
    (grad_key, grad_value), grad_query_blocks = lax.scan(
        backward_block, (zeros_full, zeros_full), (starts, lse_blocks)
    )
    grad_query = jnp.moveaxis(grad_query_blocks, 0, 1).reshape(row_count, seq_len, H, DH)
    grad_heads_query, grad_dims_query = split_factors(grad_query, heads_query, dims_query, RQ)
    grad_heads_key, grad_dims_key = split_factors(grad_key, heads_key, dims_key, RK)
    grad_heads_value, grad_dims_value = split_factors(grad_value, heads_value, dims_value, RK)
    grad_dims_query = rotate_back(grad_dims_query, cosine_table, sine_table)
    grad_dims_key = rotate_back(grad_dims_key, cosine_table, sine_table)
    factor_pairs = (
        (grad_heads_query, query_heads_w),
        (grad_dims_query, query_dims_w),
        (grad_heads_key, key_heads_w),
        (grad_dims_key, key_dims_w),
        (grad_heads_value, value_heads_w),
        (grad_dims_value, value_dims_w),
    )
    grad_flats = []
    grad_normed = jnp.zeros((token_count, D), jnp.float32)
    for grad_factor, weight in factor_pairs:
        grad_flat = grad_factor.reshape(token_count, weight.shape[1]).astype(jnp.bfloat16)
        grad_flats.append(grad_flat)
        grad_normed = grad_normed + back_dot(grad_flat, weight)
    gained_one = grad_normed * gain_one.astype(jnp.float32)
    grad_norm_gain = jnp.sum(grad_normed * inputs_flat * scale_one, axis=0)
    grad_inputs = (
        grad_middle
        + scale_one * gained_one
        - inputs_flat * scale_one**3 * jnp.mean(gained_one * inputs_flat, axis=-1, keepdims=True)
    )
    grad_tokens = grad_inputs.astype(jnp.bfloat16).reshape(tokens.shape)
    normed_cols = normed
    packed_grad = jnp.concatenate(
        [outer_sum(normed_cols, jnp.concatenate(grad_flats, axis=1))]
        + [grad_norm_gain[:, None], grad_mlp_gain[:, None]]
        + [jnp.zeros((D, PACKED - edges[-1] - 2), jnp.float32)],
        axis=1,
    )
    low = lambda v: v.astype(jnp.bfloat16)
    gate_out, up_out, down_out, output_out, packed_out = scatter(
        dims,
        [
            low(outer_sum(normed_two, grad_gate)),
            low(outer_sum(normed_two, grad_up)),
            low(outer_sum(inner_act, cotangent)),
            low(outer_sum(mixed_heads, grad_branch)),
            low(packed_grad),
        ],
        1,
    )
    parts_out = [packed_out[:, lo:hi] for lo, hi in zip(edges, edges[1:])]
    return (
        output,
        grad_tokens,
        packed_out[:, edges[-1]],
        *parts_out,
        output_out,
        packed_out[:, edges[-1] + 1],
        gate_out,
        up_out,
        down_out,
    )


def solution(mesh):
    return jax.shard_map(
        functools.partial(on_device, grid_of(mesh)),
        mesh=mesh,
        in_specs=(
            P(("dp", "fsdp"), None, None),
            P(("dp", "fsdp"), None),
            P(("dp", "fsdp")),
            P(("dp", "fsdp"), None),
            P(("dp", "fsdp"), None),
            P(("dp", "fsdp"), None),
            P(("dp", "fsdp"), None),
            P(("dp", "fsdp"), None),
            P(("dp", "fsdp"), None),
            P(("dp", "fsdp"), None),
            P(("dp", "fsdp")),
            P(("dp", "fsdp"), None),
            P(("dp", "fsdp"), None),
            P(("dp", "fsdp"), None),
            P(("dp", "fsdp"), None, None),
        ),
        out_specs=(
            P(("dp", "fsdp"), None, None),
            P(("dp", "fsdp"), None, None),
            P(("dp", "fsdp")),
            P(("dp", "fsdp"), None),
            P(("dp", "fsdp"), None),
            P(("dp", "fsdp"), None),
            P(("dp", "fsdp"), None),
            P(("dp", "fsdp"), None),
            P(("dp", "fsdp"), None),
            P(("dp", "fsdp"), None),
            P(("dp", "fsdp")),
            P(("dp", "fsdp"), None),
            P(("dp", "fsdp"), None),
            P(("dp", "fsdp"), None),
        ),
        check_vma=False,
    )
```

```python
import functools
import math

import jax
import jax.numpy as jnp
import numpy as np
from jax import lax
from jax.experimental import pallas as pl
from jax.experimental.pallas import tpu as pltpu
from jax.sharding import PartitionSpec as P

MESH = pl.DeviceIdType.MESH
D, H, DH, RQ, RK = 1024, 16, 64, 6, 2
PACKED = 896
DIMS, HEADS = 640, 128
BLOCK = 256
BACK = 512
NEG = -1e30
epsilon = 1e-06
theta_base = 10000.0
f32, bf16 = jnp.float32, jnp.bfloat16
NT = (((1,), (1,)), ((), ()))
NN = (((1,), (0,)), ((), ()))
TN = (((0,), (0,)), ((), ()))


def dot(a, b, dims=NN):
    return lax.dot_general(a, b, dims, preferred_element_type=f32)


def params(**kw):
    return pltpu.CompilerParams(vmem_limit_bytes=56 << 20, **kw)


def rope_tables(seq_len):
    half = DH // 2
    position = np.arange(seq_len, dtype=np.float32)
    inverse = np.exp(-math.log(theta_base) * 2.0 * np.arange(half, dtype=np.float32) / np.float32(2.0 * half)).astype(np.float32)
    angle = (position[:, None] * inverse[None, :]).astype(np.float32)
    cosine, sine = np.cos(angle), np.sin(angle)
    return (np.concatenate([cosine] * 4, 1), np.concatenate([-sine, sine] * 2, 1))


def spread_table():
    out = np.zeros((8, 2 * HEADS, H * DH), np.float32)
    for j in range(8):
        for h in range(H):
            out[j, [j * H + h, HEADS + j * H + h], h * DH:(h + 1) * DH] = 1.0
    return out.astype(jnp.bfloat16)


def low_lane(shape):
    return lax.rem(lax.broadcasted_iota(jnp.int32, shape, 1), 128) < 64


def first_half(shape):
    return lax.rem(lax.broadcasted_iota(jnp.int32, shape, 1), 64) < 32


def turn(x, cosine, sine):
    partner = jnp.where(first_half(x.shape), pltpu.roll(x, 96, 1), pltpu.roll(x, 32, 1))
    return x * cosine + partner * sine


def split_bf16(x):
    hi = x.astype(bf16)
    return jnp.concatenate([hi, (x - hi.astype(f32)).astype(bf16)], axis=1)


def twice(x, rank):
    rolled = pltpu.roll(x, 64, 1)
    low = low_lane(x.shape)
    return jnp.where(low, x, rolled) if rank % 2 == 0 else jnp.where(low, rolled, x)


def wide(x):
    return jnp.concatenate([x] * (H * DH // 128), axis=1)


def rms(x):
    return lax.rsqrt(jnp.mean(x * x, axis=-1, keepdims=True) + epsilon)


FACTORS = ((0, RQ, 0), (RQ, RK, 3), (0, RK, 4))


def factors_kernel(tokens, gain, weight, cosine, sine, spread, normed, factors, query, key, value):
    x = tokens[...].astype(f32)
    n = (x * rms(x) * gain[...]).astype(bf16)
    normed[...] = n
    f = dot(n, weight[...])
    pairs = [f[:, 128 * i:128 * i + 128] for i in range(DIMS // 128)]
    pairs = [turn(p, cosine[...], sine[...]) if i < 4 else p for i, p in enumerate(pairs)]
    for i, p in enumerate(pairs):
        factors[:, 128 * i:128 * i + 128] = p
    factors[:, DIMS:] = f[:, DIMS:]
    heads_qk = split_bf16(f[:, DIMS:DIMS + HEADS])
    heads_v = split_bf16(f[:, DIMS + HEADS:])
    for out, heads, (at, ranks, pair), scale in zip(
        (query, key, value), (heads_qk, heads_qk, heads_v), FACTORS, (0.125, 1.0, 1.0)
    ):
        total = None
        for r in range(ranks):
            term = dot(heads, spread[at + r]) * wide(twice(pairs[pair + r // 2], r))
            total = term if total is None else total + term
        rounded = (total * (1.0 / ranks)).astype(bf16)
        out[...] = rounded * jnp.asarray(scale, bf16) if scale != 1.0 else rounded


def make_factors(tokens, gain, weight, tables):
    cosine, sine, spread = tables
    seq = tokens.shape[0]
    row = lambda width: pl.BlockSpec((BLOCK, width), lambda i: (i, 0))
    whole = lambda a: pl.BlockSpec(a.shape, lambda i: (0,) * a.ndim)
    return pl.pallas_call(
        factors_kernel,
        grid=(seq // BLOCK,),
        out_shape=[
            jax.ShapeDtypeStruct((seq, D), bf16),
            jax.ShapeDtypeStruct((seq, PACKED), f32),
        ] + [jax.ShapeDtypeStruct((seq, H * DH), bf16)] * 3,
        in_specs=[row(D), whole(gain), whole(weight), row(128), row(128), whole(spread)],
        out_specs=[row(D), row(PACKED)] + [row(H * DH)] * 3,
        compiler_params=params(),
        name="factors",
    )(tokens, gain, weight, cosine, sine, spread)


def allowed_t(doc_col, doc_row, k0, kn, q0, qn):
    same = doc_col[k0:k0 + kn, :] == doc_row[:, q0:q0 + qn]
    if k0 + kn - 1 > q0:
        k_at = k0 + lax.broadcasted_iota(jnp.int32, (kn, qn), 0)
        q_at = q0 + lax.broadcasted_iota(jnp.int32, (kn, qn), 1)
        same = same & (k_at <= q_at)
    return same


def halves(x):
    low = low_lane(x.shape)
    zero = jnp.zeros_like(x)
    return jnp.where(low, x, zero), jnp.where(low, zero, x)


def attend_kernel(doc_col, doc_row, query, key, value, mixed, lse):
    seq = query.shape[0]
    v_half = halves(value[...])
    for q0 in range(0, seq, BLOCK):
        lo = max(0, q0 - BACK)
        kn = q0 + BLOCK - lo
        ok = allowed_t(doc_col, doc_row, lo, kn, q0, BLOCK)
        probs = []
        for h, q in enumerate(halves(query[q0:q0 + BLOCK, :])):
            s = jnp.where(ok, dot(key[lo:lo + kn, :], q, NT), NEG)
            top = jnp.max(s, axis=0, keepdims=True)
            e = jnp.exp(s - top)
            total = jnp.sum(e, axis=0, keepdims=True)
            probs.append((e * (1.0 / total)).astype(bf16))
            lse[0, h:h + 1, q0:q0 + BLOCK] = top + jnp.log(total)
        values = jnp.concatenate([v[lo:lo + kn] for v in v_half], axis=0)
        mixed[q0:q0 + BLOCK, :] = dot(jnp.concatenate(probs, axis=0), values, TN).astype(bf16)


def attend(doc_col, doc_row, query, key, value):
    seq = query.shape[0]
    pairs = H // 2
    whole = lambda a: pl.BlockSpec(a.shape, lambda i: (0,) * a.ndim)
    pair = pl.BlockSpec((seq, 128), lambda i: (0, i))
    return pl.pallas_call(
        attend_kernel,
        grid=(pairs,),
        out_shape=[jax.ShapeDtypeStruct((seq, H * DH), bf16), jax.ShapeDtypeStruct((pairs, 2, seq), f32)],
        in_specs=[whole(doc_col), whole(doc_row), pair, pair, pair],
        out_specs=[pair, pl.BlockSpec((1, 2, seq), lambda i: (i, 0, 0))],
        compiler_params=params(),
        name="attend",
    )(doc_col, doc_row, query, key, value)


def attend_back_kernel(doc_col, doc_row, query, key, value, grad, lse, g_query, g_key, g_value):
    seq = query.shape[0]
    k_half = halves(key[...])
    for q0 in range(0, seq, BLOCK):
        lo = max(0, q0 - BACK)
        kn = q0 + BLOCK - lo
        ok = allowed_t(doc_col, doc_row, lo, kn, q0, BLOCK)
        ps, ds = [], []
        q_half, g_half = halves(query[q0:q0 + BLOCK, :]), halves(grad[q0:q0 + BLOCK, :])
        for h in (0, 1):
            s = dot(key[lo:lo + kn, :], q_half[h], NT)
            p = jnp.where(ok, jnp.exp(s - lse[0, h:h + 1, q0:q0 + BLOCK]), 0.0)
            pd = p * dot(value[lo:lo + kn, :], g_half[h], NT)
            ps.append(p.astype(bf16))
            ds.append((pd - p * jnp.sum(pd, axis=0, keepdims=True)).astype(bf16))
        to_value = dot(jnp.concatenate(ps, 1), jnp.concatenate(g_half, 0))
        to_key = dot(jnp.concatenate(ds, 1), jnp.concatenate(q_half, 0))
        if q0 > lo:
            g_value[lo:q0, :] += to_value[:q0 - lo]
            g_key[lo:q0, :] += to_key[:q0 - lo]
        g_value[q0:q0 + BLOCK, :] = to_value[q0 - lo:]
        g_key[q0:q0 + BLOCK, :] = to_key[q0 - lo:]
        keys = jnp.concatenate([k[lo:lo + kn] for k in k_half], 0)
        g_query[q0:q0 + BLOCK, :] = dot(jnp.concatenate(ds, 0), keys, TN) * 0.125


def attend_back(doc_col, doc_row, query, key, value, grad, lse):
    seq = query.shape[0]
    pairs = H // 2
    whole = lambda a: pl.BlockSpec(a.shape, lambda i: (0,) * a.ndim)
    pair = pl.BlockSpec((seq, 128), lambda i: (0, i))
    return pl.pallas_call(
        attend_back_kernel,
        grid=(pairs,),
        out_shape=[jax.ShapeDtypeStruct((seq, H * DH), f32)] * 3,
        in_specs=[whole(doc_col), whole(doc_row)] + [pair] * 4 + [pl.BlockSpec((1, 2, seq), lambda i: (i, 0, 0))],
        out_specs=[pair] * 3,
        compiler_params=params(),
        name="attend_back",
    )(doc_col, doc_row, query, key, value, grad, lse)


def factors_back_kernel(tokens, gain, weight, cosine, sine, spread, factors, g_query, g_key, g_value, g_middle,
                        g_factors, g_tokens, g_gain):
    pairs = [factors[:, 128 * i:128 * i + 128] for i in range(DIMS // 128)]
    heads_qk = split_bf16(factors[:, DIMS:DIMS + HEADS])
    heads_v = split_bf16(factors[:, DIMS + HEADS:])
    g_heads = [None, None]
    for grad, heads, which, (at, ranks, pair) in zip(
        (g_query, g_key, g_value), (heads_qk, heads_qk, heads_v), (0, 0, 1), FACTORS
    ):
        g = grad[...] * (1.0 / ranks)
        folded = []
        for r in range(ranks):
            product = (g * wide(twice(pairs[pair + r // 2], r))).astype(bf16)
            part = dot(product, spread[at + r, :HEADS, :], NT)
            g_heads[which] = part if g_heads[which] is None else g_heads[which] + part
            full = g * dot(heads, spread[at + r])
            folded.append(sum(full[:, 128 * i:128 * i + 128] for i in range(H * DH // 128)))
        for r in range(0, ranks, 2):
            a, b = folded[r], folded[r + 1]
            low = low_lane(a.shape)
            mine = jnp.where(low, a, b)
            other = jnp.where(low, pltpu.roll(a, 64, 1), pltpu.roll(b, 64, 1))
            both = mine + other
            i = pair + r // 2
            if i < 4:
                both = turn(both, cosine[...], -sine[...])
            g_factors[:, 128 * i:128 * i + 128] = both.astype(bf16)
    g_factors[:, DIMS:DIMS + HEADS] = g_heads[0].astype(bf16)
    g_factors[:, DIMS + HEADS:] = g_heads[1].astype(bf16)
    g_normed = dot(g_factors[...], weight[...], NT)
    x = tokens[...].astype(f32)
    r1 = rms(x)
    u = g_normed * gain[...]
    part = jnp.sum(g_normed * x * r1, axis=0, keepdims=True)

    @pl.when(pl.program_id(0) == 0)
    def _():
        g_gain[...] = part

    @pl.when(pl.program_id(0) > 0)
    def _():
        g_gain[...] += part

    g_tokens[...] = (g_middle[...] + r1 * u - x * (r1 * r1 * r1 * jnp.mean(u * x, axis=-1, keepdims=True))).astype(bf16)


def factors_back(tokens, gain, weight, tables, factors, g_query, g_key, g_value, g_middle):
    cosine, sine, spread = tables
    seq = tokens.shape[0]
    row = lambda width: pl.BlockSpec((BLOCK, width), lambda i: (i, 0))
    whole = lambda a: pl.BlockSpec(a.shape, lambda i: (0,) * a.ndim)
    return pl.pallas_call(
        factors_back_kernel,
        grid=(seq // BLOCK,),
        out_shape=[
            jax.ShapeDtypeStruct((seq, PACKED), bf16),
            jax.ShapeDtypeStruct((seq, D), bf16),
            jax.ShapeDtypeStruct((1, D), f32),
        ],
        in_specs=[row(D), whole(gain), whole(weight), row(128), row(128), whole(spread), row(PACKED)]
        + [row(H * DH)] * 3 + [row(D)],
        out_specs=[row(PACKED), row(D), pl.BlockSpec((1, D), lambda i: (0, 0))],
        compiler_params=params(),
        name="factors_back",
    )(tokens, gain, weight, cosine, sine, spread, factors, g_query, g_key, g_value, g_middle)

ANY = pl.BlockSpec(memory_space=pl.ANY)


def grid_of(mesh):
    nd, nf = mesh.shape["dp"], mesh.shape["fsdp"]
    nc = math.gcd(2, nd)
    nz = math.gcd(4, nf)
    return (nd // nc, nc, nz, nf // nz)


class Place:
    def __init__(self, dims):
        self.dims = dims
        ny, nc, nz, nx = dims
        dp, fs = lax.axis_index("dp"), lax.axis_index("fsdp")
        self.y, self.c = lax.div(dp, nc), lax.rem(dp, nc)
        self.z, self.x = lax.div(fs, nx), lax.rem(fs, nx)

    def at(self, axis, k):
        n = self.dims["yczx".index(axis)]
        return lax.rem(getattr(self, axis) + k + n, n)

    def device(self, axis=None, k=0):
        ny, nc, nz, nx = self.dims
        put = {a: getattr(self, a) for a in "yczx"}
        if axis is not None:
            put[axis] = self.at(axis, k)
        return (put["y"] * nc + put["c"], put["z"] * nx + put["x"])


def peers_of(dims):
    ny, nc, nz, nx = dims
    return [(a, k) for a, n in (("y", ny), ("c", nc), ("z", nz), ("x", nx)) for k in range(1, n)]


def enter(place):
    barrier = pltpu.get_barrier_semaphore()
    peers = peers_of(place.dims)
    for axis, k in peers:
        pl.semaphore_signal(barrier, inc=1, device_id=place.device(axis, k), device_id_type=MESH)
    pl.semaphore_wait(barrier, len(peers))


class Gather:
    def __init__(self, place, src, dst, sems, i):
        self.p, self.src, self.dst, self.i = place, src, dst, i
        self.local, self.zs, self.zr, self.as_, self.ar, self.bs, self.br, self.cs, self.cr = sems

    @staticmethod
    def sem_shapes(dims, n):
        ny, nc, nz, nx = dims
        dma = pltpu.SemaphoreType.DMA
        m = max(nx, ny) - 1
        one = lambda k: dma((n, max(1, k)))
        return [dma((n,)), one(nz - 1), one(nz - 1), one(m), one(m), one(m), one(m), one(nx + ny - 1), one(nx + ny - 1)]

    def copy(self, ref_src, ref_dst, send, recv, axis, k):
        return pltpu.make_async_remote_copy(
            src_ref=ref_src, dst_ref=ref_dst, send_sem=send, recv_sem=recv,
            device_id=self.p.device(axis, k), device_id_type=MESH,
        )

    def z_copies(self):
        p, i = self.p, self.i
        nz = p.dims[2]
        mine = self.dst.at[p.y, p.c, p.z, p.x]
        def one(k, back):
            if back:
                ref = self.dst.at[p.y, p.c, p.at("z", -k), p.x]
                return self.copy(ref, ref, self.zs.at[i, k - 1], self.zr.at[i, k - 1], "z", k)
            return self.copy(self.src, mine, self.zs.at[i, k - 1], self.zr.at[i, k - 1], "z", k)

        return [[functools.partial(one, k, back) for k in range(1, nz)] for back in (False, True)]

    def part(self, first, step, y, x, c):
        every = slice(None)
        if step == 0:
            return self.dst.at[y, c, :, x]
        return self.dst.at[y, c] if first == "x" else self.dst.at[:, c, :, x]

    def side_copies(self, first, step):
        p, i = self.p, self.i
        axis = first if step == 0 else {"x": "y", "y": "x"}[first]
        n = p.dims["yczx".index(axis)]
        s, r = ((self.as_, self.ar), (self.bs, self.br))[step]

        def one(k, back):
            y, x = p.y, p.x
            if back:
                y, x = (p.y, p.at("x", -k)) if axis == "x" else (p.at("y", -k), p.x)
            ref = self.part(first, step, y, x, p.c)
            return self.copy(ref, ref, s.at[i, k - 1], r.at[i, k - 1], axis, k)

        return [[functools.partial(one, k, back) for k in range(1, n)] for back in (False, True)]

    def core_copies(self, first, c):
        p, i = self.p, self.i
        second = {"x": "y", "y": "x"}[first]
        lists, j = [], 0
        for step, axis in ((0, None), (0, first), (1, second)):
            now = []
            count = 1 if axis is None else p.dims["yczx".index(axis)] - 1
            for k in range(1, count + 1):
                def one(axis=axis, step=step, k=k, j=j):
                    y = p.at("y", -k) if axis == "y" else p.y
                    x = p.at("x", -k) if axis == "x" else p.x
                    ref = self.part(first, step, y, x, c)
                    return self.copy(ref, ref, self.cs.at[i, j], self.cr.at[i, j], "c", 1)

                now.append(one)
                j += 1
            lists.append(now)
        return lists

    def start(self):
        p = self.p
        mine = self.dst.at[p.y, p.c, p.z, p.x]
        pltpu.make_async_copy(self.src, mine, self.local.at[self.i]).start()
        for copy in self.z_copies()[0]:
            copy().start()

    def by_core(self, body):
        if self.p.dims[1] == 1:
            body("x")
            return
        pl.when(self.p.c == 0)(lambda: body("x"))
        pl.when(self.p.c == 1)(lambda: body("y"))

    def after_z(self):
        p = self.p
        mine = self.dst.at[p.y, p.c, p.z, p.x]
        pltpu.make_async_copy(self.src, mine, self.local.at[self.i]).wait()
        for copy in self.z_copies()[1]:
            copy().wait_recv()

        def body(first):
            for copy in self.side_copies(first, 0)[0]:
                copy().start()
            if p.dims[1] > 1:
                for copy in self.core_copies(first, p.c)[0]:
                    copy().start()

        self.by_core(body)

    def after_first(self):
        p = self.p

        def body(first):
            for copy in self.side_copies(first, 0)[1]:
                copy().wait_recv()
            for copy in self.side_copies(first, 1)[0]:
                copy().start()
            if p.dims[1] > 1:
                for copy in self.core_copies(first, p.c)[1]:
                    copy().start()

        self.by_core(body)

    def after_second(self):
        p = self.p

        def body(first):
            for copy in self.side_copies(first, 1)[1]:
                copy().wait_recv()
            if p.dims[1] > 1:
                for copy in self.core_copies(first, p.c)[2]:
                    copy().start()

        self.by_core(body)

    def finish(self):
        p = self.p
        for copy in self.z_copies()[0]:
            copy().wait_send()

        def body(first):
            for step in (0, 1):
                for copy in self.side_copies(first, step)[0]:
                    copy().wait_send()
            if p.dims[1] > 1:
                for now in self.core_copies(first, p.c):
                    for copy in now:
                        copy().wait_send()
                other = {"x": "y", "y": "x"}[first]
                for now in self.core_copies(other, p.at("c", 1)):
                    for copy in now:
                        copy().wait_recv()

        self.by_core(body)

    def stages(self):
        return [self.start, self.after_z, self.after_first, self.after_second, self.finish]


def gather_kernel(dims, n, *refs):
    place = Place(dims)
    src, dst, sems = refs[:n], refs[n:2 * n], refs[2 * n:]
    enter(place)
    jobs = [Gather(place, src[i], dst[i], sems, i).stages() for i in range(n)]
    run_stages(jobs)


def gather(dims, arrays, collective_id):
    n = len(arrays)
    outs = pl.pallas_call(
        functools.partial(gather_kernel, dims, n),
        out_shape=[jax.ShapeDtypeStruct(dims + a.shape, a.dtype) for a in arrays],
        in_specs=[ANY] * n,
        out_specs=[ANY] * n,
        scratch_shapes=Gather.sem_shapes(dims, n),
        compiler_params=pltpu.CompilerParams(collective_id=collective_id, has_side_effects=True),
        name="gather_weights",
    )(*arrays)
    return [o.reshape((-1,) + a.shape[1:]) for o, a in zip(outs, arrays)]


class Scatter:
    def __init__(self, place, src, out, bufs, sems, i):
        self.p, self.src, self.out, self.i = place, src, out, i
        self.own, self.from_core, self.from_a, self.from_b, self.from_z = bufs
        self.local, self.cs, self.cr, self.as_, self.ar, self.bs, self.br, self.zs, self.zr = sems

    @staticmethod
    def sem_shapes(dims, n):
        ny, nc, nz, nx = dims
        dma = pltpu.SemaphoreType.DMA
        m = max(nx, ny, 2) - 1
        return [dma((n, nx))] * 3 + [dma((n, m))] * 4 + [dma((n, max(1, nz - 1)))] * 2

    @staticmethod
    def buf_shapes(dims, block):
        ny, nc, nz, nx = dims
        m = max(nx, ny, 2)
        buf = lambda *s: pltpu.VMEM(s + block, jnp.bfloat16)
        return [buf(ny, nx, nz), buf(ny, nx, nz), buf(m - 1, m, nz), buf(m - 1, nz), buf(max(1, nz - 1))]

    def copy(self, src, dst, send, recv, axis, k):
        return pltpu.make_async_remote_copy(
            src_ref=src, dst_ref=dst, send_sem=send, recv_sem=recv,
            device_id=self.p.device(axis, k), device_id_type=MESH,
        )

    def loads(self):
        p, i = self.p, self.i
        for x in range(p.dims[3]):
            yield lambda x=x: pltpu.make_async_copy(self.src.at[:, p.c, :, x], self.own.at[:, x], self.local.at[i, x])

    def core_copies(self):
        p, i = self.p, self.i
        if p.dims[1] == 1:
            return
        for x in range(p.dims[3]):
            yield lambda x=x: self.copy(
                self.src.at[:, p.at("c", 1), :, x], self.from_core.at[:, x], self.cs.at[i, x], self.cr.at[i, x], "c", 1)

    def a_copies(self, first):
        p, i = self.p, self.i
        ny, nc, nz, nx = p.dims
        for k in range(1, ny if first == "y" else nx):
            def copy(k=k):
                if first == "y":
                    src, dst = self.own.at[p.at("y", k)], self.from_a.at[k - 1, pl.ds(0, nx)]
                else:
                    src, dst = self.own.at[:, p.at("x", k)], self.from_a.at[k - 1, pl.ds(0, ny)]
                return self.copy(src, dst, self.as_.at[i, k - 1], self.ar.at[i, k - 1], first, k)
            yield copy

    def b_copies(self, first):
        p, i = self.p, self.i
        ny, nc, nz, nx = p.dims
        second = {"x": "y", "y": "x"}[first]
        for k in range(1, ny if second == "y" else nx):
            def copy(k=k):
                src = self.own.at[p.at("y", k), p.x] if second == "y" else self.own.at[p.y, p.at("x", k)]
                return self.copy(src, self.from_b.at[k - 1], self.bs.at[i, k - 1], self.br.at[i, k - 1], second, k)
            yield copy

    def z_copies(self):
        p, i = self.p, self.i
        for k in range(1, p.dims[2]):
            yield lambda k=k: self.copy(
                self.own.at[p.y, p.x, p.at("z", k)], self.from_z.at[k - 1], self.zs.at[i, k - 1], self.zr.at[i, k - 1], "z", k)

    def by_core(self, body):
        if self.p.dims[1] == 1:
            body("y")
            return
        pl.when(self.p.c == 0)(lambda: body("y"))
        pl.when(self.p.c == 1)(lambda: body("x"))

    @staticmethod
    def add(total, terms):
        value = total[...].astype(jnp.float32)
        for term in terms:
            value = value + term[...].astype(jnp.float32)
        return value

    def start(self):
        for copy in self.core_copies():
            copy().start()
        for copy in self.loads():
            copy().start()

    def after_core(self):
        p = self.p
        ny, nc, nz, nx = p.dims
        for copy in self.loads():
            copy().wait()
        for copy in self.core_copies():
            copy().wait_recv()
        if nc > 1:
            def body(t, carry):
                at = (lax.div(t, nx * nz), lax.rem(lax.div(t, nz), nx), lax.rem(t, nz))
                self.own[at] = self.add(self.own.at[at], [self.from_core.at[at]]).astype(jnp.bfloat16)
                return carry
            lax.fori_loop(0, ny * nx * nz, body, 0)

        def go(first):
            for copy in self.a_copies(first):
                copy().start()
        self.by_core(go)

    def after_a(self):
        p = self.p
        ny, nc, nz, nx = p.dims

        def go(first):
            for copy in self.a_copies(first):
                copy().wait_recv()
            n = ny if first == "y" else nx

            def body(t, carry):
                j, z = lax.div(t, nz), lax.rem(t, nz)
                at = (p.y, j, z) if first == "y" else (j, p.x, z)
                terms = [self.from_a.at[k, j, z] for k in range(n - 1)]
                self.own[at] = self.add(self.own.at[at], terms).astype(jnp.bfloat16)
                return carry
            if n > 1:
                lax.fori_loop(0, (nx if first == "y" else ny) * nz, body, 0)
            for copy in self.b_copies(first):
                copy().start()
        self.by_core(go)

    def after_b(self):
        p = self.p
        ny, nc, nz, nx = p.dims

        def go(first):
            for copy in self.b_copies(first):
                copy().wait_recv()
            n = nx if first == "y" else ny

            def body(z, carry):
                at = (p.y, p.x, z)
                terms = [self.from_b.at[k, z] for k in range(n - 1)]
                self.own[at] = self.add(self.own.at[at], terms).astype(jnp.bfloat16)
                return carry
            if n > 1:
                lax.fori_loop(0, nz, body, 0)
        self.by_core(go)
        for copy in self.z_copies():
            copy().start()

    def after_z(self):
        p = self.p
        for copy in self.z_copies():
            copy().wait_recv()
        terms = [self.from_z.at[k] for k in range(p.dims[2] - 1)]
        self.out[...] = self.add(self.own.at[p.y, p.x, p.z], terms)

    def finish(self):
        for copy in self.core_copies():
            copy().wait_send()

        def go(first):
            for copy in self.a_copies(first):
                copy().wait_send()
            for copy in self.b_copies(first):
                copy().wait_send()
        self.by_core(go)
        for copy in self.z_copies():
            copy().wait_send()

    def stages(self):
        return [self.start, self.after_core, self.after_a, self.after_b, self.after_z, self.finish]


def run_stages(jobs):
    n, depth = len(jobs), len(jobs[0])
    for t in range(n + depth - 1):
        for i in range(n):
            if 0 <= t - i < depth:
                jobs[i][t - i]()


def scatter_kernel(dims, n, *refs):
    place = Place(dims)
    src, out, rest = refs[:n], refs[n:2 * n], refs[2 * n:]
    bufs, sems = rest[:5 * n], rest[5 * n:]
    enter(place)
    run_stages([Scatter(place, src[i], out[i], bufs[5 * i:5 * i + 5], sems, i).stages() for i in range(n)])


def scatter(dims, arrays, collective_id):
    n = len(arrays)
    devices = math.prod(dims)
    blocks = [(a.shape[0] // devices,) + a.shape[1:] for a in arrays]
    shaped = [a.reshape(dims + b) for a, b in zip(arrays, blocks)]
    scratch = []
    for b in blocks:
        scratch += Scatter.buf_shapes(dims, b)
    return pl.pallas_call(
        functools.partial(scatter_kernel, dims, n),
        out_shape=[jax.ShapeDtypeStruct(b, jnp.float32) for b in blocks],
        in_specs=[ANY] * n,
        out_specs=[pl.BlockSpec(memory_space=pltpu.VMEM)] * n,
        scratch_shapes=scratch + Scatter.sem_shapes(dims, n),
        compiler_params=pltpu.CompilerParams(
            collective_id=collective_id, has_side_effects=True, vmem_limit_bytes=56 << 20),
        name="scatter_gradients",
    )(*shaped)


def on_device(
    dims,
    tokens,
    doc_ids,
    norm_gain,
    w_query_heads,
    w_query_dims,
    w_key_heads,
    w_key_dims,
    w_value_heads,
    w_value_dims,
    w_output,
    mlp_gain,
    w_gate,
    w_up,
    w_down,
    out_grad,
):
    seq_len = tokens.shape[0] * tokens.shape[1]
    tables = tuple(jnp.asarray(t) for t in rope_tables(seq_len) + (spread_table(),))
    parts = (w_query_dims, w_key_dims, w_value_dims, w_query_heads, w_key_heads, w_value_heads)
    edges = [0]
    for part in parts:
        edges.append(edges[-1] + part.shape[1])
    gains_at = edges[-1]
    packed = jnp.concatenate(
        parts
        + (norm_gain[:, None], mlp_gain[:, None])
        + (jnp.zeros((norm_gain.shape[0], PACKED - gains_at - 2), bf16),),
        axis=1,
    )
    packed_w, output_w, gate_w, up_w, down_w = gather(
        dims, [packed, w_output, w_gate, w_up, w_down], 0
    )
    gain_one, gain_two = [packed_w[:, gains_at + i].astype(f32).reshape(1, D) for i in (0, 1)]

    inputs = tokens.reshape(seq_len, D)
    doc_row, doc_col = doc_ids.reshape(1, seq_len), doc_ids.reshape(seq_len, 1)
    normed, factors, query, key, value = make_factors(inputs, gain_one, packed_w, tables)
    mixed, lse = attend(doc_col, doc_row, query, key, value)

    middle = inputs.astype(f32) + dot(mixed, output_w)
    scale_two = rms(middle)
    normed_two = (middle * scale_two * gain_two).astype(bf16)
    gate_proj, up_proj = dot(normed_two, gate_w), dot(normed_two, up_w)
    sigmoid_gate = jax.nn.sigmoid(gate_proj)
    silu_gate = gate_proj * sigmoid_gate
    inner_act = (silu_gate * up_proj).astype(bf16)
    output = (middle + dot(inner_act, down_w)).astype(bf16)

    cotangent = out_grad.reshape(seq_len, D)
    grad_inner = dot(cotangent, down_w, NT)
    grad_gate = (
        grad_inner * up_proj * sigmoid_gate * (1.0 + gate_proj * (1.0 - sigmoid_gate))
    ).astype(bf16)
    grad_up = (grad_inner * silu_gate).astype(bf16)
    grad_normed_two = dot(grad_gate, gate_w, NT) + dot(grad_up, up_w, NT)
    gained_two = grad_normed_two * gain_two
    grad_mlp_gain = jnp.sum(grad_normed_two * middle * scale_two, axis=0)
    grad_middle = (
        cotangent.astype(f32)
        + scale_two * gained_two
        - middle * scale_two**3 * jnp.mean(gained_two * middle, axis=-1, keepdims=True)
    )
    grad_branch = grad_middle.astype(bf16)
    grad_mixed = dot(grad_branch, output_w, NT).astype(bf16)

    grad_query, grad_key, grad_value = attend_back(
        doc_col, doc_row, query, key, value, grad_mixed, lse
    )
    grad_factors, grad_tokens, grad_norm_gain = factors_back(
        inputs, gain_one, packed_w, tables, factors, grad_query, grad_key, grad_value, grad_middle
    )
    outer_sum = lambda left, right: dot(left, right, TN).astype(bf16)
    gains = jnp.stack([grad_norm_gain[0], grad_mlp_gain], axis=1).astype(bf16)
    packed_grad = lax.dynamic_update_slice(outer_sum(normed, grad_factors), gains, (0, gains_at))
    gate_out, up_out, down_out, output_out, packed_out = scatter(
        dims,
        [
            outer_sum(normed_two, grad_gate),
            outer_sum(normed_two, grad_up),
            outer_sum(inner_act, cotangent),
            outer_sum(mixed, grad_branch),
            packed_grad,
        ],
        1,
    )
    dims_and_heads = [packed_out[:, lo:hi] for lo, hi in zip(edges, edges[1:])]
    grads = [g for pair in zip(dims_and_heads[3:], dims_and_heads[:3]) for g in pair]
    return (
        output.reshape(tokens.shape),
        grad_tokens.reshape(tokens.shape),
        packed_out[:, gains_at],
        *grads,
        output_out,
        packed_out[:, gains_at + 1],
        gate_out,
        up_out,
        down_out,
    )


def solution(mesh):
    rows, matrix, vector = P(("dp", "fsdp"), None, None), P(("dp", "fsdp"), None), P(("dp", "fsdp"))
    return jax.shard_map(
        functools.partial(on_device, grid_of(mesh)),
        mesh=mesh,
        in_specs=(rows, matrix, vector) + (matrix,) * 7 + (vector,) + (matrix,) * 3 + (rows,),
        out_specs=(rows, rows, vector) + (matrix,) * 7 + (vector,) + (matrix,) * 3,
        check_vma=False,
    )
```

```python
import functools
import math

import jax
import jax.numpy as jnp
import numpy as np
from jax import lax
from jax.experimental import pallas as pl
from jax.experimental.pallas import tpu as pltpu
from jax.sharding import PartitionSpec as P

MESH = pl.DeviceIdType.MESH
D, H, DH, RQ, RK = 1024, 16, 64, 6, 2
PACKED = 896
DIMS, HEADS = 640, 128
BLOCK = 256
BACK = 512
NEG = -1e30
epsilon = 1e-06
theta_base = 10000.0
f32, bf16 = jnp.float32, jnp.bfloat16
NT = (((1,), (1,)), ((), ()))
NN = (((1,), (0,)), ((), ()))
TN = (((0,), (0,)), ((), ()))


def dot(a, b, dims=NN):
    return lax.dot_general(a, b, dims, preferred_element_type=f32)


def params(**kw):
    return pltpu.CompilerParams(vmem_limit_bytes=56 << 20, **kw)


def rope_tables(seq_len):
    half = DH // 2
    position = np.arange(seq_len, dtype=np.float32)
    inverse = np.exp(-math.log(theta_base) * 2.0 * np.arange(half, dtype=np.float32) / np.float32(2.0 * half)).astype(np.float32)
    angle = (position[:, None] * inverse[None, :]).astype(np.float32)
    cosine, sine = np.cos(angle), np.sin(angle)
    return (np.concatenate([cosine] * 4, 1), np.concatenate([-sine, sine] * 2, 1))


def spread_table():
    out = np.zeros((8, 2 * HEADS, H * DH), np.float32)
    for j in range(8):
        for h in range(H):
            out[j, [j * H + h, HEADS + j * H + h], h * DH:(h + 1) * DH] = 1.0
    return out.astype(jnp.bfloat16)


def low_lane(shape):
    return lax.rem(lax.broadcasted_iota(jnp.int32, shape, 1), 128) < 64


def first_half(shape):
    return lax.rem(lax.broadcasted_iota(jnp.int32, shape, 1), 64) < 32


def turn(x, cosine, sine):
    partner = jnp.where(first_half(x.shape), pltpu.roll(x, 96, 1), pltpu.roll(x, 32, 1))
    return x * cosine + partner * sine


def split_bf16(x):
    hi = x.astype(bf16)
    return jnp.concatenate([hi, (x - hi.astype(f32)).astype(bf16)], axis=1)


def twice(x, rank):
    rolled = pltpu.roll(x, 64, 1)
    low = low_lane(x.shape)
    return jnp.where(low, x, rolled) if rank % 2 == 0 else jnp.where(low, rolled, x)


def wide(x):
    return jnp.concatenate([x] * (H * DH // 128), axis=1)


def rms(x):
    return lax.rsqrt(jnp.mean(x * x, axis=-1, keepdims=True) + epsilon)


FACTORS = ((0, RQ, 0), (RQ, RK, 3), (0, RK, 4))


def factors_kernel(tokens, gain, weight, cosine, sine, spread, normed, factors, query, key, value):
    x = tokens[...].astype(f32)
    n = (x * rms(x) * gain[...]).astype(bf16)
    normed[...] = n
    f = dot(n, weight[...])
    pairs = [f[:, 128 * i:128 * i + 128] for i in range(DIMS // 128)]
    pairs = [turn(p, cosine[...], sine[...]) if i < 4 else p for i, p in enumerate(pairs)]
    for i, p in enumerate(pairs):
        factors[:, 128 * i:128 * i + 128] = p
    factors[:, DIMS:] = f[:, DIMS:]
    heads_qk = split_bf16(f[:, DIMS:DIMS + HEADS])
    heads_v = split_bf16(f[:, DIMS + HEADS:])
    for out, heads, (at, ranks, pair), scale in zip(
        (query, key, value), (heads_qk, heads_qk, heads_v), FACTORS, (0.125, 1.0, 1.0)
    ):
        total = None
        for r in range(ranks):
            term = dot(heads, spread[at + r]) * wide(twice(pairs[pair + r // 2], r))
            total = term if total is None else total + term
        rounded = (total * (1.0 / ranks)).astype(bf16)
        out[...] = rounded * jnp.asarray(scale, bf16) if scale != 1.0 else rounded


def make_factors(tokens, gain, weight, tables):
    cosine, sine, spread = tables
    seq = tokens.shape[0]
    row = lambda width: pl.BlockSpec((BLOCK, width), lambda i: (i, 0))
    whole = lambda a: pl.BlockSpec(a.shape, lambda i: (0,) * a.ndim)
    return pl.pallas_call(
        factors_kernel,
        grid=(seq // BLOCK,),
        out_shape=[
            jax.ShapeDtypeStruct((seq, D), bf16),
            jax.ShapeDtypeStruct((seq, PACKED), f32),
        ] + [jax.ShapeDtypeStruct((seq, H * DH), bf16)] * 3,
        in_specs=[row(D), whole(gain), whole(weight), row(128), row(128), whole(spread)],
        out_specs=[row(D), row(PACKED)] + [row(H * DH)] * 3,
        compiler_params=params(),
        name="factors",
    )(tokens, gain, weight, cosine, sine, spread)


def allowed_t(doc_col, doc_row, k0, kn, q0, qn):
    same = doc_col[k0:k0 + kn, :] == doc_row[:, q0:q0 + qn]
    if k0 + kn - 1 > q0:
        k_at = k0 + lax.broadcasted_iota(jnp.int32, (kn, qn), 0)
        q_at = q0 + lax.broadcasted_iota(jnp.int32, (kn, qn), 1)
        same = same & (k_at <= q_at)
    return same


def halves(x):
    low = low_lane(x.shape)
    zero = jnp.zeros_like(x)
    return jnp.where(low, x, zero), jnp.where(low, zero, x)


def attend_kernel(doc_col, doc_row, query, key, value, mixed, lse):
    seq = query.shape[0]
    v_half = halves(value[...])
    for q0 in range(0, seq, BLOCK):
        lo = max(0, q0 - BACK)
        kn = q0 + BLOCK - lo
        ok = allowed_t(doc_col, doc_row, lo, kn, q0, BLOCK)
        probs = []
        for h, q in enumerate(halves(query[q0:q0 + BLOCK, :])):
            s = jnp.where(ok, dot(key[lo:lo + kn, :], q, NT), NEG)
            top = jnp.max(s, axis=0, keepdims=True)
            e = jnp.exp(s - top)
            total = jnp.sum(e, axis=0, keepdims=True)
            probs.append((e * (1.0 / total)).astype(bf16))
            lse[0, h:h + 1, q0:q0 + BLOCK] = top + jnp.log(total)
        values = jnp.concatenate([v[lo:lo + kn] for v in v_half], axis=0)
        mixed[q0:q0 + BLOCK, :] = dot(jnp.concatenate(probs, axis=0), values, TN).astype(bf16)


def attend(doc_col, doc_row, query, key, value):
    seq = query.shape[0]
    pairs = H // 2
    whole = lambda a: pl.BlockSpec(a.shape, lambda i: (0,) * a.ndim)
    pair = pl.BlockSpec((seq, 128), lambda i: (0, i))
    return pl.pallas_call(
        attend_kernel,
        grid=(pairs,),
        out_shape=[jax.ShapeDtypeStruct((seq, H * DH), bf16), jax.ShapeDtypeStruct((pairs, 2, seq), f32)],
        in_specs=[whole(doc_col), whole(doc_row), pair, pair, pair],
        out_specs=[pair, pl.BlockSpec((1, 2, seq), lambda i: (i, 0, 0))],
        compiler_params=params(),
        name="attend",
    )(doc_col, doc_row, query, key, value)


def attend_back_kernel(doc_col, doc_row, query, key, value, grad, lse, g_query, g_key, g_value):
    seq = query.shape[0]
    k_half = halves(key[...])
    for q0 in range(0, seq, BLOCK):
        lo = max(0, q0 - BACK)
        kn = q0 + BLOCK - lo
        ok = allowed_t(doc_col, doc_row, lo, kn, q0, BLOCK)
        ps, ds = [], []
        q_half, g_half = halves(query[q0:q0 + BLOCK, :]), halves(grad[q0:q0 + BLOCK, :])
        for h in (0, 1):
            s = dot(key[lo:lo + kn, :], q_half[h], NT)
            p = jnp.where(ok, jnp.exp(s - lse[0, h:h + 1, q0:q0 + BLOCK]), 0.0)
            pd = p * dot(value[lo:lo + kn, :], g_half[h], NT)
            ps.append(p.astype(bf16))
            ds.append((pd - p * jnp.sum(pd, axis=0, keepdims=True)).astype(bf16))
        to_value = dot(jnp.concatenate(ps, 1), jnp.concatenate(g_half, 0))
        to_key = dot(jnp.concatenate(ds, 1), jnp.concatenate(q_half, 0))
        if q0 > lo:
            g_value[lo:q0, :] += to_value[:q0 - lo]
            g_key[lo:q0, :] += to_key[:q0 - lo]
        g_value[q0:q0 + BLOCK, :] = to_value[q0 - lo:]
        g_key[q0:q0 + BLOCK, :] = to_key[q0 - lo:]
        keys = jnp.concatenate([k[lo:lo + kn] for k in k_half], 0)
        g_query[q0:q0 + BLOCK, :] = dot(jnp.concatenate(ds, 0), keys, TN) * 0.125


def attend_back(doc_col, doc_row, query, key, value, grad, lse):
    seq = query.shape[0]
    pairs = H // 2
    whole = lambda a: pl.BlockSpec(a.shape, lambda i: (0,) * a.ndim)
    pair = pl.BlockSpec((seq, 128), lambda i: (0, i))
    return pl.pallas_call(
        attend_back_kernel,
        grid=(pairs,),
        out_shape=[jax.ShapeDtypeStruct((seq, H * DH), f32)] * 3,
        in_specs=[whole(doc_col), whole(doc_row)] + [pair] * 4 + [pl.BlockSpec((1, 2, seq), lambda i: (i, 0, 0))],
        out_specs=[pair] * 3,
        compiler_params=params(),
        name="attend_back",
    )(doc_col, doc_row, query, key, value, grad, lse)


def factors_back_kernel(tokens, gain, weight, cosine, sine, spread, factors, g_query, g_key, g_value, g_middle,
                        g_factors, g_tokens, g_gain):
    pairs = [factors[:, 128 * i:128 * i + 128] for i in range(DIMS // 128)]
    heads_qk = split_bf16(factors[:, DIMS:DIMS + HEADS])
    heads_v = split_bf16(factors[:, DIMS + HEADS:])
    g_heads = [None, None]
    for grad, heads, which, (at, ranks, pair) in zip(
        (g_query, g_key, g_value), (heads_qk, heads_qk, heads_v), (0, 0, 1), FACTORS
    ):
        g = grad[...] * (1.0 / ranks)
        folded = []
        for r in range(ranks):
            product = (g * wide(twice(pairs[pair + r // 2], r))).astype(bf16)
            part = dot(product, spread[at + r, :HEADS, :], NT)
            g_heads[which] = part if g_heads[which] is None else g_heads[which] + part
            full = g * dot(heads, spread[at + r])
            folded.append(sum(full[:, 128 * i:128 * i + 128] for i in range(H * DH // 128)))
        for r in range(0, ranks, 2):
            a, b = folded[r], folded[r + 1]
            low = low_lane(a.shape)
            mine = jnp.where(low, a, b)
            other = jnp.where(low, pltpu.roll(a, 64, 1), pltpu.roll(b, 64, 1))
            both = mine + other
            i = pair + r // 2
            if i < 4:
                both = turn(both, cosine[...], -sine[...])
            g_factors[:, 128 * i:128 * i + 128] = both.astype(bf16)
    g_factors[:, DIMS:DIMS + HEADS] = g_heads[0].astype(bf16)
    g_factors[:, DIMS + HEADS:] = g_heads[1].astype(bf16)
    g_normed = dot(g_factors[...], weight[...], NT)
    x = tokens[...].astype(f32)
    r1 = rms(x)
    u = g_normed * gain[...]
    part = jnp.sum(g_normed * x * r1, axis=0, keepdims=True)

    @pl.when(pl.program_id(0) == 0)
    def _():
        g_gain[...] = part

    @pl.when(pl.program_id(0) > 0)
    def _():
        g_gain[...] += part

    g_tokens[...] = (g_middle[...] + r1 * u - x * (r1 * r1 * r1 * jnp.mean(u * x, axis=-1, keepdims=True))).astype(bf16)


def factors_back(tokens, gain, weight, tables, factors, g_query, g_key, g_value, g_middle):
    cosine, sine, spread = tables
    seq = tokens.shape[0]
    row = lambda width: pl.BlockSpec((BLOCK, width), lambda i: (i, 0))
    whole = lambda a: pl.BlockSpec(a.shape, lambda i: (0,) * a.ndim)
    return pl.pallas_call(
        factors_back_kernel,
        grid=(seq // BLOCK,),
        out_shape=[
            jax.ShapeDtypeStruct((seq, PACKED), bf16),
            jax.ShapeDtypeStruct((seq, D), bf16),
            jax.ShapeDtypeStruct((1, D), f32),
        ],
        in_specs=[row(D), whole(gain), whole(weight), row(128), row(128), whole(spread), row(PACKED)]
        + [row(H * DH)] * 3 + [row(D)],
        out_specs=[row(PACKED), row(D), pl.BlockSpec((1, D), lambda i: (0, 0))],
        compiler_params=params(),
        name="factors_back",
    )(tokens, gain, weight, cosine, sine, spread, factors, g_query, g_key, g_value, g_middle)

ANY = pl.BlockSpec(memory_space=pl.ANY)


def grid_of(mesh):
    nd, nf = mesh.shape["dp"], mesh.shape["fsdp"]
    nc = math.gcd(2, nd)
    nz = math.gcd(4, nf)
    return (nd // nc, nc, nz, nf // nz)


class Place:
    def __init__(self, dims):
        self.dims = dims
        ny, nc, nz, nx = dims
        dp, fs = lax.axis_index("dp"), lax.axis_index("fsdp")
        self.y, self.c = lax.div(dp, nc), lax.rem(dp, nc)
        self.z, self.x = lax.div(fs, nx), lax.rem(fs, nx)

    def at(self, axis, k):
        n = self.dims["yczx".index(axis)]
        return lax.rem(getattr(self, axis) + k + n, n)

    def device(self, axis=None, k=0):
        ny, nc, nz, nx = self.dims
        put = {a: getattr(self, a) for a in "yczx"}
        if axis is not None:
            put[axis] = self.at(axis, k)
        return (put["y"] * nc + put["c"], put["z"] * nx + put["x"])


def peers_of(dims):
    ny, nc, nz, nx = dims
    return [(a, k) for a, n in (("y", ny), ("c", nc), ("z", nz), ("x", nx)) for k in range(1, n)]


def enter(place):
    barrier = pltpu.get_barrier_semaphore()
    peers = peers_of(place.dims)
    for axis, k in peers:
        pl.semaphore_signal(barrier, inc=1, device_id=place.device(axis, k), device_id_type=MESH)
    pl.semaphore_wait(barrier, len(peers))


class Gather:
    def __init__(self, place, src, dst, sems, i):
        self.p, self.src, self.dst, self.i = place, src, dst, i
        self.local, self.zs, self.zr, self.as_, self.ar, self.bs, self.br, self.cs, self.cr = sems

    @staticmethod
    def sem_shapes(dims, n):
        ny, nc, nz, nx = dims
        dma = pltpu.SemaphoreType.DMA
        m = max(nx, ny) - 1
        one = lambda k: dma((n, max(1, k)))
        return [dma((n,)), one(nz - 1), one(nz - 1), one(m), one(m), one(m), one(m), one(nx + ny - 1), one(nx + ny - 1)]

    def copy(self, ref_src, ref_dst, send, recv, axis, k):
        return pltpu.make_async_remote_copy(
            src_ref=ref_src, dst_ref=ref_dst, send_sem=send, recv_sem=recv,
            device_id=self.p.device(axis, k), device_id_type=MESH,
        )

    def z_copies(self):
        p, i = self.p, self.i
        nz = p.dims[2]
        mine = self.dst.at[p.y, p.c, p.z, p.x]
        def one(k, back):
            if back:
                ref = self.dst.at[p.y, p.c, p.at("z", -k), p.x]
                return self.copy(ref, ref, self.zs.at[i, k - 1], self.zr.at[i, k - 1], "z", k)
            return self.copy(self.src, mine, self.zs.at[i, k - 1], self.zr.at[i, k - 1], "z", k)

        return [[functools.partial(one, k, back) for k in range(1, nz)] for back in (False, True)]

    def part(self, first, step, y, x, c):
        every = slice(None)
        if step == 0:
            return self.dst.at[y, c, :, x]
        return self.dst.at[y, c] if first == "x" else self.dst.at[:, c, :, x]

    def side_copies(self, first, step):
        p, i = self.p, self.i
        axis = first if step == 0 else {"x": "y", "y": "x"}[first]
        n = p.dims["yczx".index(axis)]
        s, r = ((self.as_, self.ar), (self.bs, self.br))[step]

        def one(k, back):
            y, x = p.y, p.x
            if back:
                y, x = (p.y, p.at("x", -k)) if axis == "x" else (p.at("y", -k), p.x)
            ref = self.part(first, step, y, x, p.c)
            return self.copy(ref, ref, s.at[i, k - 1], r.at[i, k - 1], axis, k)

        return [[functools.partial(one, k, back) for k in range(1, n)] for back in (False, True)]

    def core_copies(self, first, c):
        p, i = self.p, self.i
        second = {"x": "y", "y": "x"}[first]
        lists, j = [], 0
        for step, axis in ((0, None), (0, first), (1, second)):
            now = []
            count = 1 if axis is None else p.dims["yczx".index(axis)] - 1
            for k in range(1, count + 1):
                def one(axis=axis, step=step, k=k, j=j):
                    y = p.at("y", -k) if axis == "y" else p.y
                    x = p.at("x", -k) if axis == "x" else p.x
                    ref = self.part(first, step, y, x, c)
                    return self.copy(ref, ref, self.cs.at[i, j], self.cr.at[i, j], "c", 1)

                now.append(one)
                j += 1
            lists.append(now)
        return lists

    def start(self):
        p = self.p
        mine = self.dst.at[p.y, p.c, p.z, p.x]
        pltpu.make_async_copy(self.src, mine, self.local.at[self.i]).start()
        for copy in self.z_copies()[0]:
            copy().start()

    def by_core(self, body):
        if self.p.dims[1] == 1:
            body("x")
            return
        pl.when(self.p.c == 0)(lambda: body("x"))
        pl.when(self.p.c == 1)(lambda: body("y"))

    def after_z(self):
        p = self.p
        mine = self.dst.at[p.y, p.c, p.z, p.x]
        pltpu.make_async_copy(self.src, mine, self.local.at[self.i]).wait()
        for copy in self.z_copies()[1]:
            copy().wait_recv()

        def body(first):
            for copy in self.side_copies(first, 0)[0]:
                copy().start()
            if p.dims[1] > 1:
                for copy in self.core_copies(first, p.c)[0]:
                    copy().start()

        self.by_core(body)

    def after_first(self):
        p = self.p

        def body(first):
            for copy in self.side_copies(first, 0)[1]:
                copy().wait_recv()
            for copy in self.side_copies(first, 1)[0]:
                copy().start()
            if p.dims[1] > 1:
                for copy in self.core_copies(first, p.c)[1]:
                    copy().start()

        self.by_core(body)

    def after_second(self):
        p = self.p

        def body(first):
            for copy in self.side_copies(first, 1)[1]:
                copy().wait_recv()
            if p.dims[1] > 1:
                for copy in self.core_copies(first, p.c)[2]:
                    copy().start()

        self.by_core(body)

    def finish(self):
        p = self.p
        for copy in self.z_copies()[0]:
            copy().wait_send()

        def body(first):
            for step in (0, 1):
                for copy in self.side_copies(first, step)[0]:
                    copy().wait_send()
            if p.dims[1] > 1:
                for now in self.core_copies(first, p.c):
                    for copy in now:
                        copy().wait_send()
                other = {"x": "y", "y": "x"}[first]
                for now in self.core_copies(other, p.at("c", 1)):
                    for copy in now:
                        copy().wait_recv()

        self.by_core(body)

    def stages(self):
        return [self.start, self.after_z, self.after_first, self.after_second, self.finish]


def gather_kernel(dims, n, *refs):
    place = Place(dims)
    src, dst, sems = refs[:n], refs[n:2 * n], refs[2 * n:]
    enter(place)
    jobs = [Gather(place, src[i], dst[i], sems, i).stages() for i in range(n)]
    run_stages(jobs)


def gather(dims, arrays, collective_id):
    n = len(arrays)
    outs = pl.pallas_call(
        functools.partial(gather_kernel, dims, n),
        out_shape=[jax.ShapeDtypeStruct(dims + a.shape, a.dtype) for a in arrays],
        in_specs=[ANY] * n,
        out_specs=[ANY] * n,
        scratch_shapes=Gather.sem_shapes(dims, n),
        compiler_params=pltpu.CompilerParams(collective_id=collective_id, has_side_effects=True),
        name="gather_weights",
    )(*arrays)
    return [o.reshape((-1,) + a.shape[1:]) for o, a in zip(outs, arrays)]


class Scatter:
    def __init__(self, place, held, out, bufs, sems, i, src=None):
        self.p, self.src, self.out, self.i = place, src, out, i
        self.own, self.away = (held, None) if src is not None else (held.at[place.c], held.at[place.at("c", 1)])
        self.from_core, self.from_a, self.from_b, self.from_z = bufs
        self.local, self.cs, self.cr, self.as_, self.ar, self.bs, self.br, self.zs, self.zr = sems

    @staticmethod
    def sem_shapes(dims, n):
        ny, nc, nz, nx = dims
        dma = pltpu.SemaphoreType.DMA
        m = max(nx, ny, 2) - 1
        return [dma((n, nx))] * 3 + [dma((n, m))] * 4 + [dma((n, max(1, nz - 1)))] * 2

    @staticmethod
    def buf_shapes(dims, block, lead=()):
        ny, nc, nz, nx = dims
        m = max(nx, ny, 2)
        buf = lambda *s: pltpu.VMEM(lead + s + block, jnp.bfloat16)
        return [buf(ny, nx, nz), buf(m - 1, m, nz), buf(m - 1, nz), buf(max(1, nz - 1))]

    def copy(self, src, dst, send, recv, axis, k):
        return pltpu.make_async_remote_copy(
            src_ref=src, dst_ref=dst, send_sem=send, recv_sem=recv,
            device_id=self.p.device(axis, k), device_id_type=MESH,
        )

    def loads(self):
        p, i = self.p, self.i
        if self.src is None:
            return
        for x in range(p.dims[3]):
            yield lambda x=x: pltpu.make_async_copy(self.src.at[:, p.c, :, x], self.own.at[:, x], self.local.at[i, x])

    def core_copies(self):
        p, i = self.p, self.i
        if p.dims[1] == 1:
            return
        if self.src is None:
            yield lambda: self.copy(self.away, self.from_core, self.cs.at[i, 0], self.cr.at[i, 0], "c", 1)
            return
        for x in range(p.dims[3]):
            yield lambda x=x: self.copy(
                self.src.at[:, p.at("c", 1), :, x], self.from_core.at[:, x], self.cs.at[i, x], self.cr.at[i, x], "c", 1)

    def a_copies(self, first):
        p, i = self.p, self.i
        ny, nc, nz, nx = p.dims
        for k in range(1, ny if first == "y" else nx):
            def copy(k=k):
                if first == "y":
                    src, dst = self.own.at[p.at("y", k)], self.from_a.at[k - 1, pl.ds(0, nx)]
                else:
                    src, dst = self.own.at[:, p.at("x", k)], self.from_a.at[k - 1, pl.ds(0, ny)]
                return self.copy(src, dst, self.as_.at[i, k - 1], self.ar.at[i, k - 1], first, k)
            yield copy

    def b_copies(self, first):
        p, i = self.p, self.i
        ny, nc, nz, nx = p.dims
        second = {"x": "y", "y": "x"}[first]
        for k in range(1, ny if second == "y" else nx):
            def copy(k=k):
                src = self.own.at[p.at("y", k), p.x] if second == "y" else self.own.at[p.y, p.at("x", k)]
                return self.copy(src, self.from_b.at[k - 1], self.bs.at[i, k - 1], self.br.at[i, k - 1], second, k)
            yield copy

    def z_copies(self):
        p, i = self.p, self.i
        for k in range(1, p.dims[2]):
            yield lambda k=k: self.copy(
                self.own.at[p.y, p.x, p.at("z", k)], self.from_z.at[k - 1], self.zs.at[i, k - 1], self.zr.at[i, k - 1], "z", k)

    def by_core(self, body):
        if self.p.dims[1] == 1:
            body("y")
            return
        pl.when(self.p.c == 0)(lambda: body("y"))
        pl.when(self.p.c == 1)(lambda: body("x"))

    @staticmethod
    def add(into, terms):
        if len(terms) == 1:
            into[...] = into[...] + terms[0][...]
        elif terms:
            value = into[...].astype(jnp.float32)
            for term in terms:
                value = value + term[...].astype(jnp.float32)
            into[...] = value.astype(jnp.bfloat16)

    def start(self):
        for copy in self.core_copies():
            copy().start()
        for copy in self.loads():
            copy().start()

    def after_core(self):
        p = self.p
        ny, nc, nz, nx = p.dims
        for copy in self.loads():
            copy().wait()
        for copy in self.core_copies():
            copy().wait_recv()
        if nc > 1:
            def body(y, carry):
                self.add(self.own.at[y], [self.from_core.at[y]])
                return carry
            lax.fori_loop(0, ny, body, 0)

        def go(first):
            for copy in self.a_copies(first):
                copy().start()
        self.by_core(go)

    def after_a(self):
        p = self.p
        ny, nc, nz, nx = p.dims

        def go(first):
            for copy in self.a_copies(first):
                copy().wait_recv()
            n = ny if first == "y" else nx

            def body(j, carry):
                at = (p.y, j) if first == "y" else (j, p.x)
                self.add(self.own.at[at], [self.from_a.at[k, j] for k in range(n - 1)])
                return carry
            lax.fori_loop(0, nx if first == "y" else ny, body, 0)
            for copy in self.b_copies(first):
                copy().start()
        self.by_core(go)

    def after_b(self):
        p = self.p
        ny, nc, nz, nx = p.dims

        def go(first):
            for copy in self.b_copies(first):
                copy().wait_recv()
            n = nx if first == "y" else ny

            self.add(self.own.at[p.y, p.x], [self.from_b.at[k] for k in range(n - 1)])
        self.by_core(go)
        for copy in self.z_copies():
            copy().start()

    def after_z(self):
        p = self.p
        for copy in self.z_copies():
            copy().wait_recv()
        value = self.own[p.y, p.x, p.z].astype(jnp.float32)
        for k in range(p.dims[2] - 1):
            value = value + self.from_z[k].astype(jnp.float32)
        self.out[...] = value

    def finish(self):
        for copy in self.core_copies():
            copy().wait_send()

        def go(first):
            for copy in self.a_copies(first):
                copy().wait_send()
            for copy in self.b_copies(first):
                copy().wait_send()
        self.by_core(go)
        for copy in self.z_copies():
            copy().wait_send()

    def stages(self):
        return [self.start, self.after_core, self.after_a, self.after_b, self.after_z, self.finish]


def run_stages(jobs):
    n, depth = len(jobs), len(jobs[0])
    for t in range(n + depth - 1):
        for i in range(n):
            if 0 <= t - i < depth:
                jobs[i][t - i]()


def scatter_kernel(dims, n, *refs):
    place = Place(dims)
    src, out, rest = refs[:n], refs[n:2 * n], refs[2 * n:]
    bufs, sems = rest[:5 * n], rest[5 * n:]
    enter(place)
    run_stages([
        Scatter(place, bufs[5 * i], out[i], bufs[5 * i + 1:5 * i + 5], sems, i, src[i]).stages() for i in range(n)
    ])


def scatter(dims, arrays, collective_id):
    n = len(arrays)
    devices = math.prod(dims)
    blocks = [(a.shape[0] // devices,) + a.shape[1:] for a in arrays]
    shaped = [a.reshape(dims + b) for a, b in zip(arrays, blocks)]
    scratch = []
    ny, nc, nz, nx = dims
    for b in blocks:
        scratch += [pltpu.VMEM((ny, nx, nz) + b, jnp.bfloat16)] + Scatter.buf_shapes(dims, b)
    return pl.pallas_call(
        functools.partial(scatter_kernel, dims, n),
        out_shape=[jax.ShapeDtypeStruct(b, jnp.float32) for b in blocks],
        in_specs=[ANY] * n,
        out_specs=[pl.BlockSpec(memory_space=pltpu.VMEM)] * n,
        scratch_shapes=scratch + Scatter.sem_shapes(dims, n),
        compiler_params=pltpu.CompilerParams(
            collective_id=collective_id, has_side_effects=True, vmem_limit_bytes=56 << 20),
        name="scatter_gradients",
    )(*shaped)


READY = 3
CHUNK = 256
SLOTS = 4
TOKENS = 512


def mlp_kernel(dims, chunks, ready, *refs):
    (middle, normed, cot, gain, down, early, local_gu, output, g_middle, g_gain, g_gate_up, g_down, gathered,
     normed_t, total, inner_s, grads_s, weights, held, from_core, from_a, from_b, from_z, load) = refs[:24]
    sems = refs[24:]
    ng = len(Gather.sem_shapes(dims, 1))
    place = Place(dims)
    j = pl.program_id(0)
    seq = normed.shape[0]
    block = local_gu.shape[1]
    ny, nc, nz, nx = dims

    def gather_at(m):
        return Gather(place, local_gu.at[m], gathered.at[m - ready], sems[:ng], m - ready)

    def scatter_at(m):
        bufs = [b.at[m] for b in (from_core, from_a, from_b, from_z)]
        return Scatter(place, held.at[lax.rem(m, SLOTS)], g_gate_up.at[m], bufs, sems[ng:], m)

    def do(m, first, body):
        if isinstance(m, int):
            if first <= m < chunks:
                body(m)
            return
        pl.when((m >= first) & (m < chunks))(lambda: body(m))

    def fetch(m, slot, start):
        def go(src):
            copy = pltpu.make_async_copy(src, weights.at[slot], load.at[slot])
            copy.start() if start else copy.wait()
        if start:
            pl.when(m < ready)(lambda: go(early.at[jnp.minimum(m, ready - 1)]))
            pl.when((m >= ready) & (m < chunks))(lambda: go(gathered.at[jnp.clip(m - ready, 0, chunks - ready - 1)]))
        else:
            go(early.at[0])

    def tick_a(j):
        do(j + 4, ready + 2, lambda m: gather_at(m).start())
        do(j + 1, ready, lambda m: gather_at(m).after_second())
        do(j + 2, ready, lambda m: gather_at(m).after_first())
        do(j - 3, 0, lambda m: scatter_at(m).after_b())

    def tick_b(j):
        do(j - 1, 0, lambda m: scatter_at(m).after_core())
        do(j + 3, ready, lambda m: gather_at(m).after_z())
        do(j - 2, 0, lambda m: scatter_at(m).after_a())
        do(j + 1, ready, lambda m: gather_at(m).finish())

    def tick_c(j):
        do(j, 0, lambda m: scatter_at(m).start())
        do(j - 3, 0, lambda m: scatter_at(m).after_z())
        do(j - 3, 0, lambda m: scatter_at(m).finish())

    @pl.when(j == 0)
    def _():
        fetch(0, 0, True)
        enter(place)
        for m in range(ready, min(ready + 2, chunks)):
            gather_at(m).start()
        normed_t[...] = normed[...].T

    slot = lax.rem(j, 2)
    fetch(j, slot, False)
    w = weights.at[slot]
    weight = lambda: w[...].reshape(D, -1)

    def tokens_part(t):
        r = slice(t * TOKENS, (t + 1) * TOKENS)
        both = dot(normed[r, :], weight())
        gate, up = both[:, :CHUNK], both[:, CHUNK:]
        sig = jax.nn.sigmoid(gate)
        silu = gate * sig
        inner = (silu * up).astype(bf16)
        inner_s[r, :] = inner
        g_inner = dot(cot[r, :], down[...], NT)
        g_gate = (g_inner * up * sig * (1.0 + gate * (1.0 - sig))).astype(bf16)
        grads = jnp.concatenate([g_gate, (g_inner * silu).astype(bf16)], axis=1)
        grads_s[r, :] = grads
        out, back = dot(inner, down[...]), dot(grads, weight(), NT)

        @pl.when(j == 0)
        def _():
            total[r, :] = out
            g_middle[r, :] = back

        @pl.when(j > 0)
        def _():
            total[r, :] += out
            g_middle[r, :] += back

    parts = seq // TOKENS
    tick_a(j)
    for t in range(parts):
        tokens_part(t)
        if t == parts // 2 - 1 or parts == 1:
            tick_b(j)
            fetch(j + 1, 1 - slot, True)
    g_weights = dot(normed_t[...], grads_s[...]).astype(bf16)
    at = held.at[lax.rem(j, SLOTS)]
    for y in range(ny):
        for c in range(nc):
            for z in range(nz):
                for x in range(nx):
                    row = (((y * nc + c) * nz + z) * nx + x) * block
                    at[c, y, x, z] = g_weights[row:row + block]
    tick_c(j)
    g_down[...] = dot(inner_s[...], cot[...], TN).astype(bf16)

    @pl.when(j == chunks - 1)
    def _():
        for t in range(seq // 256):
            r = slice(t * 256, t * 256 + 256)
            m = middle[r, :]
            s = rms(m)
            output[r, :] = (m + total[r, :]).astype(bf16)
            g_normed = g_middle[r, :]
            u = g_normed * gain[...]
            g_middle[r, :] = cot[r, :].astype(f32) + s * u - m * (s * s * s * jnp.mean(u * m, axis=-1, keepdims=True))
            part = jnp.sum(g_normed * m * s, axis=0, keepdims=True)
            if t == 0:
                g_gain[...] = part
            else:
                g_gain[...] += part
        for k in range(3):
            tick_a(chunks + k)
            tick_b(chunks + k)
            tick_c(chunks + k)


def mlp(dims, middle, normed, cot, gain, down, early, local_gu, collective_id):
    chunks, block, width = local_gu.shape
    ready = early.shape[0]
    seq = normed.shape[0]
    ny, nc, nz, nx = dims
    whole = lambda *s: pl.BlockSpec(s, lambda i: (0,) * len(s))
    vmem = lambda s, t: pltpu.VMEM(s, t)
    return pl.pallas_call(
        functools.partial(mlp_kernel, dims, chunks, ready),
        grid=(chunks,),
        out_shape=[
            jax.ShapeDtypeStruct((seq, D), bf16),
            jax.ShapeDtypeStruct((seq, D), f32),
            jax.ShapeDtypeStruct((1, D), f32),
            jax.ShapeDtypeStruct((chunks, block, width), f32),
            jax.ShapeDtypeStruct((chunks * CHUNK, D), bf16),
            jax.ShapeDtypeStruct((chunks - ready,) + dims + (block, width), bf16),
        ],
        in_specs=[whole(seq, D), whole(seq, D), whole(seq, D), whole(1, D), pl.BlockSpec((CHUNK, D), lambda i: (i, 0)), ANY, ANY],
        out_specs=[whole(seq, D), whole(seq, D), whole(1, D), whole(chunks, block, width),
                   pl.BlockSpec((CHUNK, D), lambda i: (i, 0)), ANY],
        scratch_shapes=[
            vmem((D, seq), bf16), vmem((seq, D), f32), vmem((seq, CHUNK), bf16), vmem((seq, width), bf16),
            vmem((2,) + dims + (block, width), bf16), vmem((SLOTS, nc, ny, nx, nz, block, width), bf16),
        ] + Scatter.buf_shapes(dims, (block, width), (chunks,)) + [pltpu.SemaphoreType.DMA((2,))]
        + Gather.sem_shapes(dims, chunks - ready) + Scatter.sem_shapes(dims, chunks),
        compiler_params=pltpu.CompilerParams(
            collective_id=collective_id, has_side_effects=True, vmem_limit_bytes=62 << 20),
        name="mlp",
    )(middle, normed, cot, gain, down, early, local_gu)


def plain_mlp(middle, normed_two, cotangent, gain, gate_w, up_w, down_w):
    gate, up = dot(normed_two, gate_w), dot(normed_two, up_w)
    sig = jax.nn.sigmoid(gate)
    silu = gate * sig
    inner = (silu * up).astype(bf16)
    output = (middle + dot(inner, down_w)).astype(bf16)
    grad_inner = dot(cotangent, down_w, NT)
    grad_gate = (grad_inner * up * sig * (1.0 + gate * (1.0 - sig))).astype(bf16)
    grad_up = (grad_inner * silu).astype(bf16)
    grad_normed = dot(grad_gate, gate_w, NT) + dot(grad_up, up_w, NT)
    scale = rms(middle)
    gained = grad_normed * gain
    grad_middle = (
        cotangent.astype(f32)
        + scale * gained
        - middle * scale**3 * jnp.mean(gained * middle, axis=-1, keepdims=True)
    )
    grad_gain = jnp.sum(grad_normed * middle * scale, axis=0, keepdims=True)
    outer_sum = lambda left, right: dot(left, right, TN).astype(bf16)
    return (
        output, grad_middle, grad_gain,
        outer_sum(inner, cotangent), outer_sum(normed_two, grad_gate), outer_sum(normed_two, grad_up),
    )


def on_device(
    dims,
    tokens,
    doc_ids,
    norm_gain,
    w_query_heads,
    w_query_dims,
    w_key_heads,
    w_key_dims,
    w_value_heads,
    w_value_dims,
    w_output,
    mlp_gain,
    w_gate,
    w_up,
    w_down,
    out_grad,
):
    seq_len = tokens.shape[0] * tokens.shape[1]
    tables = tuple(jnp.asarray(t) for t in rope_tables(seq_len) + (spread_table(),))
    parts = (w_query_dims, w_key_dims, w_value_dims, w_query_heads, w_key_heads, w_value_heads)
    edges = [0]
    for part in parts:
        edges.append(edges[-1] + part.shape[1])
    gains_at = edges[-1]
    packed = jnp.concatenate(
        parts
        + (norm_gain[:, None], mlp_gain[:, None])
        + (jnp.zeros((norm_gain.shape[0], PACKED - gains_at - 2), bf16),),
        axis=1,
    )
    block = w_gate.shape[0]
    fused = block % 16 == 0 and w_gate.shape[1] % CHUNK == 0 and seq_len % TOKENS == 0
    if fused:
        chunked = lambda w: w.reshape(block, -1, CHUNK).transpose(1, 0, 2)
        gate_up = jnp.concatenate([chunked(w_gate), chunked(w_up)], axis=2)
        packed_w, output_w, down_w, *early = gather(
            dims, [packed, w_output, w_down] + [gate_up[i] for i in range(READY)], 0
        )
        early = jnp.stack(early).reshape((READY,) + dims + gate_up.shape[1:])
    else:
        packed_w, output_w, gate_w, up_w, down_w = gather(
            dims, [packed, w_output, w_gate, w_up, w_down], 0
        )
    gain_one, gain_two = [packed_w[:, gains_at + i].astype(f32).reshape(1, D) for i in (0, 1)]

    inputs = tokens.reshape(seq_len, D)
    doc_row, doc_col = doc_ids.reshape(1, seq_len), doc_ids.reshape(seq_len, 1)
    normed, factors, query, key, value = make_factors(inputs, gain_one, packed_w, tables)
    mixed, lse = attend(doc_col, doc_row, query, key, value)

    outer_sum = lambda left, right: dot(left, right, TN).astype(bf16)
    middle = inputs.astype(f32) + dot(mixed, output_w)
    normed_two = (middle * rms(middle) * gain_two).astype(bf16)
    cotangent = out_grad.reshape(seq_len, D)
    if fused:
        output, grad_middle, grad_mlp_gain, gate_up_out, grad_down, _ = mlp(
            dims, middle, normed_two, cotangent, gain_two, down_w, early, gate_up, 1
        )
        mlp_grads = [grad_down]
    else:
        output, grad_middle, grad_mlp_gain, *mlp_grads = plain_mlp(
            middle, normed_two, cotangent, gain_two, gate_w, up_w, down_w
        )
    grad_branch = grad_middle.astype(bf16)
    grad_mixed = dot(grad_branch, output_w, NT).astype(bf16)

    grad_query, grad_key, grad_value = attend_back(
        doc_col, doc_row, query, key, value, grad_mixed, lse
    )
    grad_factors, grad_tokens, grad_norm_gain = factors_back(
        inputs, gain_one, packed_w, tables, factors, grad_query, grad_key, grad_value, grad_middle
    )
    gains = jnp.stack([grad_norm_gain[0], grad_mlp_gain[0]], axis=1).astype(bf16)
    packed_grad = lax.dynamic_update_slice(outer_sum(normed, grad_factors), gains, (0, gains_at))
    *mlp_out, output_out, packed_out = scatter(
        dims, mlp_grads + [outer_sum(mixed, grad_branch), packed_grad], 2
    )
    if fused:
        whole = lambda g: g.transpose(1, 0, 2).reshape(block, -1)
        mlp_out += [whole(gate_up_out[:, :, :CHUNK]), whole(gate_up_out[:, :, CHUNK:])]
    down_out, gate_out, up_out = mlp_out
    dims_and_heads = [packed_out[:, lo:hi] for lo, hi in zip(edges, edges[1:])]
    grads = [g for pair in zip(dims_and_heads[3:], dims_and_heads[:3]) for g in pair]
    return (
        output.reshape(tokens.shape),
        grad_tokens.reshape(tokens.shape),
        packed_out[:, gains_at],
        *grads,
        output_out,
        packed_out[:, gains_at + 1],
        gate_out,
        up_out,
        down_out,
    )


def solution(mesh):
    rows, matrix, vector = P(("dp", "fsdp"), None, None), P(("dp", "fsdp"), None), P(("dp", "fsdp"))
    return jax.shard_map(
        functools.partial(on_device, grid_of(mesh)),
        mesh=mesh,
        in_specs=(rows, matrix, vector) + (matrix,) * 7 + (vector,) + (matrix,) * 3 + (rows,),
        out_specs=(rows, rows, vector) + (matrix,) * 7 + (vector,) + (matrix,) * 3,
        check_vma=False,
    )
```

```python
import functools
import math

import jax
import jax.numpy as jnp
import numpy as np
from jax import lax
from jax.experimental import pallas as pl
from jax.experimental.pallas import tpu as pltpu
from jax.sharding import PartitionSpec as P

MESH = pl.DeviceIdType.MESH
D, H, DH, RQ, RK = 1024, 16, 64, 6, 2
PACKED = 896
DIMS, HEADS = 640, 128
BLOCK = 256
BACK = 512
NEG = -1e30
epsilon = 1e-06
theta_base = 10000.0
f32, bf16 = jnp.float32, jnp.bfloat16
NT = (((1,), (1,)), ((), ()))
NN = (((1,), (0,)), ((), ()))
TN = (((0,), (0,)), ((), ()))


def dot(a, b, dims=NN):
    return lax.dot_general(a, b, dims, preferred_element_type=f32)


def params(**kw):
    return pltpu.CompilerParams(vmem_limit_bytes=56 << 20, **kw)


def rope_tables(seq_len):
    half = DH // 2
    position = np.arange(seq_len, dtype=np.float32)
    inverse = np.exp(-math.log(theta_base) * 2.0 * np.arange(half, dtype=np.float32) / np.float32(2.0 * half)).astype(np.float32)
    angle = (position[:, None] * inverse[None, :]).astype(np.float32)
    cosine, sine = np.cos(angle), np.sin(angle)
    return (np.concatenate([cosine] * 4, 1), np.concatenate([-sine, sine] * 2, 1))


def spread_table():
    out = np.zeros((8, 2 * HEADS, H * DH), np.float32)
    for j in range(8):
        for h in range(H):
            out[j, [j * H + h, HEADS + j * H + h], h * DH:(h + 1) * DH] = 1.0
    return out.astype(jnp.bfloat16)


def low_lane(shape):
    return lax.rem(lax.broadcasted_iota(jnp.int32, shape, 1), 128) < 64


def first_half(shape):
    return lax.rem(lax.broadcasted_iota(jnp.int32, shape, 1), 64) < 32


def turn(x, cosine, sine):
    partner = jnp.where(first_half(x.shape), pltpu.roll(x, 96, 1), pltpu.roll(x, 32, 1))
    return x * cosine + partner * sine


def split_bf16(x):
    hi = x.astype(bf16)
    return jnp.concatenate([hi, (x - hi.astype(f32)).astype(bf16)], axis=1)


def twice(x, rank):
    rolled = pltpu.roll(x, 64, 1)
    low = low_lane(x.shape)
    return jnp.where(low, x, rolled) if rank % 2 == 0 else jnp.where(low, rolled, x)


def wide(x):
    return jnp.concatenate([x] * (H * DH // 128), axis=1)


def rms(x):
    return lax.rsqrt(jnp.mean(x * x, axis=-1, keepdims=True) + epsilon)


FACTORS = ((0, RQ, 0), (RQ, RK, 3), (0, RK, 4))


def factors_step(tokens, gain, weight, cosine, sine, spread, normed, factors, query, key, value):
    x = tokens[...].astype(f32)
    n = (x * rms(x) * gain).astype(bf16)
    normed[...] = n
    f = dot(n, weight)
    pairs = [f[:, 128 * i:128 * i + 128] for i in range(DIMS // 128)]
    pairs = [turn(p, cosine[...], sine[...]) if i < 4 else p for i, p in enumerate(pairs)]
    for i, p in enumerate(pairs):
        factors[:, 128 * i:128 * i + 128] = p
    factors[:, DIMS:] = f[:, DIMS:]
    heads_qk = split_bf16(f[:, DIMS:DIMS + HEADS])
    heads_v = split_bf16(f[:, DIMS + HEADS:])
    for out, heads, (at, ranks, pair), scale in zip(
        (query, key, value), (heads_qk, heads_qk, heads_v), FACTORS, (0.125, 1.0, 1.0)
    ):
        total = None
        for r in range(ranks):
            term = dot(heads, spread[at + r]) * wide(twice(pairs[pair + r // 2], r))
            total = term if total is None else total + term
        rounded = (total * (1.0 / ranks)).astype(bf16)
        rounded = rounded * jnp.asarray(scale, bf16) if scale != 1.0 else rounded
        for p, ref in enumerate(out):
            ref[...] = rounded[:, 128 * p:128 * p + 128]


def factors_kernel(tokens, gain, weight, cosine, sine, spread, normed, factors, query, key, value):
    outs = [[r.at[p] for p in range(H // 2)] for r in (query, key, value)]
    factors_step(tokens, gain[...], weight[...], cosine, sine, spread, normed, factors, *outs)


def make_factors(tokens, gain, weight, tables):
    cosine, sine, spread = tables
    seq = tokens.shape[0]
    row = lambda width: pl.BlockSpec((BLOCK, width), lambda i: (i, 0))
    whole = lambda a: pl.BlockSpec(a.shape, lambda i: (0,) * a.ndim)
    return pl.pallas_call(
        factors_kernel,
        grid=(seq // BLOCK,),
        out_shape=[
            jax.ShapeDtypeStruct((seq, D), bf16),
            jax.ShapeDtypeStruct((seq, PACKED), f32),
        ] + [jax.ShapeDtypeStruct((H // 2, seq, 128), bf16)] * 3,
        in_specs=[row(D), whole(gain), whole(weight), row(128), row(128), whole(spread)],
        out_specs=[row(D), row(PACKED)] + [pl.BlockSpec((H // 2, BLOCK, 128), lambda i: (0, i, 0))] * 3,
        compiler_params=params(),
        name="factors",
    )(tokens, gain, weight, cosine, sine, spread)


def allowed_t(doc_col, doc_row, k0, kn, q0, qn):
    same = doc_col[k0:k0 + kn, :] == doc_row[:, q0:q0 + qn]
    if k0 + kn - 1 > q0:
        k_at = k0 + lax.broadcasted_iota(jnp.int32, (kn, qn), 0)
        q_at = q0 + lax.broadcasted_iota(jnp.int32, (kn, qn), 1)
        same = same & (k_at <= q_at)
    return same


def halves(x):
    low = low_lane(x.shape)
    zero = jnp.zeros_like(x)
    return jnp.where(low, x, zero), jnp.where(low, zero, x)


def attend_kernel(doc_col, doc_row, query, key, value, mixed, lse):
    seq = query.shape[0]
    v_half = halves(value[...])
    for q0 in range(0, seq, BLOCK):
        lo = max(0, q0 - BACK)
        kn = q0 + BLOCK - lo
        ok = allowed_t(doc_col, doc_row, lo, kn, q0, BLOCK)
        probs = []
        for h, q in enumerate(halves(query[q0:q0 + BLOCK, :])):
            s = jnp.where(ok, dot(key[lo:lo + kn, :], q, NT), NEG)
            top = jnp.max(s, axis=0, keepdims=True)
            e = jnp.exp(s - top)
            total = jnp.sum(e, axis=0, keepdims=True)
            probs.append((e * (1.0 / total)).astype(bf16))
            lse[0, h:h + 1, q0:q0 + BLOCK] = top + jnp.log(total)
        values = jnp.concatenate([v[lo:lo + kn] for v in v_half], axis=0)
        mixed[q0:q0 + BLOCK, :] = dot(jnp.concatenate(probs, axis=0), values, TN).astype(bf16)


def attend(doc_col, doc_row, query, key, value):
    pairs, seq, _ = query.shape
    whole = lambda a: pl.BlockSpec(a.shape, lambda i: (0,) * a.ndim)
    pair = pl.BlockSpec((seq, 128), lambda i: (0, i))
    return pl.pallas_call(
        lambda dc, dr, q, k, v, *outs: attend_kernel(dc, dr, q.at[0], k.at[0], v.at[0], *outs),
        grid=(pairs,),
        out_shape=[jax.ShapeDtypeStruct((seq, H * DH), bf16), jax.ShapeDtypeStruct((pairs, 2, seq), f32)],
        in_specs=[whole(doc_col), whole(doc_row)] + [pl.BlockSpec((1, seq, 128), lambda i: (i, 0, 0))] * 3,
        out_specs=[pair, pl.BlockSpec((1, 2, seq), lambda i: (i, 0, 0))],
        compiler_params=params(),
        name="attend",
    )(doc_col, doc_row, query, key, value)


def attend_back_kernel(doc_col, doc_row, query, key, value, grad, lse, g_query, g_key, g_value):
    seq = query.shape[0]
    k_half = halves(key[...])
    for q0 in range(0, seq, BLOCK):
        lo = max(0, q0 - BACK)
        kn = q0 + BLOCK - lo
        ok = allowed_t(doc_col, doc_row, lo, kn, q0, BLOCK)
        ps, ds = [], []
        q_half, g_half = halves(query[q0:q0 + BLOCK, :]), halves(grad[q0:q0 + BLOCK, :])
        for h in (0, 1):
            s = dot(key[lo:lo + kn, :], q_half[h], NT)
            p = jnp.where(ok, jnp.exp(s - lse[0, h:h + 1, q0:q0 + BLOCK]), 0.0)
            pd = p * dot(value[lo:lo + kn, :], g_half[h], NT)
            ps.append(p.astype(bf16))
            ds.append((pd - p * jnp.sum(pd, axis=0, keepdims=True)).astype(bf16))
        to_value = dot(jnp.concatenate(ps, 1), jnp.concatenate(g_half, 0))
        to_key = dot(jnp.concatenate(ds, 1), jnp.concatenate(q_half, 0))
        if q0 > lo:
            g_value[lo:q0, :] += to_value[:q0 - lo]
            g_key[lo:q0, :] += to_key[:q0 - lo]
        g_value[q0:q0 + BLOCK, :] = to_value[q0 - lo:]
        g_key[q0:q0 + BLOCK, :] = to_key[q0 - lo:]
        keys = jnp.concatenate([k[lo:lo + kn] for k in k_half], 0)
        g_query[q0:q0 + BLOCK, :] = dot(jnp.concatenate(ds, 0), keys, TN) * 0.125


def attend_back(doc_col, doc_row, query, key, value, grad, lse):
    pairs, seq, _ = query.shape
    whole = lambda a: pl.BlockSpec(a.shape, lambda i: (0,) * a.ndim)
    pair = pl.BlockSpec((seq, 128), lambda i: (0, i))
    return pl.pallas_call(
        lambda dc, dr, q, k, v, *rest: attend_back_kernel(dc, dr, q.at[0], k.at[0], v.at[0], *rest),
        grid=(pairs,),
        out_shape=[jax.ShapeDtypeStruct((seq, H * DH), f32)] * 3,
        in_specs=[whole(doc_col), whole(doc_row)] + [pl.BlockSpec((1, seq, 128), lambda i: (i, 0, 0))] * 3 + [pair, pl.BlockSpec((1, 2, seq), lambda i: (i, 0, 0))],
        out_specs=[pair] * 3,
        compiler_params=params(),
        name="attend_back",
    )(doc_col, doc_row, query, key, value, grad, lse)


def factors_back_step(step, tokens, gain, weight, cosine, sine, spread, factors, g_query, g_key, g_value, g_middle,
                      g_factors, g_tokens, g_gain):
    pairs = [factors[:, 128 * i:128 * i + 128] for i in range(DIMS // 128)]
    heads_qk = split_bf16(factors[:, DIMS:DIMS + HEADS])
    heads_v = split_bf16(factors[:, DIMS + HEADS:])
    g_heads = [None, None]
    for grad, heads, which, (at, ranks, pair) in zip(
        (g_query, g_key, g_value), (heads_qk, heads_qk, heads_v), (0, 0, 1), FACTORS
    ):
        g = grad * (1.0 / ranks)
        folded = []
        for r in range(ranks):
            product = (g * wide(twice(pairs[pair + r // 2], r))).astype(bf16)
            part = dot(product, spread[at + r, :HEADS, :], NT)
            g_heads[which] = part if g_heads[which] is None else g_heads[which] + part
            full = g * dot(heads, spread[at + r])
            folded.append(sum(full[:, 128 * i:128 * i + 128] for i in range(H * DH // 128)))
        for r in range(0, ranks, 2):
            a, b = folded[r], folded[r + 1]
            low = low_lane(a.shape)
            mine = jnp.where(low, a, b)
            other = jnp.where(low, pltpu.roll(a, 64, 1), pltpu.roll(b, 64, 1))
            both = mine + other
            i = pair + r // 2
            if i < 4:
                both = turn(both, cosine[...], -sine[...])
            g_factors[:, 128 * i:128 * i + 128] = both.astype(bf16)
    g_factors[:, DIMS:DIMS + HEADS] = g_heads[0].astype(bf16)
    g_factors[:, DIMS + HEADS:] = g_heads[1].astype(bf16)
    g_normed = dot(g_factors[...], weight, NT)
    x = tokens[...].astype(f32)
    r1 = rms(x)
    u = g_normed * gain
    part = jnp.sum(g_normed * x * r1, axis=0, keepdims=True)

    @pl.when(step == 0)
    def _():
        g_gain[...] = part

    @pl.when(step > 0)
    def _():
        g_gain[...] += part

    g_tokens[...] = (g_middle[...] + r1 * u - x * (r1 * r1 * r1 * jnp.mean(u * x, axis=-1, keepdims=True))).astype(bf16)


def factors_back_kernel(tokens, gain, weight, cosine, sine, spread, factors, g_query, g_key, g_value, *rest):
    factors_back_step(pl.program_id(0), tokens, gain[...], weight[...], cosine, sine, spread, factors,
                      g_query[...], g_key[...], g_value[...], *rest)


def factors_back(tokens, gain, weight, tables, factors, g_query, g_key, g_value, g_middle):
    cosine, sine, spread = tables
    seq = tokens.shape[0]
    row = lambda width: pl.BlockSpec((BLOCK, width), lambda i: (i, 0))
    whole = lambda a: pl.BlockSpec(a.shape, lambda i: (0,) * a.ndim)
    return pl.pallas_call(
        factors_back_kernel,
        grid=(seq // BLOCK,),
        out_shape=[
            jax.ShapeDtypeStruct((seq, PACKED), bf16),
            jax.ShapeDtypeStruct((seq, D), bf16),
            jax.ShapeDtypeStruct((1, D), f32),
        ],
        in_specs=[row(D), whole(gain), whole(weight), row(128), row(128), whole(spread), row(PACKED)]
        + [row(H * DH)] * 3 + [row(D)],
        out_specs=[row(PACKED), row(D), pl.BlockSpec((1, D), lambda i: (0, 0))],
        compiler_params=params(),
        name="factors_back",
    )(tokens, gain, weight, cosine, sine, spread, factors, g_query, g_key, g_value, g_middle)

ANY = pl.BlockSpec(memory_space=pl.ANY)


def grid_of(mesh):
    nd, nf = mesh.shape["dp"], mesh.shape["fsdp"]
    nc = math.gcd(2, nd)
    nz = math.gcd(4, nf)
    return (nd // nc, nc, nz, nf // nz)


class Place:
    def __init__(self, dims):
        self.dims = dims
        ny, nc, nz, nx = dims
        dp, fs = lax.axis_index("dp"), lax.axis_index("fsdp")
        self.y, self.c = lax.div(dp, nc), lax.rem(dp, nc)
        self.z, self.x = lax.div(fs, nx), lax.rem(fs, nx)

    def at(self, axis, k):
        n = self.dims["yczx".index(axis)]
        return lax.rem(getattr(self, axis) + k + n, n)

    def device(self, axis=None, k=0):
        ny, nc, nz, nx = self.dims
        put = {a: getattr(self, a) for a in "yczx"}
        if axis is not None:
            put[axis] = self.at(axis, k)
        return (put["y"] * nc + put["c"], put["z"] * nx + put["x"])


def peers_of(dims):
    ny, nc, nz, nx = dims
    return [(a, k) for a, n in (("y", ny), ("c", nc), ("z", nz), ("x", nx)) for k in range(1, n)]


def enter(place):
    barrier = pltpu.get_barrier_semaphore()
    peers = peers_of(place.dims)
    for axis, k in peers:
        pl.semaphore_signal(barrier, inc=1, device_id=place.device(axis, k), device_id_type=MESH)
    pl.semaphore_wait(barrier, len(peers))


class Gather:
    def __init__(self, place, src, dst, sems, i):
        self.p, self.src, self.dst, self.i = place, src, dst, i
        self.local, self.zs, self.zr, self.as_, self.ar, self.bs, self.br, self.cs, self.cr = sems

    @staticmethod
    def sem_shapes(dims, n):
        ny, nc, nz, nx = dims
        dma = pltpu.SemaphoreType.DMA
        m = max(nx, ny) - 1
        one = lambda k: dma((n, max(1, k)))
        return [dma((n,)), one(nz - 1), one(nz - 1), one(m), one(m), one(m), one(m), one(nx + ny - 1), one(nx + ny - 1)]

    def copy(self, ref_src, ref_dst, send, recv, axis, k):
        return pltpu.make_async_remote_copy(
            src_ref=ref_src, dst_ref=ref_dst, send_sem=send, recv_sem=recv,
            device_id=self.p.device(axis, k), device_id_type=MESH,
        )

    def z_copies(self):
        p, i = self.p, self.i
        nz = p.dims[2]
        mine = self.dst.at[p.y, p.c, p.z, p.x]
        def one(k, back):
            if back:
                ref = self.dst.at[p.y, p.c, p.at("z", -k), p.x]
                return self.copy(ref, ref, self.zs.at[i, k - 1], self.zr.at[i, k - 1], "z", k)
            return self.copy(self.src, mine, self.zs.at[i, k - 1], self.zr.at[i, k - 1], "z", k)

        return [[functools.partial(one, k, back) for k in range(1, nz)] for back in (False, True)]

    def part(self, first, step, y, x, c):
        every = slice(None)
        if step == 0:
            return self.dst.at[y, c, :, x]
        return self.dst.at[y, c] if first == "x" else self.dst.at[:, c, :, x]

    def side_copies(self, first, step):
        p, i = self.p, self.i
        axis = first if step == 0 else {"x": "y", "y": "x"}[first]
        n = p.dims["yczx".index(axis)]
        s, r = ((self.as_, self.ar), (self.bs, self.br))[step]

        def one(k, back):
            y, x = p.y, p.x
            if back:
                y, x = (p.y, p.at("x", -k)) if axis == "x" else (p.at("y", -k), p.x)
            ref = self.part(first, step, y, x, p.c)
            return self.copy(ref, ref, s.at[i, k - 1], r.at[i, k - 1], axis, k)

        return [[functools.partial(one, k, back) for k in range(1, n)] for back in (False, True)]

    def core_copies(self, first, c):
        p, i = self.p, self.i
        second = {"x": "y", "y": "x"}[first]
        lists, j = [], 0
        for step, axis in ((0, None), (0, first), (1, second)):
            now = []
            count = 1 if axis is None else p.dims["yczx".index(axis)] - 1
            for k in range(1, count + 1):
                def one(axis=axis, step=step, k=k, j=j):
                    y = p.at("y", -k) if axis == "y" else p.y
                    x = p.at("x", -k) if axis == "x" else p.x
                    ref = self.part(first, step, y, x, c)
                    return self.copy(ref, ref, self.cs.at[i, j], self.cr.at[i, j], "c", 1)

                now.append(one)
                j += 1
            lists.append(now)
        return lists

    def start(self):
        p = self.p
        mine = self.dst.at[p.y, p.c, p.z, p.x]
        pltpu.make_async_copy(self.src, mine, self.local.at[self.i]).start()
        for copy in self.z_copies()[0]:
            copy().start()

    def by_core(self, body):
        if self.p.dims[1] == 1:
            body("x")
            return
        pl.when(self.p.c == 0)(lambda: body("x"))
        pl.when(self.p.c == 1)(lambda: body("y"))

    def after_z(self):
        p = self.p
        mine = self.dst.at[p.y, p.c, p.z, p.x]
        pltpu.make_async_copy(self.src, mine, self.local.at[self.i]).wait()
        for copy in self.z_copies()[1]:
            copy().wait_recv()

        def body(first):
            for copy in self.side_copies(first, 0)[0]:
                copy().start()
            if p.dims[1] > 1:
                for copy in self.core_copies(first, p.c)[0]:
                    copy().start()

        self.by_core(body)

    def after_first(self):
        p = self.p

        def body(first):
            for copy in self.side_copies(first, 0)[1]:
                copy().wait_recv()
            for copy in self.side_copies(first, 1)[0]:
                copy().start()
            if p.dims[1] > 1:
                for copy in self.core_copies(first, p.c)[1]:
                    copy().start()

        self.by_core(body)

    def after_second(self):
        p = self.p

        def body(first):
            for copy in self.side_copies(first, 1)[1]:
                copy().wait_recv()
            if p.dims[1] > 1:
                for copy in self.core_copies(first, p.c)[2]:
                    copy().start()

        self.by_core(body)

    def finish(self):
        p = self.p
        for copy in self.z_copies()[0]:
            copy().wait_send()

        def body(first):
            for step in (0, 1):
                for copy in self.side_copies(first, step)[0]:
                    copy().wait_send()
            if p.dims[1] > 1:
                for now in self.core_copies(first, p.c):
                    for copy in now:
                        copy().wait_send()
                other = {"x": "y", "y": "x"}[first]
                for now in self.core_copies(other, p.at("c", 1)):
                    for copy in now:
                        copy().wait_recv()

        self.by_core(body)

    def stages(self):
        return [self.start, self.after_z, self.after_first, self.after_second, self.finish]


def gather_kernel(dims, n, *refs):
    place = Place(dims)
    src, dst, sems = refs[:n], refs[n:2 * n], refs[2 * n:]
    enter(place)
    jobs = [Gather(place, src[i], dst[i], sems, i).stages() for i in range(n)]
    run_stages(jobs)


def gather(dims, arrays, collective_id):
    n = len(arrays)
    outs = pl.pallas_call(
        functools.partial(gather_kernel, dims, n),
        out_shape=[jax.ShapeDtypeStruct(dims + a.shape, a.dtype) for a in arrays],
        in_specs=[ANY] * n,
        out_specs=[ANY] * n,
        scratch_shapes=Gather.sem_shapes(dims, n),
        compiler_params=pltpu.CompilerParams(collective_id=collective_id, has_side_effects=True),
        name="gather_weights",
    )(*arrays)
    return [o.reshape((-1,) + a.shape[1:]) for o, a in zip(outs, arrays)]


class Scatter:
    def __init__(self, place, held, out, bufs, sems, i, src=None):
        self.p, self.src, self.out, self.i = place, src, out, i
        self.own, self.away = (held, None) if src is not None else (held.at[place.c], held.at[place.at("c", 1)])
        self.from_core, self.from_a, self.from_b, self.from_z = bufs
        self.local, self.cs, self.cr, self.as_, self.ar, self.bs, self.br, self.zs, self.zr = sems

    @staticmethod
    def sem_shapes(dims, n):
        ny, nc, nz, nx = dims
        dma = pltpu.SemaphoreType.DMA
        m = max(nx, ny, 2) - 1
        return [dma((n, nx))] * 3 + [dma((n, m))] * 4 + [dma((n, max(1, nz - 1)))] * 2

    @staticmethod
    def buf_shapes(dims, block, lead=()):
        ny, nc, nz, nx = dims
        m = max(nx, ny, 2)
        buf = lambda *s: pltpu.VMEM(lead + s + block, jnp.bfloat16)
        return [buf(ny, nx, nz), buf(m - 1, m, nz), buf(m - 1, nz), buf(max(1, nz - 1))]

    def copy(self, src, dst, send, recv, axis, k):
        return pltpu.make_async_remote_copy(
            src_ref=src, dst_ref=dst, send_sem=send, recv_sem=recv,
            device_id=self.p.device(axis, k), device_id_type=MESH,
        )

    def loads(self):
        p, i = self.p, self.i
        if self.src is None:
            return
        for x in range(p.dims[3]):
            yield lambda x=x: pltpu.make_async_copy(self.src.at[:, p.c, :, x], self.own.at[:, x], self.local.at[i, x])

    def core_copies(self):
        p, i = self.p, self.i
        if p.dims[1] == 1:
            return
        if self.src is None:
            yield lambda: self.copy(self.away, self.from_core, self.cs.at[i, 0], self.cr.at[i, 0], "c", 1)
            return
        for x in range(p.dims[3]):
            yield lambda x=x: self.copy(
                self.src.at[:, p.at("c", 1), :, x], self.from_core.at[:, x], self.cs.at[i, x], self.cr.at[i, x], "c", 1)

    def a_copies(self, first):
        p, i = self.p, self.i
        ny, nc, nz, nx = p.dims
        for k in range(1, ny if first == "y" else nx):
            def copy(k=k):
                if first == "y":
                    src, dst = self.own.at[p.at("y", k)], self.from_a.at[k - 1, pl.ds(0, nx)]
                else:
                    src, dst = self.own.at[:, p.at("x", k)], self.from_a.at[k - 1, pl.ds(0, ny)]
                return self.copy(src, dst, self.as_.at[i, k - 1], self.ar.at[i, k - 1], first, k)
            yield copy

    def b_copies(self, first):
        p, i = self.p, self.i
        ny, nc, nz, nx = p.dims
        second = {"x": "y", "y": "x"}[first]
        for k in range(1, ny if second == "y" else nx):
            def copy(k=k):
                src = self.own.at[p.at("y", k), p.x] if second == "y" else self.own.at[p.y, p.at("x", k)]
                return self.copy(src, self.from_b.at[k - 1], self.bs.at[i, k - 1], self.br.at[i, k - 1], second, k)
            yield copy

    def z_copies(self):
        p, i = self.p, self.i
        for k in range(1, p.dims[2]):
            yield lambda k=k: self.copy(
                self.own.at[p.y, p.x, p.at("z", k)], self.from_z.at[k - 1], self.zs.at[i, k - 1], self.zr.at[i, k - 1], "z", k)

    def by_core(self, body):
        if self.p.dims[1] == 1:
            body("y")
            return
        pl.when(self.p.c == 0)(lambda: body("y"))
        pl.when(self.p.c == 1)(lambda: body("x"))

    @staticmethod
    def add(into, terms):
        if len(terms) == 1:
            into[...] = into[...] + terms[0][...]
        elif terms:
            value = into[...].astype(jnp.float32)
            for term in terms:
                value = value + term[...].astype(jnp.float32)
            into[...] = value.astype(jnp.bfloat16)

    def start(self):
        for copy in self.core_copies():
            copy().start()
        for copy in self.loads():
            copy().start()

    def after_core(self):
        p = self.p
        ny, nc, nz, nx = p.dims
        for copy in self.loads():
            copy().wait()
        for copy in self.core_copies():
            copy().wait_recv()
        if nc > 1:
            def body(y, carry):
                self.add(self.own.at[y], [self.from_core.at[y]])
                return carry
            lax.fori_loop(0, ny, body, 0)

        def go(first):
            for copy in self.a_copies(first):
                copy().start()
        self.by_core(go)

    def after_a(self):
        p = self.p
        ny, nc, nz, nx = p.dims

        def go(first):
            for copy in self.a_copies(first):
                copy().wait_recv()
            n = ny if first == "y" else nx

            def body(j, carry):
                at = (p.y, j) if first == "y" else (j, p.x)
                self.add(self.own.at[at], [self.from_a.at[k, j] for k in range(n - 1)])
                return carry
            lax.fori_loop(0, nx if first == "y" else ny, body, 0)
            for copy in self.b_copies(first):
                copy().start()
        self.by_core(go)

    def after_b(self):
        p = self.p
        ny, nc, nz, nx = p.dims

        def go(first):
            for copy in self.b_copies(first):
                copy().wait_recv()
            n = nx if first == "y" else ny

            self.add(self.own.at[p.y, p.x], [self.from_b.at[k] for k in range(n - 1)])
        self.by_core(go)
        for copy in self.z_copies():
            copy().start()

    def after_z(self):
        p = self.p
        for copy in self.z_copies():
            copy().wait_recv()
        value = self.own[p.y, p.x, p.z].astype(jnp.float32)
        for k in range(p.dims[2] - 1):
            value = value + self.from_z[k].astype(jnp.float32)
        self.out[...] = value

    def finish(self):
        for copy in self.core_copies():
            copy().wait_send()

        def go(first):
            for copy in self.a_copies(first):
                copy().wait_send()
            for copy in self.b_copies(first):
                copy().wait_send()
        self.by_core(go)
        for copy in self.z_copies():
            copy().wait_send()

    def stages(self):
        return [self.start, self.after_core, self.after_a, self.after_b, self.after_z, self.finish]


def run_stages(jobs):
    n, depth = len(jobs), len(jobs[0])
    for t in range(n + depth - 1):
        for i in range(n):
            if 0 <= t - i < depth:
                jobs[i][t - i]()


def scatter_kernel(dims, n, *refs):
    place = Place(dims)
    src, out, rest = refs[:n], refs[n:2 * n], refs[2 * n:]
    bufs, sems = rest[:5 * n], rest[5 * n:]
    enter(place)
    run_stages([
        Scatter(place, bufs[5 * i], out[i], bufs[5 * i + 1:5 * i + 5], sems, i, src[i]).stages() for i in range(n)
    ])


def scatter(dims, arrays, collective_id):
    n = len(arrays)
    devices = math.prod(dims)
    blocks = [(a.shape[0] // devices,) + a.shape[1:] for a in arrays]
    shaped = [a.reshape(dims + b) for a, b in zip(arrays, blocks)]
    scratch = []
    ny, nc, nz, nx = dims
    for b in blocks:
        scratch += [pltpu.VMEM((ny, nx, nz) + b, jnp.bfloat16)] + Scatter.buf_shapes(dims, b)
    return pl.pallas_call(
        functools.partial(scatter_kernel, dims, n),
        out_shape=[jax.ShapeDtypeStruct(b, jnp.float32) for b in blocks],
        in_specs=[ANY] * n,
        out_specs=[pl.BlockSpec(memory_space=pltpu.VMEM)] * n,
        scratch_shapes=scratch + Scatter.sem_shapes(dims, n),
        compiler_params=pltpu.CompilerParams(
            collective_id=collective_id, has_side_effects=True, vmem_limit_bytes=56 << 20),
        name="scatter_gradients",
    )(*shaped)


READY = 3
CHUNK = 256
SLOTS = 4
TOKENS = 512


def mlp_kernel(dims, chunks, ready, *refs):
    (middle, normed, cot, gain, down, early, local_gu, output, g_middle, g_gain, g_gate_up, g_down, gathered,
     normed_t, total, inner_s, grads_s, weights, held, from_core, from_a, from_b, from_z, load) = refs[:24]
    sems = refs[24:]
    ng = len(Gather.sem_shapes(dims, 1))
    place = Place(dims)
    j = pl.program_id(0)
    seq = normed.shape[0]
    block = local_gu.shape[1]
    ny, nc, nz, nx = dims

    def gather_at(m):
        return Gather(place, local_gu.at[m], gathered.at[m - ready], sems[:ng], m - ready)

    def scatter_at(m):
        bufs = [b.at[m] for b in (from_core, from_a, from_b, from_z)]
        return Scatter(place, held.at[lax.rem(m, SLOTS)], g_gate_up.at[m], bufs, sems[ng:], m)

    def do(m, first, body):
        if isinstance(m, int):
            if first <= m < chunks:
                body(m)
            return
        pl.when((m >= first) & (m < chunks))(lambda: body(m))

    def fetch(m, slot, start):
        def go(src):
            copy = pltpu.make_async_copy(src, weights.at[slot], load.at[slot])
            copy.start() if start else copy.wait()
        if start:
            pl.when(m < ready)(lambda: go(early.at[jnp.minimum(m, ready - 1)]))
            pl.when((m >= ready) & (m < chunks))(lambda: go(gathered.at[jnp.clip(m - ready, 0, chunks - ready - 1)]))
        else:
            go(early.at[0])

    def tick_a(j):
        do(j + 4, ready + 2, lambda m: gather_at(m).start())
        do(j + 1, ready, lambda m: gather_at(m).after_second())
        do(j + 2, ready, lambda m: gather_at(m).after_first())
        do(j - 3, 0, lambda m: scatter_at(m).after_b())

    def tick_b(j):
        do(j - 1, 0, lambda m: scatter_at(m).after_core())
        do(j + 3, ready, lambda m: gather_at(m).after_z())
        do(j - 2, 0, lambda m: scatter_at(m).after_a())
        do(j + 1, ready, lambda m: gather_at(m).finish())

    def tick_c(j):
        do(j, 0, lambda m: scatter_at(m).start())
        do(j - 3, 0, lambda m: scatter_at(m).after_z())
        do(j - 3, 0, lambda m: scatter_at(m).finish())

    @pl.when(j == 0)
    def _():
        fetch(0, 0, True)
        enter(place)
        for m in range(ready, min(ready + 2, chunks)):
            gather_at(m).start()
        normed_t[...] = normed[...].T

    slot = lax.rem(j, 2)
    fetch(j, slot, False)
    w = weights.at[slot]
    weight = lambda: w[...].reshape(D, -1)

    def tokens_part(t):
        r = slice(t * TOKENS, (t + 1) * TOKENS)
        both = dot(normed[r, :], weight())
        gate, up = both[:, :CHUNK], both[:, CHUNK:]
        sig = jax.nn.sigmoid(gate)
        silu = gate * sig
        inner = (silu * up).astype(bf16)
        inner_s[r, :] = inner
        g_inner = dot(cot[r, :], down[...], NT)
        g_gate = (g_inner * up * sig * (1.0 + gate * (1.0 - sig))).astype(bf16)
        grads = jnp.concatenate([g_gate, (g_inner * silu).astype(bf16)], axis=1)
        grads_s[r, :] = grads
        out, back = dot(inner, down[...]), dot(grads, weight(), NT)

        @pl.when(j == 0)
        def _():
            total[r, :] = out
            g_middle[r, :] = back

        @pl.when(j > 0)
        def _():
            total[r, :] += out
            g_middle[r, :] += back

    parts = seq // TOKENS
    tick_a(j)
    for t in range(parts):
        tokens_part(t)
        if t == parts // 2 - 1 or parts == 1:
            tick_b(j)
            fetch(j + 1, 1 - slot, True)
    g_weights = dot(normed_t[...], grads_s[...]).astype(bf16)
    at = held.at[lax.rem(j, SLOTS)]
    for y in range(ny):
        for c in range(nc):
            for z in range(nz):
                for x in range(nx):
                    row = (((y * nc + c) * nz + z) * nx + x) * block
                    at[c, y, x, z] = g_weights[row:row + block]
    tick_c(j)
    g_down[...] = dot(inner_s[...], cot[...], TN).astype(bf16)

    @pl.when(j == chunks - 1)
    def _():
        for t in range(seq // 256):
            r = slice(t * 256, t * 256 + 256)
            m = middle[r, :]
            s = rms(m)
            output[r, :] = (m + total[r, :]).astype(bf16)
            g_normed = g_middle[r, :]
            u = g_normed * gain[...]
            g_middle[r, :] = cot[r, :].astype(f32) + s * u - m * (s * s * s * jnp.mean(u * m, axis=-1, keepdims=True))
            part = jnp.sum(g_normed * m * s, axis=0, keepdims=True)
            if t == 0:
                g_gain[...] = part
            else:
                g_gain[...] += part
        for k in range(3):
            tick_a(chunks + k)
            tick_b(chunks + k)
            tick_c(chunks + k)


def mlp(dims, middle, normed, cot, gain, down, early, local_gu, collective_id):
    chunks, block, width = local_gu.shape
    ready = early.shape[0]
    seq = normed.shape[0]
    ny, nc, nz, nx = dims
    whole = lambda *s: pl.BlockSpec(s, lambda i: (0,) * len(s))
    vmem = lambda s, t: pltpu.VMEM(s, t)
    return pl.pallas_call(
        functools.partial(mlp_kernel, dims, chunks, ready),
        grid=(chunks,),
        out_shape=[
            jax.ShapeDtypeStruct((seq, D), bf16),
            jax.ShapeDtypeStruct((seq, D), f32),
            jax.ShapeDtypeStruct((1, D), f32),
            jax.ShapeDtypeStruct((chunks, block, width), f32),
            jax.ShapeDtypeStruct((chunks * CHUNK, D), bf16),
            jax.ShapeDtypeStruct((chunks - ready,) + dims + (block, width), bf16),
        ],
        in_specs=[whole(seq, D), whole(seq, D), whole(seq, D), whole(1, D), pl.BlockSpec((CHUNK, D), lambda i: (i, 0)), ANY, ANY],
        out_specs=[whole(seq, D), whole(seq, D), whole(1, D), whole(chunks, block, width),
                   pl.BlockSpec((CHUNK, D), lambda i: (i, 0)), ANY],
        scratch_shapes=[
            vmem((D, seq), bf16), vmem((seq, D), f32), vmem((seq, CHUNK), bf16), vmem((seq, width), bf16),
            vmem((2,) + dims + (block, width), bf16), vmem((SLOTS, nc, ny, nx, nz, block, width), bf16),
        ] + Scatter.buf_shapes(dims, (block, width), (chunks,)) + [pltpu.SemaphoreType.DMA((2,))]
        + Gather.sem_shapes(dims, chunks - ready) + Scatter.sem_shapes(dims, chunks),
        compiler_params=pltpu.CompilerParams(
            collective_id=collective_id, has_side_effects=True, vmem_limit_bytes=62 << 20),
        name="mlp",
    )(middle, normed, cot, gain, down, early, local_gu)


STEPS = 4
PAIRS = H // 2


def spread_ticks(ticks, slots):
    plan = [[] for _ in range(slots)]
    for n, tick in enumerate(ticks):
        plan[n * slots // len(ticks)].append(tick)
    return plan


def tick_list(jobs):
    n, depth = len(jobs), len(jobs[0])
    return [[jobs[i][t - i] for i in range(n) if 0 <= t - i < depth] for t in range(n + depth - 1)]


def run_tick(tick):
    for stage in tick:
        stage()


def windows(width, size):
    return [pl.ds(at, size) for at in range(0, width, size)]


def forward_kernel(dims, ready, *refs):
    (tokens, doc_col, doc_row, cosine, sine, spread, packed, w_out, w_down, gate_up,
     normed, factors, query, key, value, mixed, lse, gains, packed_all, out_all, down_all, early,
     weight, load) = refs[:24]
    sems = refs[24:]
    place = Place(dims)
    step = pl.program_id(0)
    pairs = [(packed, packed_all), (w_out, out_all)]
    for cols in windows(w_down.shape[1], 256):
        pairs.append((w_down.at[:, cols], down_all.at[:, :, :, :, :, cols]))
    pairs += [(gate_up.at[m], early.at[m]) for m in range(ready)]
    ticks = tick_list([Gather(place, s, d, sems, i).stages() for i, (s, d) in enumerate(pairs)])

    @pl.when(step == 0)
    def _():
        enter(place)
        for tick in ticks[:5]:
            run_tick(tick)
        copy = pltpu.make_async_copy(packed_all, weight, load)
        copy.start()
        copy.wait()
        w = weight[...].reshape(D, PACKED)
        gains[...] = w[:, DIMS + HEADS:].astype(f32).T[2 * H:2 * H + 8]

    @pl.when(step < STEPS)
    def _():
        rows = pl.ds(pl.multiple_of(jnp.minimum(step, STEPS - 1) * BLOCK, BLOCK), BLOCK)
        outs = [[r.at[p, rows] for p in range(PAIRS)] for r in (query, key, value)]
        factors_step(tokens, gains[0:1, :], weight[...].reshape(D, PACKED), cosine, sine, spread, normed, factors, *outs)

    @pl.when(step >= STEPS)
    def _():
        p = jnp.maximum(step - STEPS, 0)
        attend_kernel(doc_col, doc_row, query.at[p], key.at[p], value.at[p], mixed, lse)

    for at, todo in enumerate(spread_ticks(ticks[5:], STEPS + PAIRS - 1)):
        if todo:
            @pl.when(step == at + 1)
            def _(todo=todo):
                for tick in todo:
                    run_tick(tick)


def forward(dims, tokens, doc_col, doc_row, tables, packed, w_out, w_down, gate_up, ready, collective_id):
    cosine, sine, spread = tables
    seq = tokens.shape[0]
    whole = lambda *s: pl.BlockSpec(s, lambda i: (0,) * len(s), pipeline_mode=pl.Buffered(1))
    kept = lambda *s: pl.BlockSpec(s, lambda i: (0,) * len(s))
    row = lambda width: pl.BlockSpec((seq // STEPS, width), lambda i: (jnp.minimum(i, STEPS - 1), 0))
    after = lambda i: jnp.maximum(i - STEPS, 0)
    full = lambda a: jax.ShapeDtypeStruct(dims + a.shape, a.dtype)
    jobs = 2 + w_down.shape[1] // 256 + ready
    return pl.pallas_call(
        functools.partial(forward_kernel, dims, ready),
        grid=(STEPS + PAIRS,),
        out_shape=[
            jax.ShapeDtypeStruct((seq, D), bf16),
            jax.ShapeDtypeStruct((seq, PACKED), f32),
        ] + [jax.ShapeDtypeStruct((PAIRS, seq, 128), bf16)] * 3 + [
            jax.ShapeDtypeStruct((seq, H * DH), bf16),
            jax.ShapeDtypeStruct((PAIRS, 2, seq), f32),
            jax.ShapeDtypeStruct((8, D), f32),
            full(packed), full(w_out), full(w_down),
            jax.ShapeDtypeStruct((ready,) + dims + gate_up.shape[1:], bf16),
        ],
        in_specs=[row(D), whole(seq, 1), whole(1, seq), row(128), row(128), whole(*spread.shape)] + [ANY] * 4,
        out_specs=[row(D), row(PACKED)] + [kept(PAIRS, seq, 128)] * 3 + [
            pl.BlockSpec((seq, 128), lambda i: (0, after(i))),
            pl.BlockSpec((1, 2, seq), lambda i: (after(i), 0, 0)),
            kept(8, D),
        ] + [ANY] * 4,
        scratch_shapes=[pltpu.VMEM(dims + packed.shape, bf16), pltpu.SemaphoreType.DMA]
        + Gather.sem_shapes(dims, jobs),
        compiler_params=pltpu.CompilerParams(
            collective_id=collective_id, has_side_effects=True, vmem_limit_bytes=58 << 20),
        name="forward",
    )(tokens, doc_col, doc_row, cosine, sine, spread, packed, w_out, w_down, gate_up)


def backward_kernel(dims, widths, *refs):
    (doc_col, doc_row, query, key, value, grad, lse, tokens, gain, packed_all, cosine, sine, spread, factors, g_middle,
     normed, g_gain_two, g_down, g_out) = refs[:19]
    g_tokens, down_out, out_out, gains_out = refs[19:23]
    packed_out = refs[23:23 + len(widths)]
    at = 23 + len(widths)
    g_query, g_key, g_value, weight, g_factors, g_gain, reduced, load = refs[at:at + 8]
    bufs = refs[at + 8:at + 8 + 15]
    sems = refs[at + 23:]
    place = Place(dims)
    ny, nc, nz, nx = dims
    step = pl.program_id(0)
    block = packed_all.shape[4]
    fetch = lambda: pltpu.make_async_copy(packed_all, weight, load)
    jobs = []
    for n, cols in enumerate(windows(g_out.shape[-1], 512)):
        own = [b.at[n] for b in bufs[0:5]]
        jobs.append(Scatter(place, own[0], out_out.at[:, cols], own[1:], sems, len(jobs), g_out.at[:, :, :, :, :, cols]))
    for n, cols in enumerate(windows(g_down.shape[-1], 256)):
        own = [b.at[n] for b in bufs[5:10]]
        jobs.append(Scatter(place, own[0], down_out.at[:, cols], own[1:], sems, len(jobs), g_down.at[:, :, :, :, :, cols]))
    last = Scatter(place, bufs[10], reduced, bufs[11:15], sems, len(jobs))
    ticks = tick_list([job.stages() for job in jobs])
    total = PAIRS + STEPS

    @pl.when(step == 0)
    def _():
        fetch().start()
        enter(place)
        run_tick(ticks[0])

    @pl.when(step < PAIRS)
    def _():
        p = jnp.minimum(step, PAIRS - 1)
        attend_back_kernel(doc_col, doc_row, query.at[0], key.at[0], value.at[0], grad, lse,
                           g_query.at[p], g_key.at[p], g_value.at[p])

    pl.when(step == PAIRS)(lambda: fetch().wait())

    @pl.when(step >= PAIRS)
    def _():
        t = jnp.maximum(step - PAIRS, 0)
        rows = pl.ds(pl.multiple_of(t * BLOCK, BLOCK), BLOCK)
        grads = [jnp.concatenate([g[p, rows, :] for p in range(PAIRS)], axis=1) for g in (g_query, g_key, g_value)]
        factors_back_step(t, tokens, gain[0:1, :], weight[...].reshape(D, PACKED), cosine, sine, spread, factors, *grads,
                          g_middle, g_factors.at[rows], g_tokens, g_gain)

    for n, todo in enumerate(spread_ticks(ticks[1:], total - 1)):
        if todo:
            @pl.when(step == n)
            def _(todo=todo):
                for tick in todo:
                    run_tick(tick)

    @pl.when(step == total - 1)
    def _():
        g_weight = dot(normed[...], g_factors[...], TN)
        column = lambda row: jnp.broadcast_to(row, (128, D)).T
        lane = lax.broadcasted_iota(jnp.int32, (D, 128), 1)
        tail = g_weight[:, DIMS + HEADS:]
        tail = jnp.where(lane == 2 * H, column(g_gain[...]), jnp.where(lane == 2 * H + 1, column(g_gain_two[...]), tail))
        g_weight = jnp.concatenate([g_weight[:, :DIMS + HEADS], tail], axis=1).astype(bf16)
        for y in range(ny):
            for c in range(nc):
                for z in range(nz):
                    for x in range(nx):
                        row = (((y * nc + c) * nz + z) * nx + x) * block
                        bufs[10][c, y, x, z] = g_weight[row:row + block]
        for stage in last.stages():
            stage()
        at = 0
        for out, width in zip(packed_out, widths):
            out[...] = reduced[:, at:at + width]
            at += width
        gains_out[...] = reduced[:, at:at + 2]


def backward(dims, widths, doc_col, doc_row, query, key, value, grad, lse, tokens, gains, packed_all, tables, factors,
             g_middle, normed, g_gain_two, g_down, g_out, collective_id):
    cosine, sine, spread = tables
    seq = tokens.shape[0]
    ny, nc, nz, nx = dims
    block = packed_all.shape[4]
    whole = lambda *s: pl.BlockSpec(s, lambda i: (0,) * len(s), pipeline_mode=pl.Buffered(1))
    kept = lambda *s: pl.BlockSpec(s, lambda i: (0,) * len(s))
    before = lambda i: jnp.minimum(i, PAIRS - 1)
    after = lambda i: jnp.maximum(i - PAIRS, 0)
    pair = pl.BlockSpec((1, seq, 128), lambda i: (before(i), 0, 0))
    row = lambda width: pl.BlockSpec((seq // STEPS, width), lambda i: (after(i), 0))
    down_block, out_block = g_down.shape[4], g_out.shape[4]
    downs, outs = g_down.shape[-1] // 256, g_out.shape[-1] // 512
    buffers = []
    for lead, b in (((outs,), (out_block, 512)), ((downs,), (down_block, 256))):
        buffers += [pltpu.VMEM(lead + (ny, nx, nz) + b, bf16)] + Scatter.buf_shapes(dims, b, lead)
    buffers += [pltpu.VMEM((nc, ny, nx, nz, block, PACKED), bf16)] + Scatter.buf_shapes(dims, (block, PACKED))
    shape = lambda *s: jax.ShapeDtypeStruct(s, f32)
    return pl.pallas_call(
        functools.partial(backward_kernel, dims, widths),
        grid=(PAIRS + STEPS,),
        out_shape=[jax.ShapeDtypeStruct((seq, D), bf16), shape(down_block, g_down.shape[-1]),
                   shape(out_block, g_out.shape[-1]), shape(block, 2)] + [shape(block, w) for w in widths],
        in_specs=[whole(seq, 1), whole(1, seq), pair, pair, pair, pl.BlockSpec((seq, 128), lambda i: (0, before(i))),
                  pl.BlockSpec((1, 2, seq), lambda i: (before(i), 0, 0)), row(D), whole(8, D), ANY, row(128), row(128),
                  whole(*spread.shape), row(PACKED), row(D), whole(seq, D), whole(1, D), ANY, ANY],
        out_specs=[row(D), kept(down_block, g_down.shape[-1]), kept(out_block, g_out.shape[-1]), kept(block, 2)]
        + [kept(block, w) for w in widths],
        scratch_shapes=[pltpu.VMEM((PAIRS, seq, 128), f32)] * 3 + [
            pltpu.VMEM(dims + (block, PACKED), bf16), pltpu.VMEM((seq, PACKED), bf16), pltpu.VMEM((1, D), f32),
            pltpu.VMEM((block, PACKED), f32), pltpu.SemaphoreType.DMA,
        ] + buffers + Scatter.sem_shapes(dims, downs + outs + 1),
        compiler_params=pltpu.CompilerParams(
            collective_id=collective_id, has_side_effects=True, vmem_limit_bytes=62 << 20),
        name="backward",
    )(doc_col, doc_row, query, key, value, grad, lse, tokens, gains, packed_all, cosine, sine, spread, factors,
      g_middle, normed, g_gain_two, g_down, g_out)


def plain_mlp(middle, normed_two, cotangent, gain, gate_w, up_w, down_w):
    gate, up = dot(normed_two, gate_w), dot(normed_two, up_w)
    sig = jax.nn.sigmoid(gate)
    silu = gate * sig
    inner = (silu * up).astype(bf16)
    output = (middle + dot(inner, down_w)).astype(bf16)
    grad_inner = dot(cotangent, down_w, NT)
    grad_gate = (grad_inner * up * sig * (1.0 + gate * (1.0 - sig))).astype(bf16)
    grad_up = (grad_inner * silu).astype(bf16)
    grad_normed = dot(grad_gate, gate_w, NT) + dot(grad_up, up_w, NT)
    scale = rms(middle)
    gained = grad_normed * gain
    grad_middle = (
        cotangent.astype(f32)
        + scale * gained
        - middle * scale**3 * jnp.mean(gained * middle, axis=-1, keepdims=True)
    )
    grad_gain = jnp.sum(grad_normed * middle * scale, axis=0, keepdims=True)
    outer_sum = lambda left, right: dot(left, right, TN).astype(bf16)
    return (
        output, grad_middle, grad_gain,
        outer_sum(inner, cotangent), outer_sum(normed_two, grad_gate), outer_sum(normed_two, grad_up),
    )


def on_device(
    dims,
    tokens,
    doc_ids,
    norm_gain,
    w_query_heads,
    w_query_dims,
    w_key_heads,
    w_key_dims,
    w_value_heads,
    w_value_dims,
    w_output,
    mlp_gain,
    w_gate,
    w_up,
    w_down,
    out_grad,
):
    seq_len = tokens.shape[0] * tokens.shape[1]
    tables = tuple(jnp.asarray(t) for t in rope_tables(seq_len) + (spread_table(),))
    parts = (w_query_dims, w_key_dims, w_value_dims, w_query_heads, w_key_heads, w_value_heads)
    edges = [0]
    for part in parts:
        edges.append(edges[-1] + part.shape[1])
    gains_at = edges[-1]
    packed = jnp.concatenate(
        parts
        + (norm_gain[:, None], mlp_gain[:, None])
        + (jnp.zeros((norm_gain.shape[0], PACKED - gains_at - 2), bf16),),
        axis=1,
    )
    inputs, cotangent = tokens.reshape(seq_len, D), out_grad.reshape(seq_len, D)
    doc_row, doc_col = doc_ids.reshape(1, seq_len), doc_ids.reshape(seq_len, 1)
    outer_sum = lambda left, right: dot(left, right, TN).astype(bf16)
    block = w_gate.shape[0]
    if block % 16 == 0 and w_gate.shape[1] % CHUNK == 0 and seq_len % TOKENS == 0:
        chunked = lambda w: w.reshape(block, -1, CHUNK).transpose(1, 0, 2)
        gate_up = jnp.concatenate([chunked(w_gate), chunked(w_up)], axis=2)
        (normed, factors, query, key, value, mixed, lse, gains, packed_w, output_w, down_w, early) = forward(
            dims, inputs, doc_col, doc_row, tables, packed, w_output, w_down, gate_up, READY, 0
        )
        output_w, gain_two = output_w.reshape(-1, D), gains[1:2]
        middle = inputs.astype(f32) + dot(mixed, output_w)
        normed_two = (middle * rms(middle) * gain_two).astype(bf16)
        output, grad_middle, grad_mlp_gain, gate_up_out, grad_down, _ = mlp(
            dims, middle, normed_two, cotangent, gain_two, down_w.reshape(-1, D), early, gate_up, 1
        )
        grad_branch = grad_middle.astype(bf16)
        grad_mixed = dot(grad_branch, output_w, NT).astype(bf16)
        devices_first = lambda g: g.reshape(dims + (-1,) + g.shape[1:])
        grad_tokens, down_out, output_out, gains_out, *parts_out = backward(
            dims, [part.shape[1] for part in parts], doc_col, doc_row, query, key, value, grad_mixed, lse, inputs,
            gains, packed_w, tables, factors, grad_middle, normed, grad_mlp_gain,
            devices_first(grad_down), devices_first(outer_sum(mixed, grad_branch)), 2,
        )
        whole = lambda g: g.transpose(1, 0, 2).reshape(block, -1)
        gate_out, up_out = whole(gate_up_out[:, :, :CHUNK]), whole(gate_up_out[:, :, CHUNK:])
        grads = [g for pair in zip(parts_out[3:], parts_out[:3]) for g in pair]
        return (
            output.reshape(tokens.shape), grad_tokens.reshape(tokens.shape), gains_out[:, 0], *grads,
            output_out, gains_out[:, 1], gate_out, up_out, down_out,
        )

    packed_w, output_w, gate_w, up_w, down_w = gather(
        dims, [packed, w_output, w_gate, w_up, w_down], 0
    )
    gain_one, gain_two = [packed_w[:, gains_at + i].astype(f32).reshape(1, D) for i in (0, 1)]
    normed, factors, query, key, value = make_factors(inputs, gain_one, packed_w, tables)
    mixed, lse = attend(doc_col, doc_row, query, key, value)
    middle = inputs.astype(f32) + dot(mixed, output_w)
    normed_two = (middle * rms(middle) * gain_two).astype(bf16)
    output, grad_middle, grad_mlp_gain, *mlp_grads = plain_mlp(
        middle, normed_two, cotangent, gain_two, gate_w, up_w, down_w
    )
    grad_branch = grad_middle.astype(bf16)
    grad_mixed = dot(grad_branch, output_w, NT).astype(bf16)

    grad_query, grad_key, grad_value = attend_back(
        doc_col, doc_row, query, key, value, grad_mixed, lse
    )
    grad_factors, grad_tokens, grad_norm_gain = factors_back(
        inputs, gain_one, packed_w, tables, factors, grad_query, grad_key, grad_value, grad_middle
    )
    gains = jnp.stack([grad_norm_gain[0], grad_mlp_gain[0]], axis=1).astype(bf16)
    packed_grad = lax.dynamic_update_slice(outer_sum(normed, grad_factors), gains, (0, gains_at))
    *mlp_out, output_out, packed_out = scatter(
        dims, mlp_grads + [outer_sum(mixed, grad_branch), packed_grad], 2
    )
    down_out, gate_out, up_out = mlp_out
    dims_and_heads = [packed_out[:, lo:hi] for lo, hi in zip(edges, edges[1:])]
    grads = [g for pair in zip(dims_and_heads[3:], dims_and_heads[:3]) for g in pair]
    return (
        output.reshape(tokens.shape),
        grad_tokens.reshape(tokens.shape),
        packed_out[:, gains_at],
        *grads,
        output_out,
        packed_out[:, gains_at + 1],
        gate_out,
        up_out,
        down_out,
    )


def solution(mesh):
    rows, matrix, vector = P(("dp", "fsdp"), None, None), P(("dp", "fsdp"), None), P(("dp", "fsdp"))
    return jax.shard_map(
        functools.partial(on_device, grid_of(mesh)),
        mesh=mesh,
        in_specs=(rows, matrix, vector) + (matrix,) * 7 + (vector,) + (matrix,) * 3 + (rows,),
        out_specs=(rows, rows, vector) + (matrix,) * 7 + (vector,) + (matrix,) * 3,
        check_vma=False,
    )
```

```python
import functools
import math

import jax
import jax.numpy as jnp
import numpy as np
from jax import lax
from jax.experimental import pallas as pl
from jax.experimental.pallas import tpu as pltpu
from jax.sharding import PartitionSpec as P

MESH = pl.DeviceIdType.MESH
D, H, DH, RQ, RK = 1024, 16, 64, 6, 2
PACKED = 896
DIMS, HEADS = 640, 128
BLOCK = 256
BACK = 512
NEG = -1e30
epsilon = 1e-06
theta_base = 10000.0
f32, bf16 = jnp.float32, jnp.bfloat16
NT = (((1,), (1,)), ((), ()))
NN = (((1,), (0,)), ((), ()))
TN = (((0,), (0,)), ((), ()))


def dot(a, b, dims=NN):
    return lax.dot_general(a, b, dims, preferred_element_type=f32)


def params(**kw):
    return pltpu.CompilerParams(vmem_limit_bytes=56 << 20, **kw)


def rope_tables(seq_len):
    half = DH // 2
    position = np.arange(seq_len, dtype=np.float32)
    inverse = np.exp(-math.log(theta_base) * 2.0 * np.arange(half, dtype=np.float32) / np.float32(2.0 * half)).astype(np.float32)
    angle = (position[:, None] * inverse[None, :]).astype(np.float32)
    cosine, sine = np.cos(angle), np.sin(angle)
    return (np.concatenate([cosine] * 4, 1), np.concatenate([-sine, sine] * 2, 1))


def spread_table():
    out = np.zeros((8, 2 * HEADS, H * DH), np.float32)
    for j in range(8):
        for h in range(H):
            out[j, [j * H + h, HEADS + j * H + h], h * DH:(h + 1) * DH] = 1.0
    return out.astype(jnp.bfloat16)


def low_lane(shape):
    return lax.rem(lax.broadcasted_iota(jnp.int32, shape, 1), 128) < 64


def first_half(shape):
    return lax.rem(lax.broadcasted_iota(jnp.int32, shape, 1), 64) < 32


def turn(x, cosine, sine):
    partner = jnp.where(first_half(x.shape), pltpu.roll(x, 96, 1), pltpu.roll(x, 32, 1))
    return x * cosine + partner * sine


def split_bf16(x):
    hi = x.astype(bf16)
    return jnp.concatenate([hi, (x - hi.astype(f32)).astype(bf16)], axis=1)


def twice(x, rank):
    rolled = pltpu.roll(x, 64, 1)
    low = low_lane(x.shape)
    return jnp.where(low, x, rolled) if rank % 2 == 0 else jnp.where(low, rolled, x)


def wide(x):
    return jnp.concatenate([x] * (H * DH // 128), axis=1)


def rms(x):
    return lax.rsqrt(jnp.mean(x * x, axis=-1, keepdims=True) + epsilon)


FACTORS = ((0, RQ, 0), (RQ, RK, 3), (0, RK, 4))


def factors_step(tokens, gain, weight, cosine, sine, spread, normed, factors, query, key, value):
    x = tokens[...].astype(f32)
    n = (x * rms(x) * gain).astype(bf16)
    normed[...] = n
    f = dot(n, weight)
    pairs = [f[:, 128 * i:128 * i + 128] for i in range(DIMS // 128)]
    pairs = [turn(p, cosine[...], sine[...]) if i < 4 else p for i, p in enumerate(pairs)]
    for i, p in enumerate(pairs):
        factors[:, 128 * i:128 * i + 128] = p
    factors[:, DIMS:] = f[:, DIMS:]
    heads_qk = split_bf16(f[:, DIMS:DIMS + HEADS])
    heads_v = split_bf16(f[:, DIMS + HEADS:])
    for out, heads, (at, ranks, pair), scale in zip(
        (query, key, value), (heads_qk, heads_qk, heads_v), FACTORS, (0.125, 1.0, 1.0)
    ):
        total = None
        for r in range(ranks):
            term = dot(heads, spread[at + r]) * wide(twice(pairs[pair + r // 2], r))
            total = term if total is None else total + term
        rounded = (total * (1.0 / ranks)).astype(bf16)
        rounded = rounded * jnp.asarray(scale, bf16) if scale != 1.0 else rounded
        for p, ref in enumerate(out):
            ref[...] = rounded[:, 128 * p:128 * p + 128]


def factors_kernel(tokens, gain, weight, cosine, sine, spread, normed, factors, query, key, value):
    outs = [[r.at[p] for p in range(H // 2)] for r in (query, key, value)]
    factors_step(tokens, gain[...], weight[...], cosine, sine, spread, normed, factors, *outs)


def make_factors(tokens, gain, weight, tables):
    cosine, sine, spread = tables
    seq = tokens.shape[0]
    row = lambda width: pl.BlockSpec((BLOCK, width), lambda i: (i, 0))
    whole = lambda a: pl.BlockSpec(a.shape, lambda i: (0,) * a.ndim)
    return pl.pallas_call(
        factors_kernel,
        grid=(seq // BLOCK,),
        out_shape=[
            jax.ShapeDtypeStruct((seq, D), bf16),
            jax.ShapeDtypeStruct((seq, PACKED), f32),
        ] + [jax.ShapeDtypeStruct((H // 2, seq, 128), bf16)] * 3,
        in_specs=[row(D), whole(gain), whole(weight), row(128), row(128), whole(spread)],
        out_specs=[row(D), row(PACKED)] + [pl.BlockSpec((H // 2, BLOCK, 128), lambda i: (0, i, 0))] * 3,
        compiler_params=params(),
        name="factors",
    )(tokens, gain, weight, cosine, sine, spread)


def allowed_t(doc_col, doc_row, k0, kn, q0, qn):
    same = doc_col[k0:k0 + kn, :] == doc_row[:, q0:q0 + qn]
    if k0 + kn - 1 > q0:
        k_at = k0 + lax.broadcasted_iota(jnp.int32, (kn, qn), 0)
        q_at = q0 + lax.broadcasted_iota(jnp.int32, (kn, qn), 1)
        same = same & (k_at <= q_at)
    return same


def halves(x):
    low = low_lane(x.shape)
    zero = jnp.zeros_like(x)
    return jnp.where(low, x, zero), jnp.where(low, zero, x)


def attend_kernel(doc_col, doc_row, query, key, value, mixed, lse):
    seq = query.shape[0]
    v_half = halves(value[...])
    for q0 in range(0, seq, BLOCK):
        lo = max(0, q0 - BACK)
        kn = q0 + BLOCK - lo
        ok = allowed_t(doc_col, doc_row, lo, kn, q0, BLOCK)
        probs = []
        for h, q in enumerate(halves(query[q0:q0 + BLOCK, :])):
            s = jnp.where(ok, dot(key[lo:lo + kn, :], q, NT), NEG)
            top = jnp.max(s, axis=0, keepdims=True)
            e = jnp.exp(s - top)
            total = jnp.sum(e, axis=0, keepdims=True)
            probs.append((e * (1.0 / total)).astype(bf16))
            lse[0, h:h + 1, q0:q0 + BLOCK] = top + jnp.log(total)
        values = jnp.concatenate([v[lo:lo + kn] for v in v_half], axis=0)
        mixed[q0:q0 + BLOCK, :] = dot(jnp.concatenate(probs, axis=0), values, TN).astype(bf16)


def attend(doc_col, doc_row, query, key, value):
    pairs, seq, _ = query.shape
    whole = lambda a: pl.BlockSpec(a.shape, lambda i: (0,) * a.ndim)
    pair = pl.BlockSpec((seq, 128), lambda i: (0, i))
    return pl.pallas_call(
        lambda dc, dr, q, k, v, *outs: attend_kernel(dc, dr, q.at[0], k.at[0], v.at[0], *outs),
        grid=(pairs,),
        out_shape=[jax.ShapeDtypeStruct((seq, H * DH), bf16), jax.ShapeDtypeStruct((pairs, 2, seq), f32)],
        in_specs=[whole(doc_col), whole(doc_row)] + [pl.BlockSpec((1, seq, 128), lambda i: (i, 0, 0))] * 3,
        out_specs=[pair, pl.BlockSpec((1, 2, seq), lambda i: (i, 0, 0))],
        compiler_params=params(),
        name="attend",
    )(doc_col, doc_row, query, key, value)


def attend_back_kernel(doc_col, doc_row, query, key, value, grad, lse, g_query, g_key, g_value):
    seq = query.shape[0]
    k_half = halves(key[...])
    for q0 in range(0, seq, BLOCK):
        lo = max(0, q0 - BACK)
        kn = q0 + BLOCK - lo
        ok = allowed_t(doc_col, doc_row, lo, kn, q0, BLOCK)
        ps, ds = [], []
        q_half, g_half = halves(query[q0:q0 + BLOCK, :]), halves(grad[q0:q0 + BLOCK, :])
        for h in (0, 1):
            s = dot(key[lo:lo + kn, :], q_half[h], NT)
            p = jnp.where(ok, jnp.exp(s - lse[0, h:h + 1, q0:q0 + BLOCK]), 0.0)
            pd = p * dot(value[lo:lo + kn, :], g_half[h], NT)
            ps.append(p.astype(bf16))
            ds.append((pd - p * jnp.sum(pd, axis=0, keepdims=True)).astype(bf16))
        to_value = dot(jnp.concatenate(ps, 1), jnp.concatenate(g_half, 0))
        to_key = dot(jnp.concatenate(ds, 1), jnp.concatenate(q_half, 0))
        if q0 > lo:
            g_value[lo:q0, :] += to_value[:q0 - lo]
            g_key[lo:q0, :] += to_key[:q0 - lo]
        g_value[q0:q0 + BLOCK, :] = to_value[q0 - lo:]
        g_key[q0:q0 + BLOCK, :] = to_key[q0 - lo:]
        keys = jnp.concatenate([k[lo:lo + kn] for k in k_half], 0)
        g_query[q0:q0 + BLOCK, :] = dot(jnp.concatenate(ds, 0), keys, TN) * 0.125


def attend_back(doc_col, doc_row, query, key, value, grad, lse):
    pairs, seq, _ = query.shape
    whole = lambda a: pl.BlockSpec(a.shape, lambda i: (0,) * a.ndim)
    pair = pl.BlockSpec((seq, 128), lambda i: (0, i))
    return pl.pallas_call(
        lambda dc, dr, q, k, v, *rest: attend_back_kernel(dc, dr, q.at[0], k.at[0], v.at[0], *rest),
        grid=(pairs,),
        out_shape=[jax.ShapeDtypeStruct((seq, H * DH), f32)] * 3,
        in_specs=[whole(doc_col), whole(doc_row)] + [pl.BlockSpec((1, seq, 128), lambda i: (i, 0, 0))] * 3 + [pair, pl.BlockSpec((1, 2, seq), lambda i: (i, 0, 0))],
        out_specs=[pair] * 3,
        compiler_params=params(),
        name="attend_back",
    )(doc_col, doc_row, query, key, value, grad, lse)


def factors_back_step(step, tokens, gain, weight, cosine, sine, spread, factors, g_query, g_key, g_value, g_middle,
                      g_factors, g_tokens, g_gain):
    pairs = [factors[:, 128 * i:128 * i + 128] for i in range(DIMS // 128)]
    heads_qk = split_bf16(factors[:, DIMS:DIMS + HEADS])
    heads_v = split_bf16(factors[:, DIMS + HEADS:])
    g_heads = [None, None]
    for grad, heads, which, (at, ranks, pair) in zip(
        (g_query, g_key, g_value), (heads_qk, heads_qk, heads_v), (0, 0, 1), FACTORS
    ):
        g = grad * (1.0 / ranks)
        folded = []
        for r in range(ranks):
            product = (g * wide(twice(pairs[pair + r // 2], r))).astype(bf16)
            part = dot(product, spread[at + r, :HEADS, :], NT)
            g_heads[which] = part if g_heads[which] is None else g_heads[which] + part
            full = g * dot(heads, spread[at + r])
            folded.append(sum(full[:, 128 * i:128 * i + 128] for i in range(H * DH // 128)))
        for r in range(0, ranks, 2):
            a, b = folded[r], folded[r + 1]
            low = low_lane(a.shape)
            mine = jnp.where(low, a, b)
            other = jnp.where(low, pltpu.roll(a, 64, 1), pltpu.roll(b, 64, 1))
            both = mine + other
            i = pair + r // 2
            if i < 4:
                both = turn(both, cosine[...], -sine[...])
            g_factors[:, 128 * i:128 * i + 128] = both.astype(bf16)
    g_factors[:, DIMS:DIMS + HEADS] = g_heads[0].astype(bf16)
    g_factors[:, DIMS + HEADS:] = g_heads[1].astype(bf16)
    g_normed = dot(g_factors[...], weight, NT)
    x = tokens[...].astype(f32)
    r1 = rms(x)
    u = g_normed * gain
    part = jnp.sum(g_normed * x * r1, axis=0, keepdims=True)

    @pl.when(step == 0)
    def _():
        g_gain[...] = part

    @pl.when(step > 0)
    def _():
        g_gain[...] += part

    g_tokens[...] = (g_middle[...] + r1 * u - x * (r1 * r1 * r1 * jnp.mean(u * x, axis=-1, keepdims=True))).astype(bf16)


def factors_back_kernel(tokens, gain, weight, cosine, sine, spread, factors, g_query, g_key, g_value, *rest):
    factors_back_step(pl.program_id(0), tokens, gain[...], weight[...], cosine, sine, spread, factors,
                      g_query[...], g_key[...], g_value[...], *rest)


def factors_back(tokens, gain, weight, tables, factors, g_query, g_key, g_value, g_middle):
    cosine, sine, spread = tables
    seq = tokens.shape[0]
    row = lambda width: pl.BlockSpec((BLOCK, width), lambda i: (i, 0))
    whole = lambda a: pl.BlockSpec(a.shape, lambda i: (0,) * a.ndim)
    return pl.pallas_call(
        factors_back_kernel,
        grid=(seq // BLOCK,),
        out_shape=[
            jax.ShapeDtypeStruct((seq, PACKED), bf16),
            jax.ShapeDtypeStruct((seq, D), bf16),
            jax.ShapeDtypeStruct((1, D), f32),
        ],
        in_specs=[row(D), whole(gain), whole(weight), row(128), row(128), whole(spread), row(PACKED)]
        + [row(H * DH)] * 3 + [row(D)],
        out_specs=[row(PACKED), row(D), pl.BlockSpec((1, D), lambda i: (0, 0))],
        compiler_params=params(),
        name="factors_back",
    )(tokens, gain, weight, cosine, sine, spread, factors, g_query, g_key, g_value, g_middle)

ANY = pl.BlockSpec(memory_space=pl.ANY)


def grid_of(mesh):
    nd, nf = mesh.shape["dp"], mesh.shape["fsdp"]
    nc = math.gcd(2, nd)
    nz = math.gcd(4, nf)
    return (nd // nc, nc, nz, nf // nz)


class Place:
    def __init__(self, dims):
        self.dims = dims
        ny, nc, nz, nx = dims
        dp, fs = lax.axis_index("dp"), lax.axis_index("fsdp")
        self.y, self.c = lax.div(dp, nc), lax.rem(dp, nc)
        self.z, self.x = lax.div(fs, nx), lax.rem(fs, nx)

    def at(self, axis, k):
        n = self.dims["yczx".index(axis)]
        return lax.rem(getattr(self, axis) + k + n, n)

    def device(self, axis=None, k=0):
        ny, nc, nz, nx = self.dims
        put = {a: getattr(self, a) for a in "yczx"}
        if axis is not None:
            put[axis] = self.at(axis, k)
        return (put["y"] * nc + put["c"], put["z"] * nx + put["x"])


def peers_of(dims):
    ny, nc, nz, nx = dims
    return [(a, k) for a, n in (("y", ny), ("c", nc), ("z", nz), ("x", nx)) for k in range(1, n)]


def enter(place):
    barrier = pltpu.get_barrier_semaphore()
    peers = peers_of(place.dims)
    for axis, k in peers:
        pl.semaphore_signal(barrier, inc=1, device_id=place.device(axis, k), device_id_type=MESH)
    pl.semaphore_wait(barrier, len(peers))


class Gather:
    def __init__(self, place, src, dst, sems, i):
        self.p, self.src, self.dst, self.i = place, src, dst, i
        self.local, self.zs, self.zr, self.as_, self.ar, self.bs, self.br, self.cs, self.cr = sems

    @staticmethod
    def sem_shapes(dims, n):
        ny, nc, nz, nx = dims
        dma = pltpu.SemaphoreType.DMA
        m = max(nx, ny) - 1
        one = lambda k: dma((n, max(1, k)))
        return [dma((n,)), one(nz - 1), one(nz - 1), one(m), one(m), one(m), one(m), one(nx + ny - 1), one(nx + ny - 1)]

    def copy(self, ref_src, ref_dst, send, recv, axis, k):
        return pltpu.make_async_remote_copy(
            src_ref=ref_src, dst_ref=ref_dst, send_sem=send, recv_sem=recv,
            device_id=self.p.device(axis, k), device_id_type=MESH,
        )

    def z_copies(self):
        p, i = self.p, self.i
        nz = p.dims[2]
        mine = self.dst.at[p.y, p.c, p.z, p.x]
        def one(k, back):
            if back:
                ref = self.dst.at[p.y, p.c, p.at("z", -k), p.x]
                return self.copy(ref, ref, self.zs.at[i, k - 1], self.zr.at[i, k - 1], "z", k)
            return self.copy(self.src, mine, self.zs.at[i, k - 1], self.zr.at[i, k - 1], "z", k)

        return [[functools.partial(one, k, back) for k in range(1, nz)] for back in (False, True)]

    def part(self, first, step, y, x, c):
        every = slice(None)
        if step == 0:
            return self.dst.at[y, c, :, x]
        return self.dst.at[y, c] if first == "x" else self.dst.at[:, c, :, x]

    def side_copies(self, first, step):
        p, i = self.p, self.i
        axis = first if step == 0 else {"x": "y", "y": "x"}[first]
        n = p.dims["yczx".index(axis)]
        s, r = ((self.as_, self.ar), (self.bs, self.br))[step]

        def one(k, back):
            y, x = p.y, p.x
            if back:
                y, x = (p.y, p.at("x", -k)) if axis == "x" else (p.at("y", -k), p.x)
            ref = self.part(first, step, y, x, p.c)
            return self.copy(ref, ref, s.at[i, k - 1], r.at[i, k - 1], axis, k)

        return [[functools.partial(one, k, back) for k in range(1, n)] for back in (False, True)]

    def core_copies(self, first, c):
        p, i = self.p, self.i
        second = {"x": "y", "y": "x"}[first]
        lists, j = [], 0
        for step, axis in ((0, None), (0, first), (1, second)):
            now = []
            count = 1 if axis is None else p.dims["yczx".index(axis)] - 1
            for k in range(1, count + 1):
                def one(axis=axis, step=step, k=k, j=j):
                    y = p.at("y", -k) if axis == "y" else p.y
                    x = p.at("x", -k) if axis == "x" else p.x
                    ref = self.part(first, step, y, x, c)
                    return self.copy(ref, ref, self.cs.at[i, j], self.cr.at[i, j], "c", 1)

                now.append(one)
                j += 1
            lists.append(now)
        return lists

    def start(self):
        p = self.p
        mine = self.dst.at[p.y, p.c, p.z, p.x]
        pltpu.make_async_copy(self.src, mine, self.local.at[self.i]).start()
        for copy in self.z_copies()[0]:
            copy().start()

    def by_core(self, body):
        if self.p.dims[1] == 1:
            body("x")
            return
        pl.when(self.p.c == 0)(lambda: body("x"))
        pl.when(self.p.c == 1)(lambda: body("y"))

    def after_z(self):
        p = self.p
        mine = self.dst.at[p.y, p.c, p.z, p.x]
        pltpu.make_async_copy(self.src, mine, self.local.at[self.i]).wait()
        for copy in self.z_copies()[1]:
            copy().wait_recv()

        def body(first):
            for copy in self.side_copies(first, 0)[0]:
                copy().start()
            if p.dims[1] > 1:
                for copy in self.core_copies(first, p.c)[0]:
                    copy().start()

        self.by_core(body)

    def after_first(self):
        p = self.p

        def body(first):
            for copy in self.side_copies(first, 0)[1]:
                copy().wait_recv()
            for copy in self.side_copies(first, 1)[0]:
                copy().start()
            if p.dims[1] > 1:
                for copy in self.core_copies(first, p.c)[1]:
                    copy().start()

        self.by_core(body)

    def after_second(self):
        p = self.p

        def body(first):
            for copy in self.side_copies(first, 1)[1]:
                copy().wait_recv()
            if p.dims[1] > 1:
                for copy in self.core_copies(first, p.c)[2]:
                    copy().start()

        self.by_core(body)

    def finish(self):
        p = self.p
        for copy in self.z_copies()[0]:
            copy().wait_send()

        def body(first):
            for step in (0, 1):
                for copy in self.side_copies(first, step)[0]:
                    copy().wait_send()
            if p.dims[1] > 1:
                for now in self.core_copies(first, p.c):
                    for copy in now:
                        copy().wait_send()
                other = {"x": "y", "y": "x"}[first]
                for now in self.core_copies(other, p.at("c", 1)):
                    for copy in now:
                        copy().wait_recv()

        self.by_core(body)

    def stages(self):
        return [self.start, self.after_z, self.after_first, self.after_second, self.finish]


def gather_kernel(dims, n, *refs):
    place = Place(dims)
    src, dst, sems = refs[:n], refs[n:2 * n], refs[2 * n:]
    enter(place)
    jobs = [Gather(place, src[i], dst[i], sems, i).stages() for i in range(n)]
    run_stages(jobs)


def gather(dims, arrays, collective_id):
    n = len(arrays)
    outs = pl.pallas_call(
        functools.partial(gather_kernel, dims, n),
        out_shape=[jax.ShapeDtypeStruct(dims + a.shape, a.dtype) for a in arrays],
        in_specs=[ANY] * n,
        out_specs=[ANY] * n,
        scratch_shapes=Gather.sem_shapes(dims, n),
        compiler_params=pltpu.CompilerParams(collective_id=collective_id, has_side_effects=True),
        name="gather_weights",
    )(*arrays)
    return [o.reshape((-1,) + a.shape[1:]) for o, a in zip(outs, arrays)]


class Scatter:
    def __init__(self, place, held, out, bufs, sems, i, src=None):
        self.p, self.src, self.out, self.i = place, src, out, i
        self.own, self.away = (held, None) if src is not None else (held.at[place.c], held.at[place.at("c", 1)])
        self.from_core, self.from_a, self.from_b, self.from_z = bufs
        self.local, self.cs, self.cr, self.as_, self.ar, self.bs, self.br, self.zs, self.zr = sems

    @staticmethod
    def sem_shapes(dims, n):
        ny, nc, nz, nx = dims
        dma = pltpu.SemaphoreType.DMA
        m = max(nx, ny, 2) - 1
        return [dma((n, nx))] * 3 + [dma((n, m))] * 4 + [dma((n, max(1, nz - 1)))] * 2

    @staticmethod
    def buf_shapes(dims, block, lead=()):
        ny, nc, nz, nx = dims
        m = max(nx, ny, 2)
        buf = lambda *s: pltpu.VMEM(lead + s + block, jnp.bfloat16)
        return [buf(ny, nx, nz), buf(m - 1, m, nz), buf(m - 1, nz), buf(max(1, nz - 1))]

    def copy(self, src, dst, send, recv, axis, k):
        return pltpu.make_async_remote_copy(
            src_ref=src, dst_ref=dst, send_sem=send, recv_sem=recv,
            device_id=self.p.device(axis, k), device_id_type=MESH,
        )

    def loads(self):
        p, i = self.p, self.i
        if self.src is None:
            return
        for x in range(p.dims[3]):
            yield lambda x=x: pltpu.make_async_copy(self.src.at[:, p.c, :, x], self.own.at[:, x], self.local.at[i, x])

    def core_copies(self):
        p, i = self.p, self.i
        if p.dims[1] == 1:
            return
        if self.src is None:
            yield lambda: self.copy(self.away, self.from_core, self.cs.at[i, 0], self.cr.at[i, 0], "c", 1)
            return
        for x in range(p.dims[3]):
            yield lambda x=x: self.copy(
                self.src.at[:, p.at("c", 1), :, x], self.from_core.at[:, x], self.cs.at[i, x], self.cr.at[i, x], "c", 1)

    def a_copies(self, first):
        p, i = self.p, self.i
        ny, nc, nz, nx = p.dims
        for k in range(1, ny if first == "y" else nx):
            def copy(k=k):
                if first == "y":
                    src, dst = self.own.at[p.at("y", k)], self.from_a.at[k - 1, pl.ds(0, nx)]
                else:
                    src, dst = self.own.at[:, p.at("x", k)], self.from_a.at[k - 1, pl.ds(0, ny)]
                return self.copy(src, dst, self.as_.at[i, k - 1], self.ar.at[i, k - 1], first, k)
            yield copy

    def b_copies(self, first):
        p, i = self.p, self.i
        ny, nc, nz, nx = p.dims
        second = {"x": "y", "y": "x"}[first]
        for k in range(1, ny if second == "y" else nx):
            def copy(k=k):
                src = self.own.at[p.at("y", k), p.x] if second == "y" else self.own.at[p.y, p.at("x", k)]
                return self.copy(src, self.from_b.at[k - 1], self.bs.at[i, k - 1], self.br.at[i, k - 1], second, k)
            yield copy

    def z_copies(self):
        p, i = self.p, self.i
        for k in range(1, p.dims[2]):
            yield lambda k=k: self.copy(
                self.own.at[p.y, p.x, p.at("z", k)], self.from_z.at[k - 1], self.zs.at[i, k - 1], self.zr.at[i, k - 1], "z", k)

    def by_core(self, body):
        if self.p.dims[1] == 1:
            body("y")
            return
        pl.when(self.p.c == 0)(lambda: body("y"))
        pl.when(self.p.c == 1)(lambda: body("x"))

    @staticmethod
    def add(into, terms):
        if len(terms) == 1:
            into[...] = into[...] + terms[0][...]
        elif terms:
            value = into[...].astype(jnp.float32)
            for term in terms:
                value = value + term[...].astype(jnp.float32)
            into[...] = value.astype(jnp.bfloat16)

    def start(self):
        for copy in self.core_copies():
            copy().start()
        for copy in self.loads():
            copy().start()

    def after_core(self):
        p = self.p
        ny, nc, nz, nx = p.dims
        for copy in self.loads():
            copy().wait()
        for copy in self.core_copies():
            copy().wait_recv()
        if nc > 1:
            def body(y, carry):
                self.add(self.own.at[y], [self.from_core.at[y]])
                return carry
            lax.fori_loop(0, ny, body, 0)

        def go(first):
            for copy in self.a_copies(first):
                copy().start()
        self.by_core(go)

    def after_a(self):
        p = self.p
        ny, nc, nz, nx = p.dims

        def go(first):
            for copy in self.a_copies(first):
                copy().wait_recv()
            n = ny if first == "y" else nx

            def body(j, carry):
                at = (p.y, j) if first == "y" else (j, p.x)
                self.add(self.own.at[at], [self.from_a.at[k, j] for k in range(n - 1)])
                return carry
            lax.fori_loop(0, nx if first == "y" else ny, body, 0)
            for copy in self.b_copies(first):
                copy().start()
        self.by_core(go)

    def after_b(self):
        p = self.p
        ny, nc, nz, nx = p.dims

        def go(first):
            for copy in self.b_copies(first):
                copy().wait_recv()
            n = nx if first == "y" else ny

            self.add(self.own.at[p.y, p.x], [self.from_b.at[k] for k in range(n - 1)])
        self.by_core(go)
        for copy in self.z_copies():
            copy().start()

    def after_z(self):
        p = self.p
        for copy in self.z_copies():
            copy().wait_recv()
        value = self.own[p.y, p.x, p.z].astype(jnp.float32)
        for k in range(p.dims[2] - 1):
            value = value + self.from_z[k].astype(jnp.float32)
        self.out[...] = value

    def finish(self):
        for copy in self.core_copies():
            copy().wait_send()

        def go(first):
            for copy in self.a_copies(first):
                copy().wait_send()
            for copy in self.b_copies(first):
                copy().wait_send()
        self.by_core(go)
        for copy in self.z_copies():
            copy().wait_send()

    def stages(self):
        return [self.start, self.after_core, self.after_a, self.after_b, self.after_z, self.finish]


def run_stages(jobs):
    n, depth = len(jobs), len(jobs[0])
    for t in range(n + depth - 1):
        for i in range(n):
            if 0 <= t - i < depth:
                jobs[i][t - i]()


def scatter_kernel(dims, n, *refs):
    place = Place(dims)
    src, out, rest = refs[:n], refs[n:2 * n], refs[2 * n:]
    bufs, sems = rest[:5 * n], rest[5 * n:]
    enter(place)
    run_stages([
        Scatter(place, bufs[5 * i], out[i], bufs[5 * i + 1:5 * i + 5], sems, i, src[i]).stages() for i in range(n)
    ])


def scatter(dims, arrays, collective_id):
    n = len(arrays)
    devices = math.prod(dims)
    blocks = [(a.shape[0] // devices,) + a.shape[1:] for a in arrays]
    shaped = [a.reshape(dims + b) for a, b in zip(arrays, blocks)]
    scratch = []
    ny, nc, nz, nx = dims
    for b in blocks:
        scratch += [pltpu.VMEM((ny, nx, nz) + b, jnp.bfloat16)] + Scatter.buf_shapes(dims, b)
    return pl.pallas_call(
        functools.partial(scatter_kernel, dims, n),
        out_shape=[jax.ShapeDtypeStruct(b, jnp.float32) for b in blocks],
        in_specs=[ANY] * n,
        out_specs=[pl.BlockSpec(memory_space=pltpu.VMEM)] * n,
        scratch_shapes=scratch + Scatter.sem_shapes(dims, n),
        compiler_params=pltpu.CompilerParams(
            collective_id=collective_id, has_side_effects=True, vmem_limit_bytes=56 << 20),
        name="scatter_gradients",
    )(*shaped)


READY = 3
SENT = 7
CHUNK = 256
SLOTS = 4
TOKENS = 512


def mlp_kernel(dims, chunks, ready, sent, *refs):
    (middle, normed, cot, gain, down, early, local_gu, output, g_middle, g_gain, g_gate_up, g_down, late, gathered,
     normed_t, total, inner_s, grads_s, weights, held, from_core, from_a, from_b, from_z, load) = refs[:25]
    sems = refs[25:]
    ng = len(Gather.sem_shapes(dims, 1))
    place = Place(dims)
    j = pl.program_id(0)
    seq = normed.shape[0]
    block = local_gu.shape[1]
    ny, nc, nz, nx = dims

    def gather_at(m):
        return Gather(place, local_gu.at[m], gathered.at[m - ready], sems[:ng], m - ready)

    def scatter_at(m):
        bufs = [b.at[m] for b in (from_core, from_a, from_b, from_z)]
        return Scatter(place, held.at[lax.rem(m, SLOTS)], g_gate_up.at[m], bufs, sems[ng:], m)

    def do(m, first, last, body):
        if isinstance(m, int):
            if first <= m < last:
                body(m)
            return
        pl.when((m >= first) & (m < last))(lambda: body(m))

    def fetch(m, slot, start):
        def go(src):
            copy = pltpu.make_async_copy(src, weights.at[slot], load.at[slot])
            copy.start() if start else copy.wait()
        if start:
            pl.when(m < ready)(lambda: go(early.at[jnp.minimum(m, ready - 1)]))
            pl.when((m >= ready) & (m < chunks))(lambda: go(gathered.at[jnp.clip(m - ready, 0, chunks - ready - 1)]))
        else:
            go(early.at[0])

    def tick_a(j):
        do(j - 4, 0, sent, lambda m: scatter_at(m).after_z())
        do(j - 4, 0, sent, lambda m: scatter_at(m).finish())
        do(j + 1, ready, chunks, lambda m: gather_at(m).after_second())
        do(j + 2, ready, chunks, lambda m: gather_at(m).after_first())
        do(j + 5, ready + 2, chunks, lambda m: gather_at(m).start())

    def tick_b(j):
        do(j - 3, 0, sent, lambda m: scatter_at(m).after_b())
        do(j - 2, 0, sent, lambda m: scatter_at(m).after_a())
        do(j - 1, 0, sent, lambda m: scatter_at(m).after_core())
        do(j + 1, ready, chunks, lambda m: gather_at(m).finish())
        do(j + 3, ready, min(ready + 1, chunks), lambda m: gather_at(m).after_z())

    def tick_c(j):
        do(j, 0, sent, lambda m: scatter_at(m).start())
        do(j + 4, ready + 1, chunks, lambda m: gather_at(m).after_z())

    @pl.when(j == 0)
    def _():
        fetch(0, 0, True)
        enter(place)
        for m in range(ready, min(ready + 2, chunks)):
            gather_at(m).start()
        normed_t[...] = normed[...].T

    slot = lax.rem(j, 2)
    fetch(j, slot, False)
    w = weights.at[slot]
    down_weight = lambda: jnp.concatenate([down[n] for n in range(down.shape[0])], axis=1)
    weight = lambda: w[...].reshape(D, -1)

    def tokens_part(t):
        r = slice(t * TOKENS, (t + 1) * TOKENS)
        both = dot(normed[r, :], weight())
        gate, up = both[:, :CHUNK], both[:, CHUNK:]
        sig = jax.nn.sigmoid(gate)
        silu = gate * sig
        inner = (silu * up).astype(bf16)
        inner_s[r, :] = inner
        g_inner = dot(cot[r, :], down_weight(), NT)
        g_gate = (g_inner * up * sig * (1.0 + gate * (1.0 - sig))).astype(bf16)
        grads = jnp.concatenate([g_gate, (g_inner * silu).astype(bf16)], axis=1)
        grads_s[r, :] = grads
        out, back = dot(inner, down_weight()), dot(grads, weight(), NT)

        @pl.when(j == 0)
        def _():
            total[r, :] = out
            g_middle[r, :] = back

        @pl.when(j > 0)
        def _():
            total[r, :] += out
            g_middle[r, :] += back

    parts = seq // TOKENS
    tick_a(j)
    for t in range(parts):
        tokens_part(t)
        if t == parts // 2 - 1 or parts == 1:
            tick_b(j)
            fetch(j + 1, 1 - slot, True)
    g_weights = dot(normed_t[...], grads_s[...]).astype(bf16)

    @pl.when(j < sent)
    def _():
        at = held.at[lax.rem(j, SLOTS)]
        for y in range(ny):
            for c in range(nc):
                for z in range(nz):
                    for x in range(nx):
                        row = (((y * nc + c) * nz + z) * nx + x) * block
                        at[c, y, x, z] = g_weights[row:row + block]

    @pl.when(j >= sent)
    def _():
        late[0] = g_weights

    tick_c(j)
    g_down_now = dot(inner_s[...], cot[...], TN).astype(bf16)
    for n in range(g_down.shape[0]):
        g_down[n] = g_down_now[:, n * g_down.shape[2]:(n + 1) * g_down.shape[2]]

    @pl.when(j == chunks - 1)
    def _():
        for t in range(seq // 256):
            r = slice(t * 256, t * 256 + 256)
            m = middle[r, :]
            s = rms(m)
            output[r, :] = (m + total[r, :]).astype(bf16)
            g_normed = g_middle[r, :]
            u = g_normed * gain[1:2, :]
            g_middle[r, :] = cot[r, :].astype(f32) + s * u - m * (s * s * s * jnp.mean(u * m, axis=-1, keepdims=True))
            part = jnp.sum(g_normed * m * s, axis=0, keepdims=True)
            if t == 0:
                g_gain[...] = part
            else:
                g_gain[...] += part
        for k in range(max(0, sent + 4 - chunks)):
            tick_a(chunks + k)
            tick_b(chunks + k)
            tick_c(chunks + k)


def mlp(dims, middle, normed, cot, gain, down, early, local_gu, sent, collective_id):
    chunks, block, width = local_gu.shape
    ready = early.shape[0]
    seq = normed.shape[0]
    ny, nc, nz, nx = dims
    whole = lambda *s: pl.BlockSpec(s, lambda i: (0,) * len(s))
    vmem = lambda s, t: pltpu.VMEM(s, t)
    return pl.pallas_call(
        functools.partial(mlp_kernel, dims, chunks, ready, sent),
        grid=(chunks,),
        out_shape=[
            jax.ShapeDtypeStruct((seq, D), bf16),
            jax.ShapeDtypeStruct((seq, D), f32),
            jax.ShapeDtypeStruct((1, D), f32),
            jax.ShapeDtypeStruct((sent, block, width), f32),
            jax.ShapeDtypeStruct(down.shape, bf16),
            jax.ShapeDtypeStruct((chunks - sent, D, width), bf16),
            jax.ShapeDtypeStruct((chunks - ready,) + dims + (block, width), bf16),
        ],
        in_specs=[whole(seq, D), whole(seq, D), whole(seq, D), whole(8, D), pl.BlockSpec((down.shape[0], CHUNK, down.shape[2]), lambda i: (0, i, 0)), ANY, ANY],
        out_specs=[whole(seq, D), whole(seq, D), whole(1, D), whole(sent, block, width),
                   pl.BlockSpec((down.shape[0], CHUNK, down.shape[2]), lambda i: (0, i, 0)),
                   pl.BlockSpec((1, D, width), lambda i: (jnp.maximum(i - sent, 0), 0, 0)), ANY],
        scratch_shapes=[
            vmem((D, seq), bf16), vmem((seq, D), f32), vmem((seq, CHUNK), bf16), vmem((seq, width), bf16),
            vmem((2,) + dims + (block, width), bf16), vmem((SLOTS, nc, ny, nx, nz, block, width), bf16),
        ] + Scatter.buf_shapes(dims, (block, width), (sent,)) + [pltpu.SemaphoreType.DMA((2,))]
        + Gather.sem_shapes(dims, chunks - ready) + Scatter.sem_shapes(dims, sent),
        compiler_params=pltpu.CompilerParams(
            collective_id=collective_id, has_side_effects=True, vmem_limit_bytes=62 << 20),
        name="mlp",
    )(middle, normed, cot, gain, down, early, local_gu)


STEPS = 4
AHEAD = 4
PAIRS = H // 2


def spread_ticks(ticks, slots):
    plan = [[] for _ in range(slots)]
    for n, tick in enumerate(ticks):
        plan[n * slots // len(ticks)].append(tick)
    return plan


def tick_list(jobs, gap=1):
    n, depth = len(jobs), len(jobs[0])
    return [[jobs[i][(t - i) // gap] for i in range(n) if 0 <= t - i < gap * depth and (t - i) % gap == 0]
            for t in range(n + gap * (depth - 1))]


def run_tick(tick):
    for stage in tick:
        stage()


def windows(width, size):
    return [pl.ds(at, size) for at in range(0, width, size)]


def forward_kernel(dims, ready, *refs):
    (tokens, doc_col, doc_row, cosine, sine, spread, packed, w_out, w_down, gate_up,
     normed, factors, query, key, value, mixed, lse, gains, middle, normed_two, packed_all, out_all, down_all, early,
     weight, out_weight, load) = refs[:27]
    sems = refs[27:]
    place = Place(dims)
    step = pl.program_id(0)
    part = lambda src, dst, rows: (src.at[rows], dst.at[:, :, :, :, rows])
    first = [part(packed, packed_all, rows) for rows in windows(packed.shape[0], 16)]
    pairs = [part(w_out, out_all, rows) for rows in windows(w_out.shape[0], 16)]
    pairs += [(w_down.at[n], down_all.at[n]) for n in range(w_down.shape[0])]
    pairs += [(gate_up.at[m], early.at[m]) for m in range(ready)]
    jobs = [Gather(place, s, d, sems, i).stages() for i, (s, d) in enumerate(first + pairs)]
    first, rest = jobs[:len(first)], jobs[len(first):]
    ticks = tick_list([job[1:] for job in rest], 2)
    for n, job in enumerate(rest[AHEAD:]):
        ticks[n].append(job[0])
    fetch_out = lambda: pltpu.make_async_copy(out_all, out_weight, load)

    @pl.when(step == 0)
    def _():
        enter(place)
        for job in first + rest[:AHEAD]:
            job[0]()
        for tick in tick_list([job[1:] for job in first]):
            run_tick(tick)
        copy = pltpu.make_async_copy(packed_all, weight, load)
        copy.start()
        copy.wait()
        w = weight[...].reshape(D, PACKED)
        gains[...] = w[:, DIMS + HEADS:].astype(f32).T[2 * H:2 * H + 8]

    @pl.when(step < STEPS)
    def _():
        rows = pl.ds(pl.multiple_of(jnp.minimum(step, STEPS - 1) * BLOCK, BLOCK), BLOCK)
        outs = [[r.at[p, rows] for p in range(PAIRS)] for r in (query, key, value)]
        factors_step(tokens, gains[0:1, :], weight[...].reshape(D, PACKED), cosine, sine, spread, normed, factors, *outs)

    @pl.when((step >= STEPS) & (step < STEPS + PAIRS))
    def _():
        p = jnp.clip(step - STEPS, 0, PAIRS - 1)
        cols = pl.ds(pl.multiple_of(p * 128, 128), 128)
        attend_kernel(doc_col, doc_row, query.at[p], key.at[p], value.at[p], mixed.at[:, cols], lse)

    pl.when(step == STEPS + PAIRS - 1)(lambda: fetch_out().start())
    pl.when(step == STEPS + PAIRS)(lambda: fetch_out().wait())

    @pl.when(step >= STEPS + PAIRS)
    def _():
        t = jnp.maximum(step - STEPS - PAIRS, 0)
        rows = pl.ds(pl.multiple_of(t * BLOCK, BLOCK), BLOCK)
        m = tokens[...].astype(f32) + dot(mixed[rows, :], out_weight[...].reshape(H * DH, D))
        middle[...] = m
        normed_two[...] = (m * rms(m) * gains[1:2, :]).astype(bf16)

    for at, todo in enumerate(spread_ticks(ticks, 2 * STEPS + PAIRS)):
        if todo:
            @pl.when(step == at)
            def _(todo=todo):
                for tick in todo:
                    run_tick(tick)


def forward(dims, tokens, doc_col, doc_row, tables, packed, w_out, w_down, gate_up, ready, collective_id):
    cosine, sine, spread = tables
    seq = tokens.shape[0]
    whole = lambda *s: pl.BlockSpec(s, lambda i: (0,) * len(s), pipeline_mode=pl.Buffered(1))
    kept = lambda *s: pl.BlockSpec(s, lambda i: (0,) * len(s))
    row = lambda width: pl.BlockSpec((BLOCK, width), lambda i: (jnp.minimum(i, STEPS - 1), 0))
    again = lambda i: jnp.maximum(i - STEPS - PAIRS, 0)
    after = lambda i: jnp.clip(i - STEPS, 0, PAIRS - 1)
    ends = pl.BlockSpec((BLOCK, D), lambda i: (jnp.where(i < STEPS, i, again(i)), 0))
    last = pl.BlockSpec((BLOCK, D), lambda i: (again(i), 0))
    full = lambda a: jax.ShapeDtypeStruct(dims + a.shape, a.dtype)
    jobs = packed.shape[0] // 16 + w_out.shape[0] // 16 + w_down.shape[0] + ready
    return pl.pallas_call(
        functools.partial(forward_kernel, dims, ready),
        grid=(2 * STEPS + PAIRS,),
        out_shape=[
            jax.ShapeDtypeStruct((seq, D), bf16),
            jax.ShapeDtypeStruct((seq, PACKED), f32),
        ] + [jax.ShapeDtypeStruct((PAIRS, seq, 128), bf16)] * 3 + [
            jax.ShapeDtypeStruct((seq, H * DH), bf16),
            jax.ShapeDtypeStruct((PAIRS, 2, seq), f32),
            jax.ShapeDtypeStruct((8, D), f32),
            jax.ShapeDtypeStruct((seq, D), f32), jax.ShapeDtypeStruct((seq, D), bf16),
            full(packed), full(w_out), jax.ShapeDtypeStruct(w_down.shape[:1] + dims + w_down.shape[1:], bf16),
            jax.ShapeDtypeStruct((ready,) + dims + gate_up.shape[1:], bf16),
        ],
        in_specs=[ends, whole(seq, 1), whole(1, seq), row(128), row(128), whole(*spread.shape)] + [ANY] * 4,
        out_specs=[row(D), row(PACKED)] + [kept(PAIRS, seq, 128)] * 3 + [
            kept(seq, H * DH),
            pl.BlockSpec((1, 2, seq), lambda i: (after(i), 0, 0)),
            kept(8, D), last, last,
        ] + [ANY] * 4,
        scratch_shapes=[pltpu.VMEM(dims + packed.shape, bf16), pltpu.VMEM(dims + w_out.shape, bf16), pltpu.SemaphoreType.DMA]
        + Gather.sem_shapes(dims, jobs),
        compiler_params=pltpu.CompilerParams(
            collective_id=collective_id, has_side_effects=True, vmem_limit_bytes=58 << 20),
        name="forward",
    )(tokens, doc_col, doc_row, cosine, sine, spread, packed, w_out, w_down, gate_up)


def backward_kernel(dims, widths, *refs):
    (doc_col, doc_row, query, key, value, grad, lse, tokens, gain, packed_all, cosine, sine, spread, factors, g_middle,
     normed, g_gain_two, g_down, g_out, g_late) = refs[:20]
    g_tokens, down_out, out_out, late_out, gains_out = refs[20:25]
    packed_out = refs[25:25 + len(widths)]
    at = 25 + len(widths)
    g_query, g_key, g_value, weight, g_factors, g_gain, reduced, load = refs[at:at + 8]
    bufs = refs[at + 8:at + 8 + 20]
    sems = refs[at + 28:]
    place = Place(dims)
    ny, nc, nz, nx = dims
    step = pl.program_id(0)
    block = packed_all.shape[4]
    fetch = lambda: pltpu.make_async_copy(packed_all, weight, load)
    jobs = []
    for n, rows in enumerate(windows(out_out.shape[0], 16)):
        own = [b.at[n] for b in bufs[0:5]]
        jobs.append(Scatter(place, own[0], out_out.at[rows], own[1:], sems, len(jobs), g_out.at[:, :, :, :, rows]))
    for n in range(down_out.shape[0]):
        own = [b.at[n] for b in bufs[5:10]]
        jobs.append(Scatter(place, own[0], down_out.at[n], own[1:], sems, len(jobs), g_down.at[n]))
    for n in range(late_out.shape[0]):
        own = [b.at[n] for b in bufs[15:20]]
        jobs.append(Scatter(place, own[0], late_out.at[n], own[1:], sems, len(jobs), g_late.at[n]))
    last = []
    for n, rows in enumerate(windows(block, 16)):
        own = [b.at[n] for b in bufs[10:15]]
        last.append(Scatter(place, own[0], reduced.at[rows], own[1:], sems, len(jobs) + n))
    ticks = tick_list([job.stages()[1:] for job in jobs], 2)
    total = PAIRS + STEPS

    @pl.when(step == 0)
    def _():
        fetch().start()
        enter(place)
        for job in jobs:
            job.start()

    @pl.when(step < PAIRS)
    def _():
        p = jnp.minimum(step, PAIRS - 1)
        attend_back_kernel(doc_col, doc_row, query.at[0], key.at[0], value.at[0], grad, lse,
                           g_query.at[p], g_key.at[p], g_value.at[p])

    pl.when(step == PAIRS)(lambda: fetch().wait())

    @pl.when(step >= PAIRS)
    def _():
        t = jnp.maximum(step - PAIRS, 0)
        rows = pl.ds(pl.multiple_of(t * BLOCK, BLOCK), BLOCK)
        grads = [jnp.concatenate([g[p, rows, :] for p in range(PAIRS)], axis=1) for g in (g_query, g_key, g_value)]
        factors_back_step(t, tokens, gain[0:1, :], weight[...].reshape(D, PACKED), cosine, sine, spread, factors, *grads,
                          g_middle, g_factors.at[rows], g_tokens, g_gain)

    for n, todo in enumerate(spread_ticks(ticks, total)):
        if todo:
            @pl.when(step == n)
            def _(todo=todo):
                for tick in todo:
                    run_tick(tick)

    @pl.when(step == total - 1)
    def _():
        g_weight = dot(normed[...], g_factors[...], TN)
        column = lambda row: jnp.broadcast_to(row, (128, D)).T
        lane = lax.broadcasted_iota(jnp.int32, (D, 128), 1)
        tail = g_weight[:, DIMS + HEADS:]
        tail = jnp.where(lane == 2 * H, column(g_gain[...]), jnp.where(lane == 2 * H + 1, column(g_gain_two[...]), tail))
        g_weight = jnp.concatenate([g_weight[:, :DIMS + HEADS], tail], axis=1).astype(bf16)
        for y in range(ny):
            for c in range(nc):
                for z in range(nz):
                    for x in range(nx):
                        row = (((y * nc + c) * nz + z) * nx + x) * block
                        for n in range(block // 16):
                            bufs[10][n, c, y, x, z] = g_weight[row + 16 * n:row + 16 * n + 16]
        for tick in tick_list([job.stages() for job in last]):
            run_tick(tick)
        at = 0
        for out, width in zip(packed_out, widths):
            out[...] = reduced[:, at:at + width]
            at += width
        gains_out[...] = reduced[:, at:at + 2]


def backward(dims, widths, doc_col, doc_row, query, key, value, grad, lse, tokens, gains, packed_all, tables, factors,
             g_middle, normed, g_gain_two, g_down, g_out, g_late, collective_id):
    cosine, sine, spread = tables
    seq = tokens.shape[0]
    ny, nc, nz, nx = dims
    block = packed_all.shape[4]
    whole = lambda *s: pl.BlockSpec(s, lambda i: (0,) * len(s), pipeline_mode=pl.Buffered(1))
    kept = lambda *s: pl.BlockSpec(s, lambda i: (0,) * len(s))
    before = lambda i: jnp.minimum(i, PAIRS - 1)
    after = lambda i: jnp.maximum(i - PAIRS, 0)
    pair = pl.BlockSpec((1, seq, 128), lambda i: (before(i), 0, 0))
    row = lambda width: pl.BlockSpec((seq // STEPS, width), lambda i: (after(i), 0))
    buffers = []
    groups = ((g_out.shape[4] // 16, (16, D)), (g_down.shape[0], g_down.shape[5:]), (block // 16, (16, PACKED)),
              (g_late.shape[0], g_late.shape[5:]))
    for n, (many, b) in enumerate(groups):
        held = (nc, ny, nx, nz) if n == 2 else (ny, nx, nz)
        buffers += [pltpu.VMEM((many,) + held + b, bf16)] + Scatter.buf_shapes(dims, b, (many,))
    outs = [(g_down.shape[0],) + g_down.shape[5:], (g_out.shape[4], D), (g_late.shape[0],) + g_late.shape[5:], (block, 2)]
    outs += [(block, w) for w in widths]
    shape = lambda *s: jax.ShapeDtypeStruct(s, f32)
    return pl.pallas_call(
        functools.partial(backward_kernel, dims, widths),
        grid=(PAIRS + STEPS,),
        out_shape=[jax.ShapeDtypeStruct((seq, D), bf16)] + [shape(*s) for s in outs],
        in_specs=[whole(seq, 1), whole(1, seq), pair, pair, pair, pl.BlockSpec((seq, 128), lambda i: (0, before(i))),
                  pl.BlockSpec((1, 2, seq), lambda i: (before(i), 0, 0)), row(D), whole(8, D), ANY, row(128), row(128),
                  whole(*spread.shape), row(PACKED), row(D), whole(seq, D), whole(1, D), ANY, ANY, ANY],
        out_specs=[row(D)] + [kept(*s) for s in outs],
        scratch_shapes=[pltpu.VMEM((PAIRS, seq, 128), f32)] * 3 + [
            pltpu.VMEM(dims + (block, PACKED), bf16), pltpu.VMEM((seq, PACKED), bf16), pltpu.VMEM((1, D), f32),
            pltpu.VMEM((block, PACKED), f32), pltpu.SemaphoreType.DMA,
        ] + buffers + Scatter.sem_shapes(dims, sum(many for many, _ in groups)),
        compiler_params=pltpu.CompilerParams(
            collective_id=collective_id, has_side_effects=True, vmem_limit_bytes=62 << 20),
        name="backward",
    )(doc_col, doc_row, query, key, value, grad, lse, tokens, gains, packed_all, cosine, sine, spread, factors,
      g_middle, normed, g_gain_two, g_down, g_out, g_late)


def plain_mlp(middle, normed_two, cotangent, gain, gate_w, up_w, down_w):
    gate, up = dot(normed_two, gate_w), dot(normed_two, up_w)
    sig = jax.nn.sigmoid(gate)
    silu = gate * sig
    inner = (silu * up).astype(bf16)
    output = (middle + dot(inner, down_w)).astype(bf16)
    grad_inner = dot(cotangent, down_w, NT)
    grad_gate = (grad_inner * up * sig * (1.0 + gate * (1.0 - sig))).astype(bf16)
    grad_up = (grad_inner * silu).astype(bf16)
    grad_normed = dot(grad_gate, gate_w, NT) + dot(grad_up, up_w, NT)
    scale = rms(middle)
    gained = grad_normed * gain
    grad_middle = (
        cotangent.astype(f32)
        + scale * gained
        - middle * scale**3 * jnp.mean(gained * middle, axis=-1, keepdims=True)
    )
    grad_gain = jnp.sum(grad_normed * middle * scale, axis=0, keepdims=True)
    outer_sum = lambda left, right: dot(left, right, TN).astype(bf16)
    return (
        output, grad_middle, grad_gain,
        outer_sum(inner, cotangent), outer_sum(normed_two, grad_gate), outer_sum(normed_two, grad_up),
    )


def on_device(
    dims,
    tokens,
    doc_ids,
    norm_gain,
    w_query_heads,
    w_query_dims,
    w_key_heads,
    w_key_dims,
    w_value_heads,
    w_value_dims,
    w_output,
    mlp_gain,
    w_gate,
    w_up,
    w_down,
    out_grad,
):
    seq_len = tokens.shape[0] * tokens.shape[1]
    tables = tuple(jnp.asarray(t) for t in rope_tables(seq_len) + (spread_table(),))
    parts = (w_query_dims, w_key_dims, w_value_dims, w_query_heads, w_key_heads, w_value_heads)
    edges = [0]
    for part in parts:
        edges.append(edges[-1] + part.shape[1])
    gains_at = edges[-1]
    packed = jnp.concatenate(
        parts
        + (norm_gain[:, None], mlp_gain[:, None])
        + (jnp.zeros((norm_gain.shape[0], PACKED - gains_at - 2), bf16),),
        axis=1,
    )
    inputs, cotangent = tokens.reshape(seq_len, D), out_grad.reshape(seq_len, D)
    doc_row, doc_col = doc_ids.reshape(1, seq_len), doc_ids.reshape(seq_len, 1)
    outer_sum = lambda left, right: dot(left, right, TN).astype(bf16)
    block = w_gate.shape[0]
    if block % 16 == 0 and w_gate.shape[1] % CHUNK == 0 and seq_len % TOKENS == 0:
        chunked = lambda w: w.reshape(w.shape[0], -1, CHUNK).transpose(1, 0, 2)
        whole = lambda g: g.transpose(1, 0, 2).reshape(g.shape[1], -1)
        gate_up = jnp.concatenate([chunked(w_gate), chunked(w_up)], axis=2)
        (normed, factors, query, key, value, mixed, lse, gains, middle, normed_two,
         packed_w, output_w, down_w, early) = forward(
            dims, inputs, doc_col, doc_row, tables, packed, w_output, chunked(w_down), gate_up, READY, 0
        )
        output_w = output_w.reshape(-1, D)
        output, grad_middle, grad_mlp_gain, gate_up_out, grad_down, grad_late, _ = mlp(
            dims, middle, normed_two, cotangent, gains, down_w.reshape(down_w.shape[0], -1, CHUNK), early, gate_up, SENT, 1
        )
        grad_branch = grad_middle.astype(bf16)
        grad_mixed = dot(grad_branch, output_w, NT).astype(bf16)
        grad_tokens, down_out, output_out, late_out, gains_out, *parts_out = backward(
            dims, [part.shape[1] for part in parts], doc_col, doc_row, query, key, value, grad_mixed, lse, inputs,
            gains, packed_w, tables, factors, grad_middle, normed, grad_mlp_gain,
            grad_down.reshape(down_w.shape), outer_sum(mixed, grad_branch).reshape(dims + w_output.shape),
            grad_late.reshape((-1,) + dims + gate_up.shape[1:]), 2,
        )
        gate_up_out = jnp.concatenate([gate_up_out, late_out])
        gate_out, up_out = whole(gate_up_out[:, :, :CHUNK]), whole(gate_up_out[:, :, CHUNK:])
        grads = [g for pair in zip(parts_out[3:], parts_out[:3]) for g in pair]
        return (
            output.reshape(tokens.shape), grad_tokens.reshape(tokens.shape), gains_out[:, 0], *grads,
            output_out, gains_out[:, 1], gate_out, up_out, whole(down_out),
        )

    packed_w, output_w, gate_w, up_w, down_w = gather(
        dims, [packed, w_output, w_gate, w_up, w_down], 0
    )
    gain_one, gain_two = [packed_w[:, gains_at + i].astype(f32).reshape(1, D) for i in (0, 1)]
    normed, factors, query, key, value = make_factors(inputs, gain_one, packed_w, tables)
    mixed, lse = attend(doc_col, doc_row, query, key, value)
    middle = inputs.astype(f32) + dot(mixed, output_w)
    normed_two = (middle * rms(middle) * gain_two).astype(bf16)
    output, grad_middle, grad_mlp_gain, *mlp_grads = plain_mlp(
        middle, normed_two, cotangent, gain_two, gate_w, up_w, down_w
    )
    grad_branch = grad_middle.astype(bf16)
    grad_mixed = dot(grad_branch, output_w, NT).astype(bf16)

    grad_query, grad_key, grad_value = attend_back(
        doc_col, doc_row, query, key, value, grad_mixed, lse
    )
    grad_factors, grad_tokens, grad_norm_gain = factors_back(
        inputs, gain_one, packed_w, tables, factors, grad_query, grad_key, grad_value, grad_middle
    )
    gains = jnp.stack([grad_norm_gain[0], grad_mlp_gain[0]], axis=1).astype(bf16)
    packed_grad = lax.dynamic_update_slice(outer_sum(normed, grad_factors), gains, (0, gains_at))
    *mlp_out, output_out, packed_out = scatter(
        dims, mlp_grads + [outer_sum(mixed, grad_branch), packed_grad], 2
    )
    down_out, gate_out, up_out = mlp_out
    dims_and_heads = [packed_out[:, lo:hi] for lo, hi in zip(edges, edges[1:])]
    grads = [g for pair in zip(dims_and_heads[3:], dims_and_heads[:3]) for g in pair]
    return (
        output.reshape(tokens.shape),
        grad_tokens.reshape(tokens.shape),
        packed_out[:, gains_at],
        *grads,
        output_out,
        packed_out[:, gains_at + 1],
        gate_out,
        up_out,
        down_out,
    )


def solution(mesh):
    rows, matrix, vector = P(("dp", "fsdp"), None, None), P(("dp", "fsdp"), None), P(("dp", "fsdp"))
    return jax.shard_map(
        functools.partial(on_device, grid_of(mesh)),
        mesh=mesh,
        in_specs=(rows, matrix, vector) + (matrix,) * 7 + (vector,) + (matrix,) * 3 + (rows,),
        out_specs=(rows, rows, vector) + (matrix,) * 7 + (vector,) + (matrix,) * 3,
        check_vma=False,
    )
```

```python
import functools
import math

import jax
import jax.numpy as jnp
import numpy as np
from jax import lax
from jax.experimental import pallas as pl
from jax.experimental.pallas import tpu as pltpu
from jax.sharding import PartitionSpec as P

MESH = pl.DeviceIdType.MESH
D, H, DH, RQ, RK = 1024, 16, 64, 6, 2
PACKED = 896
DIMS, HEADS = 640, 128
BLOCK = 256
BACK = 512
NEG = -1e30
epsilon = 1e-06
theta_base = 10000.0
f32, bf16 = jnp.float32, jnp.bfloat16
NT = (((1,), (1,)), ((), ()))
NN = (((1,), (0,)), ((), ()))
TN = (((0,), (0,)), ((), ()))


def dot(a, b, dims=NN):
    return lax.dot_general(a, b, dims, preferred_element_type=f32)


def params(**kw):
    return pltpu.CompilerParams(vmem_limit_bytes=56 << 20, **kw)


def rope_tables(seq_len):
    half = DH // 2
    position = np.arange(seq_len, dtype=np.float32)
    inverse = np.exp(-math.log(theta_base) * 2.0 * np.arange(half, dtype=np.float32) / np.float32(2.0 * half)).astype(np.float32)
    angle = (position[:, None] * inverse[None, :]).astype(np.float32)
    cosine, sine = np.cos(angle), np.sin(angle)
    return (np.concatenate([cosine] * 4, 1), np.concatenate([-sine, sine] * 2, 1))


def spread_table():
    out = np.zeros((8, 2 * HEADS, H * DH), np.float32)
    for j in range(8):
        for h in range(H):
            out[j, [j * H + h, HEADS + j * H + h], h * DH:(h + 1) * DH] = 1.0
    return out.astype(jnp.bfloat16)


def low_lane(shape):
    return lax.rem(lax.broadcasted_iota(jnp.int32, shape, 1), 128) < 64


def first_half(shape):
    return lax.rem(lax.broadcasted_iota(jnp.int32, shape, 1), 64) < 32


def turn(x, cosine, sine):
    partner = jnp.where(first_half(x.shape), pltpu.roll(x, 96, 1), pltpu.roll(x, 32, 1))
    return x * cosine + partner * sine


def split_bf16(x):
    hi = x.astype(bf16)
    return jnp.concatenate([hi, (x - hi.astype(f32)).astype(bf16)], axis=1)


def twice(x, rank):
    rolled = pltpu.roll(x, 64, 1)
    low = low_lane(x.shape)
    return jnp.where(low, x, rolled) if rank % 2 == 0 else jnp.where(low, rolled, x)


def wide(x):
    return jnp.concatenate([x] * (H * DH // 128), axis=1)


def rms(x):
    return lax.rsqrt(jnp.mean(x * x, axis=-1, keepdims=True) + epsilon)


FACTORS = ((0, RQ, 0), (RQ, RK, 3), (0, RK, 4))


def factors_step(tokens, gain, weight, cosine, sine, spread, normed, factors, query, key, value):
    x = tokens[...].astype(f32)
    n = (x * rms(x) * gain).astype(bf16)
    normed[...] = n
    f = dot(n, weight)
    pairs = [f[:, 128 * i:128 * i + 128] for i in range(DIMS // 128)]
    pairs = [turn(p, cosine[...], sine[...]) if i < 4 else p for i, p in enumerate(pairs)]
    for i, p in enumerate(pairs):
        factors[:, 128 * i:128 * i + 128] = p
    factors[:, DIMS:] = f[:, DIMS:]
    heads_qk = split_bf16(f[:, DIMS:DIMS + HEADS])
    heads_v = split_bf16(f[:, DIMS + HEADS:])
    for out, heads, (at, ranks, pair), scale in zip(
        (query, key, value), (heads_qk, heads_qk, heads_v), FACTORS, (0.125, 1.0, 1.0)
    ):
        total = None
        for r in range(ranks):
            term = dot(heads, spread[at + r]) * wide(twice(pairs[pair + r // 2], r))
            total = term if total is None else total + term
        rounded = (total * (1.0 / ranks)).astype(bf16)
        rounded = rounded * jnp.asarray(scale, bf16) if scale != 1.0 else rounded
        for p, ref in enumerate(out):
            ref[...] = rounded[:, 128 * p:128 * p + 128]


def factors_kernel(tokens, gain, weight, cosine, sine, spread, normed, factors, query, key, value):
    outs = [[r.at[p] for p in range(H // 2)] for r in (query, key, value)]
    factors_step(tokens, gain[...], weight[...], cosine, sine, spread, normed, factors, *outs)


def make_factors(tokens, gain, weight, tables):
    cosine, sine, spread = tables
    seq = tokens.shape[0]
    row = lambda width: pl.BlockSpec((BLOCK, width), lambda i: (i, 0))
    whole = lambda a: pl.BlockSpec(a.shape, lambda i: (0,) * a.ndim)
    return pl.pallas_call(
        factors_kernel,
        grid=(seq // BLOCK,),
        out_shape=[
            jax.ShapeDtypeStruct((seq, D), bf16),
            jax.ShapeDtypeStruct((seq, PACKED), f32),
        ] + [jax.ShapeDtypeStruct((H // 2, seq, 128), bf16)] * 3,
        in_specs=[row(D), whole(gain), whole(weight), row(128), row(128), whole(spread)],
        out_specs=[row(D), row(PACKED)] + [pl.BlockSpec((H // 2, BLOCK, 128), lambda i: (0, i, 0))] * 3,
        compiler_params=params(),
        name="factors",
    )(tokens, gain, weight, cosine, sine, spread)


def allowed_t(doc_col, doc_row, k0, kn, q0, qn):
    same = doc_col[k0:k0 + kn, 0:1].astype(f32) == doc_row[:, q0:q0 + qn].astype(f32)
    if k0 + kn - 1 > q0:
        k_at = k0 + lax.broadcasted_iota(jnp.int32, (kn, qn), 0)
        q_at = q0 + lax.broadcasted_iota(jnp.int32, (kn, qn), 1)
        same = same & (k_at <= q_at)
    return same


def halves(x):
    low = low_lane(x.shape)
    zero = jnp.zeros_like(x)
    return jnp.where(low, x, zero), jnp.where(low, zero, x)


def attend_kernel(doc_col, doc_row, query, key, value, mixed, lse):
    seq = query.shape[0]
    v_half = halves(value[...])
    for q0 in range(0, seq, BLOCK):
        lo = max(0, q0 - BACK)
        kn = q0 + BLOCK - lo
        ok = allowed_t(doc_col, doc_row, lo, kn, q0, BLOCK)
        probs = []
        for h, q in enumerate(halves(query[q0:q0 + BLOCK, :])):
            s = jnp.where(ok, dot(key[lo:lo + kn, :], q, NT), NEG)
            top = jnp.max(s, axis=0, keepdims=True)
            e = jnp.exp(s - top)
            total = jnp.sum(e, axis=0, keepdims=True)
            probs.append((e * (1.0 / total)).astype(bf16))
            lse[0, h:h + 1, q0:q0 + BLOCK] = top + jnp.log(total)
        values = jnp.concatenate([v[lo:lo + kn] for v in v_half], axis=0)
        mixed[q0:q0 + BLOCK, :] = dot(jnp.concatenate(probs, axis=0), values, TN).astype(bf16)


def attend(doc_col, doc_row, query, key, value):
    pairs, seq, _ = query.shape
    whole = lambda a: pl.BlockSpec(a.shape, lambda i: (0,) * a.ndim)
    pair = pl.BlockSpec((seq, 128), lambda i: (0, i))
    return pl.pallas_call(
        lambda dc, dr, q, k, v, *outs: attend_kernel(dc, dr, q.at[0], k.at[0], v.at[0], *outs),
        grid=(pairs,),
        out_shape=[jax.ShapeDtypeStruct((seq, H * DH), bf16), jax.ShapeDtypeStruct((pairs, 2, seq), f32)],
        in_specs=[whole(doc_col), whole(doc_row)] + [pl.BlockSpec((1, seq, 128), lambda i: (i, 0, 0))] * 3,
        out_specs=[pair, pl.BlockSpec((1, 2, seq), lambda i: (i, 0, 0))],
        compiler_params=params(),
        name="attend",
    )(doc_col, doc_row, query, key, value)


def attend_back_kernel(doc_col, doc_row, query, key, value, grad, lse, g_query, g_key, g_value):
    seq = query.shape[0]
    k_half = halves(key[...])
    for q0 in range(0, seq, BLOCK):
        lo = max(0, q0 - BACK)
        kn = q0 + BLOCK - lo
        ok = allowed_t(doc_col, doc_row, lo, kn, q0, BLOCK)
        ps, ds = [], []
        q_half, g_half = halves(query[q0:q0 + BLOCK, :]), halves(grad[q0:q0 + BLOCK, :])
        for h in (0, 1):
            s = dot(key[lo:lo + kn, :], q_half[h], NT)
            p = jnp.where(ok, jnp.exp(s - lse[0, h:h + 1, q0:q0 + BLOCK]), 0.0)
            pd = p * dot(value[lo:lo + kn, :], g_half[h], NT)
            ps.append(p.astype(bf16))
            ds.append((pd - p * jnp.sum(pd, axis=0, keepdims=True)).astype(bf16))
        to_value = dot(jnp.concatenate(ps, 1), jnp.concatenate(g_half, 0))
        to_key = dot(jnp.concatenate(ds, 1), jnp.concatenate(q_half, 0))
        if q0 > lo:
            g_value[lo:q0, :] += to_value[:q0 - lo]
            g_key[lo:q0, :] += to_key[:q0 - lo]
        g_value[q0:q0 + BLOCK, :] = to_value[q0 - lo:]
        g_key[q0:q0 + BLOCK, :] = to_key[q0 - lo:]
        keys = jnp.concatenate([k[lo:lo + kn] for k in k_half], 0)
        g_query[q0:q0 + BLOCK, :] = dot(jnp.concatenate(ds, 0), keys, TN) * 0.125


def attend_back(doc_col, doc_row, query, key, value, grad, lse):
    pairs, seq, _ = query.shape
    whole = lambda a: pl.BlockSpec(a.shape, lambda i: (0,) * a.ndim)
    pair = pl.BlockSpec((seq, 128), lambda i: (0, i))
    return pl.pallas_call(
        lambda dc, dr, q, k, v, *rest: attend_back_kernel(dc, dr, q.at[0], k.at[0], v.at[0], *rest),
        grid=(pairs,),
        out_shape=[jax.ShapeDtypeStruct((seq, H * DH), f32)] * 3,
        in_specs=[whole(doc_col), whole(doc_row)] + [pl.BlockSpec((1, seq, 128), lambda i: (i, 0, 0))] * 3 + [pair, pl.BlockSpec((1, 2, seq), lambda i: (i, 0, 0))],
        out_specs=[pair] * 3,
        compiler_params=params(),
        name="attend_back",
    )(doc_col, doc_row, query, key, value, grad, lse)


def factors_back_step(cosine, sine, spread, factors, g_query, g_key, g_value, g_factors):
    pairs = [factors[:, 128 * i:128 * i + 128] for i in range(DIMS // 128)]
    heads_qk = split_bf16(factors[:, DIMS:DIMS + HEADS])
    heads_v = split_bf16(factors[:, DIMS + HEADS:])
    g_heads = [None, None]
    for grad, heads, which, (at, ranks, pair) in zip(
        (g_query, g_key, g_value), (heads_qk, heads_qk, heads_v), (0, 0, 1), FACTORS
    ):
        g = grad * (1.0 / ranks)
        folded = []
        for r in range(ranks):
            product = (g * wide(twice(pairs[pair + r // 2], r))).astype(bf16)
            part = dot(product, spread[at + r, :HEADS, :], NT)
            g_heads[which] = part if g_heads[which] is None else g_heads[which] + part
            full = g * dot(heads, spread[at + r])
            folded.append(sum(full[:, 128 * i:128 * i + 128] for i in range(H * DH // 128)))
        for r in range(0, ranks, 2):
            a, b = folded[r], folded[r + 1]
            low = low_lane(a.shape)
            mine = jnp.where(low, a, b)
            other = jnp.where(low, pltpu.roll(a, 64, 1), pltpu.roll(b, 64, 1))
            both = mine + other
            i = pair + r // 2
            if i < 4:
                both = turn(both, cosine[...], -sine[...])
            g_factors[:, 128 * i:128 * i + 128] = both.astype(bf16)
    g_factors[:, DIMS:DIMS + HEADS] = g_heads[0].astype(bf16)
    g_factors[:, DIMS + HEADS:] = g_heads[1].astype(bf16)


def tokens_back_step(step, tokens, gain, weight, g_factors, g_middle, g_tokens, g_gain):
    g_normed = dot(g_factors[...], weight, NT)
    x = tokens[...].astype(f32)
    r1 = rms(x)
    u = g_normed * gain
    part = jnp.sum(g_normed * x * r1, axis=0, keepdims=True)

    @pl.when(step == 0)
    def _():
        g_gain[...] = part

    @pl.when(step > 0)
    def _():
        g_gain[...] += part

    g_tokens[...] = (g_middle[...] + r1 * u - x * (r1 * r1 * r1 * jnp.mean(u * x, axis=-1, keepdims=True))).astype(bf16)


def factors_back_kernel(tokens, gain, weight, cosine, sine, spread, factors, g_query, g_key, g_value, g_middle,
                        g_factors, g_tokens, g_gain):
    factors_back_step(cosine, sine, spread, factors, g_query[...], g_key[...], g_value[...], g_factors)
    tokens_back_step(pl.program_id(0), tokens, gain[...], weight[...], g_factors, g_middle, g_tokens, g_gain)


def factors_back(tokens, gain, weight, tables, factors, g_query, g_key, g_value, g_middle):
    cosine, sine, spread = tables
    seq = tokens.shape[0]
    row = lambda width: pl.BlockSpec((BLOCK, width), lambda i: (i, 0))
    whole = lambda a: pl.BlockSpec(a.shape, lambda i: (0,) * a.ndim)
    return pl.pallas_call(
        factors_back_kernel,
        grid=(seq // BLOCK,),
        out_shape=[
            jax.ShapeDtypeStruct((seq, PACKED), bf16),
            jax.ShapeDtypeStruct((seq, D), bf16),
            jax.ShapeDtypeStruct((1, D), f32),
        ],
        in_specs=[row(D), whole(gain), whole(weight), row(128), row(128), whole(spread), row(PACKED)]
        + [row(H * DH)] * 3 + [row(D)],
        out_specs=[row(PACKED), row(D), pl.BlockSpec((1, D), lambda i: (0, 0))],
        compiler_params=params(),
        name="factors_back",
    )(tokens, gain, weight, cosine, sine, spread, factors, g_query, g_key, g_value, g_middle)

ANY = pl.BlockSpec(memory_space=pl.ANY)


def grid_of(mesh):
    nd, nf = mesh.shape["dp"], mesh.shape["fsdp"]
    nc = math.gcd(2, nd)
    nz = math.gcd(4, nf)
    return (nd // nc, nc, nz, nf // nz)


class Place:
    def __init__(self, dims):
        self.dims = dims
        ny, nc, nz, nx = dims
        dp, fs = lax.axis_index("dp"), lax.axis_index("fsdp")
        self.y, self.c = lax.div(dp, nc), lax.rem(dp, nc)
        self.z, self.x = lax.div(fs, nx), lax.rem(fs, nx)

    def at(self, axis, k):
        n = self.dims["yczx".index(axis)]
        return lax.rem(getattr(self, axis) + k + n, n)

    def device(self, axis=None, k=0):
        ny, nc, nz, nx = self.dims
        put = {a: getattr(self, a) for a in "yczx"}
        if axis is not None:
            put[axis] = self.at(axis, k)
        return (put["y"] * nc + put["c"], put["z"] * nx + put["x"])


def peers_of(dims):
    ny, nc, nz, nx = dims
    return [(a, k) for a, n in (("y", ny), ("c", nc), ("z", nz), ("x", nx)) for k in range(1, n)]


def enter(place):
    barrier = pltpu.get_barrier_semaphore()
    peers = peers_of(place.dims)
    for axis, k in peers:
        pl.semaphore_signal(barrier, inc=1, device_id=place.device(axis, k), device_id_type=MESH)
    pl.semaphore_wait(barrier, len(peers))


class Gather:
    def __init__(self, place, src, dst, sems, i):
        self.p, self.src, self.dst, self.i = place, src, dst, i
        self.local, self.zs, self.zr, self.as_, self.ar, self.bs, self.br, self.cs, self.cr = sems

    @staticmethod
    def sem_shapes(dims, n):
        ny, nc, nz, nx = dims
        dma = pltpu.SemaphoreType.DMA
        m = max(nx, ny) - 1
        one = lambda k: dma((n, max(1, k)))
        return [dma((n,)), one(nz - 1), one(nz - 1), one(m), one(m), one(m), one(m), one(nx + ny - 1), one(nx + ny - 1)]

    def copy(self, ref_src, ref_dst, send, recv, axis, k):
        return pltpu.make_async_remote_copy(
            src_ref=ref_src, dst_ref=ref_dst, send_sem=send, recv_sem=recv,
            device_id=self.p.device(axis, k), device_id_type=MESH,
        )

    def z_copies(self):
        p, i = self.p, self.i
        nz = p.dims[2]
        mine = self.dst.at[p.y, p.c, p.z, p.x]
        def one(k, back):
            if back:
                ref = self.dst.at[p.y, p.c, p.at("z", -k), p.x]
                return self.copy(ref, ref, self.zs.at[i, k - 1], self.zr.at[i, k - 1], "z", k)
            return self.copy(self.src, mine, self.zs.at[i, k - 1], self.zr.at[i, k - 1], "z", k)

        return [[functools.partial(one, k, back) for k in range(1, nz)] for back in (False, True)]

    def part(self, first, step, y, x, c):
        every = slice(None)
        if step == 0:
            return self.dst.at[y, c, :, x]
        return self.dst.at[y, c] if first == "x" else self.dst.at[:, c, :, x]

    def side_copies(self, first, step):
        p, i = self.p, self.i
        axis = first if step == 0 else {"x": "y", "y": "x"}[first]
        n = p.dims["yczx".index(axis)]
        s, r = ((self.as_, self.ar), (self.bs, self.br))[step]

        def one(k, back):
            y, x = p.y, p.x
            if back:
                y, x = (p.y, p.at("x", -k)) if axis == "x" else (p.at("y", -k), p.x)
            ref = self.part(first, step, y, x, p.c)
            return self.copy(ref, ref, s.at[i, k - 1], r.at[i, k - 1], axis, k)

        return [[functools.partial(one, k, back) for k in range(1, n)] for back in (False, True)]

    def core_copies(self, first, c):
        p, i = self.p, self.i
        second = {"x": "y", "y": "x"}[first]
        lists, j = [], 0
        for step, axis in ((0, None), (0, first), (1, second)):
            now = []
            count = 1 if axis is None else p.dims["yczx".index(axis)] - 1
            for k in range(1, count + 1):
                def one(axis=axis, step=step, k=k, j=j):
                    y = p.at("y", -k) if axis == "y" else p.y
                    x = p.at("x", -k) if axis == "x" else p.x
                    ref = self.part(first, step, y, x, c)
                    return self.copy(ref, ref, self.cs.at[i, j], self.cr.at[i, j], "c", 1)

                now.append(one)
                j += 1
            lists.append(now)
        return lists

    def start(self):
        p = self.p
        mine = self.dst.at[p.y, p.c, p.z, p.x]
        pltpu.make_async_copy(self.src, mine, self.local.at[self.i]).start()
        for copy in self.z_copies()[0]:
            copy().start()

    def by_core(self, body):
        if self.p.dims[1] == 1:
            body("x")
            return
        pl.when(self.p.c == 0)(lambda: body("x"))
        pl.when(self.p.c == 1)(lambda: body("y"))

    def after_z(self):
        p = self.p
        mine = self.dst.at[p.y, p.c, p.z, p.x]
        pltpu.make_async_copy(self.src, mine, self.local.at[self.i]).wait()
        for copy in self.z_copies()[1]:
            copy().wait_recv()

        def body(first):
            for copy in self.side_copies(first, 0)[0]:
                copy().start()
            if p.dims[1] > 1:
                for copy in self.core_copies(first, p.c)[0]:
                    copy().start()

        self.by_core(body)

    def after_first(self):
        p = self.p

        def body(first):
            for copy in self.side_copies(first, 0)[1]:
                copy().wait_recv()
            for copy in self.side_copies(first, 1)[0]:
                copy().start()
            if p.dims[1] > 1:
                for copy in self.core_copies(first, p.c)[1]:
                    copy().start()

        self.by_core(body)

    def after_second(self):
        p = self.p

        def body(first):
            for copy in self.side_copies(first, 1)[1]:
                copy().wait_recv()
            if p.dims[1] > 1:
                for copy in self.core_copies(first, p.c)[2]:
                    copy().start()

        self.by_core(body)

    def finish(self):
        p = self.p
        for copy in self.z_copies()[0]:
            copy().wait_send()

        def body(first):
            for step in (0, 1):
                for copy in self.side_copies(first, step)[0]:
                    copy().wait_send()
            if p.dims[1] > 1:
                for now in self.core_copies(first, p.c):
                    for copy in now:
                        copy().wait_send()
                other = {"x": "y", "y": "x"}[first]
                for now in self.core_copies(other, p.at("c", 1)):
                    for copy in now:
                        copy().wait_recv()

        self.by_core(body)

    def stages(self):
        return [self.start, self.after_z, self.after_first, self.after_second, self.finish]


def gather_kernel(dims, n, *refs):
    place = Place(dims)
    src, dst, sems = refs[:n], refs[n:2 * n], refs[2 * n:]
    enter(place)
    jobs = [Gather(place, src[i], dst[i], sems, i).stages() for i in range(n)]
    run_stages(jobs)


def gather(dims, arrays, collective_id):
    n = len(arrays)
    outs = pl.pallas_call(
        functools.partial(gather_kernel, dims, n),
        out_shape=[jax.ShapeDtypeStruct(dims + a.shape, a.dtype) for a in arrays],
        in_specs=[ANY] * n,
        out_specs=[ANY] * n,
        scratch_shapes=Gather.sem_shapes(dims, n),
        compiler_params=pltpu.CompilerParams(collective_id=collective_id, has_side_effects=True),
        name="gather_weights",
    )(*arrays)
    return [o.reshape((-1,) + a.shape[1:]) for o, a in zip(outs, arrays)]


class Scatter:
    def __init__(self, place, held, out, bufs, sems, i, src=None):
        self.p, self.src, self.out, self.i = place, src, out, i
        self.own, self.away = (held, None) if src is not None else (held.at[place.c], held.at[place.at("c", 1)])
        self.from_core, self.from_a, self.from_b, self.from_z = bufs
        self.local, self.cs, self.cr, self.as_, self.ar, self.bs, self.br, self.zs, self.zr = sems

    @staticmethod
    def sem_shapes(dims, n):
        ny, nc, nz, nx = dims
        dma = pltpu.SemaphoreType.DMA
        m = max(nx, ny, 2) - 1
        return [dma((n, nx))] * 3 + [dma((n, m))] * 4 + [dma((n, max(1, nz - 1)))] * 2

    @staticmethod
    def buf_shapes(dims, block, lead=()):
        ny, nc, nz, nx = dims
        m = max(nx, ny, 2)
        buf = lambda *s: pltpu.VMEM(lead + s + block, jnp.bfloat16)
        return [buf(ny, nx, nz), buf(m - 1, m, nz), buf(m - 1, nz), buf(max(1, nz - 1))]

    def copy(self, src, dst, send, recv, axis, k):
        return pltpu.make_async_remote_copy(
            src_ref=src, dst_ref=dst, send_sem=send, recv_sem=recv,
            device_id=self.p.device(axis, k), device_id_type=MESH,
        )

    def loads(self):
        p, i = self.p, self.i
        if self.src is None:
            return
        for x in range(p.dims[3]):
            yield lambda x=x: pltpu.make_async_copy(self.src.at[:, p.c, :, x], self.own.at[:, x], self.local.at[i, x])

    def core_copies(self):
        p, i = self.p, self.i
        if p.dims[1] == 1:
            return
        if self.src is None:
            yield lambda: self.copy(self.away, self.from_core, self.cs.at[i, 0], self.cr.at[i, 0], "c", 1)
            return
        for x in range(p.dims[3]):
            yield lambda x=x: self.copy(
                self.src.at[:, p.at("c", 1), :, x], self.from_core.at[:, x], self.cs.at[i, x], self.cr.at[i, x], "c", 1)

    def a_copies(self, first):
        p, i = self.p, self.i
        ny, nc, nz, nx = p.dims
        for k in range(1, ny if first == "y" else nx):
            def copy(k=k):
                if first == "y":
                    src, dst = self.own.at[p.at("y", k)], self.from_a.at[k - 1, pl.ds(0, nx)]
                else:
                    src, dst = self.own.at[:, p.at("x", k)], self.from_a.at[k - 1, pl.ds(0, ny)]
                return self.copy(src, dst, self.as_.at[i, k - 1], self.ar.at[i, k - 1], first, k)
            yield copy

    def b_copies(self, first):
        p, i = self.p, self.i
        ny, nc, nz, nx = p.dims
        second = {"x": "y", "y": "x"}[first]
        for k in range(1, ny if second == "y" else nx):
            def copy(k=k):
                src = self.own.at[p.at("y", k), p.x] if second == "y" else self.own.at[p.y, p.at("x", k)]
                return self.copy(src, self.from_b.at[k - 1], self.bs.at[i, k - 1], self.br.at[i, k - 1], second, k)
            yield copy

    def z_copies(self):
        p, i = self.p, self.i
        for k in range(1, p.dims[2]):
            yield lambda k=k: self.copy(
                self.own.at[p.y, p.x, p.at("z", k)], self.from_z.at[k - 1], self.zs.at[i, k - 1], self.zr.at[i, k - 1], "z", k)

    def by_core(self, body):
        if self.p.dims[1] == 1:
            body("y")
            return
        pl.when(self.p.c == 0)(lambda: body("y"))
        pl.when(self.p.c == 1)(lambda: body("x"))

    @staticmethod
    def add(into, terms):
        if len(terms) == 1:
            into[...] = into[...] + terms[0][...]
        elif terms:
            value = into[...].astype(jnp.float32)
            for term in terms:
                value = value + term[...].astype(jnp.float32)
            into[...] = value.astype(jnp.bfloat16)

    def start(self):
        for copy in self.core_copies():
            copy().start()
        for copy in self.loads():
            copy().start()

    def after_core(self):
        p = self.p
        ny, nc, nz, nx = p.dims
        for copy in self.loads():
            copy().wait()
        for copy in self.core_copies():
            copy().wait_recv()
        if nc > 1:
            def body(y, carry):
                self.add(self.own.at[y], [self.from_core.at[y]])
                return carry
            lax.fori_loop(0, ny, body, 0)

        def go(first):
            for copy in self.a_copies(first):
                copy().start()
        self.by_core(go)

    def after_a(self):
        p = self.p
        ny, nc, nz, nx = p.dims

        def go(first):
            for copy in self.a_copies(first):
                copy().wait_recv()
            n = ny if first == "y" else nx

            def body(j, carry):
                at = (p.y, j) if first == "y" else (j, p.x)
                self.add(self.own.at[at], [self.from_a.at[k, j] for k in range(n - 1)])
                return carry
            lax.fori_loop(0, nx if first == "y" else ny, body, 0)
            for copy in self.b_copies(first):
                copy().start()
        self.by_core(go)

    def after_b(self):
        p = self.p
        ny, nc, nz, nx = p.dims

        def go(first):
            for copy in self.b_copies(first):
                copy().wait_recv()
            n = nx if first == "y" else ny

            self.add(self.own.at[p.y, p.x], [self.from_b.at[k] for k in range(n - 1)])
        self.by_core(go)
        for copy in self.z_copies():
            copy().start()

    def after_z(self):
        p = self.p
        for copy in self.z_copies():
            copy().wait_recv()
        value = self.own[p.y, p.x, p.z].astype(jnp.float32)
        for k in range(p.dims[2] - 1):
            value = value + self.from_z[k].astype(jnp.float32)
        self.out[...] = value

    def finish(self):
        for copy in self.core_copies():
            copy().wait_send()

        def go(first):
            for copy in self.a_copies(first):
                copy().wait_send()
            for copy in self.b_copies(first):
                copy().wait_send()
        self.by_core(go)
        for copy in self.z_copies():
            copy().wait_send()

    def stages(self):
        return [self.start, self.after_core, self.after_a, self.after_b, self.after_z, self.finish]


def run_stages(jobs):
    n, depth = len(jobs), len(jobs[0])
    for t in range(n + depth - 1):
        for i in range(n):
            if 0 <= t - i < depth:
                jobs[i][t - i]()


def scatter_kernel(dims, n, *refs):
    place = Place(dims)
    src, out, rest = refs[:n], refs[n:2 * n], refs[2 * n:]
    bufs, sems = rest[:5 * n], rest[5 * n:]
    enter(place)
    run_stages([
        Scatter(place, bufs[5 * i], out[i], bufs[5 * i + 1:5 * i + 5], sems, i, src[i]).stages() for i in range(n)
    ])


def scatter(dims, arrays, collective_id):
    n = len(arrays)
    devices = math.prod(dims)
    blocks = [(a.shape[0] // devices,) + a.shape[1:] for a in arrays]
    shaped = [a.reshape(dims + b) for a, b in zip(arrays, blocks)]
    scratch = []
    ny, nc, nz, nx = dims
    for b in blocks:
        scratch += [pltpu.VMEM((ny, nx, nz) + b, jnp.bfloat16)] + Scatter.buf_shapes(dims, b)
    return pl.pallas_call(
        functools.partial(scatter_kernel, dims, n),
        out_shape=[jax.ShapeDtypeStruct(b, jnp.float32) for b in blocks],
        in_specs=[ANY] * n,
        out_specs=[pl.BlockSpec(memory_space=pltpu.VMEM)] * n,
        scratch_shapes=scratch + Scatter.sem_shapes(dims, n),
        compiler_params=pltpu.CompilerParams(
            collective_id=collective_id, has_side_effects=True, vmem_limit_bytes=56 << 20),
        name="scatter_gradients",
    )(*shaped)


READY = 3
SENT = 7
CHUNK = 256
SLOTS = 4
TOKENS = 512


def mlp_kernel(dims, chunks, ready, sent, *refs):
    (middle, normed, cot, gain, down, early, local_gu, output, g_middle, g_branch, g_gain, g_gate_up, g_down, late, gathered,
     normed_t, total, inner_s, grads_s, weights, held, from_core, from_a, from_b, from_z, load) = refs[:26]
    sems = refs[26:]
    ng = len(Gather.sem_shapes(dims, 1))
    place = Place(dims)
    j = pl.program_id(0)
    seq = normed.shape[0]
    block = local_gu.shape[1]
    ny, nc, nz, nx = dims

    def gather_at(m):
        return Gather(place, local_gu.at[m], gathered.at[m - ready], sems[:ng], m - ready)

    def scatter_at(m):
        bufs = [b.at[m] for b in (from_core, from_a, from_b, from_z)]
        return Scatter(place, held.at[lax.rem(m, SLOTS)], g_gate_up.at[m], bufs, sems[ng:], m)

    def do(m, first, last, body):
        if isinstance(m, int):
            if first <= m < last:
                body(m)
            return
        pl.when((m >= first) & (m < last))(lambda: body(m))

    def fetch(m, slot, start):
        def go(src):
            copy = pltpu.make_async_copy(src, weights.at[slot], load.at[slot])
            copy.start() if start else copy.wait()
        if start:
            pl.when(m < ready)(lambda: go(early.at[jnp.minimum(m, ready - 1)]))
            pl.when((m >= ready) & (m < chunks))(lambda: go(gathered.at[jnp.clip(m - ready, 0, chunks - ready - 1)]))
        else:
            go(early.at[0])

    def tick_a(j):
        do(j - 4, 0, sent, lambda m: scatter_at(m).after_z())
        do(j - 4, 0, sent, lambda m: scatter_at(m).finish())
        do(j + 1, ready, chunks, lambda m: gather_at(m).after_second())
        do(j + 2, ready, chunks, lambda m: gather_at(m).after_first())
        do(j + 5, ready + 2, chunks, lambda m: gather_at(m).start())

    def tick_b(j):
        do(j - 3, 0, sent, lambda m: scatter_at(m).after_b())
        do(j - 2, 0, sent, lambda m: scatter_at(m).after_a())
        do(j - 1, 0, sent, lambda m: scatter_at(m).after_core())
        do(j + 1, ready, chunks, lambda m: gather_at(m).finish())
        do(j + 3, ready, min(ready + 1, chunks), lambda m: gather_at(m).after_z())

    def tick_c(j):
        do(j, 0, sent, lambda m: scatter_at(m).start())
        do(j + 4, ready + 1, chunks, lambda m: gather_at(m).after_z())

    @pl.when(j == 0)
    def _():
        fetch(0, 0, True)
        enter(place)
        for m in range(ready, min(ready + 2, chunks)):
            gather_at(m).start()
        normed_t[...] = normed[...].T

    slot = lax.rem(j, 2)
    fetch(j, slot, False)
    w = weights.at[slot]
    down_weight = lambda: jnp.concatenate([down[n] for n in range(down.shape[0])], axis=1)
    weight = lambda: w[...].reshape(D, -1)

    def tokens_part(t):
        r = slice(t * TOKENS, (t + 1) * TOKENS)
        both = dot(normed[r, :], weight())
        gate, up = both[:, :CHUNK], both[:, CHUNK:]
        sig = jax.nn.sigmoid(gate)
        silu = gate * sig
        inner = (silu * up).astype(bf16)
        inner_s[r, :] = inner
        g_inner = dot(cot[r, :], down_weight(), NT)
        g_gate = (g_inner * up * sig * (1.0 + gate * (1.0 - sig))).astype(bf16)
        grads = jnp.concatenate([g_gate, (g_inner * silu).astype(bf16)], axis=1)
        grads_s[r, :] = grads
        out, back = dot(inner, down_weight()), dot(grads, weight(), NT)

        @pl.when(j == 0)
        def _():
            total[r, :] = out
            g_middle[r, :] = back

        @pl.when(j > 0)
        def _():
            total[r, :] += out
            g_middle[r, :] += back

    parts = seq // TOKENS
    tick_a(j)
    for t in range(parts):
        tokens_part(t)
        if t == parts // 2 - 1 or parts == 1:
            tick_b(j)
            fetch(j + 1, 1 - slot, True)
    g_weights = dot(normed_t[...], grads_s[...]).astype(bf16)

    @pl.when(j < sent)
    def _():
        at = held.at[lax.rem(j, SLOTS)]
        for y in range(ny):
            for c in range(nc):
                for z in range(nz):
                    for x in range(nx):
                        row = (((y * nc + c) * nz + z) * nx + x) * block
                        at[c, y, x, z] = g_weights[row:row + block]

    @pl.when(j >= sent)
    def _():
        late[0] = g_weights

    tick_c(j)
    g_down_now = dot(inner_s[...], cot[...], TN).astype(bf16)
    for n in range(g_down.shape[0]):
        g_down[n] = g_down_now[:, n * g_down.shape[2]:(n + 1) * g_down.shape[2]]

    @pl.when(j == chunks - 1)
    def _():
        for t in range(seq // 256):
            r = slice(t * 256, t * 256 + 256)
            m = middle[r, :]
            s = rms(m)
            output[r, :] = (m + total[r, :]).astype(bf16)
            g_normed = g_middle[r, :]
            u = g_normed * gain[1:2, :]
            g_now = cot[r, :].astype(f32) + s * u - m * (s * s * s * jnp.mean(u * m, axis=-1, keepdims=True))
            g_middle[r, :] = g_now
            g_branch[r, :] = g_now.astype(bf16)
            part = jnp.sum(g_normed * m * s, axis=0, keepdims=True)
            if t == 0:
                g_gain[...] = part
            else:
                g_gain[...] += part
        for k in range(max(0, sent + 4 - chunks)):
            tick_a(chunks + k)
            tick_b(chunks + k)
            tick_c(chunks + k)


def mlp(dims, middle, normed, cot, gain, down, early, local_gu, sent, collective_id):
    chunks, block, width = local_gu.shape
    ready = early.shape[0]
    seq = normed.shape[0]
    ny, nc, nz, nx = dims
    whole = lambda *s: pl.BlockSpec(s, lambda i: (0,) * len(s))
    vmem = lambda s, t: pltpu.VMEM(s, t)
    return pl.pallas_call(
        functools.partial(mlp_kernel, dims, chunks, ready, sent),
        grid=(chunks,),
        out_shape=[
            jax.ShapeDtypeStruct((seq, D), bf16),
            jax.ShapeDtypeStruct((seq, D), f32),
            jax.ShapeDtypeStruct((seq, D), bf16),
            jax.ShapeDtypeStruct((1, D), f32),
            jax.ShapeDtypeStruct((sent, block, width), f32),
            jax.ShapeDtypeStruct(down.shape, bf16),
            jax.ShapeDtypeStruct((chunks - sent, D, width), bf16),
            jax.ShapeDtypeStruct((chunks - ready,) + dims + (block, width), bf16),
        ],
        in_specs=[whole(seq, D), whole(seq, D), whole(seq, D), whole(8, D), pl.BlockSpec((down.shape[0], CHUNK, down.shape[2]), lambda i: (0, i, 0)), ANY, ANY],
        out_specs=[whole(seq, D)] * 3 + [whole(1, D), whole(sent, block, width),
                   pl.BlockSpec((down.shape[0], CHUNK, down.shape[2]), lambda i: (0, i, 0)),
                   pl.BlockSpec((1, D, width), lambda i: (jnp.maximum(i - sent, 0), 0, 0)), ANY],
        scratch_shapes=[
            vmem((D, seq), bf16), vmem((seq, D), f32), vmem((seq, CHUNK), bf16), vmem((seq, width), bf16),
            vmem((2,) + dims + (block, width), bf16), vmem((SLOTS, nc, ny, nx, nz, block, width), bf16),
        ] + Scatter.buf_shapes(dims, (block, width), (sent,)) + [pltpu.SemaphoreType.DMA((2,))]
        + Gather.sem_shapes(dims, chunks - ready) + Scatter.sem_shapes(dims, sent),
        compiler_params=pltpu.CompilerParams(
            collective_id=collective_id, has_side_effects=True, vmem_limit_bytes=62 << 20),
        name="mlp",
    )(middle, normed, cot, gain, down, early, local_gu)


STEPS = 4
AHEAD = 4
SPREAD = (8, 2 * HEADS, H * DH)
FB, FD, FG, BB, BD, BG = 1, 0.7, 2, 0, 0.35, 2
PAIRS = H // 2


def spread_ticks(ticks, slots, busy, drain):
    plan = [[] for _ in range(slots)]
    total = busy + drain * (len(ticks) - busy)
    at = 0.0
    for n, tick in enumerate(ticks):
        at += 1.0 if n < busy else drain
        plan[min(slots - 1, int(at * slots / total))].append(tick)
    return plan


def tick_list(jobs, gap=1):
    n, depth = len(jobs), len(jobs[0])
    return [[jobs[i][(t - i) // gap] for i in range(n) if 0 <= t - i < gap * depth and (t - i) % gap == 0]
            for t in range(n + gap * (depth - 1))]


def run_tick(tick):
    for stage in tick:
        stage()


def fill_spread(spread):
    row = lax.rem(lax.broadcasted_iota(jnp.int32, spread.shape[1:], 0), HEADS)
    offset = row - lax.div(lax.broadcasted_iota(jnp.int32, spread.shape[1:], 1), DH)
    for j in range(spread.shape[0]):
        spread[j] = jnp.where(offset == j * H, 1.0, 0.0).astype(bf16)


def windows(width, size):
    return [pl.ds(at, size) for at in range(0, width, size)]


def forward_kernel(dims, ready, *refs):
    (tokens, doc_row, cosine, sine, packed, w_out, w_down, gate_up,
     normed, factors, query, key, value, mixed, lse, gains, middle, normed_two, packed_all, out_all, down_all, early,
     weight, out_weight, doc_col, spread, load) = refs[:27]
    sems = refs[27:]
    place = Place(dims)
    step = pl.program_id(0)
    part = lambda src, dst, rows: (src.at[rows], dst.at[:, :, :, :, rows])
    first = [part(packed, packed_all, rows) for rows in windows(packed.shape[0], 16)]
    pairs = [part(w_out, out_all, rows) for rows in windows(w_out.shape[0], 16)]
    pairs += [(w_down.at[n], down_all.at[n]) for n in range(w_down.shape[0])]
    pairs += [(gate_up.at[m], early.at[m]) for m in range(ready)]
    jobs = [Gather(place, s, d, sems, i).stages() for i, (s, d) in enumerate(first + pairs)]
    first, rest = jobs[:len(first)], jobs[len(first):]
    ticks = tick_list([job[1:] for job in rest], FG)
    for n, job in enumerate(rest[AHEAD:]):
        ticks[n].append(job[0])
    fetch_out = lambda: pltpu.make_async_copy(out_all, out_weight, load)

    @pl.when(step == 0)
    def _():
        doc_col[...] = jnp.broadcast_to(doc_row[...].astype(f32), (8, doc_row.shape[1])).T
        enter(place)
        for job in first + rest[:AHEAD]:
            job[0]()
        fill_spread(spread)
        for tick in tick_list([job[1:] for job in first]):
            run_tick(tick)
        copy = pltpu.make_async_copy(packed_all, weight, load)
        copy.start()
        copy.wait()
        w = weight[...].reshape(D, PACKED)
        gains[...] = w[:, DIMS + HEADS:].astype(f32).T[2 * H:2 * H + 8]

    @pl.when(step < STEPS)
    def _():
        rows = pl.ds(pl.multiple_of(jnp.minimum(step, STEPS - 1) * BLOCK, BLOCK), BLOCK)
        outs = [[r.at[p, rows] for p in range(PAIRS)] for r in (query, key, value)]
        factors_step(tokens, gains[0:1, :], weight[...].reshape(D, PACKED), cosine, sine, spread, normed, factors, *outs)

    @pl.when((step >= STEPS) & (step < STEPS + PAIRS))
    def _():
        p = jnp.clip(step - STEPS, 0, PAIRS - 1)
        cols = pl.ds(pl.multiple_of(p * 128, 128), 128)
        attend_kernel(doc_col, doc_row, query.at[p], key.at[p], value.at[p], mixed.at[:, cols], lse)

    pl.when(step == STEPS + PAIRS - 1)(lambda: fetch_out().start())
    pl.when(step == STEPS + PAIRS)(lambda: fetch_out().wait())

    @pl.when(step >= STEPS + PAIRS)
    def _():
        t = jnp.maximum(step - STEPS - PAIRS, 0)
        rows = pl.ds(pl.multiple_of(t * BLOCK, BLOCK), BLOCK)
        m = tokens[...].astype(f32) + dot(mixed[rows, :], out_weight[...].reshape(H * DH, D))
        middle[...] = m
        normed_two[...] = (m * rms(m) * gains[1:2, :]).astype(bf16)

    for at, todo in enumerate(spread_ticks(ticks, 2 * STEPS + PAIRS, len(rest) + FB, FD)):
        if todo:
            @pl.when(step == at)
            def _(todo=todo):
                for tick in todo:
                    run_tick(tick)


def forward(dims, tokens, doc_row, tables, packed, w_out, w_down, gate_up, ready, collective_id):
    cosine, sine = tables
    seq = tokens.shape[0]
    whole = lambda *s: pl.BlockSpec(s, lambda i: (0,) * len(s), pipeline_mode=pl.Buffered(1))
    kept = lambda *s: pl.BlockSpec(s, lambda i: (0,) * len(s))
    row = lambda width: pl.BlockSpec((BLOCK, width), lambda i: (jnp.minimum(i, STEPS - 1), 0))
    again = lambda i: jnp.maximum(i - STEPS - PAIRS, 0)
    after = lambda i: jnp.clip(i - STEPS, 0, PAIRS - 1)
    ends = pl.BlockSpec((BLOCK, D), lambda i: (jnp.where(i < STEPS, i, again(i)), 0))
    last = pl.BlockSpec((BLOCK, D), lambda i: (again(i), 0))
    full = lambda a: jax.ShapeDtypeStruct(dims + a.shape, a.dtype)
    jobs = packed.shape[0] // 16 + w_out.shape[0] // 16 + w_down.shape[0] + ready
    return pl.pallas_call(
        functools.partial(forward_kernel, dims, ready),
        grid=(2 * STEPS + PAIRS,),
        out_shape=[
            jax.ShapeDtypeStruct((seq, D), bf16),
            jax.ShapeDtypeStruct((seq, PACKED), f32),
        ] + [jax.ShapeDtypeStruct((PAIRS, seq, 128), bf16)] * 3 + [
            jax.ShapeDtypeStruct((seq, H * DH), bf16),
            jax.ShapeDtypeStruct((PAIRS, 2, seq), f32),
            jax.ShapeDtypeStruct((8, D), f32),
            jax.ShapeDtypeStruct((seq, D), f32), jax.ShapeDtypeStruct((seq, D), bf16),
            full(packed), full(w_out), jax.ShapeDtypeStruct(w_down.shape[:1] + dims + w_down.shape[1:], bf16),
            jax.ShapeDtypeStruct((ready,) + dims + gate_up.shape[1:], bf16),
        ],
        in_specs=[ends, whole(1, seq), row(128), row(128)] + [ANY] * 4,
        out_specs=[row(D), row(PACKED)] + [kept(PAIRS, seq, 128)] * 3 + [
            kept(seq, H * DH),
            pl.BlockSpec((1, 2, seq), lambda i: (after(i), 0, 0)),
            kept(8, D), last, last,
        ] + [ANY] * 4,
        scratch_shapes=[pltpu.VMEM(dims + packed.shape, bf16), pltpu.VMEM(dims + w_out.shape, bf16), pltpu.VMEM((seq, 8), f32), pltpu.VMEM(SPREAD, bf16), pltpu.SemaphoreType.DMA]
        + Gather.sem_shapes(dims, jobs),
        compiler_params=pltpu.CompilerParams(
            collective_id=collective_id, has_side_effects=True, vmem_limit_bytes=58 << 20),
        name="forward",
    )(tokens, doc_row, cosine, sine, packed, w_out, w_down, gate_up)


def backward_kernel(dims, *refs):
    (doc_row, query, key, value, grad, lse, tokens, gain, packed_all, cosine, sine, factors, g_middle,
     normed, g_gain_two, g_down, g_out, g_late) = refs[:18]
    g_tokens, down_out, out_out, late_out, reduced = refs[18:23]
    at = 23
    g_query, g_key, g_value, weight, g_factors, g_gain, doc_col, spread, load = refs[at:at + 9]
    bufs = refs[at + 9:at + 9 + 20]
    sems = refs[at + 29:]
    place = Place(dims)
    ny, nc, nz, nx = dims
    step = pl.program_id(0)
    block = packed_all.shape[4]
    fetch = lambda: pltpu.make_async_copy(packed_all, weight, load)
    jobs = []
    for n, rows in enumerate(windows(out_out.shape[0], 16)):
        own = [b.at[n] for b in bufs[0:5]]
        jobs.append(Scatter(place, own[0], out_out.at[rows], own[1:], sems, len(jobs), g_out.at[:, :, :, :, rows]))
    for n in range(down_out.shape[0]):
        own = [b.at[n] for b in bufs[5:10]]
        jobs.append(Scatter(place, own[0], down_out.at[n], own[1:], sems, len(jobs), g_down.at[n]))
    for n in range(late_out.shape[0]):
        own = [b.at[n] for b in bufs[15:20]]
        jobs.append(Scatter(place, own[0], late_out.at[n], own[1:], sems, len(jobs), g_late.at[n]))
    last = []
    for n, rows in enumerate(windows(block, 16)):
        own = [b.at[n] for b in bufs[10:15]]
        last.append(Scatter(place, own[0], reduced.at[rows], own[1:], sems, len(jobs) + n))
    ticks = tick_list([job.stages()[1:] for job in jobs], BG)
    total = PAIRS + STEPS

    @pl.when(step == 0)
    def _():
        fetch().start()
        doc_col[...] = jnp.broadcast_to(doc_row[...].astype(f32), (8, doc_row.shape[1])).T
        enter(place)
        for job in jobs:
            job.start()
        fill_spread(spread)

    @pl.when(step < PAIRS)
    def _():
        p = jnp.minimum(step, PAIRS - 1)
        attend_back_kernel(doc_col, doc_row, query.at[0], key.at[0], value.at[0], grad, lse,
                           g_query.at[p], g_key.at[p], g_value.at[p])

    pl.when(step == PAIRS)(lambda: fetch().wait())

    @pl.when(step >= PAIRS)
    def _():
        t = jnp.maximum(step - PAIRS, 0)
        rows = pl.ds(pl.multiple_of(t * BLOCK, BLOCK), BLOCK)
        grads = [jnp.concatenate([g[p, rows, :] for p in range(PAIRS)], axis=1) for g in (g_query, g_key, g_value)]
        factors_back_step(cosine, sine, spread, factors, *grads, g_factors.at[rows])
        tokens_back_step(t, tokens, gain[0:1, :], weight[...].reshape(D, PACKED), g_factors.at[rows], g_middle, g_tokens, g_gain)

    for n, todo in enumerate(spread_ticks(ticks, total, len(jobs) + BB, BD)):
        if todo:
            @pl.when(step == n)
            def _(todo=todo):
                for tick in todo:
                    run_tick(tick)

    @pl.when(step == total - 1)
    def _():
        g_weight = dot(normed[...], g_factors[...], TN)
        column = lambda row: jnp.broadcast_to(row, (128, D)).T
        lane = lax.broadcasted_iota(jnp.int32, (D, 128), 1)
        tail = g_weight[:, DIMS + HEADS:]
        tail = jnp.where(lane == 2 * H, column(g_gain[...]), jnp.where(lane == 2 * H + 1, column(g_gain_two[...]), tail))
        g_weight = jnp.concatenate([g_weight[:, :DIMS + HEADS], tail], axis=1).astype(bf16)
        for y in range(ny):
            for c in range(nc):
                for z in range(nz):
                    for x in range(nx):
                        row = (((y * nc + c) * nz + z) * nx + x) * block
                        for n in range(block // 16):
                            bufs[10][n, c, y, x, z] = g_weight[row + 16 * n:row + 16 * n + 16]
        for tick in tick_list([job.stages() for job in last]):
            run_tick(tick)


def backward(dims, doc_row, query, key, value, grad, lse, tokens, gains, packed_all, tables, factors,
             g_middle, normed, g_gain_two, g_down, g_out, g_late, collective_id):
    cosine, sine = tables
    seq = tokens.shape[0]
    ny, nc, nz, nx = dims
    block = packed_all.shape[4]
    whole = lambda *s: pl.BlockSpec(s, lambda i: (0,) * len(s), pipeline_mode=pl.Buffered(1))
    kept = lambda *s: pl.BlockSpec(s, lambda i: (0,) * len(s))
    before = lambda i: jnp.minimum(i, PAIRS - 1)
    after = lambda i: jnp.maximum(i - PAIRS, 0)
    pair = pl.BlockSpec((1, seq, 128), lambda i: (before(i), 0, 0))
    row = lambda width: pl.BlockSpec((seq // STEPS, width), lambda i: (after(i), 0))
    buffers = []
    groups = ((g_out.shape[4] // 16, (16, D)), (g_down.shape[0], g_down.shape[5:]), (block // 16, (16, PACKED)),
              (g_late.shape[0], g_late.shape[5:]))
    for n, (many, b) in enumerate(groups):
        held = (nc, ny, nx, nz) if n == 2 else (ny, nx, nz)
        buffers += [pltpu.VMEM((many,) + held + b, bf16)] + Scatter.buf_shapes(dims, b, (many,))
    outs = [(g_down.shape[0],) + g_down.shape[5:], (g_out.shape[4], D), (g_late.shape[0],) + g_late.shape[5:], (block, PACKED)]
    shape = lambda *s: jax.ShapeDtypeStruct(s, f32)
    return pl.pallas_call(
        functools.partial(backward_kernel, dims),
        grid=(PAIRS + STEPS,),
        out_shape=[jax.ShapeDtypeStruct((seq, D), bf16)] + [shape(*s) for s in outs],
        in_specs=[whole(1, seq), pair, pair, pair, pl.BlockSpec((seq, 128), lambda i: (0, before(i))),
                  pl.BlockSpec((1, 2, seq), lambda i: (before(i), 0, 0)), row(D), whole(8, D), ANY, row(128), row(128),
                  row(PACKED), row(D), whole(seq, D), whole(1, D), ANY, ANY, ANY],
        out_specs=[row(D)] + [kept(*s) for s in outs],
        scratch_shapes=[pltpu.VMEM((PAIRS, seq, 128), f32)] * 3 + [
            pltpu.VMEM(dims + (block, PACKED), bf16), pltpu.VMEM((seq, PACKED), bf16), pltpu.VMEM((1, D), f32),
            pltpu.VMEM((seq, 8), f32), pltpu.VMEM(SPREAD, bf16), pltpu.SemaphoreType.DMA,
        ] + buffers + Scatter.sem_shapes(dims, sum(many for many, _ in groups)),
        compiler_params=pltpu.CompilerParams(
            collective_id=collective_id, has_side_effects=True, vmem_limit_bytes=62 << 20),
        name="backward",
    )(doc_row, query, key, value, grad, lse, tokens, gains, packed_all, cosine, sine, factors,
      g_middle, normed, g_gain_two, g_down, g_out, g_late)


def pack_kernel(packed, down, gate_up, w_down, w_gate, w_up, *parts):
    at = 0
    for part in parts[:-2]:
        packed[:, at:at + part.shape[1]] = part[...]
        at += part.shape[1]
    rows = jnp.concatenate([gain[...].astype(f32) for gain in parts[-2:]] + [jnp.zeros((6, packed.shape[0]), f32)], axis=0)
    packed[:, at:at + 8] = rows.T.astype(bf16)
    packed[:, at + 8:] = jnp.zeros((packed.shape[0], PACKED - at - 8), bf16)
    for n in range(down.shape[0]):
        down[n] = w_down[:, n * CHUNK:(n + 1) * CHUNK]
    for n in range(gate_up.shape[0]):
        gate_up[n, :, :CHUNK] = w_gate[:, n * CHUNK:(n + 1) * CHUNK]
        gate_up[n, :, CHUNK:] = w_up[:, n * CHUNK:(n + 1) * CHUNK]


def pack(parts, gains, w_down, w_gate, w_up):
    block, hidden = w_gate.shape
    shape = lambda *s: jax.ShapeDtypeStruct(s, bf16)
    return pl.pallas_call(
        lambda *refs: pack_kernel(*refs[-3:], *refs[:-3]),
        out_shape=[shape(block, PACKED), shape(w_down.shape[1] // CHUNK, w_down.shape[0], CHUNK),
                   shape(hidden // CHUNK, block, 2 * CHUNK)],
        compiler_params=params(),
        name="pack",
    )(w_down, w_gate, w_up, *parts, *[g.reshape(1, block) for g in gains])


def unpack_kernel(widths, packed, down, sent, late, out, *refs):
    results, moved, outs, (held, sems) = refs[:2], refs[-4:-2], refs[2:-4], refs[-2:]
    *parts, gain_one, gain_two, w_down, w_gate, w_up, w_out = outs
    rows = windows(results[0].shape[0], 256)
    at = [(i, n, r) for i in (0, 1) for n, r in enumerate(rows)]
    loads = [lambda i=i, n=n, r=r: pltpu.make_async_copy(results[i].at[r], held.at[i, r], sems.at[0, i, n]) for i, n, r in at]
    stores = [lambda i=i, n=n, r=r: pltpu.make_async_copy(held.at[i, r], moved[i].at[r], sems.at[1, i, n]) for i, n, r in at]
    for load in loads:
        load().start()
    w_out[...] = out[...]
    at = 0
    for part, width in zip(parts, widths):
        part[...] = packed[:, at:at + width]
        at += width
    tail = packed[:, DIMS + HEADS:].T
    gain_one[...] = tail[at - DIMS - HEADS:at - DIMS - HEADS + 1]
    gain_two[...] = tail[at - DIMS - HEADS + 1:at - DIMS - HEADS + 2]
    for load, store in zip(loads, stores):
        load().wait()
        store().start()
    for n in range(down.shape[0]):
        w_down[:, n * CHUNK:(n + 1) * CHUNK] = down[n]
    for n in range(sent.shape[0] + late.shape[0]):
        both = sent[n] if n < sent.shape[0] else late[n - sent.shape[0]]
        w_gate[:, n * CHUNK:(n + 1) * CHUNK] = both[:, :CHUNK]
        w_up[:, n * CHUNK:(n + 1) * CHUNK] = both[:, CHUNK:]
    for store in stores:
        store().wait()


def unpack(widths, packed, down, sent, late, out, results):
    block = packed.shape[0]
    hidden = (sent.shape[0] + late.shape[0]) * CHUNK
    shape = lambda *s: jax.ShapeDtypeStruct(s, f32)
    vmem = pl.BlockSpec(memory_space=pltpu.VMEM)
    small = [shape(block, w) for w in widths] + [shape(1, block)] * 2
    small += [shape(down.shape[1], down.shape[0] * CHUNK)] + [shape(block, hidden)] * 2 + [shape(*out.shape)]
    *parts, gain_one, gain_two, w_down, w_gate, w_up, w_out, output, g_tokens = pl.pallas_call(
        functools.partial(unpack_kernel, widths),
        out_shape=small + [jax.ShapeDtypeStruct(r.shape, r.dtype) for r in results],
        in_specs=[vmem] * 5 + [ANY] * 2,
        out_specs=[vmem] * len(small) + [ANY] * 2,
        scratch_shapes=[pltpu.VMEM((2,) + results[0].shape, bf16), pltpu.SemaphoreType.DMA((2, 2, results[0].shape[0] // 256))],
        compiler_params=params(),
        name="unpack",
    )(packed, down, sent, late, out, *results)
    return parts, gain_one.reshape(block), gain_two.reshape(block), w_down, w_gate, w_up, w_out, output, g_tokens


def plain_mlp(middle, normed_two, cotangent, gain, gate_w, up_w, down_w):
    gate, up = dot(normed_two, gate_w), dot(normed_two, up_w)
    sig = jax.nn.sigmoid(gate)
    silu = gate * sig
    inner = (silu * up).astype(bf16)
    output = (middle + dot(inner, down_w)).astype(bf16)
    grad_inner = dot(cotangent, down_w, NT)
    grad_gate = (grad_inner * up * sig * (1.0 + gate * (1.0 - sig))).astype(bf16)
    grad_up = (grad_inner * silu).astype(bf16)
    grad_normed = dot(grad_gate, gate_w, NT) + dot(grad_up, up_w, NT)
    scale = rms(middle)
    gained = grad_normed * gain
    grad_middle = (
        cotangent.astype(f32)
        + scale * gained
        - middle * scale**3 * jnp.mean(gained * middle, axis=-1, keepdims=True)
    )
    grad_gain = jnp.sum(grad_normed * middle * scale, axis=0, keepdims=True)
    outer_sum = lambda left, right: dot(left, right, TN).astype(bf16)
    return (
        output, grad_middle, grad_gain,
        outer_sum(inner, cotangent), outer_sum(normed_two, grad_gate), outer_sum(normed_two, grad_up),
    )


def on_device(
    dims,
    tokens,
    doc_ids,
    norm_gain,
    w_query_heads,
    w_query_dims,
    w_key_heads,
    w_key_dims,
    w_value_heads,
    w_value_dims,
    w_output,
    mlp_gain,
    w_gate,
    w_up,
    w_down,
    out_grad,
):
    seq_len = tokens.shape[0] * tokens.shape[1]
    tables = tuple(jnp.asarray(t) for t in rope_tables(seq_len))
    parts = (w_query_dims, w_key_dims, w_value_dims, w_query_heads, w_key_heads, w_value_heads)
    edges = [0]
    for part in parts:
        edges.append(edges[-1] + part.shape[1])
    gains_at = edges[-1]
    inputs, cotangent = tokens.reshape(seq_len, D), out_grad.reshape(seq_len, D)
    doc_row, doc_col = doc_ids.reshape(1, seq_len), doc_ids.reshape(seq_len, 1)
    outer_sum = lambda left, right: dot(left, right, TN).astype(bf16)
    block = w_gate.shape[0]
    if block % 16 == 0 and w_gate.shape[1] % CHUNK == 0 and seq_len % TOKENS == 0:
        packed, down, gate_up = pack(parts, (norm_gain, mlp_gain), w_down, w_gate, w_up)
        (normed, factors, query, key, value, mixed, lse, gains, middle, normed_two,
         packed_w, output_w, down_w, early) = forward(
            dims, inputs, doc_row, tables, packed, w_output, down, gate_up, READY, 0
        )
        output_w = output_w.reshape(-1, D)
        output, grad_middle, grad_branch, grad_mlp_gain, gate_up_out, grad_down, grad_late, _ = mlp(
            dims, middle, normed_two, cotangent, gains, down_w.reshape(down_w.shape[0], -1, CHUNK), early, gate_up, SENT, 1
        )
        grad_mixed = dot(grad_branch, output_w, NT).astype(bf16)
        grad_tokens, down_out, output_out, late_out, packed_out = backward(
            dims, doc_row, query, key, value, grad_mixed, lse, inputs,
            gains, packed_w, tables, factors, grad_middle, normed, grad_mlp_gain,
            grad_down.reshape(down_w.shape), outer_sum(mixed, grad_branch).reshape(dims + w_output.shape),
            grad_late.reshape((-1,) + dims + gate_up.shape[1:]), 2,
        )
        parts_out, gain_one_out, gain_two_out, down_out, gate_out, up_out, output_out, output, grad_tokens = unpack(
            [part.shape[1] for part in parts], packed_out, down_out, gate_up_out, late_out, output_out,
            (output, grad_tokens),
        )
        grads = [g for pair in zip(parts_out[3:], parts_out[:3]) for g in pair]
        return (
            output.reshape(tokens.shape), grad_tokens.reshape(tokens.shape), gain_one_out, *grads,
            output_out, gain_two_out, gate_out, up_out, down_out,
        )

    packed = jnp.concatenate(
        parts
        + (norm_gain[:, None], mlp_gain[:, None])
        + (jnp.zeros((norm_gain.shape[0], PACKED - gains_at - 2), bf16),),
        axis=1,
    )
    packed_w, output_w, gate_w, up_w, down_w = gather(
        dims, [packed, w_output, w_gate, w_up, w_down], 0
    )
    gain_one, gain_two = [packed_w[:, gains_at + i].astype(f32).reshape(1, D) for i in (0, 1)]
    tables += (jnp.asarray(spread_table()),)
    normed, factors, query, key, value = make_factors(inputs, gain_one, packed_w, tables)
    mixed, lse = attend(doc_col, doc_row, query, key, value)
    middle = inputs.astype(f32) + dot(mixed, output_w)
    normed_two = (middle * rms(middle) * gain_two).astype(bf16)
    output, grad_middle, grad_mlp_gain, *mlp_grads = plain_mlp(
        middle, normed_two, cotangent, gain_two, gate_w, up_w, down_w
    )
    grad_branch = grad_middle.astype(bf16)
    grad_mixed = dot(grad_branch, output_w, NT).astype(bf16)

    grad_query, grad_key, grad_value = attend_back(
        doc_col, doc_row, query, key, value, grad_mixed, lse
    )
    grad_factors, grad_tokens, grad_norm_gain = factors_back(
        inputs, gain_one, packed_w, tables, factors, grad_query, grad_key, grad_value, grad_middle
    )
    gains = jnp.stack([grad_norm_gain[0], grad_mlp_gain[0]], axis=1).astype(bf16)
    packed_grad = lax.dynamic_update_slice(outer_sum(normed, grad_factors), gains, (0, gains_at))
    *mlp_out, output_out, packed_out = scatter(
        dims, mlp_grads + [outer_sum(mixed, grad_branch), packed_grad], 2
    )
    down_out, gate_out, up_out = mlp_out
    dims_and_heads = [packed_out[:, lo:hi] for lo, hi in zip(edges, edges[1:])]
    grads = [g for pair in zip(dims_and_heads[3:], dims_and_heads[:3]) for g in pair]
    return (
        output.reshape(tokens.shape),
        grad_tokens.reshape(tokens.shape),
        packed_out[:, gains_at],
        *grads,
        output_out,
        packed_out[:, gains_at + 1],
        gate_out,
        up_out,
        down_out,
    )


def solution(mesh):
    rows, matrix, vector = P(("dp", "fsdp"), None, None), P(("dp", "fsdp"), None), P(("dp", "fsdp"))
    return jax.shard_map(
        functools.partial(on_device, grid_of(mesh)),
        mesh=mesh,
        in_specs=(rows, matrix, vector) + (matrix,) * 7 + (vector,) + (matrix,) * 3 + (rows,),
        out_specs=(rows, rows, vector) + (matrix,) * 7 + (vector,) + (matrix,) * 3,
        check_vma=False,
    )
```

```python
import functools
import math

import jax
import jax.numpy as jnp
import numpy as np
from jax import lax
from jax.experimental import pallas as pl
from jax.experimental.pallas import tpu as pltpu
from jax.sharding import PartitionSpec as P

MESH = pl.DeviceIdType.MESH
D, H, DH, RQ, RK = 1024, 16, 64, 6, 2
PACKED = 896
DIMS, HEADS = 640, 128
BLOCK = 256
BACK = 512
NEG = -1e30
epsilon = 1e-06
theta_base = 10000.0
f32, bf16 = jnp.float32, jnp.bfloat16
NT = (((1,), (1,)), ((), ()))
NN = (((1,), (0,)), ((), ()))
TN = (((0,), (0,)), ((), ()))


def dot(a, b, dims=NN):
    return lax.dot_general(a, b, dims, preferred_element_type=f32)


def params(**kw):
    return pltpu.CompilerParams(vmem_limit_bytes=56 << 20, **kw)


def rope_tables(seq_len):
    half = DH // 2
    position = np.arange(seq_len, dtype=np.float32)
    inverse = np.exp(-math.log(theta_base) * 2.0 * np.arange(half, dtype=np.float32) / np.float32(2.0 * half)).astype(np.float32)
    angle = (position[:, None] * inverse[None, :]).astype(np.float32)
    cosine, sine = np.cos(angle), np.sin(angle)
    return (np.concatenate([cosine] * 4, 1), np.concatenate([-sine, sine] * 2, 1))


def spread_table():
    out = np.zeros((8, 2 * HEADS, H * DH), np.float32)
    for j in range(8):
        for h in range(H):
            out[j, [j * H + h, HEADS + j * H + h], h * DH:(h + 1) * DH] = 1.0
    return out.astype(jnp.bfloat16)


def low_lane(shape):
    return lax.rem(lax.broadcasted_iota(jnp.int32, shape, 1), 128) < 64


def first_half(shape):
    return lax.rem(lax.broadcasted_iota(jnp.int32, shape, 1), 64) < 32


def turn(x, cosine, sine):
    partner = jnp.where(first_half(x.shape), pltpu.roll(x, 96, 1), pltpu.roll(x, 32, 1))
    return x * cosine + partner * sine


def split_bf16(x):
    hi = x.astype(bf16)
    return jnp.concatenate([hi, (x - hi.astype(f32)).astype(bf16)], axis=1)


def twice(x, rank):
    rolled = pltpu.roll(x, 64, 1)
    low = low_lane(x.shape)
    return jnp.where(low, x, rolled) if rank % 2 == 0 else jnp.where(low, rolled, x)


def wide(x):
    return jnp.concatenate([x] * (H * DH // 128), axis=1)


def rms(x):
    return lax.rsqrt(jnp.mean(x * x, axis=-1, keepdims=True) + epsilon)


FACTORS = ((0, RQ, 0), (RQ, RK, 3), (0, RK, 4))


def factors_step(tokens, gain, weight, cosine, sine, spread, normed, factors, query, key, value):
    x = tokens[...].astype(f32)
    n = (x * rms(x) * gain).astype(bf16)
    normed[...] = n
    f = dot(n, weight)
    pairs = [f[:, 128 * i:128 * i + 128] for i in range(DIMS // 128)]
    pairs = [turn(p, cosine[...], sine[...]) if i < 4 else p for i, p in enumerate(pairs)]
    for i, p in enumerate(pairs):
        factors[:, 128 * i:128 * i + 128] = p
    factors[:, DIMS:] = f[:, DIMS:]
    heads_qk = split_bf16(f[:, DIMS:DIMS + HEADS])
    heads_v = split_bf16(f[:, DIMS + HEADS:])
    for out, heads, (at, ranks, pair), scale in zip(
        (query, key, value), (heads_qk, heads_qk, heads_v), FACTORS, (0.125, 1.0, 1.0)
    ):
        total = None
        for r in range(ranks):
            term = dot(heads, spread[at + r]) * wide(twice(pairs[pair + r // 2], r))
            total = term if total is None else total + term
        rounded = (total * (1.0 / ranks)).astype(bf16)
        rounded = rounded * jnp.asarray(scale, bf16) if scale != 1.0 else rounded
        for p, ref in enumerate(out):
            ref[...] = rounded[:, 128 * p:128 * p + 128]


def factors_kernel(tokens, gain, weight, cosine, sine, spread, normed, factors, query, key, value):
    outs = [[r.at[p] for p in range(H // 2)] for r in (query, key, value)]
    factors_step(tokens, gain[...], weight[...], cosine, sine, spread, normed, factors, *outs)


def make_factors(tokens, gain, weight, tables):
    cosine, sine, spread = tables
    seq = tokens.shape[0]
    row = lambda width: pl.BlockSpec((BLOCK, width), lambda i: (i, 0))
    whole = lambda a: pl.BlockSpec(a.shape, lambda i: (0,) * a.ndim)
    return pl.pallas_call(
        factors_kernel,
        grid=(seq // BLOCK,),
        out_shape=[
            jax.ShapeDtypeStruct((seq, D), bf16),
            jax.ShapeDtypeStruct((seq, PACKED), f32),
        ] + [jax.ShapeDtypeStruct((H // 2, seq, 128), bf16)] * 3,
        in_specs=[row(D), whole(gain), whole(weight), row(128), row(128), whole(spread)],
        out_specs=[row(D), row(PACKED)] + [pl.BlockSpec((H // 2, BLOCK, 128), lambda i: (0, i, 0))] * 3,
        compiler_params=params(),
        name="factors",
    )(tokens, gain, weight, cosine, sine, spread)


def allowed_t(doc_col, doc_row, k0, kn, q0, qn):
    same = doc_col[k0:k0 + kn, 0:1].astype(f32) == doc_row[:, q0:q0 + qn].astype(f32)
    if k0 + kn - 1 > q0:
        k_at = k0 + lax.broadcasted_iota(jnp.int32, (kn, qn), 0)
        q_at = q0 + lax.broadcasted_iota(jnp.int32, (kn, qn), 1)
        same = same & (k_at <= q_at)
    return same


def halves(x):
    low = low_lane(x.shape)
    zero = jnp.zeros_like(x)
    return jnp.where(low, x, zero), jnp.where(low, zero, x)


def attend_kernel(doc_col, doc_row, query, key, value, mixed, lse):
    seq = query.shape[0]
    v_half = halves(value[...])
    for q0 in range(0, seq, BLOCK):
        lo = max(0, q0 - BACK)
        kn = q0 + BLOCK - lo
        ok = allowed_t(doc_col, doc_row, lo, kn, q0, BLOCK)
        probs = []
        for h, q in enumerate(halves(query[q0:q0 + BLOCK, :])):
            s = jnp.where(ok, dot(key[lo:lo + kn, :], q, NT), NEG)
            top = jnp.max(s, axis=0, keepdims=True)
            e = jnp.exp(s - top)
            total = jnp.sum(e, axis=0, keepdims=True)
            probs.append((e * (1.0 / total)).astype(bf16))
            lse[0, h:h + 1, q0:q0 + BLOCK] = top + jnp.log(total)
        values = jnp.concatenate([v[lo:lo + kn] for v in v_half], axis=0)
        mixed[q0:q0 + BLOCK, :] = dot(jnp.concatenate(probs, axis=0), values, TN).astype(bf16)


def attend(doc_col, doc_row, query, key, value):
    pairs, seq, _ = query.shape
    whole = lambda a: pl.BlockSpec(a.shape, lambda i: (0,) * a.ndim)
    pair = pl.BlockSpec((seq, 128), lambda i: (0, i))
    return pl.pallas_call(
        lambda dc, dr, q, k, v, *outs: attend_kernel(dc, dr, q.at[0], k.at[0], v.at[0], *outs),
        grid=(pairs,),
        out_shape=[jax.ShapeDtypeStruct((seq, H * DH), bf16), jax.ShapeDtypeStruct((pairs, 2, seq), f32)],
        in_specs=[whole(doc_col), whole(doc_row)] + [pl.BlockSpec((1, seq, 128), lambda i: (i, 0, 0))] * 3,
        out_specs=[pair, pl.BlockSpec((1, 2, seq), lambda i: (i, 0, 0))],
        compiler_params=params(),
        name="attend",
    )(doc_col, doc_row, query, key, value)


def attend_back_kernel(doc_col, doc_row, query, key, value, grad, lse, g_query, g_key, g_value):
    seq = query.shape[0]
    k_half = halves(key[...])
    for q0 in range(0, seq, BLOCK):
        lo = max(0, q0 - BACK)
        kn = q0 + BLOCK - lo
        ok = allowed_t(doc_col, doc_row, lo, kn, q0, BLOCK)
        ps, ds = [], []
        q_half, g_half = halves(query[q0:q0 + BLOCK, :]), halves(grad[q0:q0 + BLOCK, :])
        for h in (0, 1):
            s = dot(key[lo:lo + kn, :], q_half[h], NT)
            p = jnp.where(ok, jnp.exp(s - lse[0, h:h + 1, q0:q0 + BLOCK]), 0.0)
            pd = p * dot(value[lo:lo + kn, :], g_half[h], NT)
            ps.append(p.astype(bf16))
            ds.append((pd - p * jnp.sum(pd, axis=0, keepdims=True)).astype(bf16))
        to_value = dot(jnp.concatenate(ps, 1), jnp.concatenate(g_half, 0))
        to_key = dot(jnp.concatenate(ds, 1), jnp.concatenate(q_half, 0))
        if q0 > lo:
            g_value[lo:q0, :] += to_value[:q0 - lo]
            g_key[lo:q0, :] += to_key[:q0 - lo]
        g_value[q0:q0 + BLOCK, :] = to_value[q0 - lo:]
        g_key[q0:q0 + BLOCK, :] = to_key[q0 - lo:]
        keys = jnp.concatenate([k[lo:lo + kn] for k in k_half], 0)
        g_query[q0:q0 + BLOCK, :] = dot(jnp.concatenate(ds, 0), keys, TN) * 0.125


def attend_back(doc_col, doc_row, query, key, value, grad, lse):
    pairs, seq, _ = query.shape
    whole = lambda a: pl.BlockSpec(a.shape, lambda i: (0,) * a.ndim)
    pair = pl.BlockSpec((seq, 128), lambda i: (0, i))
    return pl.pallas_call(
        lambda dc, dr, q, k, v, *rest: attend_back_kernel(dc, dr, q.at[0], k.at[0], v.at[0], *rest),
        grid=(pairs,),
        out_shape=[jax.ShapeDtypeStruct((seq, H * DH), f32)] * 3,
        in_specs=[whole(doc_col), whole(doc_row)] + [pl.BlockSpec((1, seq, 128), lambda i: (i, 0, 0))] * 3 + [pair, pl.BlockSpec((1, 2, seq), lambda i: (i, 0, 0))],
        out_specs=[pair] * 3,
        compiler_params=params(),
        name="attend_back",
    )(doc_col, doc_row, query, key, value, grad, lse)


def factors_back_step(cosine, sine, spread, factors, g_query, g_key, g_value, g_factors):
    pairs = [factors[:, 128 * i:128 * i + 128] for i in range(DIMS // 128)]
    heads_qk = split_bf16(factors[:, DIMS:DIMS + HEADS])
    heads_v = split_bf16(factors[:, DIMS + HEADS:])
    g_heads = [None, None]
    for grad, heads, which, (at, ranks, pair) in zip(
        (g_query, g_key, g_value), (heads_qk, heads_qk, heads_v), (0, 0, 1), FACTORS
    ):
        g = grad * (1.0 / ranks)
        folded = []
        for r in range(ranks):
            product = (g * wide(twice(pairs[pair + r // 2], r))).astype(bf16)
            part = dot(product, spread[at + r, :HEADS, :], NT)
            g_heads[which] = part if g_heads[which] is None else g_heads[which] + part
            full = g * dot(heads, spread[at + r])
            folded.append(sum(full[:, 128 * i:128 * i + 128] for i in range(H * DH // 128)))
        for r in range(0, ranks, 2):
            a, b = folded[r], folded[r + 1]
            low = low_lane(a.shape)
            mine = jnp.where(low, a, b)
            other = jnp.where(low, pltpu.roll(a, 64, 1), pltpu.roll(b, 64, 1))
            both = mine + other
            i = pair + r // 2
            if i < 4:
                both = turn(both, cosine[...], -sine[...])
            g_factors[:, 128 * i:128 * i + 128] = both.astype(bf16)
    g_factors[:, DIMS:DIMS + HEADS] = g_heads[0].astype(bf16)
    g_factors[:, DIMS + HEADS:] = g_heads[1].astype(bf16)


def tokens_back_step(step, tokens, gain, weight, g_factors, g_middle, g_tokens, g_gain):
    g_normed = dot(g_factors[...], weight, NT)
    x = tokens[...].astype(f32)
    r1 = rms(x)
    u = g_normed * gain
    part = jnp.sum(g_normed * x * r1, axis=0, keepdims=True)

    @pl.when(step == 0)
    def _():
        g_gain[...] = part

    @pl.when(step > 0)
    def _():
        g_gain[...] += part

    g_tokens[...] = (g_middle[...] + r1 * u - x * (r1 * r1 * r1 * jnp.mean(u * x, axis=-1, keepdims=True))).astype(bf16)


def factors_back_kernel(tokens, gain, weight, cosine, sine, spread, factors, g_query, g_key, g_value, g_middle,
                        g_factors, g_tokens, g_gain):
    factors_back_step(cosine, sine, spread, factors, g_query[...], g_key[...], g_value[...], g_factors)
    tokens_back_step(pl.program_id(0), tokens, gain[...], weight[...], g_factors, g_middle, g_tokens, g_gain)


def factors_back(tokens, gain, weight, tables, factors, g_query, g_key, g_value, g_middle):
    cosine, sine, spread = tables
    seq = tokens.shape[0]
    row = lambda width: pl.BlockSpec((BLOCK, width), lambda i: (i, 0))
    whole = lambda a: pl.BlockSpec(a.shape, lambda i: (0,) * a.ndim)
    return pl.pallas_call(
        factors_back_kernel,
        grid=(seq // BLOCK,),
        out_shape=[
            jax.ShapeDtypeStruct((seq, PACKED), bf16),
            jax.ShapeDtypeStruct((seq, D), bf16),
            jax.ShapeDtypeStruct((1, D), f32),
        ],
        in_specs=[row(D), whole(gain), whole(weight), row(128), row(128), whole(spread), row(PACKED)]
        + [row(H * DH)] * 3 + [row(D)],
        out_specs=[row(PACKED), row(D), pl.BlockSpec((1, D), lambda i: (0, 0))],
        compiler_params=params(),
        name="factors_back",
    )(tokens, gain, weight, cosine, sine, spread, factors, g_query, g_key, g_value, g_middle)

ANY = pl.BlockSpec(memory_space=pl.ANY)


def grid_of(mesh):
    nd, nf = mesh.shape["dp"], mesh.shape["fsdp"]
    nc = math.gcd(2, nd)
    nz = math.gcd(4, nf)
    return (nd // nc, nc, nz, nf // nz)


class Place:
    def __init__(self, dims):
        self.dims = dims
        ny, nc, nz, nx = dims
        dp, fs = lax.axis_index("dp"), lax.axis_index("fsdp")
        self.y, self.c = lax.div(dp, nc), lax.rem(dp, nc)
        self.z, self.x = lax.div(fs, nx), lax.rem(fs, nx)

    def at(self, axis, k):
        n = self.dims["yczx".index(axis)]
        return lax.rem(getattr(self, axis) + k + n, n)

    def device(self, axis=None, k=0):
        ny, nc, nz, nx = self.dims
        put = {a: getattr(self, a) for a in "yczx"}
        if axis is not None:
            put[axis] = self.at(axis, k)
        return (put["y"] * nc + put["c"], put["z"] * nx + put["x"])


def peers_of(dims):
    ny, nc, nz, nx = dims
    return [(a, k) for a, n in (("y", ny), ("c", nc), ("z", nz), ("x", nx)) for k in range(1, n)]


def enter(place):
    barrier = pltpu.get_barrier_semaphore()
    peers = peers_of(place.dims)
    for axis, k in peers:
        pl.semaphore_signal(barrier, inc=1, device_id=place.device(axis, k), device_id_type=MESH)
    pl.semaphore_wait(barrier, len(peers))


class Gather:
    def __init__(self, place, src, dst, sems, i):
        self.p, self.src, self.dst, self.i = place, src, dst, i
        self.local, self.zs, self.zr, self.as_, self.ar, self.bs, self.br, self.cs, self.cr = sems

    @staticmethod
    def sem_shapes(dims, n):
        ny, nc, nz, nx = dims
        dma = pltpu.SemaphoreType.DMA
        m = max(nx, ny) - 1
        one = lambda k: dma((n, max(1, k)))
        return [dma((n,)), one(nz - 1), one(nz - 1), one(m), one(m), one(m), one(m), one(nx + ny - 1), one(nx + ny - 1)]

    def copy(self, ref_src, ref_dst, send, recv, axis, k):
        return pltpu.make_async_remote_copy(
            src_ref=ref_src, dst_ref=ref_dst, send_sem=send, recv_sem=recv,
            device_id=self.p.device(axis, k), device_id_type=MESH,
        )

    def z_copies(self):
        p, i = self.p, self.i
        nz = p.dims[2]
        mine = self.dst.at[p.y, p.c, p.z, p.x]
        def one(k, back):
            if back:
                ref = self.dst.at[p.y, p.c, p.at("z", -k), p.x]
                return self.copy(ref, ref, self.zs.at[i, k - 1], self.zr.at[i, k - 1], "z", k)
            return self.copy(self.src, mine, self.zs.at[i, k - 1], self.zr.at[i, k - 1], "z", k)

        return [[functools.partial(one, k, back) for k in range(1, nz)] for back in (False, True)]

    def part(self, first, step, y, x, c):
        every = slice(None)
        if step == 0:
            return self.dst.at[y, c, :, x]
        return self.dst.at[y, c] if first == "x" else self.dst.at[:, c, :, x]

    def side_copies(self, first, step):
        p, i = self.p, self.i
        axis = first if step == 0 else {"x": "y", "y": "x"}[first]
        n = p.dims["yczx".index(axis)]
        s, r = ((self.as_, self.ar), (self.bs, self.br))[step]

        def one(k, back):
            y, x = p.y, p.x
            if back:
                y, x = (p.y, p.at("x", -k)) if axis == "x" else (p.at("y", -k), p.x)
            ref = self.part(first, step, y, x, p.c)
            return self.copy(ref, ref, s.at[i, k - 1], r.at[i, k - 1], axis, k)

        return [[functools.partial(one, k, back) for k in range(1, n)] for back in (False, True)]

    def core_copies(self, first, c):
        p, i = self.p, self.i
        second = {"x": "y", "y": "x"}[first]
        lists, j = [], 0
        for step, axis in ((0, None), (0, first), (1, second)):
            now = []
            count = 1 if axis is None else p.dims["yczx".index(axis)] - 1
            for k in range(1, count + 1):
                def one(axis=axis, step=step, k=k, j=j):
                    y = p.at("y", -k) if axis == "y" else p.y
                    x = p.at("x", -k) if axis == "x" else p.x
                    ref = self.part(first, step, y, x, c)
                    return self.copy(ref, ref, self.cs.at[i, j], self.cr.at[i, j], "c", 1)

                now.append(one)
                j += 1
            lists.append(now)
        return lists

    def start(self):
        p = self.p
        mine = self.dst.at[p.y, p.c, p.z, p.x]
        pltpu.make_async_copy(self.src, mine, self.local.at[self.i]).start()
        for copy in self.z_copies()[0]:
            copy().start()

    def by_core(self, body):
        if self.p.dims[1] == 1:
            body("x")
            return
        pl.when(self.p.c == 0)(lambda: body("x"))
        pl.when(self.p.c == 1)(lambda: body("y"))

    def after_z(self):
        p = self.p
        mine = self.dst.at[p.y, p.c, p.z, p.x]
        pltpu.make_async_copy(self.src, mine, self.local.at[self.i]).wait()
        for copy in self.z_copies()[1]:
            copy().wait_recv()

        def body(first):
            for copy in self.side_copies(first, 0)[0]:
                copy().start()
            if p.dims[1] > 1:
                for copy in self.core_copies(first, p.c)[0]:
                    copy().start()

        self.by_core(body)

    def after_first(self):
        p = self.p

        def body(first):
            for copy in self.side_copies(first, 0)[1]:
                copy().wait_recv()
            for copy in self.side_copies(first, 1)[0]:
                copy().start()
            if p.dims[1] > 1:
                for copy in self.core_copies(first, p.c)[1]:
                    copy().start()

        self.by_core(body)

    def after_second(self):
        p = self.p

        def body(first):
            for copy in self.side_copies(first, 1)[1]:
                copy().wait_recv()
            if p.dims[1] > 1:
                for copy in self.core_copies(first, p.c)[2]:
                    copy().start()

        self.by_core(body)

    def finish(self):
        p = self.p
        for copy in self.z_copies()[0]:
            copy().wait_send()

        def body(first):
            for step in (0, 1):
                for copy in self.side_copies(first, step)[0]:
                    copy().wait_send()
            if p.dims[1] > 1:
                for now in self.core_copies(first, p.c):
                    for copy in now:
                        copy().wait_send()
                other = {"x": "y", "y": "x"}[first]
                for now in self.core_copies(other, p.at("c", 1)):
                    for copy in now:
                        copy().wait_recv()

        self.by_core(body)

    def stages(self):
        return [self.start, self.after_z, self.after_first, self.after_second, self.finish]


def gather_kernel(dims, n, *refs):
    place = Place(dims)
    src, dst, sems = refs[:n], refs[n:2 * n], refs[2 * n:]
    enter(place)
    jobs = [Gather(place, src[i], dst[i], sems, i).stages() for i in range(n)]
    run_stages(jobs)


def gather(dims, arrays, collective_id):
    n = len(arrays)
    outs = pl.pallas_call(
        functools.partial(gather_kernel, dims, n),
        out_shape=[jax.ShapeDtypeStruct(dims + a.shape, a.dtype) for a in arrays],
        in_specs=[ANY] * n,
        out_specs=[ANY] * n,
        scratch_shapes=Gather.sem_shapes(dims, n),
        compiler_params=pltpu.CompilerParams(collective_id=collective_id, has_side_effects=True),
        name="gather_weights",
    )(*arrays)
    return [o.reshape((-1,) + a.shape[1:]) for o, a in zip(outs, arrays)]


class Scatter:
    def __init__(self, place, held, out, bufs, sems, i, src=None):
        self.p, self.src, self.out, self.i = place, src, out, i
        self.own, self.away = (held, None) if src is not None else (held.at[place.c], held.at[place.at("c", 1)])
        self.from_core, self.from_a, self.from_b, self.from_z = bufs
        self.local, self.cs, self.cr, self.as_, self.ar, self.bs, self.br, self.zs, self.zr = sems

    @staticmethod
    def sem_shapes(dims, n):
        ny, nc, nz, nx = dims
        dma = pltpu.SemaphoreType.DMA
        m = max(nx, ny, 2) - 1
        return [dma((n, nx))] * 3 + [dma((n, m))] * 4 + [dma((n, max(1, nz - 1)))] * 2

    @staticmethod
    def buf_shapes(dims, block, lead=()):
        ny, nc, nz, nx = dims
        m = max(nx, ny, 2)
        buf = lambda *s: pltpu.VMEM(lead + s + block, jnp.bfloat16)
        return [buf(ny, nx, nz), buf(m - 1, m, nz), buf(m - 1, nz), buf(max(1, nz - 1))]

    def copy(self, src, dst, send, recv, axis, k):
        return pltpu.make_async_remote_copy(
            src_ref=src, dst_ref=dst, send_sem=send, recv_sem=recv,
            device_id=self.p.device(axis, k), device_id_type=MESH,
        )

    def loads(self):
        p, i = self.p, self.i
        if self.src is None:
            return
        for x in range(p.dims[3]):
            yield lambda x=x: pltpu.make_async_copy(self.src.at[:, p.c, :, x], self.own.at[:, x], self.local.at[i, x])

    def core_copies(self):
        p, i = self.p, self.i
        if p.dims[1] == 1:
            return
        if self.src is None:
            yield lambda: self.copy(self.away, self.from_core, self.cs.at[i, 0], self.cr.at[i, 0], "c", 1)
            return
        for x in range(p.dims[3]):
            yield lambda x=x: self.copy(
                self.src.at[:, p.at("c", 1), :, x], self.from_core.at[:, x], self.cs.at[i, x], self.cr.at[i, x], "c", 1)

    def a_copies(self, first):
        p, i = self.p, self.i
        ny, nc, nz, nx = p.dims
        for k in range(1, ny if first == "y" else nx):
            def copy(k=k):
                if first == "y":
                    src, dst = self.own.at[p.at("y", k)], self.from_a.at[k - 1, pl.ds(0, nx)]
                else:
                    src, dst = self.own.at[:, p.at("x", k)], self.from_a.at[k - 1, pl.ds(0, ny)]
                return self.copy(src, dst, self.as_.at[i, k - 1], self.ar.at[i, k - 1], first, k)
            yield copy

    def b_copies(self, first):
        p, i = self.p, self.i
        ny, nc, nz, nx = p.dims
        second = {"x": "y", "y": "x"}[first]
        for k in range(1, ny if second == "y" else nx):
            def copy(k=k):
                src = self.own.at[p.at("y", k), p.x] if second == "y" else self.own.at[p.y, p.at("x", k)]
                return self.copy(src, self.from_b.at[k - 1], self.bs.at[i, k - 1], self.br.at[i, k - 1], second, k)
            yield copy

    def z_copies(self):
        p, i = self.p, self.i
        for k in range(1, p.dims[2]):
            yield lambda k=k: self.copy(
                self.own.at[p.y, p.x, p.at("z", k)], self.from_z.at[k - 1], self.zs.at[i, k - 1], self.zr.at[i, k - 1], "z", k)

    def by_core(self, body):
        if self.p.dims[1] == 1:
            body("y")
            return
        pl.when(self.p.c == 0)(lambda: body("y"))
        pl.when(self.p.c == 1)(lambda: body("x"))

    @staticmethod
    def add(into, terms):
        if len(terms) == 1:
            into[...] = into[...] + terms[0][...]
        elif terms:
            value = into[...].astype(jnp.float32)
            for term in terms:
                value = value + term[...].astype(jnp.float32)
            into[...] = value.astype(jnp.bfloat16)

    def start(self):
        for copy in self.core_copies():
            copy().start()
        for copy in self.loads():
            copy().start()

    def after_core(self):
        p = self.p
        ny, nc, nz, nx = p.dims
        for copy in self.loads():
            copy().wait()
        for copy in self.core_copies():
            copy().wait_recv()
        if nc > 1:
            def body(y, carry):
                self.add(self.own.at[y], [self.from_core.at[y]])
                return carry
            lax.fori_loop(0, ny, body, 0)

        def go(first):
            for copy in self.a_copies(first):
                copy().start()
        self.by_core(go)

    def after_a(self):
        p = self.p
        ny, nc, nz, nx = p.dims

        def go(first):
            for copy in self.a_copies(first):
                copy().wait_recv()
            n = ny if first == "y" else nx

            def body(j, carry):
                at = (p.y, j) if first == "y" else (j, p.x)
                self.add(self.own.at[at], [self.from_a.at[k, j] for k in range(n - 1)])
                return carry
            lax.fori_loop(0, nx if first == "y" else ny, body, 0)
            for copy in self.b_copies(first):
                copy().start()
        self.by_core(go)

    def after_b(self):
        p = self.p
        ny, nc, nz, nx = p.dims

        def go(first):
            for copy in self.b_copies(first):
                copy().wait_recv()
            n = nx if first == "y" else ny

            self.add(self.own.at[p.y, p.x], [self.from_b.at[k] for k in range(n - 1)])
        self.by_core(go)
        for copy in self.z_copies():
            copy().start()

    def after_z(self):
        p = self.p
        for copy in self.z_copies():
            copy().wait_recv()
        value = self.own[p.y, p.x, p.z].astype(jnp.float32)
        for k in range(p.dims[2] - 1):
            value = value + self.from_z[k].astype(jnp.float32)
        self.out[...] = value

    def finish(self):
        for copy in self.core_copies():
            copy().wait_send()

        def go(first):
            for copy in self.a_copies(first):
                copy().wait_send()
            for copy in self.b_copies(first):
                copy().wait_send()
        self.by_core(go)
        for copy in self.z_copies():
            copy().wait_send()

    def stages(self):
        return [self.start, self.after_core, self.after_a, self.after_b, self.after_z, self.finish]


def run_stages(jobs):
    n, depth = len(jobs), len(jobs[0])
    for t in range(n + depth - 1):
        for i in range(n):
            if 0 <= t - i < depth:
                jobs[i][t - i]()


def scatter_kernel(dims, n, *refs):
    place = Place(dims)
    src, out, rest = refs[:n], refs[n:2 * n], refs[2 * n:]
    bufs, sems = rest[:5 * n], rest[5 * n:]
    enter(place)
    run_stages([
        Scatter(place, bufs[5 * i], out[i], bufs[5 * i + 1:5 * i + 5], sems, i, src[i]).stages() for i in range(n)
    ])


def scatter(dims, arrays, collective_id):
    n = len(arrays)
    devices = math.prod(dims)
    blocks = [(a.shape[0] // devices,) + a.shape[1:] for a in arrays]
    shaped = [a.reshape(dims + b) for a, b in zip(arrays, blocks)]
    scratch = []
    ny, nc, nz, nx = dims
    for b in blocks:
        scratch += [pltpu.VMEM((ny, nx, nz) + b, jnp.bfloat16)] + Scatter.buf_shapes(dims, b)
    return pl.pallas_call(
        functools.partial(scatter_kernel, dims, n),
        out_shape=[jax.ShapeDtypeStruct(b, jnp.float32) for b in blocks],
        in_specs=[ANY] * n,
        out_specs=[pl.BlockSpec(memory_space=pltpu.VMEM)] * n,
        scratch_shapes=scratch + Scatter.sem_shapes(dims, n),
        compiler_params=pltpu.CompilerParams(
            collective_id=collective_id, has_side_effects=True, vmem_limit_bytes=56 << 20),
        name="scatter_gradients",
    )(*shaped)


READY = 3
SENT = 7
CHUNK = 256
SLOTS = 4
TOKENS = 512


def mlp_kernel(dims, chunks, ready, sent, *refs):
    (middle, normed, cot, gain, down, early, local_gu, output, g_middle, g_branch, g_gain, g_gate_up, g_down, late, gathered,
     normed_t, total, inner_s, grads_s, weights, held, from_core, from_a, from_b, from_z, load) = refs[:26]
    sems = refs[26:]
    ng = len(Gather.sem_shapes(dims, 1))
    place = Place(dims)
    j = pl.program_id(0)
    seq = normed.shape[0]
    block = local_gu.shape[1]
    ny, nc, nz, nx = dims

    def gather_at(m):
        return Gather(place, local_gu.at[m], gathered.at[m - ready], sems[:ng], m - ready)

    def scatter_at(m):
        bufs = [b.at[m] for b in (from_core, from_a, from_b, from_z)]
        return Scatter(place, held.at[lax.rem(m, SLOTS)], g_gate_up.at[m], bufs, sems[ng:], m)

    def do(m, first, last, body):
        if isinstance(m, int):
            if first <= m < last:
                body(m)
            return
        pl.when((m >= first) & (m < last))(lambda: body(m))

    def fetch(m, slot, start):
        def go(src):
            copy = pltpu.make_async_copy(src, weights.at[slot], load.at[slot])
            copy.start() if start else copy.wait()
        if start:
            pl.when(m < ready)(lambda: go(early.at[jnp.minimum(m, ready - 1)]))
            pl.when((m >= ready) & (m < chunks))(lambda: go(gathered.at[jnp.clip(m - ready, 0, chunks - ready - 1)]))
        else:
            go(early.at[0])

    def tick_a(j):
        do(j - 4, 0, sent, lambda m: scatter_at(m).after_z())
        do(j - 4, 0, sent, lambda m: scatter_at(m).finish())
        do(j + 1, ready, chunks, lambda m: gather_at(m).after_second())
        do(j + 2, ready, chunks, lambda m: gather_at(m).after_first())
        do(j + 5, ready + 2, chunks, lambda m: gather_at(m).start())

    def tick_b(j):
        do(j - 3, 0, sent, lambda m: scatter_at(m).after_b())
        do(j - 2, 0, sent, lambda m: scatter_at(m).after_a())
        do(j - 1, 0, sent, lambda m: scatter_at(m).after_core())
        do(j + 1, ready, chunks, lambda m: gather_at(m).finish())
        do(j + 3, ready, min(ready + 1, chunks), lambda m: gather_at(m).after_z())

    def tick_c(j):
        do(j, 0, sent, lambda m: scatter_at(m).start())
        do(j + 4, ready + 1, chunks, lambda m: gather_at(m).after_z())

    @pl.when(j == 0)
    def _():
        fetch(0, 0, True)
        enter(place)
        for m in range(ready, min(ready + 2, chunks)):
            gather_at(m).start()
        normed_t[...] = normed[...].T

    slot = lax.rem(j, 2)
    fetch(j, slot, False)
    w = weights.at[slot]
    down_weight = lambda: jnp.concatenate([down[n] for n in range(down.shape[0])], axis=1)
    weight = lambda: w[...].reshape(D, -1)

    def tokens_part(t):
        r = slice(t * TOKENS, (t + 1) * TOKENS)
        both = dot(normed[r, :], weight())
        gate, up = both[:, :CHUNK], both[:, CHUNK:]
        sig = jax.nn.sigmoid(gate)
        silu = gate * sig
        inner = (silu * up).astype(bf16)
        inner_s[r, :] = inner
        g_inner = dot(cot[r, :], down_weight(), NT)
        g_gate = (g_inner * up * sig * (1.0 + gate * (1.0 - sig))).astype(bf16)
        grads = jnp.concatenate([g_gate, (g_inner * silu).astype(bf16)], axis=1)
        grads_s[r, :] = grads
        out, back = dot(inner, down_weight()), dot(grads, weight(), NT)

        @pl.when(j == 0)
        def _():
            total[r, :] = out
            g_middle[r, :] = back

        @pl.when(j > 0)
        def _():
            total[r, :] += out
            g_middle[r, :] += back

    parts = seq // TOKENS
    tick_a(j)
    for t in range(parts):
        tokens_part(t)
        if t == parts // 2 - 1 or parts == 1:
            tick_b(j)
            fetch(j + 1, 1 - slot, True)
    g_weights = dot(normed_t[...], grads_s[...]).astype(bf16)

    @pl.when(j < sent)
    def _():
        at = held.at[lax.rem(j, SLOTS)]
        for y in range(ny):
            for c in range(nc):
                for z in range(nz):
                    for x in range(nx):
                        row = (((y * nc + c) * nz + z) * nx + x) * block
                        at[c, y, x, z] = g_weights[row:row + block]

    @pl.when(j >= sent)
    def _():
        late[0] = g_weights

    tick_c(j)
    g_down_now = dot(inner_s[...], cot[...], TN).astype(bf16)
    for n in range(g_down.shape[0]):
        g_down[n] = g_down_now[:, n * g_down.shape[2]:(n + 1) * g_down.shape[2]]

    @pl.when(j == chunks - 1)
    def _():
        for t in range(seq // 256):
            r = slice(t * 256, t * 256 + 256)
            m = middle[r, :]
            s = rms(m)
            output[r, :] = (m + total[r, :]).astype(bf16)
            g_normed = g_middle[r, :]
            u = g_normed * gain[1:2, :]
            g_now = cot[r, :].astype(f32) + s * u - m * (s * s * s * jnp.mean(u * m, axis=-1, keepdims=True))
            g_middle[r, :] = g_now
            g_branch[r, :] = g_now.astype(bf16)
            part = jnp.sum(g_normed * m * s, axis=0, keepdims=True)
            if t == 0:
                g_gain[...] = part
            else:
                g_gain[...] += part
        for k in range(max(0, sent + 4 - chunks)):
            tick_a(chunks + k)
            tick_b(chunks + k)
            tick_c(chunks + k)


def mlp(dims, middle, normed, cot, gain, down, early, local_gu, sent, collective_id):
    chunks, block, width = local_gu.shape
    ready = early.shape[0]
    seq = normed.shape[0]
    ny, nc, nz, nx = dims
    whole = lambda *s: pl.BlockSpec(s, lambda i: (0,) * len(s))
    vmem = lambda s, t: pltpu.VMEM(s, t)
    return pl.pallas_call(
        functools.partial(mlp_kernel, dims, chunks, ready, sent),
        grid=(chunks,),
        out_shape=[
            jax.ShapeDtypeStruct((seq, D), bf16),
            jax.ShapeDtypeStruct((seq, D), f32),
            jax.ShapeDtypeStruct((seq, D), bf16),
            jax.ShapeDtypeStruct((1, D), f32),
            jax.ShapeDtypeStruct((sent, block, width), f32),
            jax.ShapeDtypeStruct(down.shape, bf16),
            jax.ShapeDtypeStruct((chunks - sent, D, width), bf16),
            jax.ShapeDtypeStruct((chunks - ready,) + dims + (block, width), bf16),
        ],
        in_specs=[whole(seq, D), whole(seq, D), whole(seq, D), whole(8, D), pl.BlockSpec((down.shape[0], CHUNK, down.shape[2]), lambda i: (0, i, 0)), ANY,
                  pl.BlockSpec(local_gu.shape, lambda i: (0, 0, 0), pipeline_mode=pl.Buffered(1))],
        out_specs=[whole(seq, D)] * 3 + [whole(1, D), whole(sent, block, width),
                   pl.BlockSpec((down.shape[0], CHUNK, down.shape[2]), lambda i: (0, i, 0)),
                   pl.BlockSpec((1, D, width), lambda i: (jnp.maximum(i - sent, 0), 0, 0)), ANY],
        scratch_shapes=[
            vmem((D, seq), bf16), vmem((seq, D), f32), vmem((seq, CHUNK), bf16), vmem((seq, width), bf16),
            vmem((2,) + dims + (block, width), bf16), vmem((SLOTS, nc, ny, nx, nz, block, width), bf16),
        ] + Scatter.buf_shapes(dims, (block, width), (sent,)) + [pltpu.SemaphoreType.DMA((2,))]
        + Gather.sem_shapes(dims, chunks - ready) + Scatter.sem_shapes(dims, sent),
        compiler_params=pltpu.CompilerParams(
            collective_id=collective_id, has_side_effects=True, vmem_limit_bytes=62 << 20),
        name="mlp",
    )(middle, normed, cot, gain, down, early, local_gu)


STEPS = 4
AHEAD = 4
SPREAD = (8, 2 * HEADS, H * DH)
FB, FD, FG, BB, BD, BG = 1, 0.7, 2, 0, 0.35, 2
PAIRS = H // 2


def spread_ticks(ticks, slots, busy, drain):
    plan = [[] for _ in range(slots)]
    total = busy + drain * (len(ticks) - busy)
    at = 0.0
    for n, tick in enumerate(ticks):
        at += 1.0 if n < busy else drain
        plan[min(slots - 1, int(at * slots / total))].append(tick)
    return plan


def tick_list(jobs, gap=1):
    n, depth = len(jobs), len(jobs[0])
    return [[jobs[i][(t - i) // gap] for i in range(n) if 0 <= t - i < gap * depth and (t - i) % gap == 0]
            for t in range(n + gap * (depth - 1))]


def run_tick(tick):
    for stage in tick:
        stage()


def fill_spread(spread):
    row = lax.rem(lax.broadcasted_iota(jnp.int32, spread.shape[1:], 0), HEADS)
    offset = row - lax.div(lax.broadcasted_iota(jnp.int32, spread.shape[1:], 1), DH)
    for j in range(spread.shape[0]):
        spread[j] = jnp.where(offset == j * H, 1.0, 0.0).astype(bf16)


def windows(width, size):
    return [pl.ds(at, size) for at in range(0, width, size)]


def forward_kernel(dims, ready, *refs):
    (tokens, doc_row, cosine, sine, packed, w_out, w_down, gate_up,
     normed, factors, query, key, value, mixed, lse, gains, middle, normed_two, packed_all, out_all, down_all, early,
     weight, out_weight, doc_col, spread, load) = refs[:27]
    sems = refs[27:]
    place = Place(dims)
    step = pl.program_id(0)
    part = lambda src, dst, rows: (src.at[rows], dst.at[:, :, :, :, rows])
    first = [part(packed, packed_all, rows) for rows in windows(packed.shape[0], 16)]
    pairs = [part(w_out, out_all, rows) for rows in windows(w_out.shape[0], 16)]
    pairs += [(w_down.at[n], down_all.at[n]) for n in range(w_down.shape[0])]
    pairs += [(gate_up.at[m], early.at[m]) for m in range(ready)]
    jobs = [Gather(place, s, d, sems, i).stages() for i, (s, d) in enumerate(first + pairs)]
    first, rest = jobs[:len(first)], jobs[len(first):]
    ticks = tick_list([job[1:] for job in rest], FG)
    for n, job in enumerate(rest[AHEAD:]):
        ticks[n].append(job[0])
    fetch_out = lambda: pltpu.make_async_copy(out_all, out_weight, load)

    @pl.when(step == 0)
    def _():
        doc_col[...] = jnp.broadcast_to(doc_row[...].astype(f32), (8, doc_row.shape[1])).T
        enter(place)
        for job in first + rest[:AHEAD]:
            job[0]()
        fill_spread(spread)
        for tick in tick_list([job[1:] for job in first]):
            run_tick(tick)
        copy = pltpu.make_async_copy(packed_all, weight, load)
        copy.start()
        copy.wait()
        w = weight[...].reshape(D, PACKED)
        gains[...] = w[:, DIMS + HEADS:].astype(f32).T[2 * H:2 * H + 8]

    @pl.when(step < STEPS)
    def _():
        rows = pl.ds(pl.multiple_of(jnp.minimum(step, STEPS - 1) * BLOCK, BLOCK), BLOCK)
        outs = [[r.at[p, rows] for p in range(PAIRS)] for r in (query, key, value)]
        factors_step(tokens, gains[0:1, :], weight[...].reshape(D, PACKED), cosine, sine, spread, normed, factors, *outs)

    @pl.when((step >= STEPS) & (step < STEPS + PAIRS))
    def _():
        p = jnp.clip(step - STEPS, 0, PAIRS - 1)
        cols = pl.ds(pl.multiple_of(p * 128, 128), 128)
        attend_kernel(doc_col, doc_row, query.at[p], key.at[p], value.at[p], mixed.at[:, cols], lse)

    pl.when(step == STEPS + PAIRS - 1)(lambda: fetch_out().start())
    pl.when(step == STEPS + PAIRS)(lambda: fetch_out().wait())

    @pl.when(step >= STEPS + PAIRS)
    def _():
        t = jnp.maximum(step - STEPS - PAIRS, 0)
        rows = pl.ds(pl.multiple_of(t * BLOCK, BLOCK), BLOCK)
        m = tokens[...].astype(f32) + dot(mixed[rows, :], out_weight[...].reshape(H * DH, D))
        middle[...] = m
        normed_two[...] = (m * rms(m) * gains[1:2, :]).astype(bf16)

    for at, todo in enumerate(spread_ticks(ticks, 2 * STEPS + PAIRS, len(rest) + FB, FD)):
        if todo:
            @pl.when(step == at)
            def _(todo=todo):
                for tick in todo:
                    run_tick(tick)


def forward(dims, tokens, doc_row, tables, packed, w_out, w_down, gate_up, ready, collective_id):
    cosine, sine = tables
    seq = tokens.shape[0]
    whole = lambda *s: pl.BlockSpec(s, lambda i: (0,) * len(s), pipeline_mode=pl.Buffered(1))
    kept = lambda *s: pl.BlockSpec(s, lambda i: (0,) * len(s))
    row = lambda width: pl.BlockSpec((BLOCK, width), lambda i: (jnp.minimum(i, STEPS - 1), 0))
    again = lambda i: jnp.maximum(i - STEPS - PAIRS, 0)
    after = lambda i: jnp.clip(i - STEPS, 0, PAIRS - 1)
    ends = pl.BlockSpec((BLOCK, D), lambda i: (jnp.where(i < STEPS, i, again(i)), 0))
    last = pl.BlockSpec((BLOCK, D), lambda i: (again(i), 0))
    full = lambda a: jax.ShapeDtypeStruct(dims + a.shape, a.dtype)
    jobs = packed.shape[0] // 16 + w_out.shape[0] // 16 + w_down.shape[0] + ready
    return pl.pallas_call(
        functools.partial(forward_kernel, dims, ready),
        grid=(2 * STEPS + PAIRS,),
        out_shape=[
            jax.ShapeDtypeStruct((seq, D), bf16),
            jax.ShapeDtypeStruct((seq, PACKED), f32),
        ] + [jax.ShapeDtypeStruct((PAIRS, seq, 128), bf16)] * 3 + [
            jax.ShapeDtypeStruct((seq, H * DH), bf16),
            jax.ShapeDtypeStruct((PAIRS, 2, seq), f32),
            jax.ShapeDtypeStruct((8, D), f32),
            jax.ShapeDtypeStruct((seq, D), f32), jax.ShapeDtypeStruct((seq, D), bf16),
            full(packed), full(w_out), jax.ShapeDtypeStruct(w_down.shape[:1] + dims + w_down.shape[1:], bf16),
            jax.ShapeDtypeStruct((ready,) + dims + gate_up.shape[1:], bf16),
        ],
        in_specs=[ends, whole(1, seq), row(128), row(128)] + [whole(*a.shape) for a in (packed, w_out, w_down, gate_up)],
        out_specs=[row(D), row(PACKED)] + [kept(PAIRS, seq, 128)] * 3 + [
            kept(seq, H * DH),
            pl.BlockSpec((1, 2, seq), lambda i: (after(i), 0, 0)),
            kept(8, D), last, last,
        ] + [ANY] * 4,
        scratch_shapes=[pltpu.VMEM(dims + packed.shape, bf16), pltpu.VMEM(dims + w_out.shape, bf16), pltpu.VMEM((seq, 8), f32), pltpu.VMEM(SPREAD, bf16), pltpu.SemaphoreType.DMA]
        + Gather.sem_shapes(dims, jobs),
        compiler_params=pltpu.CompilerParams(
            collective_id=collective_id, has_side_effects=True, vmem_limit_bytes=58 << 20),
        name="forward",
    )(tokens, doc_row, cosine, sine, packed, w_out, w_down, gate_up)


def backward_kernel(dims, *refs):
    (doc_row, query, key, value, w_out, lse, tokens, gain, packed_all, cosine, sine, factors, g_middle,
     normed, g_gain_two, g_down, mixed, g_branch, g_late) = refs[:19]
    g_tokens, down_out, out_out, late_out, reduced = refs[19:24]
    at = 24
    g_query, g_key, g_value, weight, g_factors, g_gain, doc_col, spread, two, grad, load = refs[at:at + 11]
    bufs = refs[at + 11:at + 11 + 20]
    sems = refs[at + 31:]
    place = Place(dims)
    ny, nc, nz, nx = dims
    step = pl.program_id(0)
    block = packed_all.shape[4]
    fetch = lambda: pltpu.make_async_copy(packed_all, weight, load.at[0])
    fetches = [lambda n=n, src=src: pltpu.make_async_copy(src, two.at[min(n, 1)], load.at[n + 1])
               for n, src in enumerate((g_branch, w_out, mixed))]

    def hold(held, value, start=0):
        for y in range(ny):
            for c in range(nc):
                for z in range(nz):
                    for x in range(nx):
                        row = (((y * nc + c) * nz + z) * nx + x) * block
                        for n in range(block // 16):
                            at = row + 16 * n - start
                            if 0 <= at < value.shape[0]:
                                held[n, c, y, x, z] = value[at:at + 16]

    jobs = []
    for n in range(down_out.shape[0]):
        own = [b.at[n] for b in bufs[5:10]]
        jobs.append(Scatter(place, own[0], down_out.at[n], own[1:], sems, len(jobs), g_down.at[n]))
    for n in range(late_out.shape[0]):
        own = [b.at[n] for b in bufs[15:20]]
        jobs.append(Scatter(place, own[0], late_out.at[n], own[1:], sems, len(jobs), g_late.at[n]))
    known = list(jobs)
    for n, rows in enumerate(windows(out_out.shape[0], 16)):
        own = [b.at[n] for b in bufs[0:5]]
        jobs.append(Scatter(place, own[0], out_out.at[rows], own[1:], sems, len(jobs)))
    last = []
    for n, rows in enumerate(windows(block, 16)):
        own = [b.at[n] for b in bufs[10:15]]
        last.append(Scatter(place, own[0], reduced.at[rows], own[1:], sems, len(jobs) + n))
    ticks = tick_list([job.stages()[1:] for job in jobs], BG)
    total = PAIRS + STEPS

    @pl.when(step == 0)
    def _():
        for copy in [fetch] + fetches[:2]:
            copy().start()
        doc_col[...] = jnp.broadcast_to(doc_row[...].astype(f32), (8, doc_row.shape[1])).T
        enter(place)
        for job in known:
            job.start()
        fill_spread(spread)
        fetches[0]().wait()
        fetches[1]().wait()
        for t in range(0, doc_row.shape[1], BLOCK):
            g_mixed = dot(two[0, t:t + BLOCK], two[1], NT).astype(bf16)
            for p in range(PAIRS):
                grad[p, t:t + BLOCK] = g_mixed[:, 128 * p:128 * p + 128]
        fetches[2]().start()
        fetches[2]().wait()
        for t in range(0, D, BLOCK):
            hold(bufs[0], dot(two[1, :, t:t + BLOCK], two[0], TN).astype(bf16), t)
        for job in jobs[len(known):]:
            job.start()

    @pl.when(step < PAIRS)
    def _():
        p = jnp.minimum(step, PAIRS - 1)
        attend_back_kernel(doc_col, doc_row, query.at[0], key.at[0], value.at[0], grad.at[p], lse,
                           g_query.at[p], g_key.at[p], g_value.at[p])

    pl.when(step == PAIRS)(lambda: fetch().wait())

    @pl.when(step >= PAIRS)
    def _():
        t = jnp.maximum(step - PAIRS, 0)
        rows = pl.ds(pl.multiple_of(t * BLOCK, BLOCK), BLOCK)
        grads = [jnp.concatenate([g[p, rows, :] for p in range(PAIRS)], axis=1) for g in (g_query, g_key, g_value)]
        factors_back_step(cosine, sine, spread, factors, *grads, g_factors.at[rows])
        tokens_back_step(t, tokens, gain[0:1, :], weight[...].reshape(D, PACKED), g_factors.at[rows], g_middle, g_tokens, g_gain)

    for n, todo in enumerate(spread_ticks(ticks, total, len(jobs) + BB, BD)):
        if todo:
            @pl.when(step == n)
            def _(todo=todo):
                for tick in todo:
                    run_tick(tick)

    @pl.when(step == total - 1)
    def _():
        g_weight = dot(normed[...], g_factors[...], TN)
        column = lambda row: jnp.broadcast_to(row, (128, D)).T
        lane = lax.broadcasted_iota(jnp.int32, (D, 128), 1)
        tail = g_weight[:, DIMS + HEADS:]
        tail = jnp.where(lane == 2 * H, column(g_gain[...]), jnp.where(lane == 2 * H + 1, column(g_gain_two[...]), tail))
        g_weight = jnp.concatenate([g_weight[:, :DIMS + HEADS], tail], axis=1).astype(bf16)
        hold(bufs[10], g_weight)
        for tick in tick_list([job.stages() for job in last]):
            run_tick(tick)


def backward(dims, doc_row, query, key, value, w_out, lse, tokens, gains, packed_all, tables, factors,
             g_middle, normed, g_gain_two, g_down, mixed, g_branch, g_late, collective_id):
    cosine, sine = tables
    seq = tokens.shape[0]
    ny, nc, nz, nx = dims
    block = packed_all.shape[4]
    whole = lambda *s: pl.BlockSpec(s, lambda i: (0,) * len(s), pipeline_mode=pl.Buffered(1))
    kept = lambda *s: pl.BlockSpec(s, lambda i: (0,) * len(s))
    before = lambda i: jnp.minimum(i, PAIRS - 1)
    after = lambda i: jnp.maximum(i - PAIRS, 0)
    pair = pl.BlockSpec((1, seq, 128), lambda i: (before(i), 0, 0))
    row = lambda width: pl.BlockSpec((seq // STEPS, width), lambda i: (after(i), 0))
    buffers = []
    groups = ((block // 16, (16, D)), (g_down.shape[0], g_down.shape[5:]), (block // 16, (16, PACKED)),
              (g_late.shape[0], g_late.shape[5:]))
    for n, (many, b) in enumerate(groups):
        held = (nc, ny, nx, nz) if n in (0, 2) else (ny, nx, nz)
        buffers += [pltpu.VMEM((many,) + held + b, bf16)] + Scatter.buf_shapes(dims, b, (many,))
    outs = [(g_down.shape[0],) + g_down.shape[5:], (block, D), (g_late.shape[0],) + g_late.shape[5:], (block, PACKED)]
    shape = lambda *s: jax.ShapeDtypeStruct(s, f32)
    return pl.pallas_call(
        functools.partial(backward_kernel, dims),
        grid=(PAIRS + STEPS,),
        out_shape=[jax.ShapeDtypeStruct((seq, D), bf16)] + [shape(*s) for s in outs],
        in_specs=[whole(1, seq), pair, pair, pair, ANY,
                  pl.BlockSpec((1, 2, seq), lambda i: (before(i), 0, 0)), row(D), whole(8, D), ANY, row(128), row(128),
                  row(PACKED), row(D), whole(seq, D), whole(1, D), ANY, ANY, ANY, ANY],
        out_specs=[row(D)] + [kept(*s) for s in outs],
        scratch_shapes=[pltpu.VMEM((PAIRS, seq, 128), f32)] * 3 + [
            pltpu.VMEM(dims + (block, PACKED), bf16), pltpu.VMEM((seq, PACKED), bf16), pltpu.VMEM((1, D), f32),
            pltpu.VMEM((seq, 8), f32), pltpu.VMEM(SPREAD, bf16), pltpu.VMEM((2, seq, D), bf16),
            pltpu.VMEM((PAIRS, seq, 128), bf16), pltpu.SemaphoreType.DMA((4,)),
        ] + buffers + Scatter.sem_shapes(dims, sum(many for many, _ in groups)),
        compiler_params=pltpu.CompilerParams(
            collective_id=collective_id, has_side_effects=True, vmem_limit_bytes=62 << 20),
        name="backward",
    )(doc_row, query, key, value, w_out, lse, tokens, gains, packed_all, cosine, sine, factors,
      g_middle, normed, g_gain_two, g_down, mixed, g_branch, g_late)


def pack_kernel(packed, down, gate_up, w_down, w_gate, w_up, *parts):
    at = 0
    for part in parts[:-2]:
        packed[:, at:at + part.shape[1]] = part[...]
        at += part.shape[1]
    rows = jnp.concatenate([gain[...].astype(f32) for gain in parts[-2:]] + [jnp.zeros((6, packed.shape[0]), f32)], axis=0)
    packed[:, at:at + 8] = rows.T.astype(bf16)
    packed[:, at + 8:] = jnp.zeros((packed.shape[0], PACKED - at - 8), bf16)
    for n in range(down.shape[0]):
        down[n] = w_down[:, n * CHUNK:(n + 1) * CHUNK]
    for n in range(gate_up.shape[0]):
        gate_up[n, :, :CHUNK] = w_gate[:, n * CHUNK:(n + 1) * CHUNK]
        gate_up[n, :, CHUNK:] = w_up[:, n * CHUNK:(n + 1) * CHUNK]


def pack(parts, gains, w_down, w_gate, w_up):
    block, hidden = w_gate.shape
    shape = lambda *s: jax.ShapeDtypeStruct(s, bf16)
    return pl.pallas_call(
        lambda *refs: pack_kernel(*refs[-3:], *refs[:-3]),
        out_shape=[shape(block, PACKED), shape(w_down.shape[1] // CHUNK, w_down.shape[0], CHUNK),
                   shape(hidden // CHUNK, block, 2 * CHUNK)],
        compiler_params=params(),
        name="pack",
    )(w_down, w_gate, w_up, *parts, *[g.reshape(1, block) for g in gains])


def unpack_kernel(widths, packed, down, sent, late, out, *refs):
    results, moved, outs, (held, sems) = refs[:2], refs[-4:-2], refs[2:-4], refs[-2:]
    *parts, gain_one, gain_two, w_down, w_gate, w_up, w_out = outs
    rows = windows(results[0].shape[0], 256)
    at = [(i, n, r) for i in (0, 1) for n, r in enumerate(rows)]
    loads = [lambda i=i, n=n, r=r: pltpu.make_async_copy(results[i].at[r], held.at[i, r], sems.at[0, i, n]) for i, n, r in at]
    stores = [lambda i=i, n=n, r=r: pltpu.make_async_copy(held.at[i, r], moved[i].at[r], sems.at[1, i, n]) for i, n, r in at]
    for load in loads:
        load().start()
    w_out[...] = out[...]
    at = 0
    for part, width in zip(parts, widths):
        part[...] = packed[:, at:at + width]
        at += width
    tail = packed[:, DIMS + HEADS:].T
    gain_one[...] = tail[at - DIMS - HEADS:at - DIMS - HEADS + 1]
    gain_two[...] = tail[at - DIMS - HEADS + 1:at - DIMS - HEADS + 2]
    for load, store in zip(loads, stores):
        load().wait()
        store().start()
    for n in range(down.shape[0]):
        w_down[:, n * CHUNK:(n + 1) * CHUNK] = down[n]
    for n in range(sent.shape[0] + late.shape[0]):
        both = sent[n] if n < sent.shape[0] else late[n - sent.shape[0]]
        w_gate[:, n * CHUNK:(n + 1) * CHUNK] = both[:, :CHUNK]
        w_up[:, n * CHUNK:(n + 1) * CHUNK] = both[:, CHUNK:]
    for store in stores:
        store().wait()


def unpack(widths, packed, down, sent, late, out, results):
    block = packed.shape[0]
    hidden = (sent.shape[0] + late.shape[0]) * CHUNK
    shape = lambda *s: jax.ShapeDtypeStruct(s, f32)
    vmem = pl.BlockSpec(memory_space=pltpu.VMEM)
    small = [shape(block, w) for w in widths] + [shape(1, block)] * 2
    small += [shape(down.shape[1], down.shape[0] * CHUNK)] + [shape(block, hidden)] * 2 + [shape(*out.shape)]
    *parts, gain_one, gain_two, w_down, w_gate, w_up, w_out, output, g_tokens = pl.pallas_call(
        functools.partial(unpack_kernel, widths),
        out_shape=small + [jax.ShapeDtypeStruct(r.shape, r.dtype) for r in results],
        in_specs=[vmem] * 5 + [ANY] * 2,
        out_specs=[vmem] * len(small) + [ANY] * 2,
        scratch_shapes=[pltpu.VMEM((2,) + results[0].shape, bf16), pltpu.SemaphoreType.DMA((2, 2, results[0].shape[0] // 256))],
        compiler_params=params(),
        name="unpack",
    )(packed, down, sent, late, out, *results)
    return parts, gain_one.reshape(block), gain_two.reshape(block), w_down, w_gate, w_up, w_out, output, g_tokens


def plain_mlp(middle, normed_two, cotangent, gain, gate_w, up_w, down_w):
    gate, up = dot(normed_two, gate_w), dot(normed_two, up_w)
    sig = jax.nn.sigmoid(gate)
    silu = gate * sig
    inner = (silu * up).astype(bf16)
    output = (middle + dot(inner, down_w)).astype(bf16)
    grad_inner = dot(cotangent, down_w, NT)
    grad_gate = (grad_inner * up * sig * (1.0 + gate * (1.0 - sig))).astype(bf16)
    grad_up = (grad_inner * silu).astype(bf16)
    grad_normed = dot(grad_gate, gate_w, NT) + dot(grad_up, up_w, NT)
    scale = rms(middle)
    gained = grad_normed * gain
    grad_middle = (
        cotangent.astype(f32)
        + scale * gained
        - middle * scale**3 * jnp.mean(gained * middle, axis=-1, keepdims=True)
    )
    grad_gain = jnp.sum(grad_normed * middle * scale, axis=0, keepdims=True)
    outer_sum = lambda left, right: dot(left, right, TN).astype(bf16)
    return (
        output, grad_middle, grad_gain,
        outer_sum(inner, cotangent), outer_sum(normed_two, grad_gate), outer_sum(normed_two, grad_up),
    )


def on_device(
    dims,
    tokens,
    doc_ids,
    norm_gain,
    w_query_heads,
    w_query_dims,
    w_key_heads,
    w_key_dims,
    w_value_heads,
    w_value_dims,
    w_output,
    mlp_gain,
    w_gate,
    w_up,
    w_down,
    out_grad,
):
    seq_len = tokens.shape[0] * tokens.shape[1]
    tables = tuple(jnp.asarray(t) for t in rope_tables(seq_len))
    parts = (w_query_dims, w_key_dims, w_value_dims, w_query_heads, w_key_heads, w_value_heads)
    edges = [0]
    for part in parts:
        edges.append(edges[-1] + part.shape[1])
    gains_at = edges[-1]
    inputs, cotangent = tokens.reshape(seq_len, D), out_grad.reshape(seq_len, D)
    doc_row, doc_col = doc_ids.reshape(1, seq_len), doc_ids.reshape(seq_len, 1)
    outer_sum = lambda left, right: dot(left, right, TN).astype(bf16)
    block = w_gate.shape[0]
    if block % 16 == 0 and w_gate.shape[1] % CHUNK == 0 and seq_len % TOKENS == 0:
        packed, down, gate_up = pack(parts, (norm_gain, mlp_gain), w_down, w_gate, w_up)
        (normed, factors, query, key, value, mixed, lse, gains, middle, normed_two,
         packed_w, output_w, down_w, early) = forward(
            dims, inputs, doc_row, tables, packed, w_output, down, gate_up, READY, 0
        )
        output_w = output_w.reshape(-1, D)
        output, grad_middle, grad_branch, grad_mlp_gain, gate_up_out, grad_down, grad_late, _ = mlp(
            dims, middle, normed_two, cotangent, gains, down_w.reshape(down_w.shape[0], -1, CHUNK), early, gate_up, SENT, 1
        )
        grad_tokens, down_out, output_out, late_out, packed_out = backward(
            dims, doc_row, query, key, value, output_w, lse, inputs,
            gains, packed_w, tables, factors, grad_middle, normed, grad_mlp_gain,
            grad_down.reshape(down_w.shape), mixed, grad_branch,
            grad_late.reshape((-1,) + dims + gate_up.shape[1:]), 2,
        )
        parts_out, gain_one_out, gain_two_out, down_out, gate_out, up_out, output_out, output, grad_tokens = unpack(
            [part.shape[1] for part in parts], packed_out, down_out, gate_up_out, late_out, output_out,
            (output, grad_tokens),
        )
        grads = [g for pair in zip(parts_out[3:], parts_out[:3]) for g in pair]
        return (
            output.reshape(tokens.shape), grad_tokens.reshape(tokens.shape), gain_one_out, *grads,
            output_out, gain_two_out, gate_out, up_out, down_out,
        )

    packed = jnp.concatenate(
        parts
        + (norm_gain[:, None], mlp_gain[:, None])
        + (jnp.zeros((norm_gain.shape[0], PACKED - gains_at - 2), bf16),),
        axis=1,
    )
    packed_w, output_w, gate_w, up_w, down_w = gather(
        dims, [packed, w_output, w_gate, w_up, w_down], 0
    )
    gain_one, gain_two = [packed_w[:, gains_at + i].astype(f32).reshape(1, D) for i in (0, 1)]
    tables += (jnp.asarray(spread_table()),)
    normed, factors, query, key, value = make_factors(inputs, gain_one, packed_w, tables)
    mixed, lse = attend(doc_col, doc_row, query, key, value)
    middle = inputs.astype(f32) + dot(mixed, output_w)
    normed_two = (middle * rms(middle) * gain_two).astype(bf16)
    output, grad_middle, grad_mlp_gain, *mlp_grads = plain_mlp(
        middle, normed_two, cotangent, gain_two, gate_w, up_w, down_w
    )
    grad_branch = grad_middle.astype(bf16)
    grad_mixed = dot(grad_branch, output_w, NT).astype(bf16)

    grad_query, grad_key, grad_value = attend_back(
        doc_col, doc_row, query, key, value, grad_mixed, lse
    )
    grad_factors, grad_tokens, grad_norm_gain = factors_back(
        inputs, gain_one, packed_w, tables, factors, grad_query, grad_key, grad_value, grad_middle
    )
    gains = jnp.stack([grad_norm_gain[0], grad_mlp_gain[0]], axis=1).astype(bf16)
    packed_grad = lax.dynamic_update_slice(outer_sum(normed, grad_factors), gains, (0, gains_at))
    *mlp_out, output_out, packed_out = scatter(
        dims, mlp_grads + [outer_sum(mixed, grad_branch), packed_grad], 2
    )
    down_out, gate_out, up_out = mlp_out
    dims_and_heads = [packed_out[:, lo:hi] for lo, hi in zip(edges, edges[1:])]
    grads = [g for pair in zip(dims_and_heads[3:], dims_and_heads[:3]) for g in pair]
    return (
        output.reshape(tokens.shape),
        grad_tokens.reshape(tokens.shape),
        packed_out[:, gains_at],
        *grads,
        output_out,
        packed_out[:, gains_at + 1],
        gate_out,
        up_out,
        down_out,
    )


def solution(mesh):
    rows, matrix, vector = P(("dp", "fsdp"), None, None), P(("dp", "fsdp"), None), P(("dp", "fsdp"))
    return jax.shard_map(
        functools.partial(on_device, grid_of(mesh)),
        mesh=mesh,
        in_specs=(rows, matrix, vector) + (matrix,) * 7 + (vector,) + (matrix,) * 3 + (rows,),
        out_specs=(rows, rows, vector) + (matrix,) * 7 + (vector,) + (matrix,) * 3,
        check_vma=False,
    )
```

```python
import functools
import math

import jax
import jax.numpy as jnp
import numpy as np
from jax import lax
from jax.experimental import pallas as pl
from jax.experimental.pallas import tpu as pltpu
from jax.sharding import PartitionSpec as P

MESH = pl.DeviceIdType.MESH
D, H, DH, RQ, RK = 1024, 16, 64, 6, 2
PACKED = 896
DIMS, HEADS = 640, 128
BLOCK = 256
BACK = 512
NEG = -1e30
epsilon = 1e-06
theta_base = 10000.0
f32, bf16 = jnp.float32, jnp.bfloat16
NT = (((1,), (1,)), ((), ()))
NN = (((1,), (0,)), ((), ()))
TN = (((0,), (0,)), ((), ()))


def dot(a, b, dims=NN):
    return lax.dot_general(a, b, dims, preferred_element_type=f32)


def params(**kw):
    return pltpu.CompilerParams(vmem_limit_bytes=56 << 20, **kw)


def rope_tables(seq_len):
    half = DH // 2
    position = np.arange(seq_len, dtype=np.float32)
    inverse = np.exp(-math.log(theta_base) * 2.0 * np.arange(half, dtype=np.float32) / np.float32(2.0 * half)).astype(np.float32)
    angle = (position[:, None] * inverse[None, :]).astype(np.float32)
    cosine, sine = np.cos(angle), np.sin(angle)
    return (np.concatenate([cosine] * 4, 1), np.concatenate([-sine, sine] * 2, 1))


def spread_table():
    out = np.zeros((8, 2 * HEADS, H * DH), np.float32)
    for j in range(8):
        for h in range(H):
            out[j, [j * H + h, HEADS + j * H + h], h * DH:(h + 1) * DH] = 1.0
    return out.astype(jnp.bfloat16)


def low_lane(shape):
    return lax.rem(lax.broadcasted_iota(jnp.int32, shape, 1), 128) < 64


def first_half(shape):
    return lax.rem(lax.broadcasted_iota(jnp.int32, shape, 1), 64) < 32


def turn(x, cosine, sine):
    partner = jnp.where(first_half(x.shape), pltpu.roll(x, 96, 1), pltpu.roll(x, 32, 1))
    return x * cosine + partner * sine


def split_bf16(x):
    hi = x.astype(bf16)
    return jnp.concatenate([hi, (x - hi.astype(f32)).astype(bf16)], axis=1)


def twice(x, rank):
    rolled = pltpu.roll(x, 64, 1)
    low = low_lane(x.shape)
    return jnp.where(low, x, rolled) if rank % 2 == 0 else jnp.where(low, rolled, x)


def wide(x):
    return jnp.concatenate([x] * (H * DH // 128), axis=1)


def rms(x):
    return lax.rsqrt(jnp.mean(x * x, axis=-1, keepdims=True) + epsilon)


FACTORS = ((0, RQ, 0), (RQ, RK, 3), (0, RK, 4))


def factors_step(tokens, gain, weight, cosine, sine, spread, normed, factors, query, key, value):
    x = tokens[...].astype(f32)
    n = (x * rms(x) * gain).astype(bf16)
    normed[...] = n
    f = dot(n, weight)
    pairs = [f[:, 128 * i:128 * i + 128] for i in range(DIMS // 128)]
    pairs = [turn(p, cosine[...], sine[...]) if i < 4 else p for i, p in enumerate(pairs)]
    for i, p in enumerate(pairs):
        factors[:, 128 * i:128 * i + 128] = p
    factors[:, DIMS:] = f[:, DIMS:]
    heads_qk = split_bf16(f[:, DIMS:DIMS + HEADS])
    heads_v = split_bf16(f[:, DIMS + HEADS:])
    for out, heads, (at, ranks, pair), scale in zip(
        (query, key, value), (heads_qk, heads_qk, heads_v), FACTORS, (0.125, 1.0, 1.0)
    ):
        total = None
        for r in range(ranks):
            term = dot(heads, spread[at + r]) * wide(twice(pairs[pair + r // 2], r))
            total = term if total is None else total + term
        rounded = (total * (1.0 / ranks)).astype(bf16)
        rounded = rounded * jnp.asarray(scale, bf16) if scale != 1.0 else rounded
        for p, ref in enumerate(out):
            ref[...] = rounded[:, 128 * p:128 * p + 128]


def factors_kernel(tokens, gain, weight, cosine, sine, spread, normed, factors, query, key, value):
    outs = [[r.at[p] for p in range(H // 2)] for r in (query, key, value)]
    factors_step(tokens, gain[...], weight[...], cosine, sine, spread, normed, factors, *outs)


def make_factors(tokens, gain, weight, tables):
    cosine, sine, spread = tables
    seq = tokens.shape[0]
    row = lambda width: pl.BlockSpec((BLOCK, width), lambda i: (i, 0))
    whole = lambda a: pl.BlockSpec(a.shape, lambda i: (0,) * a.ndim)
    return pl.pallas_call(
        factors_kernel,
        grid=(seq // BLOCK,),
        out_shape=[
            jax.ShapeDtypeStruct((seq, D), bf16),
            jax.ShapeDtypeStruct((seq, PACKED), f32),
        ] + [jax.ShapeDtypeStruct((H // 2, seq, 128), bf16)] * 3,
        in_specs=[row(D), whole(gain), whole(weight), row(128), row(128), whole(spread)],
        out_specs=[row(D), row(PACKED)] + [pl.BlockSpec((H // 2, BLOCK, 128), lambda i: (0, i, 0))] * 3,
        compiler_params=params(),
        name="factors",
    )(tokens, gain, weight, cosine, sine, spread)


def allowed_t(doc_col, doc_row, k0, kn, q0, qn):
    same = doc_col[k0:k0 + kn, 0:1].astype(f32) == doc_row[:, q0:q0 + qn].astype(f32)
    if k0 + kn - 1 > q0:
        k_at = k0 + lax.broadcasted_iota(jnp.int32, (kn, qn), 0)
        q_at = q0 + lax.broadcasted_iota(jnp.int32, (kn, qn), 1)
        same = same & (k_at <= q_at)
    return same


def halves(x):
    low = low_lane(x.shape)
    zero = jnp.zeros_like(x)
    return jnp.where(low, x, zero), jnp.where(low, zero, x)


def attend_kernel(doc_col, doc_row, query, key, value, mixed, lse):
    seq = query.shape[0]
    v_half = halves(value[...])
    for q0 in range(0, seq, BLOCK):
        lo = max(0, q0 - BACK)
        kn = q0 + BLOCK - lo
        ok = allowed_t(doc_col, doc_row, lo, kn, q0, BLOCK)
        probs = []
        for h, q in enumerate(halves(query[q0:q0 + BLOCK, :])):
            s = jnp.where(ok, dot(key[lo:lo + kn, :], q, NT), NEG)
            top = jnp.max(s, axis=0, keepdims=True)
            e = jnp.exp(s - top)
            total = jnp.sum(e, axis=0, keepdims=True)
            probs.append((e * (1.0 / total)).astype(bf16))
            lse[0, h:h + 1, q0:q0 + BLOCK] = top + jnp.log(total)
        values = jnp.concatenate([v[lo:lo + kn] for v in v_half], axis=0)
        mixed[q0:q0 + BLOCK, :] = dot(jnp.concatenate(probs, axis=0), values, TN).astype(bf16)


def attend(doc_col, doc_row, query, key, value):
    pairs, seq, _ = query.shape
    whole = lambda a: pl.BlockSpec(a.shape, lambda i: (0,) * a.ndim)
    pair = pl.BlockSpec((seq, 128), lambda i: (0, i))
    return pl.pallas_call(
        lambda dc, dr, q, k, v, *outs: attend_kernel(dc, dr, q.at[0], k.at[0], v.at[0], *outs),
        grid=(pairs,),
        out_shape=[jax.ShapeDtypeStruct((seq, H * DH), bf16), jax.ShapeDtypeStruct((pairs, 2, seq), f32)],
        in_specs=[whole(doc_col), whole(doc_row)] + [pl.BlockSpec((1, seq, 128), lambda i: (i, 0, 0))] * 3,
        out_specs=[pair, pl.BlockSpec((1, 2, seq), lambda i: (i, 0, 0))],
        compiler_params=params(),
        name="attend",
    )(doc_col, doc_row, query, key, value)


def attend_back_kernel(doc_col, doc_row, query, key, value, grad, lse, g_query, g_key, g_value):
    seq = query.shape[0]
    k_half = halves(key[...])
    for q0 in range(0, seq, BLOCK):
        lo = max(0, q0 - BACK)
        kn = q0 + BLOCK - lo
        ok = allowed_t(doc_col, doc_row, lo, kn, q0, BLOCK)
        ps, ds = [], []
        q_half, g_half = halves(query[q0:q0 + BLOCK, :]), halves(grad[q0:q0 + BLOCK, :])
        for h in (0, 1):
            s = dot(key[lo:lo + kn, :], q_half[h], NT)
            p = jnp.where(ok, jnp.exp(s - lse[0, h:h + 1, q0:q0 + BLOCK]), 0.0)
            pd = p * dot(value[lo:lo + kn, :], g_half[h], NT)
            ps.append(p.astype(bf16))
            ds.append((pd - p * jnp.sum(pd, axis=0, keepdims=True)).astype(bf16))
        to_value = dot(jnp.concatenate(ps, 1), jnp.concatenate(g_half, 0))
        to_key = dot(jnp.concatenate(ds, 1), jnp.concatenate(q_half, 0))
        if q0 > lo:
            g_value[lo:q0, :] += to_value[:q0 - lo]
            g_key[lo:q0, :] += to_key[:q0 - lo]
        g_value[q0:q0 + BLOCK, :] = to_value[q0 - lo:]
        g_key[q0:q0 + BLOCK, :] = to_key[q0 - lo:]
        keys = jnp.concatenate([k[lo:lo + kn] for k in k_half], 0)
        g_query[q0:q0 + BLOCK, :] = dot(jnp.concatenate(ds, 0), keys, TN) * 0.125


def attend_back(doc_col, doc_row, query, key, value, grad, lse):
    pairs, seq, _ = query.shape
    whole = lambda a: pl.BlockSpec(a.shape, lambda i: (0,) * a.ndim)
    pair = pl.BlockSpec((seq, 128), lambda i: (0, i))
    return pl.pallas_call(
        lambda dc, dr, q, k, v, *rest: attend_back_kernel(dc, dr, q.at[0], k.at[0], v.at[0], *rest),
        grid=(pairs,),
        out_shape=[jax.ShapeDtypeStruct((seq, H * DH), f32)] * 3,
        in_specs=[whole(doc_col), whole(doc_row)] + [pl.BlockSpec((1, seq, 128), lambda i: (i, 0, 0))] * 3 + [pair, pl.BlockSpec((1, 2, seq), lambda i: (i, 0, 0))],
        out_specs=[pair] * 3,
        compiler_params=params(),
        name="attend_back",
    )(doc_col, doc_row, query, key, value, grad, lse)


def factors_back_step(cosine, sine, spread, factors, g_query, g_key, g_value, g_factors):
    pairs = [factors[:, 128 * i:128 * i + 128] for i in range(DIMS // 128)]
    heads_qk = split_bf16(factors[:, DIMS:DIMS + HEADS])
    heads_v = split_bf16(factors[:, DIMS + HEADS:])
    g_heads = [None, None]
    for grad, heads, which, (at, ranks, pair) in zip(
        (g_query, g_key, g_value), (heads_qk, heads_qk, heads_v), (0, 0, 1), FACTORS
    ):
        g = grad * (1.0 / ranks)
        folded = []
        for r in range(ranks):
            product = (g * wide(twice(pairs[pair + r // 2], r))).astype(bf16)
            part = dot(product, spread[at + r, :HEADS, :], NT)
            g_heads[which] = part if g_heads[which] is None else g_heads[which] + part
            full = g * dot(heads, spread[at + r])
            folded.append(sum(full[:, 128 * i:128 * i + 128] for i in range(H * DH // 128)))
        for r in range(0, ranks, 2):
            a, b = folded[r], folded[r + 1]
            low = low_lane(a.shape)
            mine = jnp.where(low, a, b)
            other = jnp.where(low, pltpu.roll(a, 64, 1), pltpu.roll(b, 64, 1))
            both = mine + other
            i = pair + r // 2
            if i < 4:
                both = turn(both, cosine[...], -sine[...])
            g_factors[:, 128 * i:128 * i + 128] = both.astype(bf16)
    g_factors[:, DIMS:DIMS + HEADS] = g_heads[0].astype(bf16)
    g_factors[:, DIMS + HEADS:] = g_heads[1].astype(bf16)


def tokens_back_step(step, tokens, gain, weight, g_factors, g_middle, g_tokens, g_gain):
    g_normed = dot(g_factors[...], weight, NT)
    x = tokens[...].astype(f32)
    r1 = rms(x)
    u = g_normed * gain
    part = jnp.sum(g_normed * x * r1, axis=0, keepdims=True)

    @pl.when(step == 0)
    def _():
        g_gain[...] = part

    @pl.when(step > 0)
    def _():
        g_gain[...] += part

    g_tokens[...] = (g_middle[...] + r1 * u - x * (r1 * r1 * r1 * jnp.mean(u * x, axis=-1, keepdims=True))).astype(bf16)


def factors_back_kernel(tokens, gain, weight, cosine, sine, spread, factors, g_query, g_key, g_value, g_middle,
                        g_factors, g_tokens, g_gain):
    factors_back_step(cosine, sine, spread, factors, g_query[...], g_key[...], g_value[...], g_factors)
    tokens_back_step(pl.program_id(0), tokens, gain[...], weight[...], g_factors, g_middle, g_tokens, g_gain)


def factors_back(tokens, gain, weight, tables, factors, g_query, g_key, g_value, g_middle):
    cosine, sine, spread = tables
    seq = tokens.shape[0]
    row = lambda width: pl.BlockSpec((BLOCK, width), lambda i: (i, 0))
    whole = lambda a: pl.BlockSpec(a.shape, lambda i: (0,) * a.ndim)
    return pl.pallas_call(
        factors_back_kernel,
        grid=(seq // BLOCK,),
        out_shape=[
            jax.ShapeDtypeStruct((seq, PACKED), bf16),
            jax.ShapeDtypeStruct((seq, D), bf16),
            jax.ShapeDtypeStruct((1, D), f32),
        ],
        in_specs=[row(D), whole(gain), whole(weight), row(128), row(128), whole(spread), row(PACKED)]
        + [row(H * DH)] * 3 + [row(D)],
        out_specs=[row(PACKED), row(D), pl.BlockSpec((1, D), lambda i: (0, 0))],
        compiler_params=params(),
        name="factors_back",
    )(tokens, gain, weight, cosine, sine, spread, factors, g_query, g_key, g_value, g_middle)

ANY = pl.BlockSpec(memory_space=pl.ANY)


def grid_of(mesh):
    nd, nf = mesh.shape["dp"], mesh.shape["fsdp"]
    nc = math.gcd(2, nd)
    nz = math.gcd(4, nf)
    return (nd // nc, nc, nz, nf // nz)


class Place:
    def __init__(self, dims):
        self.dims = dims
        ny, nc, nz, nx = dims
        dp, fs = lax.axis_index("dp"), lax.axis_index("fsdp")
        self.y, self.c = lax.div(dp, nc), lax.rem(dp, nc)
        self.z, self.x = lax.div(fs, nx), lax.rem(fs, nx)

    def at(self, axis, k):
        n = self.dims["yczx".index(axis)]
        return lax.rem(getattr(self, axis) + k + n, n)

    def device(self, axis=None, k=0):
        ny, nc, nz, nx = self.dims
        put = {a: getattr(self, a) for a in "yczx"}
        if axis is not None:
            put[axis] = self.at(axis, k)
        return (put["y"] * nc + put["c"], put["z"] * nx + put["x"])


def peers_of(dims):
    ny, nc, nz, nx = dims
    return [(a, k) for a, n in (("y", ny), ("c", nc), ("z", nz), ("x", nx)) for k in range(1, n)]


def enter(place):
    barrier = pltpu.get_barrier_semaphore()
    peers = peers_of(place.dims)
    for axis, k in peers:
        pl.semaphore_signal(barrier, inc=1, device_id=place.device(axis, k), device_id_type=MESH)
    pl.semaphore_wait(barrier, len(peers))


class Gather:
    def __init__(self, place, src, dst, sems, i):
        self.p, self.src, self.dst, self.i = place, src, dst, i
        self.local, self.zs, self.zr, self.as_, self.ar, self.bs, self.br, self.cs, self.cr = sems

    @staticmethod
    def sem_shapes(dims, n):
        ny, nc, nz, nx = dims
        dma = pltpu.SemaphoreType.DMA
        m = max(nx, ny) - 1
        one = lambda k: dma((n, max(1, k)))
        return [dma((n,)), one(nz - 1), one(nz - 1), one(m), one(m), one(m), one(m), one(nx + ny - 1), one(nx + ny - 1)]

    def copy(self, ref_src, ref_dst, send, recv, axis, k):
        return pltpu.make_async_remote_copy(
            src_ref=ref_src, dst_ref=ref_dst, send_sem=send, recv_sem=recv,
            device_id=self.p.device(axis, k), device_id_type=MESH,
        )

    def z_copies(self):
        p, i = self.p, self.i
        nz = p.dims[2]
        mine = self.dst.at[p.y, p.c, p.z, p.x]
        def one(k, back):
            if back:
                ref = self.dst.at[p.y, p.c, p.at("z", -k), p.x]
                return self.copy(ref, ref, self.zs.at[i, k - 1], self.zr.at[i, k - 1], "z", k)
            return self.copy(self.src, mine, self.zs.at[i, k - 1], self.zr.at[i, k - 1], "z", k)

        return [[functools.partial(one, k, back) for k in range(1, nz)] for back in (False, True)]

    def part(self, first, step, y, x, c):
        every = slice(None)
        if step == 0:
            return self.dst.at[y, c, :, x]
        return self.dst.at[y, c] if first == "x" else self.dst.at[:, c, :, x]

    def side_copies(self, first, step):
        p, i = self.p, self.i
        axis = first if step == 0 else {"x": "y", "y": "x"}[first]
        n = p.dims["yczx".index(axis)]
        s, r = ((self.as_, self.ar), (self.bs, self.br))[step]

        def one(k, back):
            y, x = p.y, p.x
            if back:
                y, x = (p.y, p.at("x", -k)) if axis == "x" else (p.at("y", -k), p.x)
            ref = self.part(first, step, y, x, p.c)
            return self.copy(ref, ref, s.at[i, k - 1], r.at[i, k - 1], axis, k)

        return [[functools.partial(one, k, back) for k in range(1, n)] for back in (False, True)]

    def core_copies(self, first, c):
        p, i = self.p, self.i
        second = {"x": "y", "y": "x"}[first]
        lists, j = [], 0
        for step, axis in ((0, None), (0, first), (1, second)):
            now = []
            count = 1 if axis is None else p.dims["yczx".index(axis)] - 1
            for k in range(1, count + 1):
                def one(axis=axis, step=step, k=k, j=j):
                    y = p.at("y", -k) if axis == "y" else p.y
                    x = p.at("x", -k) if axis == "x" else p.x
                    ref = self.part(first, step, y, x, c)
                    return self.copy(ref, ref, self.cs.at[i, j], self.cr.at[i, j], "c", 1)

                now.append(one)
                j += 1
            lists.append(now)
        return lists

    def start(self):
        p = self.p
        mine = self.dst.at[p.y, p.c, p.z, p.x]
        pltpu.make_async_copy(self.src, mine, self.local.at[self.i]).start()
        for copy in self.z_copies()[0]:
            copy().start()

    def by_core(self, body):
        if self.p.dims[1] == 1:
            body("x")
            return
        pl.when(self.p.c == 0)(lambda: body("x"))
        pl.when(self.p.c == 1)(lambda: body("y"))

    def after_z(self):
        p = self.p
        mine = self.dst.at[p.y, p.c, p.z, p.x]
        pltpu.make_async_copy(self.src, mine, self.local.at[self.i]).wait()
        for copy in self.z_copies()[1]:
            copy().wait_recv()

        def body(first):
            for copy in self.side_copies(first, 0)[0]:
                copy().start()
            if p.dims[1] > 1:
                for copy in self.core_copies(first, p.c)[0]:
                    copy().start()

        self.by_core(body)

    def after_first(self):
        p = self.p

        def body(first):
            for copy in self.side_copies(first, 0)[1]:
                copy().wait_recv()
            for copy in self.side_copies(first, 1)[0]:
                copy().start()
            if p.dims[1] > 1:
                for copy in self.core_copies(first, p.c)[1]:
                    copy().start()

        self.by_core(body)

    def after_second(self):
        p = self.p

        def body(first):
            for copy in self.side_copies(first, 1)[1]:
                copy().wait_recv()
            if p.dims[1] > 1:
                for copy in self.core_copies(first, p.c)[2]:
                    copy().start()

        self.by_core(body)

    def finish(self):
        p = self.p
        for copy in self.z_copies()[0]:
            copy().wait_send()

        def body(first):
            for step in (0, 1):
                for copy in self.side_copies(first, step)[0]:
                    copy().wait_send()
            if p.dims[1] > 1:
                for now in self.core_copies(first, p.c):
                    for copy in now:
                        copy().wait_send()
                other = {"x": "y", "y": "x"}[first]
                for now in self.core_copies(other, p.at("c", 1)):
                    for copy in now:
                        copy().wait_recv()

        self.by_core(body)

    def stages(self):
        return [self.start, self.after_z, self.after_first, self.after_second, self.finish]


def gather_kernel(dims, n, *refs):
    place = Place(dims)
    src, dst, sems = refs[:n], refs[n:2 * n], refs[2 * n:]
    enter(place)
    jobs = [Gather(place, src[i], dst[i], sems, i).stages() for i in range(n)]
    run_stages(jobs)


def gather(dims, arrays, collective_id):
    n = len(arrays)
    outs = pl.pallas_call(
        functools.partial(gather_kernel, dims, n),
        out_shape=[jax.ShapeDtypeStruct(dims + a.shape, a.dtype) for a in arrays],
        in_specs=[ANY] * n,
        out_specs=[ANY] * n,
        scratch_shapes=Gather.sem_shapes(dims, n),
        compiler_params=pltpu.CompilerParams(collective_id=collective_id, has_side_effects=True),
        name="gather_weights",
    )(*arrays)
    return [o.reshape((-1,) + a.shape[1:]) for o, a in zip(outs, arrays)]


class Scatter:
    def __init__(self, place, held, out, bufs, sems, i, src=None):
        self.p, self.src, self.out, self.i = place, src, out, i
        self.own, self.away = (held, None) if src is not None else (held.at[place.c], held.at[place.at("c", 1)])
        self.from_core, self.from_a, self.from_b, self.from_z = bufs
        self.local, self.cs, self.cr, self.as_, self.ar, self.bs, self.br, self.zs, self.zr = sems

    @staticmethod
    def sem_shapes(dims, n):
        ny, nc, nz, nx = dims
        dma = pltpu.SemaphoreType.DMA
        m = max(nx, ny, 2) - 1
        return [dma((n, nx))] * 3 + [dma((n, m))] * 4 + [dma((n, max(1, nz - 1)))] * 2

    @staticmethod
    def buf_shapes(dims, block, lead=()):
        ny, nc, nz, nx = dims
        m = max(nx, ny, 2)
        buf = lambda *s: pltpu.VMEM(lead + s + block, jnp.bfloat16)
        return [buf(ny, nx, nz), buf(m - 1, m, nz), buf(m - 1, nz), buf(max(1, nz - 1))]

    def copy(self, src, dst, send, recv, axis, k):
        return pltpu.make_async_remote_copy(
            src_ref=src, dst_ref=dst, send_sem=send, recv_sem=recv,
            device_id=self.p.device(axis, k), device_id_type=MESH,
        )

    def loads(self):
        p, i = self.p, self.i
        if self.src is None:
            return
        for x in range(p.dims[3]):
            yield lambda x=x: pltpu.make_async_copy(self.src.at[:, p.c, :, x], self.own.at[:, x], self.local.at[i, x])

    def core_copies(self):
        p, i = self.p, self.i
        if p.dims[1] == 1:
            return
        if self.src is None:
            yield lambda: self.copy(self.away, self.from_core, self.cs.at[i, 0], self.cr.at[i, 0], "c", 1)
            return
        for x in range(p.dims[3]):
            yield lambda x=x: self.copy(
                self.src.at[:, p.at("c", 1), :, x], self.from_core.at[:, x], self.cs.at[i, x], self.cr.at[i, x], "c", 1)

    def a_copies(self, first):
        p, i = self.p, self.i
        ny, nc, nz, nx = p.dims
        for k in range(1, ny if first == "y" else nx):
            def copy(k=k):
                if first == "y":
                    src, dst = self.own.at[p.at("y", k)], self.from_a.at[k - 1, pl.ds(0, nx)]
                else:
                    src, dst = self.own.at[:, p.at("x", k)], self.from_a.at[k - 1, pl.ds(0, ny)]
                return self.copy(src, dst, self.as_.at[i, k - 1], self.ar.at[i, k - 1], first, k)
            yield copy

    def b_copies(self, first):
        p, i = self.p, self.i
        ny, nc, nz, nx = p.dims
        second = {"x": "y", "y": "x"}[first]
        for k in range(1, ny if second == "y" else nx):
            def copy(k=k):
                src = self.own.at[p.at("y", k), p.x] if second == "y" else self.own.at[p.y, p.at("x", k)]
                return self.copy(src, self.from_b.at[k - 1], self.bs.at[i, k - 1], self.br.at[i, k - 1], second, k)
            yield copy

    def z_copies(self):
        p, i = self.p, self.i
        for k in range(1, p.dims[2]):
            yield lambda k=k: self.copy(
                self.own.at[p.y, p.x, p.at("z", k)], self.from_z.at[k - 1], self.zs.at[i, k - 1], self.zr.at[i, k - 1], "z", k)

    def by_core(self, body):
        if self.p.dims[1] == 1:
            body("y")
            return
        pl.when(self.p.c == 0)(lambda: body("y"))
        pl.when(self.p.c == 1)(lambda: body("x"))

    @staticmethod
    def add(into, terms):
        if len(terms) == 1:
            into[...] = into[...] + terms[0][...]
        elif terms:
            value = into[...].astype(jnp.float32)
            for term in terms:
                value = value + term[...].astype(jnp.float32)
            into[...] = value.astype(jnp.bfloat16)

    def start(self):
        for copy in self.core_copies():
            copy().start()
        for copy in self.loads():
            copy().start()

    def after_core(self):
        p = self.p
        ny, nc, nz, nx = p.dims
        for copy in self.loads():
            copy().wait()
        for copy in self.core_copies():
            copy().wait_recv()
        if nc > 1:
            def body(y, carry):
                self.add(self.own.at[y], [self.from_core.at[y]])
                return carry
            lax.fori_loop(0, ny, body, 0)

        def go(first):
            for copy in self.a_copies(first):
                copy().start()
        self.by_core(go)

    def after_a(self):
        p = self.p
        ny, nc, nz, nx = p.dims

        def go(first):
            for copy in self.a_copies(first):
                copy().wait_recv()
            n = ny if first == "y" else nx

            def body(j, carry):
                at = (p.y, j) if first == "y" else (j, p.x)
                self.add(self.own.at[at], [self.from_a.at[k, j] for k in range(n - 1)])
                return carry
            lax.fori_loop(0, nx if first == "y" else ny, body, 0)
            for copy in self.b_copies(first):
                copy().start()
        self.by_core(go)

    def after_b(self):
        p = self.p
        ny, nc, nz, nx = p.dims

        def go(first):
            for copy in self.b_copies(first):
                copy().wait_recv()
            n = nx if first == "y" else ny

            self.add(self.own.at[p.y, p.x], [self.from_b.at[k] for k in range(n - 1)])
        self.by_core(go)
        for copy in self.z_copies():
            copy().start()

    def after_z(self):
        p = self.p
        for copy in self.z_copies():
            copy().wait_recv()
        value = self.own[p.y, p.x, p.z].astype(jnp.float32)
        for k in range(p.dims[2] - 1):
            value = value + self.from_z[k].astype(jnp.float32)
        self.out[...] = value

    def finish(self):
        for copy in self.core_copies():
            copy().wait_send()

        def go(first):
            for copy in self.a_copies(first):
                copy().wait_send()
            for copy in self.b_copies(first):
                copy().wait_send()
        self.by_core(go)
        for copy in self.z_copies():
            copy().wait_send()

    def stages(self):
        return [self.start, self.after_core, self.after_a, self.after_b, self.after_z, self.finish]


def run_stages(jobs):
    n, depth = len(jobs), len(jobs[0])
    for t in range(n + depth - 1):
        for i in range(n):
            if 0 <= t - i < depth:
                jobs[i][t - i]()


def scatter_kernel(dims, n, *refs):
    place = Place(dims)
    src, out, rest = refs[:n], refs[n:2 * n], refs[2 * n:]
    bufs, sems = rest[:5 * n], rest[5 * n:]
    enter(place)
    run_stages([
        Scatter(place, bufs[5 * i], out[i], bufs[5 * i + 1:5 * i + 5], sems, i, src[i]).stages() for i in range(n)
    ])


def scatter(dims, arrays, collective_id):
    n = len(arrays)
    devices = math.prod(dims)
    blocks = [(a.shape[0] // devices,) + a.shape[1:] for a in arrays]
    shaped = [a.reshape(dims + b) for a, b in zip(arrays, blocks)]
    scratch = []
    ny, nc, nz, nx = dims
    for b in blocks:
        scratch += [pltpu.VMEM((ny, nx, nz) + b, jnp.bfloat16)] + Scatter.buf_shapes(dims, b)
    return pl.pallas_call(
        functools.partial(scatter_kernel, dims, n),
        out_shape=[jax.ShapeDtypeStruct(b, jnp.float32) for b in blocks],
        in_specs=[ANY] * n,
        out_specs=[pl.BlockSpec(memory_space=pltpu.VMEM)] * n,
        scratch_shapes=scratch + Scatter.sem_shapes(dims, n),
        compiler_params=pltpu.CompilerParams(
            collective_id=collective_id, has_side_effects=True, vmem_limit_bytes=56 << 20),
        name="scatter_gradients",
    )(*shaped)


READY = 3
SENT = 7
CHUNK = 256
SLOTS = 4
TOKENS = 512


def mlp_kernel(dims, chunks, ready, sent, *refs):
    (middle, normed, cot, gain, down, early, local_gu, output, g_middle, g_branch, g_gain, g_gate_up, g_down, late, gathered,
     normed_t, total, inner_s, grads_s, weights, held, from_core, from_a, from_b, from_z, load) = refs[:26]
    sems = refs[26:]
    ng = len(Gather.sem_shapes(dims, 1))
    place = Place(dims)
    j = pl.program_id(0)
    seq = normed.shape[0]
    block = local_gu.shape[1]
    ny, nc, nz, nx = dims

    def gather_at(m):
        return Gather(place, local_gu.at[m], gathered.at[m - ready], sems[:ng], m - ready)

    def scatter_at(m):
        bufs = [b.at[m] for b in (from_core, from_a, from_b, from_z)]
        return Scatter(place, held.at[lax.rem(m, SLOTS)], g_gate_up.at[m], bufs, sems[ng:], m)

    def do(m, first, last, body):
        if isinstance(m, int):
            if first <= m < last:
                body(m)
            return
        pl.when((m >= first) & (m < last))(lambda: body(m))

    def fetch(m, slot, start):
        def go(src):
            copy = pltpu.make_async_copy(src, weights.at[slot], load.at[slot])
            copy.start() if start else copy.wait()
        if start:
            pl.when(m < ready)(lambda: go(early.at[jnp.minimum(m, ready - 1)]))
            pl.when((m >= ready) & (m < chunks))(lambda: go(gathered.at[jnp.clip(m - ready, 0, chunks - ready - 1)]))
        else:
            go(early.at[0])

    def tick_a(j):
        do(j - 4, 0, sent, lambda m: scatter_at(m).after_z())
        do(j - 4, 0, sent, lambda m: scatter_at(m).finish())
        do(j + 1, ready, chunks, lambda m: gather_at(m).after_second())
        do(j + 2, ready, chunks, lambda m: gather_at(m).after_first())
        do(j + 5, ready + 2, chunks, lambda m: gather_at(m).start())

    def tick_b(j):
        do(j - 3, 0, sent, lambda m: scatter_at(m).after_b())
        do(j - 2, 0, sent, lambda m: scatter_at(m).after_a())
        do(j - 1, 0, sent, lambda m: scatter_at(m).after_core())
        do(j + 1, ready, chunks, lambda m: gather_at(m).finish())
        do(j + 3, ready, min(ready + 1, chunks), lambda m: gather_at(m).after_z())

    def tick_c(j):
        do(j, 0, sent, lambda m: scatter_at(m).start())
        do(j + 4, ready + 1, chunks, lambda m: gather_at(m).after_z())

    @pl.when(j == 0)
    def _():
        fetch(0, 0, True)
        enter(place)
        for m in range(ready, min(ready + 2, chunks)):
            gather_at(m).start()
        normed_t[...] = normed[...].T

    slot = lax.rem(j, 2)
    fetch(j, slot, False)
    w = weights.at[slot]
    down_weight = lambda: jnp.concatenate([down[n] for n in range(down.shape[0])], axis=1)
    weight = lambda: w[...].reshape(D, -1)

    def tokens_part(t):
        r = slice(t * TOKENS, (t + 1) * TOKENS)
        both = dot(normed[r, :], weight())
        gate, up = both[:, :CHUNK], both[:, CHUNK:]
        sig = jax.nn.sigmoid(gate)
        silu = gate * sig
        inner = (silu * up).astype(bf16)
        inner_s[r, :] = inner
        g_inner = dot(cot[r, :], down_weight(), NT)
        g_gate = (g_inner * up * sig * (1.0 + gate * (1.0 - sig))).astype(bf16)
        grads = jnp.concatenate([g_gate, (g_inner * silu).astype(bf16)], axis=1)
        grads_s[r, :] = grads
        out, back = dot(inner, down_weight()), dot(grads, weight(), NT)

        @pl.when(j == 0)
        def _():
            total[r, :] = out
            g_middle[r, :] = back

        @pl.when(j > 0)
        def _():
            total[r, :] += out
            g_middle[r, :] += back

    parts = seq // TOKENS
    tick_a(j)
    for t in range(parts):
        tokens_part(t)
        if t == parts // 2 - 1 or parts == 1:
            tick_b(j)
            fetch(j + 1, 1 - slot, True)
    g_weights = dot(normed_t[...], grads_s[...]).astype(bf16)

    @pl.when(j < sent)
    def _():
        at = held.at[lax.rem(j, SLOTS)]
        for y in range(ny):
            for c in range(nc):
                for z in range(nz):
                    for x in range(nx):
                        row = (((y * nc + c) * nz + z) * nx + x) * block
                        at[c, y, x, z] = g_weights[row:row + block]

    @pl.when(j >= sent)
    def _():
        late[0] = g_weights

    tick_c(j)
    g_down_now = dot(inner_s[...], cot[...], TN).astype(bf16)
    for n in range(g_down.shape[0]):
        g_down[n] = g_down_now[:, n * g_down.shape[2]:(n + 1) * g_down.shape[2]]

    @pl.when(j == chunks - 1)
    def _():
        for t in range(seq // 256):
            r = slice(t * 256, t * 256 + 256)
            m = middle[r, :]
            s = rms(m)
            output[r, :] = (m + total[r, :]).astype(bf16)
            g_normed = g_middle[r, :]
            u = g_normed * gain[1:2, :]
            g_now = cot[r, :].astype(f32) + s * u - m * (s * s * s * jnp.mean(u * m, axis=-1, keepdims=True))
            g_middle[r, :] = g_now
            g_branch[r, :] = g_now.astype(bf16)
            part = jnp.sum(g_normed * m * s, axis=0, keepdims=True)
            if t == 0:
                g_gain[...] = part
            else:
                g_gain[...] += part
        for k in range(max(0, sent + 4 - chunks)):
            tick_a(chunks + k)
            tick_b(chunks + k)
            tick_c(chunks + k)


def mlp(dims, middle, normed, cot, gain, down, early, local_gu, sent, collective_id):
    chunks, block, width = local_gu.shape
    ready = early.shape[0]
    seq = normed.shape[0]
    ny, nc, nz, nx = dims
    whole = lambda *s: pl.BlockSpec(s, lambda i: (0,) * len(s))
    vmem = lambda s, t: pltpu.VMEM(s, t)
    return pl.pallas_call(
        functools.partial(mlp_kernel, dims, chunks, ready, sent),
        grid=(chunks,),
        out_shape=[
            jax.ShapeDtypeStruct((seq, D), bf16),
            jax.ShapeDtypeStruct((seq, D), f32),
            jax.ShapeDtypeStruct((seq, D), bf16),
            jax.ShapeDtypeStruct((1, D), f32),
            jax.ShapeDtypeStruct((sent, block, width), f32),
            jax.ShapeDtypeStruct(down.shape, bf16),
            jax.ShapeDtypeStruct((chunks - sent, D, width), bf16),
            jax.ShapeDtypeStruct((chunks - ready,) + dims + (block, width), bf16),
        ],
        in_specs=[whole(seq, D), whole(seq, D), whole(seq, D), whole(8, D), pl.BlockSpec((down.shape[0], CHUNK, down.shape[2]), lambda i: (0, i, 0)), ANY,
                  pl.BlockSpec(local_gu.shape, lambda i: (0, 0, 0), pipeline_mode=pl.Buffered(1))],
        out_specs=[whole(seq, D)] * 3 + [whole(1, D), whole(sent, block, width),
                   pl.BlockSpec((down.shape[0], CHUNK, down.shape[2]), lambda i: (0, i, 0)),
                   pl.BlockSpec((1, D, width), lambda i: (jnp.maximum(i - sent, 0), 0, 0)), ANY],
        scratch_shapes=[
            vmem((D, seq), bf16), vmem((seq, D), f32), vmem((seq, CHUNK), bf16), vmem((seq, width), bf16),
            vmem((2,) + dims + (block, width), bf16), vmem((SLOTS, nc, ny, nx, nz, block, width), bf16),
        ] + Scatter.buf_shapes(dims, (block, width), (sent,)) + [pltpu.SemaphoreType.DMA((2,))]
        + Gather.sem_shapes(dims, chunks - ready) + Scatter.sem_shapes(dims, sent),
        compiler_params=pltpu.CompilerParams(
            collective_id=collective_id, has_side_effects=True, vmem_limit_bytes=62 << 20),
        name="mlp",
    )(middle, normed, cot, gain, down, early, local_gu)


STEPS = 4
AHEAD = 4
SPREAD = (8, 2 * HEADS, H * DH)
FB, FD, FG, BB, BD, BG = 1, 0.7, 2, 0, 0.35, 2
PAIRS = H // 2


def spread_ticks(ticks, slots, busy, drain):
    plan = [[] for _ in range(slots)]
    total = busy + drain * (len(ticks) - busy)
    at = 0.0
    for n, tick in enumerate(ticks):
        at += 1.0 if n < busy else drain
        plan[min(slots - 1, int(at * slots / total))].append(tick)
    return plan


def tick_list(jobs, gap=1):
    n, depth = len(jobs), len(jobs[0])
    return [[jobs[i][(t - i) // gap] for i in range(n) if 0 <= t - i < gap * depth and (t - i) % gap == 0]
            for t in range(n + gap * (depth - 1))]


def run_tick(tick):
    for stage in tick:
        stage()


def fill_spread(spread):
    row = lax.rem(lax.broadcasted_iota(jnp.int32, spread.shape[1:], 0), HEADS)
    offset = row - lax.div(lax.broadcasted_iota(jnp.int32, spread.shape[1:], 1), DH)
    for j in range(spread.shape[0]):
        spread[j] = jnp.where(offset == j * H, 1.0, 0.0).astype(bf16)


def windows(width, size):
    return [pl.ds(at, size) for at in range(0, width, size)]


def forward_kernel(dims, ready, *refs):
    (tokens, doc_row, cosine, sine, packed, w_out, w_down, gate_up,
     normed, factors, query, key, value, mixed, lse, gains, middle, normed_two, packed_all, out_all, down_all, early,
     weight, out_weight, doc_col, spread, load) = refs[:27]
    sems = refs[27:]
    place = Place(dims)
    step = pl.program_id(0)
    part = lambda src, dst, rows: (src.at[rows], dst.at[:, :, :, :, rows])
    first = [part(packed, packed_all, rows) for rows in windows(packed.shape[0], 16)]
    pairs = [(w_out, out_all)]
    pairs += [(w_down.at[n], down_all.at[n]) for n in range(w_down.shape[0])]
    pairs += [(gate_up.at[m], early.at[m]) for m in range(ready)]
    jobs = [Gather(place, s, d, sems, i).stages() for i, (s, d) in enumerate(first + pairs)]
    first, rest = jobs[:len(first)], jobs[len(first):]
    ticks = tick_list([job[1:] for job in rest], FG)
    for n, job in enumerate(rest[AHEAD:]):
        ticks[n].append(job[0])
    fetch_out = lambda: pltpu.make_async_copy(out_all, out_weight, load)

    @pl.when(step == 0)
    def _():
        doc_col[...] = jnp.broadcast_to(doc_row[...].astype(f32), (8, doc_row.shape[1])).T
        enter(place)
        for job in first + rest[:AHEAD]:
            job[0]()
        fill_spread(spread)
        for tick in tick_list([job[1:] for job in first]):
            run_tick(tick)
        copy = pltpu.make_async_copy(packed_all, weight, load)
        copy.start()
        copy.wait()
        w = weight[...].reshape(D, PACKED)
        gains[...] = w[:, DIMS + HEADS:].astype(f32).T[2 * H:2 * H + 8]

    @pl.when(step < STEPS)
    def _():
        rows = pl.ds(pl.multiple_of(jnp.minimum(step, STEPS - 1) * BLOCK, BLOCK), BLOCK)
        outs = [[r.at[p, rows] for p in range(PAIRS)] for r in (query, key, value)]
        factors_step(tokens, gains[0:1, :], weight[...].reshape(D, PACKED), cosine, sine, spread, normed, factors, *outs)

    @pl.when((step >= STEPS) & (step < STEPS + PAIRS))
    def _():
        p = jnp.clip(step - STEPS, 0, PAIRS - 1)
        cols = pl.ds(pl.multiple_of(p * 128, 128), 128)
        attend_kernel(doc_col, doc_row, query.at[p], key.at[p], value.at[p], mixed.at[:, cols], lse)

    pl.when(step == STEPS + PAIRS - 1)(lambda: fetch_out().start())
    pl.when(step == STEPS + PAIRS)(lambda: fetch_out().wait())

    @pl.when(step >= STEPS + PAIRS)
    def _():
        t = jnp.maximum(step - STEPS - PAIRS, 0)
        rows = pl.ds(pl.multiple_of(t * BLOCK, BLOCK), BLOCK)
        m = tokens[...].astype(f32) + dot(mixed[rows, :], out_weight[...].reshape(H * DH, D))
        middle[...] = m
        normed_two[...] = (m * rms(m) * gains[1:2, :]).astype(bf16)

    for at, todo in enumerate(spread_ticks(ticks, 2 * STEPS + PAIRS, len(rest) + FB, FD)):
        if todo:
            @pl.when(step == at)
            def _(todo=todo):
                for tick in todo:
                    run_tick(tick)


def forward(dims, tokens, doc_row, tables, packed, w_out, w_down, gate_up, ready, collective_id):
    cosine, sine = tables
    seq = tokens.shape[0]
    whole = lambda *s: pl.BlockSpec(s, lambda i: (0,) * len(s), pipeline_mode=pl.Buffered(1))
    kept = lambda *s: pl.BlockSpec(s, lambda i: (0,) * len(s))
    row = lambda width: pl.BlockSpec((BLOCK, width), lambda i: (jnp.minimum(i, STEPS - 1), 0))
    again = lambda i: jnp.maximum(i - STEPS - PAIRS, 0)
    after = lambda i: jnp.clip(i - STEPS, 0, PAIRS - 1)
    ends = pl.BlockSpec((BLOCK, D), lambda i: (jnp.where(i < STEPS, i, again(i)), 0))
    last = pl.BlockSpec((BLOCK, D), lambda i: (again(i), 0))
    full = lambda a: jax.ShapeDtypeStruct(dims + a.shape, a.dtype)
    jobs = packed.shape[0] // 16 + 1 + w_down.shape[0] + ready
    return pl.pallas_call(
        functools.partial(forward_kernel, dims, ready),
        grid=(2 * STEPS + PAIRS,),
        out_shape=[
            jax.ShapeDtypeStruct((seq, D), bf16),
            jax.ShapeDtypeStruct((seq, PACKED), f32),
        ] + [jax.ShapeDtypeStruct((PAIRS, seq, 128), bf16)] * 3 + [
            jax.ShapeDtypeStruct((seq, H * DH), bf16),
            jax.ShapeDtypeStruct((PAIRS, 2, seq), f32),
            jax.ShapeDtypeStruct((8, D), f32),
            jax.ShapeDtypeStruct((seq, D), f32), jax.ShapeDtypeStruct((seq, D), bf16),
            full(packed), full(w_out), jax.ShapeDtypeStruct(w_down.shape[:1] + dims + w_down.shape[1:], bf16),
            jax.ShapeDtypeStruct((ready,) + dims + gate_up.shape[1:], bf16),
        ],
        in_specs=[ends, whole(1, seq), row(128), row(128)] + [whole(*a.shape) for a in (packed, w_out, w_down, gate_up)],
        out_specs=[row(D), row(PACKED)] + [kept(PAIRS, seq, 128)] * 3 + [
            kept(seq, H * DH),
            pl.BlockSpec((1, 2, seq), lambda i: (after(i), 0, 0)),
            kept(8, D), last, last,
        ] + [ANY] * 4,
        scratch_shapes=[pltpu.VMEM(dims + packed.shape, bf16), pltpu.VMEM(dims + w_out.shape, bf16), pltpu.VMEM((seq, 8), f32), pltpu.VMEM(SPREAD, bf16), pltpu.SemaphoreType.DMA]
        + Gather.sem_shapes(dims, jobs),
        compiler_params=pltpu.CompilerParams(
            collective_id=collective_id, has_side_effects=True, vmem_limit_bytes=58 << 20),
        name="forward",
    )(tokens, doc_row, cosine, sine, packed, w_out, w_down, gate_up)


def backward_kernel(dims, *refs):
    (doc_row, query, key, value, w_out, lse, tokens, gain, packed_all, cosine, sine, factors, g_middle,
     normed, g_gain_two, g_down, mixed, g_branch, g_late) = refs[:19]
    g_tokens, down_out, out_out, late_out, reduced = refs[19:24]
    at = 24
    g_query, g_key, g_value, weight, g_factors, g_gain, doc_col, spread, two, grad, load = refs[at:at + 11]
    bufs = refs[at + 11:at + 11 + 20]
    sems = refs[at + 31:]
    place = Place(dims)
    ny, nc, nz, nx = dims
    step = pl.program_id(0)
    block = packed_all.shape[4]
    fetch = lambda: pltpu.make_async_copy(packed_all, weight, load.at[0])
    fetches = [lambda n=n, src=src: pltpu.make_async_copy(src, two.at[min(n, 1)], load.at[n + 1])
               for n, src in enumerate((g_branch, w_out, mixed))]

    def hold(held, value, start=0):
        for y in range(ny):
            for c in range(nc):
                for z in range(nz):
                    for x in range(nx):
                        row = (((y * nc + c) * nz + z) * nx + x) * block
                        for n in range(block // 16):
                            at = row + 16 * n - start
                            if 0 <= at < value.shape[0]:
                                held[n, c, y, x, z] = value[at:at + 16]

    jobs = []
    for n in range(down_out.shape[0]):
        own = [b.at[n] for b in bufs[5:10]]
        jobs.append(Scatter(place, own[0], down_out.at[n], own[1:], sems, len(jobs), g_down.at[n]))
    for n in range(late_out.shape[0]):
        own = [b.at[n] for b in bufs[15:20]]
        jobs.append(Scatter(place, own[0], late_out.at[n], own[1:], sems, len(jobs), g_late.at[n]))
    known = list(jobs)
    for n, rows in enumerate(windows(out_out.shape[0], 16)):
        own = [b.at[n] for b in bufs[0:5]]
        jobs.append(Scatter(place, own[0], out_out.at[rows], own[1:], sems, len(jobs)))
    last = []
    for n, rows in enumerate(windows(block, 16)):
        own = [b.at[n] for b in bufs[10:15]]
        last.append(Scatter(place, own[0], reduced.at[rows], own[1:], sems, len(jobs) + n))
    ticks = tick_list([job.stages()[1:] for job in jobs], BG)
    total = PAIRS + STEPS

    @pl.when(step == 0)
    def _():
        for copy in [fetch] + fetches[:2]:
            copy().start()
        doc_col[...] = jnp.broadcast_to(doc_row[...].astype(f32), (8, doc_row.shape[1])).T
        enter(place)
        for job in known:
            job.start()
        fill_spread(spread)
        fetches[0]().wait()
        fetches[1]().wait()
        for t in range(0, doc_row.shape[1], BLOCK):
            g_mixed = dot(two[0, t:t + BLOCK], two[1], NT).astype(bf16)
            for p in range(PAIRS):
                grad[p, t:t + BLOCK] = g_mixed[:, 128 * p:128 * p + 128]
        fetches[2]().start()
        fetches[2]().wait()
        for t in range(0, D, BLOCK):
            hold(bufs[0], dot(two[1, :, t:t + BLOCK], two[0], TN).astype(bf16), t)
        for job in jobs[len(known):]:
            job.start()

    @pl.when(step < PAIRS)
    def _():
        p = jnp.minimum(step, PAIRS - 1)
        attend_back_kernel(doc_col, doc_row, query.at[0], key.at[0], value.at[0], grad.at[p], lse,
                           g_query.at[p], g_key.at[p], g_value.at[p])

    pl.when(step == PAIRS)(lambda: fetch().wait())

    @pl.when(step >= PAIRS)
    def _():
        t = jnp.maximum(step - PAIRS, 0)
        rows = pl.ds(pl.multiple_of(t * BLOCK, BLOCK), BLOCK)
        grads = [jnp.concatenate([g[p, rows, :] for p in range(PAIRS)], axis=1) for g in (g_query, g_key, g_value)]
        factors_back_step(cosine, sine, spread, factors, *grads, g_factors.at[rows])
        tokens_back_step(t, tokens, gain[0:1, :], weight[...].reshape(D, PACKED), g_factors.at[rows], g_middle, g_tokens, g_gain)

    for n, todo in enumerate(spread_ticks(ticks, total, len(jobs) + BB, BD)):
        if todo:
            @pl.when(step == n)
            def _(todo=todo):
                for tick in todo:
                    run_tick(tick)

    @pl.when(step == total - 1)
    def _():
        g_weight = dot(normed[...], g_factors[...], TN)
        column = lambda row: jnp.broadcast_to(row, (128, D)).T
        lane = lax.broadcasted_iota(jnp.int32, (D, 128), 1)
        tail = g_weight[:, DIMS + HEADS:]
        tail = jnp.where(lane == 2 * H, column(g_gain[...]), jnp.where(lane == 2 * H + 1, column(g_gain_two[...]), tail))
        g_weight = jnp.concatenate([g_weight[:, :DIMS + HEADS], tail], axis=1).astype(bf16)
        hold(bufs[10], g_weight)
        for tick in tick_list([job.stages() for job in last]):
            run_tick(tick)


def backward(dims, doc_row, query, key, value, w_out, lse, tokens, gains, packed_all, tables, factors,
             g_middle, normed, g_gain_two, g_down, mixed, g_branch, g_late, collective_id):
    cosine, sine = tables
    seq = tokens.shape[0]
    ny, nc, nz, nx = dims
    block = packed_all.shape[4]
    whole = lambda *s: pl.BlockSpec(s, lambda i: (0,) * len(s), pipeline_mode=pl.Buffered(1))
    kept = lambda *s: pl.BlockSpec(s, lambda i: (0,) * len(s))
    before = lambda i: jnp.minimum(i, PAIRS - 1)
    after = lambda i: jnp.maximum(i - PAIRS, 0)
    pair = pl.BlockSpec((1, seq, 128), lambda i: (before(i), 0, 0))
    row = lambda width: pl.BlockSpec((seq // STEPS, width), lambda i: (after(i), 0))
    buffers = []
    groups = ((block // 16, (16, D)), (g_down.shape[0], g_down.shape[5:]), (block // 16, (16, PACKED)),
              (g_late.shape[0], g_late.shape[5:]))
    for n, (many, b) in enumerate(groups):
        held = (nc, ny, nx, nz) if n in (0, 2) else (ny, nx, nz)
        buffers += [pltpu.VMEM((many,) + held + b, bf16)] + Scatter.buf_shapes(dims, b, (many,))
    outs = [(g_down.shape[0],) + g_down.shape[5:], (block, D), (g_late.shape[0],) + g_late.shape[5:], (block, PACKED)]
    shape = lambda *s: jax.ShapeDtypeStruct(s, f32)
    return pl.pallas_call(
        functools.partial(backward_kernel, dims),
        grid=(PAIRS + STEPS,),
        out_shape=[jax.ShapeDtypeStruct((seq, D), bf16)] + [shape(*s) for s in outs],
        in_specs=[whole(1, seq), pair, pair, pair, ANY,
                  pl.BlockSpec((1, 2, seq), lambda i: (before(i), 0, 0)), row(D), whole(8, D), ANY, row(128), row(128),
                  row(PACKED), row(D), whole(seq, D), whole(1, D), ANY, ANY, ANY, ANY],
        out_specs=[row(D)] + [kept(*s) for s in outs],
        scratch_shapes=[pltpu.VMEM((PAIRS, seq, 128), f32)] * 3 + [
            pltpu.VMEM(dims + (block, PACKED), bf16), pltpu.VMEM((seq, PACKED), bf16), pltpu.VMEM((1, D), f32),
            pltpu.VMEM((seq, 8), f32), pltpu.VMEM(SPREAD, bf16), pltpu.VMEM((2, seq, D), bf16),
            pltpu.VMEM((PAIRS, seq, 128), bf16), pltpu.SemaphoreType.DMA((4,)),
        ] + buffers + Scatter.sem_shapes(dims, sum(many for many, _ in groups)),
        compiler_params=pltpu.CompilerParams(
            collective_id=collective_id, has_side_effects=True, vmem_limit_bytes=62 << 20),
        name="backward",
    )(doc_row, query, key, value, w_out, lse, tokens, gains, packed_all, cosine, sine, factors,
      g_middle, normed, g_gain_two, g_down, mixed, g_branch, g_late)


def pack_kernel(packed, down, gate_up, w_down, w_gate, w_up, *parts):
    at = 0
    for part in parts[:-2]:
        packed[:, at:at + part.shape[1]] = part[...]
        at += part.shape[1]
    rows = jnp.concatenate([gain[...].astype(f32) for gain in parts[-2:]] + [jnp.zeros((6, packed.shape[0]), f32)], axis=0)
    packed[:, at:at + 8] = rows.T.astype(bf16)
    packed[:, at + 8:] = jnp.zeros((packed.shape[0], PACKED - at - 8), bf16)
    for n in range(down.shape[0]):
        down[n] = w_down[:, n * CHUNK:(n + 1) * CHUNK]
    for n in range(gate_up.shape[0]):
        gate_up[n, :, :CHUNK] = w_gate[:, n * CHUNK:(n + 1) * CHUNK]
        gate_up[n, :, CHUNK:] = w_up[:, n * CHUNK:(n + 1) * CHUNK]


def pack(parts, gains, w_down, w_gate, w_up):
    block, hidden = w_gate.shape
    shape = lambda *s: jax.ShapeDtypeStruct(s, bf16)
    return pl.pallas_call(
        lambda *refs: pack_kernel(*refs[-3:], *refs[:-3]),
        out_shape=[shape(block, PACKED), shape(w_down.shape[1] // CHUNK, w_down.shape[0], CHUNK),
                   shape(hidden // CHUNK, block, 2 * CHUNK)],
        compiler_params=params(),
        name="pack",
    )(w_down, w_gate, w_up, *parts, *[g.reshape(1, block) for g in gains])


def unpack_kernel(widths, packed, down, sent, late, out, *refs):
    results, moved, outs, (held, sems) = refs[:2], refs[-4:-2], refs[2:-4], refs[-2:]
    *parts, gain_one, gain_two, w_down, w_gate, w_up, w_out = outs
    rows = windows(results[0].shape[0], 256)
    at = [(i, n, r) for i in (0, 1) for n, r in enumerate(rows)]
    loads = [lambda i=i, n=n, r=r: pltpu.make_async_copy(results[i].at[r], held.at[i, r], sems.at[0, i, n]) for i, n, r in at]
    stores = [lambda i=i, n=n, r=r: pltpu.make_async_copy(held.at[i, r], moved[i].at[r], sems.at[1, i, n]) for i, n, r in at]
    for load in loads:
        load().start()
    w_out[...] = out[...]
    at = 0
    for part, width in zip(parts, widths):
        part[...] = packed[:, at:at + width]
        at += width
    tail = packed[:, DIMS + HEADS:].T
    gain_one[...] = tail[at - DIMS - HEADS:at - DIMS - HEADS + 1]
    gain_two[...] = tail[at - DIMS - HEADS + 1:at - DIMS - HEADS + 2]
    for load, store in zip(loads, stores):
        load().wait()
        store().start()
    for n in range(down.shape[0]):
        w_down[:, n * CHUNK:(n + 1) * CHUNK] = down[n]
    for n in range(sent.shape[0] + late.shape[0]):
        both = sent[n] if n < sent.shape[0] else late[n - sent.shape[0]]
        w_gate[:, n * CHUNK:(n + 1) * CHUNK] = both[:, :CHUNK]
        w_up[:, n * CHUNK:(n + 1) * CHUNK] = both[:, CHUNK:]
    for store in stores:
        store().wait()


def unpack(widths, packed, down, sent, late, out, results):
    block = packed.shape[0]
    hidden = (sent.shape[0] + late.shape[0]) * CHUNK
    shape = lambda *s: jax.ShapeDtypeStruct(s, f32)
    vmem = pl.BlockSpec(memory_space=pltpu.VMEM)
    small = [shape(block, w) for w in widths] + [shape(1, block)] * 2
    small += [shape(down.shape[1], down.shape[0] * CHUNK)] + [shape(block, hidden)] * 2 + [shape(*out.shape)]
    *parts, gain_one, gain_two, w_down, w_gate, w_up, w_out, output, g_tokens = pl.pallas_call(
        functools.partial(unpack_kernel, widths),
        out_shape=small + [jax.ShapeDtypeStruct(r.shape, r.dtype) for r in results],
        in_specs=[vmem] * 5 + [ANY] * 2,
        out_specs=[vmem] * len(small) + [ANY] * 2,
        scratch_shapes=[pltpu.VMEM((2,) + results[0].shape, bf16), pltpu.SemaphoreType.DMA((2, 2, results[0].shape[0] // 256))],
        compiler_params=params(),
        name="unpack",
    )(packed, down, sent, late, out, *results)
    return parts, gain_one.reshape(block), gain_two.reshape(block), w_down, w_gate, w_up, w_out, output, g_tokens


def plain_mlp(middle, normed_two, cotangent, gain, gate_w, up_w, down_w):
    gate, up = dot(normed_two, gate_w), dot(normed_two, up_w)
    sig = jax.nn.sigmoid(gate)
    silu = gate * sig
    inner = (silu * up).astype(bf16)
    output = (middle + dot(inner, down_w)).astype(bf16)
    grad_inner = dot(cotangent, down_w, NT)
    grad_gate = (grad_inner * up * sig * (1.0 + gate * (1.0 - sig))).astype(bf16)
    grad_up = (grad_inner * silu).astype(bf16)
    grad_normed = dot(grad_gate, gate_w, NT) + dot(grad_up, up_w, NT)
    scale = rms(middle)
    gained = grad_normed * gain
    grad_middle = (
        cotangent.astype(f32)
        + scale * gained
        - middle * scale**3 * jnp.mean(gained * middle, axis=-1, keepdims=True)
    )
    grad_gain = jnp.sum(grad_normed * middle * scale, axis=0, keepdims=True)
    outer_sum = lambda left, right: dot(left, right, TN).astype(bf16)
    return (
        output, grad_middle, grad_gain,
        outer_sum(inner, cotangent), outer_sum(normed_two, grad_gate), outer_sum(normed_two, grad_up),
    )


def on_device(
    dims,
    tokens,
    doc_ids,
    norm_gain,
    w_query_heads,
    w_query_dims,
    w_key_heads,
    w_key_dims,
    w_value_heads,
    w_value_dims,
    w_output,
    mlp_gain,
    w_gate,
    w_up,
    w_down,
    out_grad,
):
    seq_len = tokens.shape[0] * tokens.shape[1]
    tables = tuple(jnp.asarray(t) for t in rope_tables(seq_len))
    parts = (w_query_dims, w_key_dims, w_value_dims, w_query_heads, w_key_heads, w_value_heads)
    edges = [0]
    for part in parts:
        edges.append(edges[-1] + part.shape[1])
    gains_at = edges[-1]
    inputs, cotangent = tokens.reshape(seq_len, D), out_grad.reshape(seq_len, D)
    doc_row, doc_col = doc_ids.reshape(1, seq_len), doc_ids.reshape(seq_len, 1)
    outer_sum = lambda left, right: dot(left, right, TN).astype(bf16)
    block = w_gate.shape[0]
    if block % 16 == 0 and w_gate.shape[1] % CHUNK == 0 and seq_len % TOKENS == 0:
        packed, down, gate_up = pack(parts, (norm_gain, mlp_gain), w_down, w_gate, w_up)
        (normed, factors, query, key, value, mixed, lse, gains, middle, normed_two,
         packed_w, output_w, down_w, early) = forward(
            dims, inputs, doc_row, tables, packed, w_output, down, gate_up, READY, 0
        )
        output_w = output_w.reshape(-1, D)
        output, grad_middle, grad_branch, grad_mlp_gain, gate_up_out, grad_down, grad_late, _ = mlp(
            dims, middle, normed_two, cotangent, gains, down_w.reshape(down_w.shape[0], -1, CHUNK), early, gate_up, SENT, 1
        )
        grad_tokens, down_out, output_out, late_out, packed_out = backward(
            dims, doc_row, query, key, value, output_w, lse, inputs,
            gains, packed_w, tables, factors, grad_middle, normed, grad_mlp_gain,
            grad_down.reshape(down_w.shape), mixed, grad_branch,
            grad_late.reshape((-1,) + dims + gate_up.shape[1:]), 2,
        )
        parts_out, gain_one_out, gain_two_out, down_out, gate_out, up_out, output_out, output, grad_tokens = unpack(
            [part.shape[1] for part in parts], packed_out, down_out, gate_up_out, late_out, output_out,
            (output, grad_tokens),
        )
        grads = [g for pair in zip(parts_out[3:], parts_out[:3]) for g in pair]
        return (
            output.reshape(tokens.shape), grad_tokens.reshape(tokens.shape), gain_one_out, *grads,
            output_out, gain_two_out, gate_out, up_out, down_out,
        )

    packed = jnp.concatenate(
        parts
        + (norm_gain[:, None], mlp_gain[:, None])
        + (jnp.zeros((norm_gain.shape[0], PACKED - gains_at - 2), bf16),),
        axis=1,
    )
    packed_w, output_w, gate_w, up_w, down_w = gather(
        dims, [packed, w_output, w_gate, w_up, w_down], 0
    )
    gain_one, gain_two = [packed_w[:, gains_at + i].astype(f32).reshape(1, D) for i in (0, 1)]
    tables += (jnp.asarray(spread_table()),)
    normed, factors, query, key, value = make_factors(inputs, gain_one, packed_w, tables)
    mixed, lse = attend(doc_col, doc_row, query, key, value)
    middle = inputs.astype(f32) + dot(mixed, output_w)
    normed_two = (middle * rms(middle) * gain_two).astype(bf16)
    output, grad_middle, grad_mlp_gain, *mlp_grads = plain_mlp(
        middle, normed_two, cotangent, gain_two, gate_w, up_w, down_w
    )
    grad_branch = grad_middle.astype(bf16)
    grad_mixed = dot(grad_branch, output_w, NT).astype(bf16)

    grad_query, grad_key, grad_value = attend_back(
        doc_col, doc_row, query, key, value, grad_mixed, lse
    )
    grad_factors, grad_tokens, grad_norm_gain = factors_back(
        inputs, gain_one, packed_w, tables, factors, grad_query, grad_key, grad_value, grad_middle
    )
    gains = jnp.stack([grad_norm_gain[0], grad_mlp_gain[0]], axis=1).astype(bf16)
    packed_grad = lax.dynamic_update_slice(outer_sum(normed, grad_factors), gains, (0, gains_at))
    *mlp_out, output_out, packed_out = scatter(
        dims, mlp_grads + [outer_sum(mixed, grad_branch), packed_grad], 2
    )
    down_out, gate_out, up_out = mlp_out
    dims_and_heads = [packed_out[:, lo:hi] for lo, hi in zip(edges, edges[1:])]
    grads = [g for pair in zip(dims_and_heads[3:], dims_and_heads[:3]) for g in pair]
    return (
        output.reshape(tokens.shape),
        grad_tokens.reshape(tokens.shape),
        packed_out[:, gains_at],
        *grads,
        output_out,
        packed_out[:, gains_at + 1],
        gate_out,
        up_out,
        down_out,
    )


def solution(mesh):
    rows, matrix, vector = P(("dp", "fsdp"), None, None), P(("dp", "fsdp"), None), P(("dp", "fsdp"))
    return jax.shard_map(
        functools.partial(on_device, grid_of(mesh)),
        mesh=mesh,
        in_specs=(rows, matrix, vector) + (matrix,) * 7 + (vector,) + (matrix,) * 3 + (rows,),
        out_specs=(rows, rows, vector) + (matrix,) * 7 + (vector,) + (matrix,) * 3,
        check_vma=False,
    )
```
